32 devices in a mesh: fsdp: 2 (over core), ctx: 16 (over z, y, x).
Axes of the slice: x: 2, y: 2, z: 4, core: 2. Of those that a mesh axis runs over, the one named last changes fastest.
Arguments:
- inputs: bfloat16 [4, 2048, 1024], P('fsdp', 'ctx'), may hold values from -6 to 6
- lengths: int32 [4], P('fsdp'), may hold values from 512 to 2048, as said below
- w_query: bfloat16 [1024, 1024], P(('fsdp', 'ctx')), may hold values from -0.375 to 0.375
- b_query: bfloat16 [1024], P(('fsdp', 'ctx')), may hold values from -3 to 3
- w_key: bfloat16 [1024, 1024], P(('fsdp', 'ctx')), may hold values from -0.1875 to 0.1875
- w_value: bfloat16 [1024, 1024], P(('fsdp', 'ctx')), may hold values from -0.1875 to 0.1875
- b_value: bfloat16 [1024], P(('fsdp', 'ctx')), may hold values from -3 to 3
- w_out: bfloat16 [1024, 1024], P(('fsdp', 'ctx')), may hold values from -1.5 to 1.5
- b_out: bfloat16 [1024], P(('fsdp', 'ctx')), may hold values from -3 to 3
- first_gain: bfloat16 [1024], P(('fsdp', 'ctx')), may hold values from 0.099609375 to 1.8984375
- first_shift: bfloat16 [1024], P(('fsdp', 'ctx')), may hold values from -3 to 3
- w_expand: bfloat16 [1024, 4096], P(('fsdp', 'ctx')), may hold values from -0.1875 to 0.1875
- b_expand: bfloat16 [4096], P(('fsdp', 'ctx')), may hold values from -3 to 3
- w_reduce: bfloat16 [4096, 1024], P(('fsdp', 'ctx')), may hold values from -0.125 to 0.125
- b_reduce: bfloat16 [1024], P(('fsdp', 'ctx')), may hold values from -3 to 3
- second_gain: bfloat16 [1024], P(('fsdp', 'ctx')), may hold values from 0.099609375 to 1.8984375
- second_shift: bfloat16 [1024], P(('fsdp', 'ctx')), may hold values from -3 to 3
- cotangent: bfloat16 [4, 2048, 1024], P('fsdp', 'ctx'), may hold values from -6 to 6
Outputs:
- layer_out: bfloat16 [4, 2048, 1024], P('fsdp', 'ctx')
- input_grad: float32 [4, 2048, 1024], P('fsdp', 'ctx')
- w_query_grad: float32 [1024, 1024], P(('fsdp', 'ctx'))
- b_query_grad: float32 [1024], P(('fsdp', 'ctx'))
- w_key_grad: float32 [1024, 1024], P(('fsdp', 'ctx'))
- w_value_grad: float32 [1024, 1024], P(('fsdp', 'ctx'))
- b_value_grad: float32 [1024], P(('fsdp', 'ctx'))
- w_out_grad: float32 [1024, 1024], P(('fsdp', 'ctx'))
- b_out_grad: float32 [1024], P(('fsdp', 'ctx'))
- first_gain_grad: float32 [1024], P(('fsdp', 'ctx'))
- first_shift_grad: float32 [1024], P(('fsdp', 'ctx'))
- w_expand_grad: float32 [1024, 4096], P(('fsdp', 'ctx'))
- b_expand_grad: float32 [4096], P(('fsdp', 'ctx'))
- w_reduce_grad: float32 [4096, 1024], P(('fsdp', 'ctx'))
- b_reduce_grad: float32 [1024], P(('fsdp', 'ctx'))
- second_gain_grad: float32 [1024], P(('fsdp', 'ctx'))
- second_shift_grad: float32 [1024], P(('fsdp', 'ctx'))
The draws below stay inside these ranges and needn't reach their ends.
Inputs may be any that keep to these rules, and one draw needn't show every extreme that they name: `lengths`: valid length of each sequence; positions from it on are padding. Exactly one sequence has 2048 valid positions.
All inputs are finite; a program needn't handle non-finite values.
Results may differ from the reference program's by a relative error of at most 0.029.
Values may be sent and summed in bfloat16 or wider, within the bound.
A program may use at most 256 MiB of HBM per device.

```python
import math
import jax
import jax.numpy as jnp
from jax import lax

D = 1024
HEADS = 16
HEAD_DIM = 64
FF = 4096
LEN = 2048
SEQS = 4


def draw_lengths(key, part):
    base_key, pick_key = jax.random.split(key, 2)
    drawn = jax.random.randint(base_key, (SEQS,), LEN // 4, LEN)
    longest = jax.random.randint(pick_key, (), 0, SEQS)
    places = jnp.arange(SEQS)
    drawn = jnp.where(places == longest, LEN, drawn)
    return drawn.astype(jnp.int32)


def shard_levels(key, dims, cuts, smallest, high):
    def one(dim, blocks):
        draws = jax.random.uniform(jax.random.fold_in(jax.random.fold_in(key, 6), dim), (blocks,), jnp.float32, smallest / len(cuts), high / len(cuts))
        return jnp.repeat(jnp.exp(draws), dims[dim] // blocks).reshape((-1,) + (1,) * (len(dims) - dim - 1))

    loudness = one(*cuts[0])
    for cut in cuts[1:]:
        loudness = loudness * one(*cut)
    return loudness


def scatter_about(stream_key, dims, deviation, reach, cuts=(), kind=jnp.bfloat16):
    values = jax.random.normal(stream_key, dims, jnp.float32) * deviation
    if len(cuts) > 0:
        values = shard_levels(stream_key, dims, cuts, -0.22, 0.18) * values
    return jnp.clip(values, min=-reach, max=reach).astype(kind)


def setup_inputs(seed: int = 0) -> dict:
    key_list = jax.random.split(jax.random.key(seed), 19)
    return {
        "inputs": scatter_about(key_list[0], (SEQS, LEN, D), 1.0, 6.0, ((0, 2), (1, 16))),
        "lengths": draw_lengths(jax.random.fold_in(key_list[18], 71), 0),
        "w_query": scatter_about(key_list[2], (D, D), (D // 4) ** -0.5, 0.375, ((0, 32),)),
        "b_query": scatter_about(key_list[3], (D,), 0.5, 3.0, ((0, 32),)),
        "w_key": scatter_about(key_list[4], (D, D), D ** -0.5, 0.1875, ((0, 32),)),
        "w_value": scatter_about(key_list[5], (D, D), D ** -0.5, 0.1875, ((0, 32),)),
        "b_value": scatter_about(key_list[6], (D,), 0.5, 3.0, ((0, 32),)),
        "w_out": scatter_about(key_list[7], (D, D), (D // 64) ** -0.5, 1.5, ((0, 32),)),
        "b_out": scatter_about(key_list[8], (D,), 0.5, 3.0, ((0, 32),)),
        "first_gain": jnp.clip(1.0 + 0.18 * jax.random.normal(key_list[9], (D,), jnp.float32), 0.099609375, 1.8984375).astype(jnp.bfloat16),
        "first_shift": scatter_about(key_list[10], (D,), 0.5, 3.0, ((0, 32),)),
        "w_expand": scatter_about(key_list[11], (D, FF), D ** -0.5, 0.1875, ((0, 32),)),
        "b_expand": scatter_about(key_list[12], (FF,), 0.5, 3.0, ((0, 32),)),
        "w_reduce": scatter_about(key_list[13], (FF, D), (FF // 2) ** -0.5, 0.125, ((0, 32),)),
        "b_reduce": scatter_about(key_list[14], (D,), 0.5, 3.0, ((0, 32),)),
        "second_gain": jnp.clip(1.0 + 0.18 * jax.random.normal(key_list[15], (D,), jnp.float32), 0.099609375, 1.8984375).astype(jnp.bfloat16),
        "second_shift": scatter_about(key_list[16], (D,), 0.5, 3.0, ((0, 32),)),
        "cotangent": scatter_about(key_list[17], (SEQS, LEN, D), 1.0, 6.0, ((0, 2), (1, 16))),
    }


@jax.custom_vjp
def low(v):
    return lax.optimization_barrier(v.astype(jnp.bfloat16)).astype(jnp.float32)

@jax.custom_vjp
def low_back(v):
    return v

def low_keep(v):
    return (low(v), None)

def low_pass(kept, grad):
    return (grad,)

def back_keep(v):
    return (v, None)

def back_low(kept, grad):
    return (low(grad),)
low.defvjp(low_keep, low_pass)
low_back.defvjp(back_keep, back_low)
highest = lax.Precision.HIGHEST
masked_score = -1e+30
epsilon = 1e-05

def layer_norm(rows_in, gain, shift):
    center = rows_in - lax.optimization_barrier(jnp.mean(rows_in, -1, keepdims=True))
    spread = lax.optimization_barrier(jnp.mean(center * center, -1, keepdims=True))
    return center * lax.rsqrt(spread + epsilon) * gain + shift

def product(left, right):
    return jnp.dot(left, right, precision=highest, preferred_element_type=jnp.float32)

def both_ways(value):
    return low(low_back(value))

def sequence_layer(params, seq_inputs, seq_length):
    full_query, bias_query, full_key, full_value, bias_value, full_out, bias_out, gain_first, shift_first, full_expand, bias_expand, full_reduce, bias_reduce, gain_second, shift_second = params
    total_rows = seq_inputs.shape[0]
    key_valid = jnp.arange(total_rows) < seq_length
    score_scale = HEAD_DIM ** (-0.5)
    queries = both_ways(product(seq_inputs, full_query) + bias_query)
    key_rows = both_ways(product(seq_inputs, full_key))
    value_rows = both_ways(product(seq_inputs, full_value) + bias_value)
    key_heads = key_rows.reshape(total_rows, HEADS, HEAD_DIM)
    value_heads = value_rows.reshape(total_rows, HEADS, HEAD_DIM)
    block_width = math.gcd(total_rows, 512)

    def query_block(block_queries):
        scores = low_back(jnp.einsum('qhd,khd->hqk', block_queries, key_heads, precision=highest) * score_scale)
        scores = jnp.where(key_valid[None, None, :], scores, masked_score)
        row_top = lax.optimization_barrier(jnp.max(scores, -1, keepdims=True))
        exponents = jnp.where(key_valid[None, None, :], jnp.exp(scores - row_top), 0.0)
        probabilities = exponents / lax.optimization_barrier(jnp.sum(exponents, -1, keepdims=True))
        return jnp.einsum('hqk,khd->qhd', low(probabilities), value_heads, precision=highest)
    query_blocks = queries.reshape(total_rows // block_width, block_width, HEADS, HEAD_DIM)
    context = lax.map(jax.checkpoint(query_block), query_blocks).reshape(total_rows, HEADS * HEAD_DIM)
    context = both_ways(context)
    attended = low_back(product(context, full_out) + bias_out)
    normed = layer_norm(seq_inputs + attended, gain_first, shift_first)
    expanded = low_back(product(low(normed), full_expand) + bias_expand)
    activated = low(jax.nn.gelu(expanded, approximate=False))
    reduced = low_back(product(activated, full_reduce) + bias_reduce)
    final_rows = layer_norm(normed + reduced, gain_second, shift_second)
    return final_rows * key_valid[:, None].astype(final_rows.dtype)

def reference(inputs, lengths, w_query, b_query, w_key, w_value, b_value, w_out, b_out, first_gain, first_shift, w_expand, b_expand, w_reduce, b_reduce, second_gain, second_shift, cotangent):
    params = tuple((weight.astype(jnp.float32) for weight in (w_query, b_query, w_key, w_value, b_value, w_out, b_out, first_gain, first_shift, w_expand, b_expand, w_reduce, b_reduce, second_gain, second_shift)))
    start_rows = inputs.astype(jnp.float32)

    def whole_layer(batch_data, weight_set):

        def one_sequence(seq_item):
            return jax.checkpoint(sequence_layer)(weight_set, seq_item[0], seq_item[1])
        return lax.map(one_sequence, (batch_data, lengths))
    result, pullback = jax.vjp(whole_layer, start_rows, params)
    input_grad, weight_grads = pullback(cotangent.astype(jnp.float32))
    return (result.astype(jnp.bfloat16), input_grad, weight_grads[0], weight_grads[1], weight_grads[2], weight_grads[3], weight_grads[4], weight_grads[5], weight_grads[6], weight_grads[7], weight_grads[8], weight_grads[9], weight_grads[10], weight_grads[11], weight_grads[12], weight_grads[13], weight_grads[14])
```

```python
from functools import partial
import math

import jax
import jax.numpy as jnp
from jax import lax
from jax.experimental import pallas as pl
from jax.experimental.pallas import tpu as pltpu
from jax.sharding import PartitionSpec as P

HEADS = 16


epsilon = 1e-05
masked_score = -1e30


def layer_norm(rows_in, gain, shift):
    center = rows_in - jnp.mean(rows_in, -1, keepdims=True)
    spread = jnp.mean(center * center, -1, keepdims=True)
    return center * lax.rsqrt(spread + epsilon) * gain + shift


def product(left, right):
    return jnp.dot(left, right, preferred_element_type=jnp.float32)


def outer_sum(left, right):
    return jnp.einsum("rd,re->de", left, right, preferred_element_type=jnp.float32)


def back_product(grad_rows, weight):
    return jnp.einsum("re,de->rd", grad_rows, weight, preferred_element_type=jnp.float32)


def over_blocks(step_fn, carry_state, pair_rows):
    key_count = pair_rows.shape[1]
    block_width = math.gcd(key_count, 512)

    def turn(turn_index, inner_state):
        block_pairs = lax.dynamic_slice_in_dim(pair_rows, turn_index * block_width, block_width, 1)
        return step_fn(inner_state, block_pairs, turn_index * block_width)

    return lax.fori_loop(0, key_count // block_width, turn, carry_state)


def general_shards(
    inputs,
    lengths,
    w_query,
    b_query,
    w_key,
    w_value,
    b_value,
    w_out,
    b_out,
    first_gain,
    first_shift,
    w_expand,
    b_expand,
    w_reduce,
    b_reduce,
    second_gain,
    second_shift,
    cotangent,
):
    gathered = (
        lax.all_gather(w_query, ("fsdp", "ctx"), axis=0, tiled=True),
        lax.all_gather(b_query, ("fsdp", "ctx"), axis=0, tiled=True),
        lax.all_gather(w_key, ("fsdp", "ctx"), axis=0, tiled=True),
        lax.all_gather(w_value, ("fsdp", "ctx"), axis=0, tiled=True),
        lax.all_gather(b_value, ("fsdp", "ctx"), axis=0, tiled=True),
        lax.all_gather(w_out, ("fsdp", "ctx"), axis=0, tiled=True),
        lax.all_gather(b_out, ("fsdp", "ctx"), axis=0, tiled=True),
        lax.all_gather(first_gain, ("fsdp", "ctx"), axis=0, tiled=True),
        lax.all_gather(first_shift, ("fsdp", "ctx"), axis=0, tiled=True),
        lax.all_gather(w_expand, ("fsdp", "ctx"), axis=0, tiled=True),
        lax.all_gather(b_expand, ("fsdp", "ctx"), axis=0, tiled=True),
        lax.all_gather(w_reduce, ("fsdp", "ctx"), axis=0, tiled=True),
        lax.all_gather(b_reduce, ("fsdp", "ctx"), axis=0, tiled=True),
        lax.all_gather(second_gain, ("fsdp", "ctx"), axis=0, tiled=True),
        lax.all_gather(second_shift, ("fsdp", "ctx"), axis=0, tiled=True),
    )
    (
        full_query,
        bias_query,
        full_key,
        full_value,
        bias_value,
        full_out,
        bias_out,
        gain_first,
        shift_first,
        full_expand,
        bias_expand,
        full_reduce,
        bias_reduce,
        gain_second,
        shift_second,
    ) = gathered
    seq_count, block_rows, model_width = inputs.shape
    total_rows = seq_count * block_rows
    head_size = model_width // HEADS
    score_scale = head_size ** (-0.5)
    own_first = lax.axis_index("ctx") * block_rows
    positions = own_first + jnp.arange(block_rows, dtype=jnp.int32)
    valid_rows = (positions[None, :] < lengths[:, None]).astype(jnp.float32).reshape(total_rows, 1)
    flat_rows = inputs.reshape(total_rows, model_width)
    queries = (product(flat_rows, full_query) + bias_query.astype(jnp.float32)).astype(jnp.bfloat16)
    key_rows = product(flat_rows, full_key).astype(jnp.bfloat16)
    value_rows = (product(flat_rows, full_value) + bias_value.astype(jnp.float32)).astype(
        jnp.bfloat16
    )
    query_heads = queries.reshape(seq_count, block_rows, HEADS, head_size)
    local_pairs = jnp.concatenate([key_rows, value_rows], -1).reshape(
        seq_count, block_rows, 2 * model_width
    )

    def key_allowed(first_row, key_count):
        return ((first_row + jnp.arange(key_count, dtype=jnp.int32))[None, :] < lengths[:, None])[
            :, None, None, :
        ]

    def split_pairs(block_pairs):
        key_count = block_pairs.shape[1]
        key_heads = block_pairs[:, :, :model_width].reshape(seq_count, key_count, HEADS, head_size)
        value_heads = block_pairs[:, :, model_width:].reshape(
            seq_count, key_count, HEADS, head_size
        )
        return (key_heads, value_heads, key_count)

    def forward_step(carry_state, block_pairs, first_row):
        running_max, running_sum, running_acc = carry_state
        key_heads, value_heads, key_count = split_pairs(block_pairs)
        allowed = key_allowed(first_row, key_count)
        scores = (
            jnp.einsum(
                "sqhd,skhd->shqk", query_heads, key_heads, preferred_element_type=jnp.float32
            )
            * score_scale
        )
        scores = jnp.where(allowed, scores, masked_score)
        new_max = jnp.maximum(running_max, jnp.max(scores, -1))
        factor = jnp.exp(running_max - new_max)
        exponents = jnp.where(allowed, jnp.exp(scores - new_max[..., None]), 0.0)
        new_sum = running_sum * factor + jnp.sum(exponents, -1)
        update = jnp.einsum(
            "shqk,skhd->sqhd",
            exponents.astype(jnp.bfloat16),
            value_heads,
            preferred_element_type=jnp.float32,
        )
        new_acc = running_acc * jnp.transpose(factor, (0, 2, 1))[..., None] + update
        return (new_max, new_sum, new_acc)

    start_state = (
        jnp.full((seq_count, HEADS, block_rows), masked_score, jnp.float32),
        jnp.zeros((seq_count, HEADS, block_rows), jnp.float32),
        jnp.zeros((seq_count, block_rows, HEADS, head_size), jnp.float32),
    )
    running_max, running_sum, running_acc = over_blocks(
        forward_step, start_state, lax.all_gather(local_pairs, "ctx", axis=1, tiled=True)
    )
    context_full = running_acc / jnp.transpose(running_sum, (0, 2, 1))[..., None]
    log_total = running_max + jnp.log(running_sum)
    context = context_full.reshape(total_rows, model_width).astype(jnp.bfloat16)
    attended = product(context, full_out) + bias_out.astype(jnp.float32)
    residual = flat_rows.astype(jnp.float32) + attended
    normed, first_pull = jax.vjp(
        layer_norm, residual, gain_first.astype(jnp.float32), shift_first.astype(jnp.float32)
    )
    normed_low = normed.astype(jnp.bfloat16)
    expanded = product(normed_low, full_expand) + bias_expand.astype(jnp.float32)
    activated, gelu_pull = jax.vjp(partial(jax.nn.gelu, approximate=False), expanded)
    activated_low = activated.astype(jnp.bfloat16)
    reduced = product(activated_low, full_reduce) + bias_reduce.astype(jnp.float32)
    final_rows, second_pull = jax.vjp(
        layer_norm,
        normed + reduced,
        gain_second.astype(jnp.float32),
        shift_second.astype(jnp.float32),
    )
    layer_out = (final_rows * valid_rows).astype(jnp.bfloat16).reshape(inputs.shape)
    d_output = cotangent.reshape(total_rows, model_width).astype(jnp.float32) * valid_rows
    d_second, second_gain_grad, second_shift_grad = second_pull(d_output)
    d_reduced = d_second.astype(jnp.bfloat16)
    reduce_grad = outer_sum(activated_low, d_reduced)
    reduce_bias_grad = jnp.sum(d_reduced.astype(jnp.float32), 0)
    (d_expanded_full,) = gelu_pull(back_product(d_reduced, full_reduce))
    d_expanded = d_expanded_full.astype(jnp.bfloat16)
    expand_grad = outer_sum(normed_low, d_expanded)
    expand_bias_grad = jnp.sum(d_expanded.astype(jnp.float32), 0)
    d_normed = d_second + back_product(d_expanded, full_expand)
    d_first, first_gain_grad, first_shift_grad = first_pull(d_normed)
    d_attended = d_first.astype(jnp.bfloat16)
    out_grad = outer_sum(context, d_attended)
    out_bias_grad = jnp.sum(d_attended.astype(jnp.float32), 0)
    d_context = back_product(d_attended, full_out).astype(jnp.bfloat16)
    d_context_heads = d_context.reshape(seq_count, block_rows, HEADS, head_size)
    delta = jnp.transpose(
        jnp.sum(d_context_heads.astype(jnp.float32) * context_full, -1), (0, 2, 1)
    )
    whole_length = block_rows * lax.axis_size("ctx")

    def score_grads(key_heads, value_heads, allowed):
        scores = (
            jnp.einsum(
                "sqhd,skhd->shqk", query_heads, key_heads, preferred_element_type=jnp.float32
            )
            * score_scale
        )
        probabilities = jnp.where(allowed, jnp.exp(scores - log_total[..., None]), 0.0)
        d_probs = jnp.einsum(
            "sqhd,skhd->shqk", d_context_heads, value_heads, preferred_element_type=jnp.float32
        )
        d_scores = (probabilities * (d_probs - delta[..., None])).astype(jnp.bfloat16)
        return (probabilities, d_scores)

    def backward_step(carry_state, block_pairs, first_row):
        grad_query, grad_pairs = carry_state
        key_heads, value_heads, key_count = split_pairs(block_pairs)
        probabilities, d_scores = score_grads(
            key_heads, value_heads, key_allowed(first_row, key_count)
        )
        grad_query = (
            grad_query
            + jnp.einsum("shqk,skhd->sqhd", d_scores, key_heads, preferred_element_type=jnp.float32)
            * score_scale
        )
        key_part = (
            jnp.einsum("shqk,sqhd->skhd", d_scores, query_heads, preferred_element_type=jnp.float32)
            * score_scale
        )
        value_part = jnp.einsum(
            "shqk,sqhd->skhd",
            probabilities.astype(jnp.bfloat16),
            d_context_heads,
            preferred_element_type=jnp.float32,
        )
        fresh = jnp.concatenate(
            [
                key_part.reshape(seq_count, key_count, model_width),
                value_part.reshape(seq_count, key_count, model_width),
            ],
            -1,
        )
        before = lax.dynamic_slice_in_dim(grad_pairs, first_row, key_count, 1)
        grad_pairs = lax.dynamic_update_slice_in_dim(grad_pairs, before + fresh, first_row, 1)
        return (grad_query, grad_pairs)

    query_zero = jnp.zeros((seq_count, block_rows, HEADS, head_size), jnp.float32)
    back_state = (query_zero, jnp.zeros((seq_count, whole_length, 2 * model_width), jnp.float32))
    back_result = over_blocks(
        backward_step, back_state, lax.all_gather(local_pairs, "ctx", axis=1, tiled=True)
    )
    grad_query = back_result[0]
    own_pairs = lax.psum_scatter(
        back_result[1].astype(jnp.bfloat16), "ctx", scatter_dimension=1, tiled=True
    ).astype(jnp.float32)
    d_keys = own_pairs[:, :, :model_width].reshape(total_rows, model_width).astype(jnp.bfloat16)
    d_values = own_pairs[:, :, model_width:].reshape(total_rows, model_width).astype(jnp.bfloat16)
    d_queries = grad_query.reshape(total_rows, model_width).astype(jnp.bfloat16)
    query_grad = outer_sum(flat_rows, d_queries)
    query_bias_grad = jnp.sum(d_queries.astype(jnp.float32), 0)
    key_grad = outer_sum(flat_rows, d_keys)
    value_grad = outer_sum(flat_rows, d_values)
    value_bias_grad = jnp.sum(d_values.astype(jnp.float32), 0)
    input_grad = (
        d_first
        + back_product(d_queries, full_query)
        + back_product(d_keys, full_key)
        + back_product(d_values, full_value)
    ).reshape(inputs.shape)
    shares = (
        lax.psum_scatter(query_grad, ("fsdp", "ctx"), scatter_dimension=0, tiled=True),
        lax.psum_scatter(query_bias_grad, ("fsdp", "ctx"), scatter_dimension=0, tiled=True),
        lax.psum_scatter(key_grad, ("fsdp", "ctx"), scatter_dimension=0, tiled=True),
        lax.psum_scatter(value_grad, ("fsdp", "ctx"), scatter_dimension=0, tiled=True),
        lax.psum_scatter(value_bias_grad, ("fsdp", "ctx"), scatter_dimension=0, tiled=True),
        lax.psum_scatter(out_grad, ("fsdp", "ctx"), scatter_dimension=0, tiled=True),
        lax.psum_scatter(out_bias_grad, ("fsdp", "ctx"), scatter_dimension=0, tiled=True),
        lax.psum_scatter(first_gain_grad, ("fsdp", "ctx"), scatter_dimension=0, tiled=True),
        lax.psum_scatter(first_shift_grad, ("fsdp", "ctx"), scatter_dimension=0, tiled=True),
        lax.psum_scatter(expand_grad, ("fsdp", "ctx"), scatter_dimension=0, tiled=True),
        lax.psum_scatter(expand_bias_grad, ("fsdp", "ctx"), scatter_dimension=0, tiled=True),
        lax.psum_scatter(reduce_grad, ("fsdp", "ctx"), scatter_dimension=0, tiled=True),
        lax.psum_scatter(reduce_bias_grad, ("fsdp", "ctx"), scatter_dimension=0, tiled=True),
        lax.psum_scatter(second_gain_grad, ("fsdp", "ctx"), scatter_dimension=0, tiled=True),
        lax.psum_scatter(second_shift_grad, ("fsdp", "ctx"), scatter_dimension=0, tiled=True),
    )
    return (
        layer_out,
        input_grad,
        shares[0],
        shares[1],
        shares[2],
        shares[3],
        shares[4],
        shares[5],
        shares[6],
        shares[7],
        shares[8],
        shares[9],
        shares[10],
        shares[11],
        shares[12],
        shares[13],
        shares[14],
    )


MESH = pl.DeviceIdType.MESH
MIB = 1024*1024

def place():
    core = lax.axis_index("fsdp"); chip = lax.axis_index("ctx")
    return core, chip

def greet(peers):
    barrier = pltpu.get_barrier_semaphore()
    for peer in peers:
        pl.semaphore_signal(barrier, inc=1, device_id=peer, device_id_type=MESH)
    pl.semaphore_wait(barrier, len(peers))

class Mover:
    def __init__(self, send_sem, recv_sem):
        self.send_sem, self.recv_sem, self.used, self.started = send_sem, recv_sem, 0, []
    def make(self, src, dst, peer):
        i = self.used; self.used += 1
        return pltpu.make_async_remote_copy(src_ref=src, dst_ref=dst, send_sem=self.send_sem.at[i],
            recv_sem=self.recv_sem.at[i], device_id=peer, device_id_type=MESH)

def flip(v, bits):
    for b in (1, 2, 4, 8):
        if bits & b:
            v = v + b - 2 * b * lax.rem(lax.div(v, b), 2)
    return v

def gather_kernel(count, *refs):
    srcs, outs = refs[:count], refs[count:2*count]
    send_sem, recv_sem, local_sem = refs[2*count:]
    core, chip = place()
    sib = (1 - core, chip)
    at = lambda bits: (core, flip(chip, bits))
    Z = (0, 4, 8, 12)
    greet([sib, at(1), at(2), at(4), at(8), at(12)])
    mine = lambda bits: core * 16 + flip(chip, bits)
    theirs = lambda bits: (1 - core) * 16 + flip(chip, bits)
    sems = {}
    def sem_of(a, tag):
        return sems.setdefault((a, tag), len(sems))
    pending = []
    def send(a, tag, src, dst, peer):
        i = sem_of(a, tag)
        c = pltpu.make_async_remote_copy(src_ref=src, dst_ref=dst, send_sem=send_sem.at[i], recv_sem=recv_sem.at[i], device_id=peer, device_id_type=MESH)
        c.start(); pending.append(c)
    def arrived(a, tag, dst):
        i = sem_of(a, tag)
        pltpu.make_async_remote_copy(src_ref=dst, dst_ref=dst, send_sem=send_sem.at[i], recv_sem=recv_sem.at[i], device_id=sib, device_id_type=MESH).wait_recv()
    locals_ = []
    for a in range(count):
        o = outs[a].at[mine(0)]
        for bits in (4, 8, 12):
            send(a, ("z", bits), srcs[a], o, at(bits))
        send(a, ("x", 0), srcs[a], o, at(1))
        send(a, ("y", 0), srcs[a], o, at(2))
        send(a, ("s", 0), srcs[a], o, sib)
        c = pltpu.make_async_copy(srcs[a], o, local_sem.at[a]); c.start(); locals_.append(c)
    for a in range(count):
        for z in (4, 8, 12):
            b = outs[a].at[mine(z)]
            arrived(a, ("z", z), b)
            send(a, ("x", z), b, b, at(1))
            send(a, ("y", z), b, b, at(2))
            send(a, ("s", z), b, b, sib)
    for a in range(count):
        half = srcs[a].shape[0] // 2
        for z in Z:
            b = outs[a].at[mine(z + 1)]
            arrived(a, ("x", z), b)
            h = outs[a].at[mine(z + 1), pl.ds(0, half)]
            send(a, ("dy", z), h, h, at(2))
            send(a, ("s", z + 1), b, b, sib)
            b = outs[a].at[mine(z + 2)]
            arrived(a, ("y", z), b)
            h = outs[a].at[mine(z + 2), pl.ds(half, half)]
            send(a, ("dx", z), h, h, at(1))
            send(a, ("s", z + 2), b, b, sib)
    for a in range(count):
        half = srcs[a].shape[0] // 2
        for z in Z:
            b = outs[a].at[mine(z + 3)]
            arrived(a, ("dy", z), outs[a].at[mine(z + 3), pl.ds(0, half)])
            arrived(a, ("dx", z), outs[a].at[mine(z + 3), pl.ds(half, half)])
            send(a, ("s", z + 3), b, b, sib)
    for a in range(count):
        for z in range(16):
            arrived(a, ("s", z), outs[a].at[theirs(z)])
    for c in pending:
        c.wait_send()
    for c in locals_:
        c.wait()

def gather_all(shards, collective_id):
    n = len(shards)
    hbm = pl.BlockSpec(memory_space=pl.ANY)
    return pl.pallas_call(
        partial(gather_kernel, n),
        out_shape=[jax.ShapeDtypeStruct((32,) + s.shape, s.dtype) for s in shards],
        in_specs=[hbm] * n, out_specs=[hbm] * n,
        scratch_shapes=[pltpu.SemaphoreType.DMA((35 * n,)), pltpu.SemaphoreType.DMA((35 * n,)), pltpu.SemaphoreType.DMA((n,))],
        compiler_params=pltpu.CompilerParams(collective_id=collective_id, has_side_effects=True),
        name="gather_weights",
    )(*shards)

def exchange_kernel(count, *refs):
    srcs, outs = refs[:count], refs[count:2*count]
    send_sem, recv_sem, local_sem = refs[2*count:]
    core, chip = place()
    greet([(core, flip(chip, b)) for b in range(1, 16)])
    copies = []
    for a in range(count):
        for b in ORDER:
            i = a * 16 + b
            to = flip(chip, b)
            c = pltpu.make_async_remote_copy(src_ref=srcs[a].at[to], dst_ref=outs[a].at[chip], send_sem=send_sem.at[i], recv_sem=recv_sem.at[i], device_id=(core, to), device_id_type=MESH)
            c.start(); copies.append((c, a, to, i))
        c0 = pltpu.make_async_copy(srcs[a].at[chip], outs[a].at[chip], local_sem.at[a]); c0.start(); copies.append((c0, None, None, None))
    for c, a, to, i in copies:
        if a is None: c.wait()
        else:
            c.wait_send()
            pltpu.make_async_remote_copy(src_ref=outs[a].at[to], dst_ref=outs[a].at[to], send_sem=send_sem.at[i], recv_sem=recv_sem.at[i], device_id=(core, to), device_id_type=MESH).wait_recv()
ORDER = (12, 8, 4, 15, 11, 7, 14, 13, 10, 9, 6, 5, 3, 2, 1)

def exchange(blocks, collective_id, space=pl.ANY):
    n = len(blocks)
    hbm = pl.BlockSpec(memory_space=space)
    return pl.pallas_call(
        partial(exchange_kernel, n),
        out_shape=[jax.ShapeDtypeStruct(s.shape, s.dtype) for s in blocks],
        in_specs=[hbm] * n, out_specs=[hbm] * n,
        scratch_shapes=[pltpu.SemaphoreType.DMA((16 * n,)), pltpu.SemaphoreType.DMA((16 * n,)), pltpu.SemaphoreType.DMA((n,))],
        compiler_params=pltpu.CompilerParams(collective_id=collective_id, has_side_effects=True),
        name="exchange_heads",
    )(*blocks)

def scatter_kernel(count, *refs):
    g, outs = refs[:count], refs[count:2*count]
    first, second, third, passed = (refs[(2+i)*count:(3+i)*count] for i in range(4))
    send_sem, recv_sem = refs[6*count:]
    core, chip = place()
    at = lambda bits: (core, flip(chip, bits))
    greet([at(1), at(2), at(4), at(8), at(12)])
    sems = {}; pending = []
    def pair(a, tag, src, dst, peer):
        i = sems.setdefault((a, tag), len(sems))
        return pltpu.make_async_remote_copy(src_ref=src, dst_ref=dst, send_sem=send_sem.at[i], recv_sem=recv_sem.at[i], device_id=peer, device_id_type=MESH)
    def send(a, tag, src, dst, peer):
        c = pair(a, tag, src, dst, peer); c.start(); pending.append(c)
    def arrived(a, tag, dst):
        pair(a, tag, dst, dst, at(1)).wait_recv()
    ORD = (12, 8, 4, 0)
    def add(rows, fn):
        step = min(rows, 16)
        @pl.loop(0, rows // step)
        def _(i):
            fn(pl.ds(pl.multiple_of(i * step, step), step))
    for a in range(count):
        half = g[a].shape[1] // 2
        lo, hi = pl.ds(0, half), pl.ds(half, half)
        for k, z in enumerate(ORD):
            diag = flip(chip, z + 3)
            send(a, ("1a", k), g[a].at[diag, lo], first[a].at[k, 0], at(2))
            send(a, ("1b", k), g[a].at[diag, hi], first[a].at[k, 1], at(1))
        for k, z in enumerate(ORD):
            send(a, ("2xh", k), g[a].at[flip(chip, z + 1), hi], second[a].at[k, 0, hi], at(1))
            send(a, ("2yl", k), g[a].at[flip(chip, z + 2), lo], second[a].at[k, 1, lo], at(2))
    for a in range(count):
        half = g[a].shape[1] // 2
        lo, hi = pl.ds(0, half), pl.ds(half, half)
        for k, z in enumerate(ORD):
            xb, yb = flip(chip, z + 1), flip(chip, z + 2)
            arrived(a, ("1a", k), first[a].at[k, 0])
            def f(rows, a=a, k=k, xb=xb):
                first[a][k, 0, rows] = first[a][k, 0, rows] + g[a][xb, rows]
            add(half, f)
            send(a, ("2xl", k), first[a].at[k, 0], second[a].at[k, 0, lo], at(1))
            arrived(a, ("1b", k), first[a].at[k, 1])
            def f(rows, a=a, k=k, yb=yb, half=half):
                first[a][k, 1, rows] = first[a][k, 1, rows] + g[a][yb, pl.ds(pl.multiple_of(rows.start + half, 8), rows.size)]
            add(half, f)
            send(a, ("2yh", k), first[a].at[k, 1], second[a].at[k, 1, hi], at(2))
    for a in range(count):
        full = g[a].shape[1]
        half = full // 2
        lo, hi = pl.ds(0, half), pl.ds(half, half)
        for k, z in enumerate(ORD):
            arrived(a, ("2xh", k), second[a].at[k, 0, hi])
            arrived(a, ("2yl", k), second[a].at[k, 1, lo])
            arrived(a, ("2xl", k), second[a].at[k, 0, lo])
            arrived(a, ("2yh", k), second[a].at[k, 1, hi])
            zb = flip(chip, z)
            def f(rows, a=a, k=k, zb=zb):
                total = g[a][zb, rows].astype(jnp.float32) + second[a][k, 0, rows].astype(jnp.float32) + second[a][k, 1, rows].astype(jnp.float32)
                if k < 3: passed[a][k, rows] = total.astype(passed[a].dtype)
                else: outs[a][rows] = total
            add(full, f)
            if k < 3:
                send(a, ("3", k), passed[a].at[k], third[a].at[k], at(z))
    for a in range(count):
        for k in range(3):
            arrived(a, ("3", k), third[a].at[k])
        def f(rows, a=a):
            outs[a][rows] = outs[a][rows] + third[a][0, rows].astype(jnp.float32) + third[a][1, rows].astype(jnp.float32) + third[a][2, rows].astype(jnp.float32)
        add(g[a].shape[1], f)
    for c in pending:
        c.wait_send()

def scatter_all(grads, collective_id):
    n = len(grads)
    v = pl.BlockSpec(memory_space=pltpu.VMEM)
    sc = []
    for lead, halve in (((4, 2), 1), ((4, 2), 0), ((3,), 0), ((3,), 0)):
        for x in grads:
            _, r, c = x.shape
            sc.append(pltpu.VMEM(lead + ((r // 2) if halve else r, c), x.dtype))
    return pl.pallas_call(
        partial(scatter_kernel, n),
        out_shape=[jax.ShapeDtypeStruct(x.shape[1:], jnp.float32) for x in grads],
        in_specs=[v] * n, out_specs=[v] * n,
        scratch_shapes=sc + [pltpu.SemaphoreType.DMA((27 * n,)), pltpu.SemaphoreType.DMA((27 * n,))],
        compiler_params=pltpu.CompilerParams(collective_id=collective_id, has_side_effects=True, vmem_limit_bytes=60 * MIB),
        name="scatter_grads",
    )(*grads)


LOG2E = math.log2(math.e)


def lanes(rows, upper):
    lane = lax.broadcasted_iota(jnp.int32, (rows, 128), 1)
    return lane >= 64 if upper else lane < 64


def nt(a, b):
    return lax.dot_general(a, b, (((1,), (1,)), ((), ())), preferred_element_type=jnp.float32)


def attend_kernel(blk, lengths_ref, r_ref, ctx_ref, full_ref, lse_ref, vt_ref):
    q = pl.program_id(0)
    total = r_ref.shape[0] * 128

    @pl.when(q == 0)
    def _():
        vt_ref[...] = r_ref[:, 2].reshape(total, 128).T

    rows = pl.ds(q * (blk // 128), blk // 128)
    parts = []
    for s in range(2):
        pair = r_ref[:, s].reshape(total, 128)
        mine = r_ref[rows, s].reshape(blk, 128)
        query = jnp.where(lanes(blk, True), pltpu.roll(mine.astype(jnp.float32), 64, 1), 0.0).astype(jnp.bfloat16)
        scores = nt(pair, query) * (0.125 * LOG2E)
        key = lax.broadcasted_iota(jnp.int32, scores.shape, 0)
        scores = jnp.where(key < lengths_ref[s], scores, masked_score)
        top = jnp.max(scores, 0, keepdims=True)
        e = jnp.exp2(scores - top)
        mass = jnp.sum(e, 0, keepdims=True)
        o = jnp.dot(vt_ref[...], e.astype(jnp.bfloat16), preferred_element_type=jnp.float32)
        parts.append(o[64 * s : 64 * s + 64] / mass)
        lse_ref[s, pl.ds(q, 1), :] = top + jnp.log2(mass)
    out = jnp.concatenate(parts, 0).T
    full_ref[...] = out
    ctx_ref[...] = out.astype(jnp.bfloat16)


def attend(lengths, blocks, blk=256):
    chips = blocks.shape[0]
    total = chips * 128
    return pl.pallas_call(
        partial(attend_kernel, blk),
        grid=(total // blk,),
        out_shape=[
            jax.ShapeDtypeStruct((total, 128), jnp.bfloat16),
            jax.ShapeDtypeStruct((total, 128), jnp.float32),
            jax.ShapeDtypeStruct((2, total // blk, blk), jnp.float32),
        ],
        in_specs=[pl.BlockSpec(memory_space=pltpu.SMEM), pl.BlockSpec(memory_space=pltpu.VMEM)],
        out_specs=[
            pl.BlockSpec((blk, 128), lambda q: (q, 0)),
            pl.BlockSpec((blk, 128), lambda q: (q, 0)),
            pl.BlockSpec((2, total // blk, blk), lambda q: (0, 0, 0)),
        ],
        scratch_shapes=[pltpu.VMEM((128, total), jnp.bfloat16)],
        compiler_params=pltpu.CompilerParams(vmem_limit_bytes=56 * MIB),
        name="attend",
    )(lengths, blocks)


def attend_back_kernel(blk, lengths_ref, r_ref, d_ref, full_ref, lse_ref, out_ref, pair_t, acc, acc_v):
    q = pl.program_id(0)
    total = r_ref.shape[0] * 128

    @pl.when(q == 0)
    def _():
        for s in range(2):
            pair_t[s] = r_ref[:, s].reshape(total, 128).T
        acc[...] = jnp.zeros_like(acc)
        acc_v[...] = jnp.zeros_like(acc_v)

    rows = pl.ds(q * (blk // 128), blk // 128)
    span = pl.ds(pl.multiple_of(q * blk, blk), blk)
    d_mine = d_ref[span]
    product_t = (d_mine.astype(jnp.float32) * full_ref[span]).T
    values = r_ref[:, 2].reshape(total, 128)
    for s in range(2):
        pair = r_ref[:, s].reshape(total, 128)
        mine = r_ref[rows, s].reshape(blk, 128)
        query = jnp.where(lanes(blk, True), pltpu.roll(mine.astype(jnp.float32), 64, 1), 0.0).astype(jnp.bfloat16)
        d_half = jnp.where(lanes(blk, s == 1), d_mine.astype(jnp.float32), 0.0).astype(jnp.bfloat16)
        delta = jnp.sum(product_t[64 * s : 64 * s + 64], 0, keepdims=True)
        scores = nt(pair, query) * (0.125 * LOG2E)
        key = lax.broadcasted_iota(jnp.int32, scores.shape, 0)
        probs = jnp.where(key < lengths_ref[s], jnp.exp2(scores - lse_ref[s, pl.ds(q, 1), :]), 0.0)
        d_probs = nt(values, d_half)
        d_scores = (probs * (d_probs - delta)).astype(jnp.bfloat16)
        acc_v[...] += jnp.dot(probs.astype(jnp.bfloat16), d_half, preferred_element_type=jnp.float32)
        acc[s] += jnp.dot(d_scores, query, preferred_element_type=jnp.float32)
        d_query = jnp.dot(pair_t[s], d_scores, preferred_element_type=jnp.float32)
        acc[s, span] += jnp.concatenate([d_query[64:], jnp.zeros((64, blk), jnp.float32)], 0).T

    @pl.when(q == pl.num_programs(0) - 1)
    def _():
        for s in range(2):
            out_ref[:, s] = (acc[s] * 0.125).astype(jnp.bfloat16).reshape(total // 128, 128, 128)
        out_ref[:, 2] = acc_v[...].astype(jnp.bfloat16).reshape(total // 128, 128, 128)


def attend_back(lengths, blocks, d_context, full, lse, blk=256):
    chips = blocks.shape[0]
    total = chips * 128
    v = pl.BlockSpec(memory_space=pltpu.VMEM)
    return pl.pallas_call(
        partial(attend_back_kernel, blk),
        grid=(total // blk,),
        out_shape=jax.ShapeDtypeStruct(blocks.shape, jnp.bfloat16),
        in_specs=[pl.BlockSpec(memory_space=pltpu.SMEM), v, v, v, v],
        out_specs=v,
        scratch_shapes=[
            pltpu.VMEM((2, 128, total), jnp.bfloat16),
            pltpu.VMEM((2, total, 128), jnp.float32),
            pltpu.VMEM((total, 128), jnp.float32),
        ],
        compiler_params=pltpu.CompilerParams(vmem_limit_bytes=56 * MIB),
        name="attend_back",
    )(lengths, blocks, d_context, full, lse)


def swap(x):
    return lax.ppermute(x, "fsdp", [(0, 1), (1, 0)])


def pack_heads(rows, seqs, count):
    return rows.reshape(seqs, count, HEADS, 64).transpose(2, 1, 0, 3).reshape(HEADS, count, seqs * 64)


def unpack_heads(blocks, seqs, count):
    return blocks.reshape(HEADS, count, seqs, 64).transpose(2, 1, 0, 3).reshape(seqs * count, HEADS * 64)


def chip_sum(left, right):
    core = lax.axis_index("fsdp")
    h = left.shape[1] // 2
    own = lax.dynamic_slice_in_dim(left, core * h, h, 1)
    other = swap(lax.dynamic_slice_in_dim(left, (1 - core) * h, h, 1))
    grad = outer_sum(own, right) + outer_sum(other, swap(right))
    return grad.astype(jnp.bfloat16).reshape(16, h // 16, right.shape[1])


def fast_shards(
    inputs,
    lengths,
    w_query,
    b_query,
    w_key,
    w_value,
    b_value,
    w_out,
    b_out,
    first_gain,
    first_shift,
    w_expand,
    b_expand,
    w_reduce,
    b_reduce,
    second_gain,
    second_shift,
    cotangent,
):
    core = lax.axis_index("fsdp")
    f32, bf16 = jnp.float32, jnp.bfloat16
    seqs, count, width = inputs.shape
    total = seqs * count
    part = width // 32
    ff = w_expand.shape[1]
    heads_of = lambda w: w.reshape(part, HEADS, 64)
    qk = jnp.concatenate([heads_of(w_query), heads_of(w_key)], -1).reshape(part, 2 * width)
    small = [b_query, b_value, b_out, first_gain, first_shift, b_expand, b_reduce, second_gain, second_shift]
    sizes = [b.shape[0] for b in small]
    vec = jnp.concatenate(small + [jnp.zeros((part * 128 - sum(sizes),), bf16)]).reshape(part, 128)
    g_qkv, g_vec, g_out, g_expand, g_reduce = gather_all(
        [jnp.concatenate([qk, w_value], 1), vec, w_out, w_expand, w_reduce], 1
    )
    full_qkv = g_qkv.reshape(width, 3 * width)
    full_out = g_out.reshape(width, width)
    full_expand = g_expand.reshape(width, ff)
    full_reduce = g_reduce.reshape(ff, width)
    flat_vec = g_vec.reshape(32, part * 128)
    offsets = [sum(sizes[:i]) for i in range(len(sizes) + 1)]
    (bias_query, bias_value, bias_out, gain_first, shift_first, bias_expand, bias_reduce, gain_second, shift_second) = [
        flat_vec[:, offsets[i] : offsets[i + 1]].reshape(-1).astype(f32) for i in range(len(sizes))
    ]
    own_first = lax.axis_index("ctx") * count
    positions = own_first + jnp.arange(count, dtype=jnp.int32)
    valid_rows = (positions[None, :] < lengths[:, None]).astype(f32).reshape(total, 1)
    flat_rows = inputs.reshape(total, width)
    bias_qk = jnp.concatenate([bias_query.reshape(HEADS, 64), jnp.zeros((HEADS, 64), f32)], 1).reshape(-1)
    qkv = (product(flat_rows, full_qkv) + jnp.concatenate([bias_qk, bias_value])).astype(bf16)
    blocks = jnp.concatenate(
        [
            qkv[:, : 2 * width].reshape(seqs, count, HEADS, 128).transpose(2, 0, 1, 3),
            pack_heads(qkv[:, 2 * width :], seqs, count)[:, None],
        ],
        1,
    )
    (blocks,) = exchange([blocks], 2)
    context_head, full_head, lse = attend(lengths, blocks)
    (context_blocks,) = exchange([context_head.reshape(16, count, 128)], 3)
    context = unpack_heads(context_blocks, seqs, count)
    attended = product(context, full_out) + bias_out
    residual = flat_rows.astype(f32) + attended
    normed, first_pull = jax.vjp(layer_norm, residual, gain_first, shift_first)
    normed_low = normed.astype(bf16)
    expanded = product(normed_low, full_expand) + bias_expand
    activated, gelu_pull = jax.vjp(partial(jax.nn.gelu, approximate=False), expanded)
    activated_low = activated.astype(bf16)
    reduced = product(activated_low, full_reduce) + bias_reduce
    final_rows, second_pull = jax.vjp(layer_norm, normed + reduced, gain_second, shift_second)
    layer_out = (final_rows * valid_rows).astype(bf16).reshape(inputs.shape)
    d_output = cotangent.reshape(total, width).astype(f32) * valid_rows
    d_second, second_gain_grad, second_shift_grad = second_pull(d_output)
    d_reduced = d_second.astype(bf16)
    reduce_grad = chip_sum(activated_low, d_reduced)
    reduce_bias_grad = jnp.sum(d_reduced.astype(f32), 0)
    (d_expanded_full,) = gelu_pull(back_product(d_reduced, full_reduce))
    d_expanded = d_expanded_full.astype(bf16)
    expand_grad = chip_sum(normed_low, d_expanded)
    expand_bias_grad = jnp.sum(d_expanded.astype(f32), 0)
    d_normed = d_second + back_product(d_expanded, full_expand)
    d_first, first_gain_grad, first_shift_grad = first_pull(d_normed)
    d_attended = d_first.astype(bf16)
    out_grad = chip_sum(context, d_attended)
    out_bias_grad = jnp.sum(d_attended.astype(f32), 0)
    d_context = back_product(d_attended, full_out).astype(bf16)
    (d_blocks,) = exchange([pack_heads(d_context, seqs, count)], 4)
    d_heads = attend_back(lengths, blocks, d_blocks.reshape(16 * count, 128), full_head, lse)
    (d_heads,) = exchange([d_heads], 5)
    d_qk = d_heads[:, :2].transpose(1, 2, 0, 3).reshape(total, 2 * width)
    d_qkv = jnp.concatenate([d_qk, unpack_heads(d_heads[:, 2], seqs, count)], 1)
    qkv_grad = chip_sum(flat_rows, d_qkv)
    input_grad = (d_first + back_product(d_qkv, full_qkv)).reshape(inputs.shape)
    qkv_bias_grad = jnp.sum(d_qkv.astype(f32), 0)
    query_bias_grad = qkv_bias_grad[: 2 * width].reshape(HEADS, 128)[:, :64].reshape(-1)
    value_bias_grad = qkv_bias_grad[2 * width :]
    small_grads = jnp.concatenate(
        [
            g.reshape(32, -1)
            for g in (
                query_bias_grad,
                value_bias_grad,
                out_bias_grad,
                first_gain_grad,
                first_shift_grad,
                expand_bias_grad,
                reduce_bias_grad,
                second_gain_grad,
                second_shift_grad,
            )
        ]
        + [jnp.zeros((32, 2048 - sum(sizes)), f32)],
        1,
    ).reshape(2, 16, 16, 128)
    vec_grad = lax.dynamic_index_in_dim(small_grads, core, 0, False) + swap(
        lax.dynamic_index_in_dim(small_grads, 1 - core, 0, False)
    )
    s_reduce, s_expand, s_out, s_vec, s_qkv = scatter_all([reduce_grad, expand_grad, out_grad, vec_grad, qkv_grad], 6)
    s_qk = s_qkv[:, : 2 * width].reshape(part, HEADS, 128)
    s_vec = s_vec.reshape(-1)
    v = [s_vec[offsets[i] : offsets[i + 1]] for i in range(len(sizes))]
    return (
        layer_out,
        input_grad,
        s_qk[:, :, :64].reshape(part, width),
        v[0],
        s_qk[:, :, 64:].reshape(part, width),
        s_qkv[:, 2 * width :],
        v[1],
        s_out,
        v[2],
        v[3],
        v[4],
        s_expand,
        v[5],
        s_reduce,
        v[6],
        v[7],
        v[8],
    )


def solution(mesh):
    fast = mesh.shape["fsdp"] == 2 and mesh.shape["ctx"] == HEADS
    shards = fast_shards if fast else general_shards
    return jax.shard_map(
        shards,
        mesh=mesh,
        in_specs=(
            P("fsdp", "ctx", None),
            P("fsdp"),
            P(("fsdp", "ctx"), None),
            P(("fsdp", "ctx")),
            P(("fsdp", "ctx"), None),
            P(("fsdp", "ctx"), None),
            P(("fsdp", "ctx")),
            P(("fsdp", "ctx"), None),
            P(("fsdp", "ctx")),
            P(("fsdp", "ctx")),
            P(("fsdp", "ctx")),
            P(("fsdp", "ctx"), None),
            P(("fsdp", "ctx")),
            P(("fsdp", "ctx"), None),
            P(("fsdp", "ctx")),
            P(("fsdp", "ctx")),
            P(("fsdp", "ctx")),
            P("fsdp", "ctx", None),
        ),
        out_specs=(
            P("fsdp", "ctx", None),
            P("fsdp", "ctx", None),
            P(("fsdp", "ctx"), None),
            P(("fsdp", "ctx")),
            P(("fsdp", "ctx"), None),
            P(("fsdp", "ctx"), None),
            P(("fsdp", "ctx")),
            P(("fsdp", "ctx"), None),
            P(("fsdp", "ctx")),
            P(("fsdp", "ctx")),
            P(("fsdp", "ctx")),
            P(("fsdp", "ctx"), None),
            P(("fsdp", "ctx")),
            P(("fsdp", "ctx"), None),
            P(("fsdp", "ctx")),
            P(("fsdp", "ctx")),
            P(("fsdp", "ctx")),
        ),
        check_vma=False,
    )
```

```python
from functools import partial
import math

import jax
import jax.numpy as jnp
from jax import lax
from jax.experimental import pallas as pl
from jax.experimental.pallas import tpu as pltpu
from jax.sharding import PartitionSpec as P

HEADS = 16


epsilon = 1e-05
masked_score = -1e30


def layer_norm(rows_in, gain, shift):
    center = rows_in - jnp.mean(rows_in, -1, keepdims=True)
    spread = jnp.mean(center * center, -1, keepdims=True)
    return center * lax.rsqrt(spread + epsilon) * gain + shift


def product(left, right):
    return jnp.dot(left, right, preferred_element_type=jnp.float32)


def outer_sum(left, right):
    return jnp.einsum("rd,re->de", left, right, preferred_element_type=jnp.float32)


def back_product(grad_rows, weight):
    return jnp.einsum("re,de->rd", grad_rows, weight, preferred_element_type=jnp.float32)


def over_blocks(step_fn, carry_state, pair_rows):
    key_count = pair_rows.shape[1]
    block_width = math.gcd(key_count, 512)

    def turn(turn_index, inner_state):
        block_pairs = lax.dynamic_slice_in_dim(pair_rows, turn_index * block_width, block_width, 1)
        return step_fn(inner_state, block_pairs, turn_index * block_width)

    return lax.fori_loop(0, key_count // block_width, turn, carry_state)


def general_shards(
    inputs,
    lengths,
    w_query,
    b_query,
    w_key,
    w_value,
    b_value,
    w_out,
    b_out,
    first_gain,
    first_shift,
    w_expand,
    b_expand,
    w_reduce,
    b_reduce,
    second_gain,
    second_shift,
    cotangent,
):
    gathered = (
        lax.all_gather(w_query, ("fsdp", "ctx"), axis=0, tiled=True),
        lax.all_gather(b_query, ("fsdp", "ctx"), axis=0, tiled=True),
        lax.all_gather(w_key, ("fsdp", "ctx"), axis=0, tiled=True),
        lax.all_gather(w_value, ("fsdp", "ctx"), axis=0, tiled=True),
        lax.all_gather(b_value, ("fsdp", "ctx"), axis=0, tiled=True),
        lax.all_gather(w_out, ("fsdp", "ctx"), axis=0, tiled=True),
        lax.all_gather(b_out, ("fsdp", "ctx"), axis=0, tiled=True),
        lax.all_gather(first_gain, ("fsdp", "ctx"), axis=0, tiled=True),
        lax.all_gather(first_shift, ("fsdp", "ctx"), axis=0, tiled=True),
        lax.all_gather(w_expand, ("fsdp", "ctx"), axis=0, tiled=True),
        lax.all_gather(b_expand, ("fsdp", "ctx"), axis=0, tiled=True),
        lax.all_gather(w_reduce, ("fsdp", "ctx"), axis=0, tiled=True),
        lax.all_gather(b_reduce, ("fsdp", "ctx"), axis=0, tiled=True),
        lax.all_gather(second_gain, ("fsdp", "ctx"), axis=0, tiled=True),
        lax.all_gather(second_shift, ("fsdp", "ctx"), axis=0, tiled=True),
    )
    (
        full_query,
        bias_query,
        full_key,
        full_value,
        bias_value,
        full_out,
        bias_out,
        gain_first,
        shift_first,
        full_expand,
        bias_expand,
        full_reduce,
        bias_reduce,
        gain_second,
        shift_second,
    ) = gathered
    seq_count, block_rows, model_width = inputs.shape
    total_rows = seq_count * block_rows
    head_size = model_width // HEADS
    score_scale = head_size ** (-0.5)
    own_first = lax.axis_index("ctx") * block_rows
    positions = own_first + jnp.arange(block_rows, dtype=jnp.int32)
    valid_rows = (positions[None, :] < lengths[:, None]).astype(jnp.float32).reshape(total_rows, 1)
    flat_rows = inputs.reshape(total_rows, model_width)
    queries = (product(flat_rows, full_query) + bias_query.astype(jnp.float32)).astype(jnp.bfloat16)
    key_rows = product(flat_rows, full_key).astype(jnp.bfloat16)
    value_rows = (product(flat_rows, full_value) + bias_value.astype(jnp.float32)).astype(
        jnp.bfloat16
    )
    query_heads = queries.reshape(seq_count, block_rows, HEADS, head_size)
    local_pairs = jnp.concatenate([key_rows, value_rows], -1).reshape(
        seq_count, block_rows, 2 * model_width
    )

    def key_allowed(first_row, key_count):
        return ((first_row + jnp.arange(key_count, dtype=jnp.int32))[None, :] < lengths[:, None])[
            :, None, None, :
        ]

    def split_pairs(block_pairs):
        key_count = block_pairs.shape[1]
        key_heads = block_pairs[:, :, :model_width].reshape(seq_count, key_count, HEADS, head_size)
        value_heads = block_pairs[:, :, model_width:].reshape(
            seq_count, key_count, HEADS, head_size
        )
        return (key_heads, value_heads, key_count)

    def forward_step(carry_state, block_pairs, first_row):
        running_max, running_sum, running_acc = carry_state
        key_heads, value_heads, key_count = split_pairs(block_pairs)
        allowed = key_allowed(first_row, key_count)
        scores = (
            jnp.einsum(
                "sqhd,skhd->shqk", query_heads, key_heads, preferred_element_type=jnp.float32
            )
            * score_scale
        )
        scores = jnp.where(allowed, scores, masked_score)
        new_max = jnp.maximum(running_max, jnp.max(scores, -1))
        factor = jnp.exp(running_max - new_max)
        exponents = jnp.where(allowed, jnp.exp(scores - new_max[..., None]), 0.0)
        new_sum = running_sum * factor + jnp.sum(exponents, -1)
        update = jnp.einsum(
            "shqk,skhd->sqhd",
            exponents.astype(jnp.bfloat16),
            value_heads,
            preferred_element_type=jnp.float32,
        )
        new_acc = running_acc * jnp.transpose(factor, (0, 2, 1))[..., None] + update
        return (new_max, new_sum, new_acc)

    start_state = (
        jnp.full((seq_count, HEADS, block_rows), masked_score, jnp.float32),
        jnp.zeros((seq_count, HEADS, block_rows), jnp.float32),
        jnp.zeros((seq_count, block_rows, HEADS, head_size), jnp.float32),
    )
    running_max, running_sum, running_acc = over_blocks(
        forward_step, start_state, lax.all_gather(local_pairs, "ctx", axis=1, tiled=True)
    )
    context_full = running_acc / jnp.transpose(running_sum, (0, 2, 1))[..., None]
    log_total = running_max + jnp.log(running_sum)
    context = context_full.reshape(total_rows, model_width).astype(jnp.bfloat16)
    attended = product(context, full_out) + bias_out.astype(jnp.float32)
    residual = flat_rows.astype(jnp.float32) + attended
    normed, first_pull = jax.vjp(
        layer_norm, residual, gain_first.astype(jnp.float32), shift_first.astype(jnp.float32)
    )
    normed_low = normed.astype(jnp.bfloat16)
    expanded = product(normed_low, full_expand) + bias_expand.astype(jnp.float32)
    activated, gelu_pull = jax.vjp(partial(jax.nn.gelu, approximate=False), expanded)
    activated_low = activated.astype(jnp.bfloat16)
    reduced = product(activated_low, full_reduce) + bias_reduce.astype(jnp.float32)
    final_rows, second_pull = jax.vjp(
        layer_norm,
        normed + reduced,
        gain_second.astype(jnp.float32),
        shift_second.astype(jnp.float32),
    )
    layer_out = (final_rows * valid_rows).astype(jnp.bfloat16).reshape(inputs.shape)
    d_output = cotangent.reshape(total_rows, model_width).astype(jnp.float32) * valid_rows
    d_second, second_gain_grad, second_shift_grad = second_pull(d_output)
    d_reduced = d_second.astype(jnp.bfloat16)
    reduce_grad = outer_sum(activated_low, d_reduced)
    reduce_bias_grad = jnp.sum(d_reduced.astype(jnp.float32), 0)
    (d_expanded_full,) = gelu_pull(back_product(d_reduced, full_reduce))
    d_expanded = d_expanded_full.astype(jnp.bfloat16)
    expand_grad = outer_sum(normed_low, d_expanded)
    expand_bias_grad = jnp.sum(d_expanded.astype(jnp.float32), 0)
    d_normed = d_second + back_product(d_expanded, full_expand)
    d_first, first_gain_grad, first_shift_grad = first_pull(d_normed)
    d_attended = d_first.astype(jnp.bfloat16)
    out_grad = outer_sum(context, d_attended)
    out_bias_grad = jnp.sum(d_attended.astype(jnp.float32), 0)
    d_context = back_product(d_attended, full_out).astype(jnp.bfloat16)
    d_context_heads = d_context.reshape(seq_count, block_rows, HEADS, head_size)
    delta = jnp.transpose(
        jnp.sum(d_context_heads.astype(jnp.float32) * context_full, -1), (0, 2, 1)
    )
    whole_length = block_rows * lax.axis_size("ctx")

    def score_grads(key_heads, value_heads, allowed):
        scores = (
            jnp.einsum(
                "sqhd,skhd->shqk", query_heads, key_heads, preferred_element_type=jnp.float32
            )
            * score_scale
        )
        probabilities = jnp.where(allowed, jnp.exp(scores - log_total[..., None]), 0.0)
        d_probs = jnp.einsum(
            "sqhd,skhd->shqk", d_context_heads, value_heads, preferred_element_type=jnp.float32
        )
        d_scores = (probabilities * (d_probs - delta[..., None])).astype(jnp.bfloat16)
        return (probabilities, d_scores)

    def backward_step(carry_state, block_pairs, first_row):
        grad_query, grad_pairs = carry_state
        key_heads, value_heads, key_count = split_pairs(block_pairs)
        probabilities, d_scores = score_grads(
            key_heads, value_heads, key_allowed(first_row, key_count)
        )
        grad_query = (
            grad_query
            + jnp.einsum("shqk,skhd->sqhd", d_scores, key_heads, preferred_element_type=jnp.float32)
            * score_scale
        )
        key_part = (
            jnp.einsum("shqk,sqhd->skhd", d_scores, query_heads, preferred_element_type=jnp.float32)
            * score_scale
        )
        value_part = jnp.einsum(
            "shqk,sqhd->skhd",
            probabilities.astype(jnp.bfloat16),
            d_context_heads,
            preferred_element_type=jnp.float32,
        )
        fresh = jnp.concatenate(
            [
                key_part.reshape(seq_count, key_count, model_width),
                value_part.reshape(seq_count, key_count, model_width),
            ],
            -1,
        )
        before = lax.dynamic_slice_in_dim(grad_pairs, first_row, key_count, 1)
        grad_pairs = lax.dynamic_update_slice_in_dim(grad_pairs, before + fresh, first_row, 1)
        return (grad_query, grad_pairs)

    query_zero = jnp.zeros((seq_count, block_rows, HEADS, head_size), jnp.float32)
    back_state = (query_zero, jnp.zeros((seq_count, whole_length, 2 * model_width), jnp.float32))
    back_result = over_blocks(
        backward_step, back_state, lax.all_gather(local_pairs, "ctx", axis=1, tiled=True)
    )
    grad_query = back_result[0]
    own_pairs = lax.psum_scatter(
        back_result[1].astype(jnp.bfloat16), "ctx", scatter_dimension=1, tiled=True
    ).astype(jnp.float32)
    d_keys = own_pairs[:, :, :model_width].reshape(total_rows, model_width).astype(jnp.bfloat16)
    d_values = own_pairs[:, :, model_width:].reshape(total_rows, model_width).astype(jnp.bfloat16)
    d_queries = grad_query.reshape(total_rows, model_width).astype(jnp.bfloat16)
    query_grad = outer_sum(flat_rows, d_queries)
    query_bias_grad = jnp.sum(d_queries.astype(jnp.float32), 0)
    key_grad = outer_sum(flat_rows, d_keys)
    value_grad = outer_sum(flat_rows, d_values)
    value_bias_grad = jnp.sum(d_values.astype(jnp.float32), 0)
    input_grad = (
        d_first
        + back_product(d_queries, full_query)
        + back_product(d_keys, full_key)
        + back_product(d_values, full_value)
    ).reshape(inputs.shape)
    shares = (
        lax.psum_scatter(query_grad, ("fsdp", "ctx"), scatter_dimension=0, tiled=True),
        lax.psum_scatter(query_bias_grad, ("fsdp", "ctx"), scatter_dimension=0, tiled=True),
        lax.psum_scatter(key_grad, ("fsdp", "ctx"), scatter_dimension=0, tiled=True),
        lax.psum_scatter(value_grad, ("fsdp", "ctx"), scatter_dimension=0, tiled=True),
        lax.psum_scatter(value_bias_grad, ("fsdp", "ctx"), scatter_dimension=0, tiled=True),
        lax.psum_scatter(out_grad, ("fsdp", "ctx"), scatter_dimension=0, tiled=True),
        lax.psum_scatter(out_bias_grad, ("fsdp", "ctx"), scatter_dimension=0, tiled=True),
        lax.psum_scatter(first_gain_grad, ("fsdp", "ctx"), scatter_dimension=0, tiled=True),
        lax.psum_scatter(first_shift_grad, ("fsdp", "ctx"), scatter_dimension=0, tiled=True),
        lax.psum_scatter(expand_grad, ("fsdp", "ctx"), scatter_dimension=0, tiled=True),
        lax.psum_scatter(expand_bias_grad, ("fsdp", "ctx"), scatter_dimension=0, tiled=True),
        lax.psum_scatter(reduce_grad, ("fsdp", "ctx"), scatter_dimension=0, tiled=True),
        lax.psum_scatter(reduce_bias_grad, ("fsdp", "ctx"), scatter_dimension=0, tiled=True),
        lax.psum_scatter(second_gain_grad, ("fsdp", "ctx"), scatter_dimension=0, tiled=True),
        lax.psum_scatter(second_shift_grad, ("fsdp", "ctx"), scatter_dimension=0, tiled=True),
    )
    return (
        layer_out,
        input_grad,
        shares[0],
        shares[1],
        shares[2],
        shares[3],
        shares[4],
        shares[5],
        shares[6],
        shares[7],
        shares[8],
        shares[9],
        shares[10],
        shares[11],
        shares[12],
        shares[13],
        shares[14],
    )


MESH = pl.DeviceIdType.MESH
MIB = 1024*1024

def place():
    core = lax.axis_index("fsdp"); chip = lax.axis_index("ctx")
    return core, chip

def greet(peers):
    barrier = pltpu.get_barrier_semaphore()
    for peer in peers:
        pl.semaphore_signal(barrier, inc=1, device_id=peer, device_id_type=MESH)
    pl.semaphore_wait(barrier, len(peers))

def flip(v, bits):
    for b in (1, 2, 4, 8):
        if bits & b:
            v = v + b - 2 * b * lax.rem(lax.div(v, b), 2)
    return v

LOG2E = math.log2(math.e)


def nt(a, b):
    return lax.dot_general(a, b, (((1,), (1,)), ((), ())), preferred_element_type=jnp.float32)


FULL_ORDER = (12, 8, 4, 15, 11, 7, 14, 13, 10, 9, 6, 5, 3, 2, 1)


class Copies:
    def __init__(self, send_sem, recv_sem):
        self.send_sem, self.recv_sem = send_sem, recv_sem
        self.names, self.sent = {}, []

    def pair(self, name, src, dst, peer):
        i = self.names.setdefault(name, len(self.names))
        return pltpu.make_async_remote_copy(
            src_ref=src,
            dst_ref=dst,
            send_sem=self.send_sem.at[i],
            recv_sem=self.recv_sem.at[i],
            device_id=peer,
            device_id_type=MESH,
        )

    def send(self, name, src, dst, peer, like):
        self.pair(name, src, dst, peer).start()
        self.sent.append((name, like))

    def arrived(self, name, dst, peer):
        self.pair(name, dst, dst, peer).wait_recv()

    def drain(self, peer):
        for name, like in self.sent:
            self.pair(name, like, like, peer).wait_send()


class Gather:
    def __init__(self, copies, name, src, out, local_sem):
        self.copies, self.name, self.src, self.out, self.local_sem = copies, name, src, out, local_sem
        self.core, self.chip = place()
        self.sib = (1 - self.core, self.chip)
        self.half = src.shape[0] // 2

    def at(self, bits):
        return (self.core, flip(self.chip, bits))

    def block(self, bits, core=None):
        return self.out.at[(self.core if core is None else core) * 16 + flip(self.chip, bits)]

    def part(self, bits, upper):
        return self.out.at[self.core * 16 + flip(self.chip, bits), pl.ds(self.half if upper else 0, self.half)]

    def send(self, tag, src, dst, peer, half=False):
        like = self.src.at[pl.ds(0, self.half)] if half else self.src
        self.copies.send((self.name, tag), src, dst, peer, like)

    def arrived(self, tag, dst):
        self.copies.arrived((self.name, tag), dst, self.sib)

    def start_z(self):
        for z in (12, 8, 4):
            self.send(("z", z), self.src, self.block(0), self.at(z))

    def start_plane(self):
        self.send(("x", 0), self.src, self.block(0), self.at(1))
        self.send(("y", 0), self.src, self.block(0), self.at(2))
        self.send(("s", 0), self.src, self.block(0), self.sib)
        self.local = pltpu.make_async_copy(self.src, self.block(0), self.local_sem)
        self.local.start()

    def on_z(self, z):
        b = self.block(z)
        self.arrived(("z", z), b)
        self.send(("x", z), b, b, self.at(1))
        self.send(("y", z), b, b, self.at(2))
        self.send(("s", z), b, b, self.sib)

    def on_plane(self, z):
        for bit, tag, further, upper in ((1, "x", 2, False), (2, "y", 1, True)):
            b = self.block(z + bit)
            self.arrived((tag, z), b)
            h = self.part(z + bit, upper)
            self.send(("d" + tag, z), h, h, self.at(further), True)
            self.send(("s", z + bit), b, b, self.sib)

    def on_diagonal(self, z):
        self.arrived(("dx", z), self.part(z + 3, False))
        self.arrived(("dy", z), self.part(z + 3, True))
        b = self.block(z + 3)
        self.send(("s", z + 3), b, b, self.sib)

    def on_sibling(self):
        for bits in range(16):
            self.arrived(("s", bits), self.block(bits, 1 - self.core))
        self.local.wait()


def load_sequence(r_ref, s, kk_ref, vt_ref=None, vv_ref=None):
    for j in range(r_ref.shape[1]):
        span = pl.ds(j * 128, 128)
        kk_ref[span] = r_ref[s, j, 64:128, :].astype(jnp.float32).T.astype(jnp.bfloat16)
        if vt_ref is not None:
            vt_ref[:, span] = r_ref[s, j, 128:192, :]
        if vv_ref is not None:
            vv_ref[span] = r_ref[s, j, 128:192, :].astype(jnp.float32).T.astype(jnp.bfloat16)


def fwd_kernel(
    x_ref, lengths_ref, s_qkv, s_bias, s_vec, s_out, s_expand, s_reduce,
    o_vec, o_out, o_expand, o_reduce, o_qkv, o_pairs, o_ctx, o_full, lse_ref,
    w_qkv, w_bias, send_blk, recv_blk, ctx_blk, ctx_recv, kk, vt,
    send_sem, recv_sem, local_sem, hsend, hrecv, csend, crecv,
):
    f32, bf16 = jnp.float32, jnp.bfloat16
    core, chip = place()
    sib = (1 - core, chip)
    greet([sib] + [(core, flip(chip, b)) for b in range(1, 16)])
    copies = Copies(send_sem, recv_sem)
    first = [
        Gather(copies, 0, s_qkv, w_qkv, local_sem.at[0]),
        Gather(copies, 1, s_bias, w_bias, local_sem.at[1]),
    ]
    rest = [
        Gather(copies, 2, s_out, o_out, local_sem.at[2]),
        Gather(copies, 3, s_vec, o_vec, local_sem.at[3]),
        Gather(copies, 4, s_expand, o_expand, local_sem.at[4]),
        Gather(copies, 5, s_reduce, o_reduce, local_sem.at[5]),
    ]
    for g in first:
        g.start_z()
        g.start_plane()
    for z in (4, 8, 12):
        for g in first:
            g.on_z(z)
    for g in rest[:3]:
        g.start_z()
    for z in (0, 4, 8, 12):
        for g in first:
            g.on_plane(z)
    for z in (0, 4, 8, 12):
        for g in first:
            g.on_diagonal(z)
    for g in first:
        g.on_sibling()
    keep = pltpu.make_async_copy(w_qkv, o_qkv, local_sem.at[6])
    keep.start()

    @pl.loop(0, 8)
    def _(p):
        w = w_qkv[:, :, pl.ds(pl.multiple_of(p * 384, 128), 384)].reshape(1024, 384)
        t = jnp.dot(x_ref[...], w, preferred_element_type=f32).T
        for i in range(2):
            h = 2 * p + i
            for part in range(3):
                rows = t[192 * i + 64 * part : 192 * i + 64 * part + 64]
                if part != 1:
                    bias = jnp.concatenate([w_bias[2 * h + k, pl.ds(0 if part == 0 else 32, 32)] for k in range(2)], 0).astype(f32)
                    rows = rows + jnp.concatenate([bias, bias], 1)
                send_blk[h, pl.ds(64 * part, 64)] = rows.astype(bf16)

    heads = []
    for s in range(2):
        for b in FULL_ORDER:
            to = flip(chip, b)
            i = s * 16 + b
            c = pltpu.make_async_remote_copy(
                src_ref=send_blk.at[to, :, pl.ds(128 * s, 128)],
                dst_ref=recv_blk.at[s, chip],
                send_sem=hsend.at[i],
                recv_sem=hrecv.at[i],
                device_id=(core, to),
                device_id_type=MESH,
            )
            c.start()
            heads.append(c)
        recv_blk[s, chip] = send_blk[chip, :, pl.ds(128 * s, 128)]

    def heads_here(s):
        for b in FULL_ORDER:
            i = s * 16 + b
            here = recv_blk.at[s, flip(chip, b)]
            pltpu.make_async_remote_copy(
                src_ref=here, dst_ref=here, send_sem=hsend.at[i], recv_sem=hrecv.at[i], device_id=sib, device_id_type=MESH
            ).wait_recv()

    for g in rest:
        g.start_plane()
    rest[3].start_z()
    events = []
    for z in (4, 8, 12):
        events.append(lambda z=z: [g.on_z(z) for g in rest[:3]])
    events.append(lambda: [g.on_plane(0) for g in rest])
    events.append(lambda: [g.on_diagonal(0) for g in rest])
    for z in (4, 8, 12):
        events.append(lambda z=z: [g.on_plane(z) for g in rest[:3]])
    for z in (4, 8, 12):
        events.append(lambda z=z: [rest[3].on_z(z)])
    for z in (4, 8, 12):
        events.append(lambda z=z: [g.on_diagonal(z) for g in rest[:3]])
    for z in (4, 8, 12):
        events.append(lambda z=z: [rest[3].on_plane(z)])
    for z in (4, 8, 12):
        events.append(lambda z=z: [rest[3].on_diagonal(z)])
    events.append(lambda: [g.on_sibling() for g in rest])

    def attend_sequence(s, during):
        load_sequence(recv_blk, s, kk, vt_ref=vt)

        @pl.loop(0, 8)
        def _(step):
            for k, event in enumerate(during):

                @pl.when(step == k)
                def _():
                    event()

            q = flip_by(step, chip // 2)
            query = jnp.concatenate([recv_blk[s, 2 * q, 0:64, :], recv_blk[s, 2 * q + 1, 0:64, :]], 1)
            scores = jnp.dot(kk[...], query, preferred_element_type=f32) * (0.125 * LOG2E)
            key = lax.broadcasted_iota(jnp.int32, scores.shape, 0)
            scores = jnp.where(key < lengths_ref[s], scores, masked_score)
            top = jnp.max(scores, 0, keepdims=True)
            e = jnp.exp2(scores - top)
            mass = jnp.sum(e, 0, keepdims=True)
            o = jnp.dot(vt[...], e.astype(bf16), preferred_element_type=f32) / mass
            lse_ref[s, pl.ds(q, 1), :] = top + jnp.log2(mass)
            o_full[s, :, pl.ds(pl.multiple_of(q * 256, 256), 256)] = o
            for i in range(2):
                to = 2 * q + i
                ctx_blk[s, to] = o[:, 128 * i : 128 * i + 128].astype(bf16)

                @pl.when(to != chip)
                def _():
                    pltpu.make_async_remote_copy(
                        src_ref=ctx_blk.at[s, to],
                        dst_ref=ctx_recv.at[chip, :, pl.ds(128 * s, 128)],
                        send_sem=csend.at[s * 16 + to],
                        recv_sem=crecv.at[s * 16 + chip],
                        device_id=(core, to),
                        device_id_type=MESH,
                    ).start()

        ctx_recv[chip, :, pl.ds(128 * s, 128)] = ctx_blk[s, chip]

    PRE, FIRST, SECOND = 2, 2, 6
    for event in events[:PRE]:
        event()
    heads_here(0)
    attend_sequence(0, events[PRE : PRE + FIRST])
    heads_here(1)
    pairs_out = pltpu.make_async_copy(recv_blk, o_pairs, local_sem.at[7])
    pairs_out.start()
    attend_sequence(1, events[PRE + FIRST : PRE + FIRST + SECOND])
    for event in events[PRE + FIRST + SECOND :]:
        event()
    for s in range(2):
        for b in range(1, 16):
            other = flip(chip, b)
            here = ctx_recv.at[other, :, pl.ds(128 * s, 128)]
            pltpu.make_async_remote_copy(
                src_ref=ctx_blk.at[s, other],
                dst_ref=here,
                send_sem=csend.at[s * 16 + other],
                recv_sem=crecv.at[s * 16 + other],
                device_id=sib,
                device_id_type=MESH,
            ).wait()
    ctx_out = pltpu.make_async_copy(ctx_recv, o_ctx, local_sem.at[8])
    ctx_out.start()
    for c in heads:
        c.wait_send()
    copies.drain(sib)
    keep.wait()
    pairs_out.wait()
    ctx_out.wait()


def flip_by(v, w):
    out = 0
    for b in (1, 2, 4):
        p, q = lax.rem(lax.div(v, b), 2), lax.rem(lax.div(w, b), 2)
        out = out + b * (p + q - 2 * p * q)
    return out


def forward_attention(rows, lengths, qkv, bias, vec, w_out, w_expand, w_reduce, collective_id):
    v, hbm = pl.BlockSpec(memory_space=pltpu.VMEM), pl.BlockSpec(memory_space=pl.ANY)
    f32, bf16 = jnp.float32, jnp.bfloat16
    gathered = lambda x: jax.ShapeDtypeStruct((32,) + x.shape, x.dtype)
    dma = pltpu.SemaphoreType.DMA
    return pl.pallas_call(
        fwd_kernel,
        out_shape=[
            gathered(vec),
            gathered(w_out),
            gathered(w_expand),
            gathered(w_reduce),
            gathered(qkv),
            jax.ShapeDtypeStruct((2, 16, 192, 128), bf16),
            jax.ShapeDtypeStruct((16, 64, 256), bf16),
            jax.ShapeDtypeStruct((2, 64, 2048), f32),
            jax.ShapeDtypeStruct((2, 8, 256), f32),
        ],
        in_specs=[v, pl.BlockSpec(memory_space=pltpu.SMEM)] + [hbm] * 6,
        out_specs=[hbm] * 7 + [v, v],
        scratch_shapes=[
            pltpu.VMEM((32,) + qkv.shape, bf16),
            pltpu.VMEM((32,) + bias.shape, bf16),
            pltpu.VMEM((16, 192, 256), bf16),
            pltpu.VMEM((2, 16, 192, 128), bf16),
            pltpu.VMEM((2, 16, 64, 128), bf16),
            pltpu.VMEM((16, 64, 256), bf16),
            pltpu.VMEM((2048, 64), bf16),
            pltpu.VMEM((64, 2048), bf16),
            dma((210,)),
            dma((210,)),
            dma((9,)),
            dma((32,)),
            dma((32,)),
            dma((32,)),
            dma((32,)),
        ],
        compiler_params=pltpu.CompilerParams(
            collective_id=collective_id, has_side_effects=True, vmem_limit_bytes=56 * MIB
        ),
        name="forward_attention",
    )(rows, lengths, qkv, bias, vec, w_out, w_expand, w_reduce)


class Scatter:
    ORDER = (12, 8, 4, 0)

    def __init__(self, copies, name, grads, out, bufs):
        self.copies, self.name, self.grads, self.out = copies, name, grads, out
        self.first, self.second, self.third, self.passed = bufs
        self.core, self.chip = place()
        self.rows = grads.shape[1]
        self.half = self.rows // 2
        self.lo, self.hi = pl.ds(0, self.half), pl.ds(self.half, self.half)
        self.first_at = [[self.first.at[k, i] for i in range(2)] for k in range(4)]
        self.second_at = [[self.second.at[k, i] for i in range(2)] for k in range(4)]
        self.third_at = [self.third.at[k] for k in range(3)]
        self.passed_at = [self.passed.at[k] for k in range(3)]

    def at(self, bits):
        return (self.core, flip(self.chip, bits))

    def send(self, tag, src, dst, bits, half=True):
        like = self.first_at[0][0] if half else self.passed_at[0]
        self.copies.send((self.name, tag), src, dst, self.at(bits), like)

    def arrived(self, tag, dst):
        self.copies.arrived((self.name, tag), dst, self.at(1))

    def add(self, rows, fn):
        step = min(rows, 16)
        if rows == step:
            fn(0, step)
            return

        def turn(i, carry):
            fn(pl.multiple_of(i * step, step), step)
            return carry

        lax.fori_loop(0, rows // step, turn, 0)

    def start(self):
        for k, z in enumerate(self.ORDER):
            diag = flip(self.chip, z + 3)
            self.send(("1a", k), self.grads.at[diag, self.lo], self.first_at[k][0], 2)
            self.send(("1b", k), self.grads.at[diag, self.hi], self.first_at[k][1], 1)

    def start_direct(self):
        for k, z in enumerate(self.ORDER):
            xb, yb = flip(self.chip, z + 1), flip(self.chip, z + 2)
            self.send(("2xh", k), self.grads.at[xb, self.hi], self.second_at[k][0].at[self.hi], 1)
            self.send(("2yl", k), self.grads.at[yb, self.lo], self.second_at[k][1].at[self.lo], 2)

    def on_first(self, k):
        z = self.ORDER[k]
        for i, (tag, bit, upper) in enumerate((("1a", 1, False), ("1b", 2, True))):
            owner = flip(self.chip, z + bit)
            here = self.first_at[k][i]
            self.arrived((tag, k), here)

            def fn(start, size):
                rows = pl.ds(start, size)
                theirs = pl.ds(start + (self.half if upper else 0), size)
                here[rows] = here[rows] + self.grads.at[owner][theirs]

            self.add(self.half, fn)
            self.send(("2" + "xy"[i] + "lh"[i], k), here, self.second_at[k][i].at[self.hi if upper else self.lo], bit)

    def on_second(self, k):
        z = self.ORDER[k]
        self.arrived(("2xh", k), self.second_at[k][0].at[self.hi])
        self.arrived(("2yl", k), self.second_at[k][1].at[self.lo])
        self.arrived(("2xl", k), self.second_at[k][0].at[self.lo])
        self.arrived(("2yh", k), self.second_at[k][1].at[self.hi])
        owner = flip(self.chip, z)

        def fn(start, size):
            rows = pl.ds(start, size)
            f32 = jnp.float32
            total = self.grads.at[owner][rows].astype(f32) + self.second_at[k][0][rows].astype(f32)
            total = total + self.second_at[k][1][rows].astype(f32)
            if k < 3:
                self.passed_at[k][rows] = total.astype(self.passed.dtype)
            else:
                self.out[rows] = total

        self.add(self.rows, fn)
        if k < 3:
            self.send(("3", k), self.passed_at[k], self.third_at[k], z, False)

    def on_third(self):
        for k in range(3):
            self.arrived(("3", k), self.third_at[k])

        def fn(start, size):
            rows = pl.ds(start, size)
            total = self.out[rows]
            for k in range(3):
                total = total + self.third_at[k][rows].astype(jnp.float32)
            self.out[rows] = total

        self.add(self.rows, fn)


def scatter_buffers(block, dtype):
    rows, cols = block
    return [
        pltpu.VMEM((4, 2, rows // 2, cols), dtype),
        pltpu.VMEM((4, 2, rows, cols), dtype),
        pltpu.VMEM((3, rows, cols), dtype),
        pltpu.VMEM((3, rows, cols), dtype),
    ]


def bwd_kernel(*refs):
    f32, bf16 = jnp.float32, jnp.bfloat16
    (lengths_ref, pairs, o_full, lse_ref, d_ctx, x_t, d_first, g_reduce, g_expand, g_out, g_vec, h_qkv) = refs[:12]
    (o_reduce, o_expand, o_out, o_vec, o_qkv, o_input, o_bias) = refs[12:19]
    bufs = [refs[19 + 4 * i : 23 + 4 * i] for i in range(5)]
    (
        g_qkv, w_qkv, d_recv, kk, vv, kt, acc, d_send, d_own, d_sib, b_own, b_sib, b_in,
        send_sem, recv_sem, local_sem, dsend, drecv, qsend, qrecv,
    ) = refs[39:]
    core, chip = place()
    sib = (1 - core, chip)
    greet([sib] + [(core, flip(chip, b)) for b in range(1, 16)])
    copies = Copies(send_sem, recv_sem)
    rest = [
        Scatter(copies, i, g, o, bufs[i])
        for i, (g, o) in enumerate(((g_reduce, o_reduce), (g_expand, o_expand), (g_out, o_out), (g_vec, o_vec)))
    ]
    last = Scatter(copies, 4, g_qkv, o_qkv, bufs[4])
    weights = pltpu.make_async_copy(h_qkv, w_qkv, local_sem.at[0])
    weights.start()
    sent = []

    def exchange_out(s, b, src, dst, sends, recvs):
        c = pltpu.make_async_remote_copy(
            src_ref=src,
            dst_ref=dst,
            send_sem=sends.at[s * 16 + b],
            recv_sem=recvs.at[s * 16 + b],
            device_id=(core, flip(chip, b)),
            device_id_type=MESH,
        )
        c.start()
        sent.append(c)

    def exchange_in(s, b, here, sends, recvs):
        pltpu.make_async_remote_copy(
            src_ref=here,
            dst_ref=here,
            send_sem=sends.at[s * 16 + b],
            recv_sem=recvs.at[s * 16 + b],
            device_id=sib,
            device_id_type=MESH,
        ).wait_recv()

    for s in range(2):
        lane = pl.ds(128 * s, 128)
        for b in FULL_ORDER:
            exchange_out(s, b, d_ctx.at[flip(chip, b), :, lane], d_recv.at[s, chip], dsend, drecv)
        d_recv[s, chip] = d_ctx[chip, :, lane]
    for r in rest:
        r.start()
    for r in rest:
        r.start_direct()
    b_own[...] = jnp.zeros_like(b_own)

    def back_sequence(s, during):
        load_sequence(pairs, s, kk, vt_ref=None, vv_ref=vv)
        for j in range(16):
            kt[:, pl.ds(j * 128, 128)] = pairs[s, j, 64:128, :]
        acc[...] = jnp.zeros_like(acc)

        @pl.loop(0, 8)
        def _(q):
            for k, event in enumerate(during):

                @pl.when(q == k)
                def _():
                    event()

            both = lambda ref, lo, hi: jnp.concatenate([ref[s, 2 * q, lo:hi, :], ref[s, 2 * q + 1, lo:hi, :]], 1)
            query, d_out = both(pairs, 0, 64), both(d_recv, 0, 64)
            span = pl.ds(pl.multiple_of(q * 256, 256), 256)
            delta = jnp.sum(d_out.astype(f32) * o_full[s, :, span], 0, keepdims=True)
            scores = jnp.dot(kk[...], query, preferred_element_type=f32) * (0.125 * LOG2E)
            key = lax.broadcasted_iota(jnp.int32, scores.shape, 0)
            probs = jnp.where(key < lengths_ref[s], jnp.exp2(scores - lse_ref[s, pl.ds(q, 1), :]), 0.0)
            d_probs = jnp.dot(vv[...], d_out, preferred_element_type=f32)
            d_scores = (probs * (d_probs - delta)).astype(bf16)
            zero = jnp.zeros((64, 256), f32)
            query_rows = jnp.concatenate([query.astype(f32), zero], 0).T.astype(bf16)
            d_rows = jnp.concatenate([zero, d_out.astype(f32)], 0).T.astype(bf16)
            acc[...] += jnp.dot(d_scores, query_rows, preferred_element_type=f32) + jnp.dot(
                probs.astype(bf16), d_rows, preferred_element_type=f32
            )
            d_query = (jnp.dot(kt[...], d_scores, preferred_element_type=f32) * 0.125).astype(bf16)
            for i in range(2):
                part = d_query[:, 128 * i : 128 * i + 128]
                d_send[s, 2 * q + i, 0:64, :] = part
                b_own[0] += part.astype(f32)

        for j in range(16):
            t = acc[pl.ds(j * 128, 128)].T
            d_send[s, j, 64:128, :] = (t[:64] * 0.125).astype(bf16)
            value = t[64:].astype(bf16)
            d_send[s, j, 128:192, :] = value
            b_own[1] += value.astype(f32)
        lane = pl.ds(128 * s, 128)
        for b in FULL_ORDER:
            exchange_out(s, b, d_send.at[s, flip(chip, b)], d_own.at[chip, :, lane], qsend, qrecv)
        d_own[chip, :, lane] = d_send[s, chip]

    events = [lambda k=k: [r.on_first(k) for r in rest] for k in range(4)]
    events += [lambda k=k: [r.on_second(k) for r in rest] for k in range(4)]
    FIRST, SECOND, WAIT = 0, 4, 2
    for b in FULL_ORDER:
        exchange_in(0, b, d_recv.at[0, flip(chip, b)], dsend, drecv)
    back_sequence(0, events[:FIRST])
    for b in FULL_ORDER:
        exchange_in(1, b, d_recv.at[1, flip(chip, b)], dsend, drecv)
    back_sequence(1, events[FIRST : FIRST + SECOND])

    copies.send("bias sib", b_own, b_sib, sib, b_own)
    for event in events[FIRST + SECOND : FIRST + SECOND + WAIT]:
        event()
    for s in range(2):
        lane = pl.ds(128 * s, 128)
        for b in FULL_ORDER:
            exchange_in(s, b, d_own.at[flip(chip, b), :, lane], qsend, qrecv)
        copies.send(("rows", s), d_own.at[:, :, lane], d_sib.at[:, :, lane], sib, d_own.at[:, :, lane])

    copies.arrived("bias sib", b_sib, sib)
    for s in range(2):
        copies.arrived(("rows", s), d_sib.at[:, :, pl.ds(128 * s, 128)], sib)

    @pl.loop(0, 8)
    def _(p):
        total = None
        for i, rows in enumerate((d_own, d_sib)):
            term = nt(x_t[:, 256 * i : 256 * i + 256], rows[pl.ds(2 * p, 2)].reshape(384, 256))
            total = term if total is None else total + term
        g_qkv[:, :, pl.ds(pl.multiple_of(p * 384, 128), 384)] = total.astype(bf16).reshape(16, 32, 384)

    last.start()
    last.start_direct()

    b_sib[...] = b_sib[...] + b_own[...]
    sender = core == lax.div(chip, 8)
    for i in range(2):
        to = lax.rem(2 * chip + i, 16)
        rows = pl.ds(32 * i, 32)
        c = pltpu.make_async_remote_copy(
            src_ref=b_sib.at[:, rows],
            dst_ref=b_in,
            send_sem=local_sem.at[1 + i],
            recv_sem=local_sem.at[3],
            device_id=(core, to),
            device_id_type=MESH,
        )

        @pl.when(sender & (to != chip))
        def _():
            c.start()

        @pl.when(sender & (to == chip))
        def _():
            b_in[...] = b_sib[:, rows]

    weights.wait()

    @pl.loop(0, 4)
    def _(i):
        w = w_qkv[pl.ds(i * 8, 8)].reshape(256, 3072)
        t = jnp.dot(w, d_own[...].reshape(3072, 256), preferred_element_type=f32).T
        cols = pl.ds(pl.multiple_of(i * 256, 256), 256)
        o_input[:, cols] = d_first[:, cols] + t

    for event in events[FIRST + SECOND + WAIT :]:
        event()
    for k in range(4):
        last.on_first(k)
    for r in rest:
        r.on_third()
    for k in range(4):
        last.on_second(k)
    last.on_third()
    for i in range(2):
        to = lax.rem(2 * chip + i, 16)

        @pl.when(sender & (to != chip))
        def _():
            pltpu.make_async_remote_copy(
                src_ref=b_sib.at[:, pl.ds(32 * i, 32)],
                dst_ref=b_in,
                send_sem=local_sem.at[1 + i],
                recv_sem=local_sem.at[3],
                device_id=(core, to),
                device_id_type=MESH,
            ).wait_send()

    @pl.when(8 * core + lax.div(chip, 2) != chip)
    def _():
        pltpu.make_async_remote_copy(
            src_ref=b_in, dst_ref=b_in, send_sem=local_sem.at[1], recv_sem=local_sem.at[3], device_id=sib, device_id_type=MESH
        ).wait_recv()

    o_bias[...] = b_in[...]
    for c in sent:
        c.wait_send()
    copies.drain(sib)


def backward_attention(lengths, pairs, o_full, lse, d_ctx, x_t, d_first, grads, w_qkv, collective_id):
    v, hbm = pl.BlockSpec(memory_space=pltpu.VMEM), pl.BlockSpec(memory_space=pl.ANY)
    f32, bf16 = jnp.float32, jnp.bfloat16
    dma = pltpu.SemaphoreType.DMA
    blocks = [(g.shape[1:], g.dtype) for g in grads] + [((32, 3072), bf16)]
    bufs = []
    for block, dtype in blocks:
        bufs += scatter_buffers(block, dtype)
    return pl.pallas_call(
        bwd_kernel,
        out_shape=[jax.ShapeDtypeStruct(block, f32) for block, _ in blocks]
        + [jax.ShapeDtypeStruct(d_first.shape, f32), jax.ShapeDtypeStruct((2, 32, 128), f32)],
        in_specs=[pl.BlockSpec(memory_space=pltpu.SMEM)] + [v] * 10 + [hbm],
        out_specs=[v] * 7,
        scratch_shapes=bufs
        + [
            pltpu.VMEM((16, 32, 3072), bf16),
            pltpu.VMEM((32, 32, 3072), bf16),
            pltpu.VMEM((2, 16, 64, 128), bf16),
            pltpu.VMEM((2048, 64), bf16),
            pltpu.VMEM((2048, 64), bf16),
            pltpu.VMEM((64, 2048), bf16),
            pltpu.VMEM((2048, 128), f32),
            pltpu.VMEM((2, 16, 192, 128), bf16),
            pltpu.VMEM((16, 192, 256), bf16),
            pltpu.VMEM((16, 192, 256), bf16),
            pltpu.VMEM((2, 64, 128), f32),
            pltpu.VMEM((2, 64, 128), f32),
            pltpu.VMEM((2, 32, 128), f32),
            dma((140,)),
            dma((140,)),
            dma((4,)),
            dma((32,)),
            dma((32,)),
            dma((32,)),
            dma((32,)),
        ],
        compiler_params=pltpu.CompilerParams(
            collective_id=collective_id, has_side_effects=True, vmem_limit_bytes=62 * MIB
        ),
        name="backward_attention",
    )(lengths, pairs, o_full, lse, d_ctx, x_t, d_first, *grads, w_qkv)


def swap(x):
    return lax.ppermute(x, "fsdp", [(0, 1), (1, 0)])


def halves(left_t):
    core = lax.axis_index("fsdp")
    h = left_t.shape[0] // 2
    own = lax.dynamic_slice_in_dim(left_t, core * h, h, 0)
    return own, swap(lax.dynamic_slice_in_dim(left_t, (1 - core) * h, h, 0))


def chip_sum(left, right):
    core = lax.axis_index("fsdp")
    h = left.shape[1] // 2
    own = lax.dynamic_slice_in_dim(left, core * h, h, 1)
    other = swap(lax.dynamic_slice_in_dim(left, (1 - core) * h, h, 1))
    grad = outer_sum(own, right) + outer_sum(other, swap(right))
    return grad.astype(jnp.bfloat16).reshape(16, h // 16, right.shape[1])


def fast_shards(
    inputs,
    lengths,
    w_query,
    b_query,
    w_key,
    w_value,
    b_value,
    w_out,
    b_out,
    first_gain,
    first_shift,
    w_expand,
    b_expand,
    w_reduce,
    b_reduce,
    second_gain,
    second_shift,
    cotangent,
):
    core = lax.axis_index("fsdp")
    f32, bf16 = jnp.float32, jnp.bfloat16
    seqs, count, width = inputs.shape
    total = seqs * count
    part = width // 32
    ff = w_expand.shape[1]
    qkv = jnp.concatenate([w.reshape(part, HEADS, 64) for w in (w_query, w_key, w_value)], -1).reshape(part, 3 * width)
    bias = jnp.concatenate([b_query, b_value])[:, None] + jnp.zeros((2 * part, 128), bf16)
    small = [b_out, first_gain, first_shift, b_expand, b_reduce, second_gain, second_shift]
    sizes = [b.shape[0] for b in small]
    vec = jnp.concatenate(small + [jnp.zeros((part * 128 - sum(sizes),), bf16)]).reshape(part, 128)
    flat_rows = inputs.reshape(total, width)
    g_vec, g_out, g_expand, g_reduce, g_qkv, pairs, context_t, o_full, lse = forward_attention(
        flat_rows, lengths, qkv, bias, vec, w_out, w_expand, w_reduce, 1
    )
    full_out = g_out.reshape(width, width)
    full_expand = g_expand.reshape(width, ff)
    full_reduce = g_reduce.reshape(ff, width)
    flat_vec = g_vec.reshape(32, part * 128)
    offsets = [sum(sizes[:i]) for i in range(len(sizes) + 1)]
    (bias_out, gain_first, shift_first, bias_expand, bias_reduce, gain_second, shift_second) = [
        flat_vec[:, offsets[i] : offsets[i + 1]].reshape(-1).astype(f32) for i in range(len(sizes))
    ]
    own_first = lax.axis_index("ctx") * count
    positions = own_first + jnp.arange(count, dtype=jnp.int32)
    valid_rows = (positions[None, :] < lengths[:, None]).astype(f32).reshape(total, 1)
    context_t = context_t.reshape(width, total)
    attended = outer_sum(context_t, full_out) + bias_out
    residual = flat_rows.astype(f32) + attended
    normed, first_pull = jax.vjp(layer_norm, residual, gain_first, shift_first)
    normed_low = normed.astype(bf16)
    expanded = product(normed_low, full_expand) + bias_expand
    activated, gelu_pull = jax.vjp(partial(jax.nn.gelu, approximate=False), expanded)
    activated_low = activated.astype(bf16)
    reduced = product(activated_low, full_reduce) + bias_reduce
    final_rows, second_pull = jax.vjp(layer_norm, normed + reduced, gain_second, shift_second)
    layer_out = (final_rows * valid_rows).astype(bf16).reshape(inputs.shape)
    d_output = cotangent.reshape(total, width).astype(f32) * valid_rows
    d_second, second_gain_grad, second_shift_grad = second_pull(d_output)
    d_reduced = d_second.astype(bf16)
    reduce_grad = chip_sum(activated_low, d_reduced)
    reduce_bias_grad = jnp.sum(d_reduced.astype(f32), 0)
    (d_expanded_full,) = gelu_pull(back_product(d_reduced, full_reduce))
    d_expanded = d_expanded_full.astype(bf16)
    expand_grad = chip_sum(normed_low, d_expanded)
    expand_bias_grad = jnp.sum(d_expanded.astype(f32), 0)
    d_normed = d_second + back_product(d_expanded, full_expand)
    d_first, first_gain_grad, first_shift_grad = first_pull(d_normed)
    d_attended = d_first.astype(bf16)
    context_own, context_other = halves(context_t)
    out_grad = product(context_own, d_attended) + product(context_other, swap(d_attended))
    out_grad = out_grad.astype(bf16).reshape(16, part, width)
    out_bias_grad = jnp.sum(d_attended.astype(f32), 0)
    d_context_t = back_product(full_out, d_attended).astype(bf16).reshape(HEADS, 64, total)
    x_t = jnp.concatenate(halves(flat_rows.T), 1)
    small_grads = jnp.concatenate(
        [
            g.reshape(32, -1)
            for g in (
                out_bias_grad,
                first_gain_grad,
                first_shift_grad,
                expand_bias_grad,
                reduce_bias_grad,
                second_gain_grad,
                second_shift_grad,
            )
        ]
        + [jnp.zeros((32, 2048 - sum(sizes)), f32)],
        1,
    ).reshape(2, 16, 16, 128)
    vec_grad = lax.dynamic_index_in_dim(small_grads, core, 0, False) + swap(
        lax.dynamic_index_in_dim(small_grads, 1 - core, 0, False)
    )
    s_reduce, s_expand, s_out, s_vec, s_qkv, input_grad, s_bias = backward_attention(
        lengths, pairs, o_full, lse, d_context_t, x_t, d_first, [reduce_grad, expand_grad, out_grad, vec_grad], g_qkv, 2
    )
    s_qkv = s_qkv.reshape(part, HEADS, 3, 64)
    s_query, s_key, s_value = (s_qkv[:, :, i].reshape(part, width) for i in range(3))
    s_bias = jnp.sum(s_bias, -1)
    s_vec = s_vec.reshape(-1)
    v = [s_vec[offsets[i] : offsets[i + 1]] for i in range(len(sizes))]
    return (
        layer_out,
        input_grad.reshape(inputs.shape),
        s_query,
        s_bias[0],
        s_key,
        s_value,
        s_bias[1],
        s_out,
        v[0],
        v[1],
        v[2],
        s_expand,
        v[3],
        s_reduce,
        v[4],
        v[5],
        v[6],
    )


def solution(mesh):
    fast = mesh.shape["fsdp"] == 2 and mesh.shape["ctx"] == HEADS
    shards = fast_shards if fast else general_shards
    return jax.shard_map(
        shards,
        mesh=mesh,
        in_specs=(
            P("fsdp", "ctx", None),
            P("fsdp"),
            P(("fsdp", "ctx"), None),
            P(("fsdp", "ctx")),
            P(("fsdp", "ctx"), None),
            P(("fsdp", "ctx"), None),
            P(("fsdp", "ctx")),
            P(("fsdp", "ctx"), None),
            P(("fsdp", "ctx")),
            P(("fsdp", "ctx")),
            P(("fsdp", "ctx")),
            P(("fsdp", "ctx"), None),
            P(("fsdp", "ctx")),
            P(("fsdp", "ctx"), None),
            P(("fsdp", "ctx")),
            P(("fsdp", "ctx")),
            P(("fsdp", "ctx")),
            P("fsdp", "ctx", None),
        ),
        out_specs=(
            P("fsdp", "ctx", None),
            P("fsdp", "ctx", None),
            P(("fsdp", "ctx"), None),
            P(("fsdp", "ctx")),
            P(("fsdp", "ctx"), None),
            P(("fsdp", "ctx"), None),
            P(("fsdp", "ctx")),
            P(("fsdp", "ctx"), None),
            P(("fsdp", "ctx")),
            P(("fsdp", "ctx")),
            P(("fsdp", "ctx")),
            P(("fsdp", "ctx"), None),
            P(("fsdp", "ctx")),
            P(("fsdp", "ctx"), None),
            P(("fsdp", "ctx")),
            P(("fsdp", "ctx")),
            P(("fsdp", "ctx")),
        ),
        check_vma=False,
    )
```

```python
from functools import partial
import math

import jax
import jax.numpy as jnp
from jax import lax
from jax.experimental import pallas as pl
from jax.experimental.pallas import tpu as pltpu
from jax.sharding import PartitionSpec as P

HEADS = 16


epsilon = 1e-05
masked_score = -1e30


def layer_norm(rows_in, gain, shift):
    center = rows_in - jnp.mean(rows_in, -1, keepdims=True)
    spread = jnp.mean(center * center, -1, keepdims=True)
    return center * lax.rsqrt(spread + epsilon) * gain + shift


def product(left, right):
    return jnp.dot(left, right, preferred_element_type=jnp.float32)


def outer_sum(left, right):
    return jnp.einsum("rd,re->de", left, right, preferred_element_type=jnp.float32)


def back_product(grad_rows, weight):
    return jnp.einsum("re,de->rd", grad_rows, weight, preferred_element_type=jnp.float32)


def over_blocks(step_fn, carry_state, pair_rows):
    key_count = pair_rows.shape[1]
    block_width = math.gcd(key_count, 512)

    def turn(turn_index, inner_state):
        block_pairs = lax.dynamic_slice_in_dim(pair_rows, turn_index * block_width, block_width, 1)
        return step_fn(inner_state, block_pairs, turn_index * block_width)

    return lax.fori_loop(0, key_count // block_width, turn, carry_state)


def general_shards(
    inputs,
    lengths,
    w_query,
    b_query,
    w_key,
    w_value,
    b_value,
    w_out,
    b_out,
    first_gain,
    first_shift,
    w_expand,
    b_expand,
    w_reduce,
    b_reduce,
    second_gain,
    second_shift,
    cotangent,
):
    gathered = (
        lax.all_gather(w_query, ("fsdp", "ctx"), axis=0, tiled=True),
        lax.all_gather(b_query, ("fsdp", "ctx"), axis=0, tiled=True),
        lax.all_gather(w_key, ("fsdp", "ctx"), axis=0, tiled=True),
        lax.all_gather(w_value, ("fsdp", "ctx"), axis=0, tiled=True),
        lax.all_gather(b_value, ("fsdp", "ctx"), axis=0, tiled=True),
        lax.all_gather(w_out, ("fsdp", "ctx"), axis=0, tiled=True),
        lax.all_gather(b_out, ("fsdp", "ctx"), axis=0, tiled=True),
        lax.all_gather(first_gain, ("fsdp", "ctx"), axis=0, tiled=True),
        lax.all_gather(first_shift, ("fsdp", "ctx"), axis=0, tiled=True),
        lax.all_gather(w_expand, ("fsdp", "ctx"), axis=0, tiled=True),
        lax.all_gather(b_expand, ("fsdp", "ctx"), axis=0, tiled=True),
        lax.all_gather(w_reduce, ("fsdp", "ctx"), axis=0, tiled=True),
        lax.all_gather(b_reduce, ("fsdp", "ctx"), axis=0, tiled=True),
        lax.all_gather(second_gain, ("fsdp", "ctx"), axis=0, tiled=True),
        lax.all_gather(second_shift, ("fsdp", "ctx"), axis=0, tiled=True),
    )
    (
        full_query,
        bias_query,
        full_key,
        full_value,
        bias_value,
        full_out,
        bias_out,
        gain_first,
        shift_first,
        full_expand,
        bias_expand,
        full_reduce,
        bias_reduce,
        gain_second,
        shift_second,
    ) = gathered
    seq_count, block_rows, model_width = inputs.shape
    total_rows = seq_count * block_rows
    head_size = model_width // HEADS
    score_scale = head_size ** (-0.5)
    own_first = lax.axis_index("ctx") * block_rows
    positions = own_first + jnp.arange(block_rows, dtype=jnp.int32)
    valid_rows = (positions[None, :] < lengths[:, None]).astype(jnp.float32).reshape(total_rows, 1)
    flat_rows = inputs.reshape(total_rows, model_width)
    queries = (product(flat_rows, full_query) + bias_query.astype(jnp.float32)).astype(jnp.bfloat16)
    key_rows = product(flat_rows, full_key).astype(jnp.bfloat16)
    value_rows = (product(flat_rows, full_value) + bias_value.astype(jnp.float32)).astype(
        jnp.bfloat16
    )
    query_heads = queries.reshape(seq_count, block_rows, HEADS, head_size)
    local_pairs = jnp.concatenate([key_rows, value_rows], -1).reshape(
        seq_count, block_rows, 2 * model_width
    )

    def key_allowed(first_row, key_count):
        return ((first_row + jnp.arange(key_count, dtype=jnp.int32))[None, :] < lengths[:, None])[
            :, None, None, :
        ]

    def split_pairs(block_pairs):
        key_count = block_pairs.shape[1]
        key_heads = block_pairs[:, :, :model_width].reshape(seq_count, key_count, HEADS, head_size)
        value_heads = block_pairs[:, :, model_width:].reshape(
            seq_count, key_count, HEADS, head_size
        )
        return (key_heads, value_heads, key_count)

    def forward_step(carry_state, block_pairs, first_row):
        running_max, running_sum, running_acc = carry_state
        key_heads, value_heads, key_count = split_pairs(block_pairs)
        allowed = key_allowed(first_row, key_count)
        scores = (
            jnp.einsum(
                "sqhd,skhd->shqk", query_heads, key_heads, preferred_element_type=jnp.float32
            )
            * score_scale
        )
        scores = jnp.where(allowed, scores, masked_score)
        new_max = jnp.maximum(running_max, jnp.max(scores, -1))
        factor = jnp.exp(running_max - new_max)
        exponents = jnp.where(allowed, jnp.exp(scores - new_max[..., None]), 0.0)
        new_sum = running_sum * factor + jnp.sum(exponents, -1)
        update = jnp.einsum(
            "shqk,skhd->sqhd",
            exponents.astype(jnp.bfloat16),
            value_heads,
            preferred_element_type=jnp.float32,
        )
        new_acc = running_acc * jnp.transpose(factor, (0, 2, 1))[..., None] + update
        return (new_max, new_sum, new_acc)

    start_state = (
        jnp.full((seq_count, HEADS, block_rows), masked_score, jnp.float32),
        jnp.zeros((seq_count, HEADS, block_rows), jnp.float32),
        jnp.zeros((seq_count, block_rows, HEADS, head_size), jnp.float32),
    )
    running_max, running_sum, running_acc = over_blocks(
        forward_step, start_state, lax.all_gather(local_pairs, "ctx", axis=1, tiled=True)
    )
    context_full = running_acc / jnp.transpose(running_sum, (0, 2, 1))[..., None]
    log_total = running_max + jnp.log(running_sum)
    context = context_full.reshape(total_rows, model_width).astype(jnp.bfloat16)
    attended = product(context, full_out) + bias_out.astype(jnp.float32)
    residual = flat_rows.astype(jnp.float32) + attended
    normed, first_pull = jax.vjp(
        layer_norm, residual, gain_first.astype(jnp.float32), shift_first.astype(jnp.float32)
    )
    normed_low = normed.astype(jnp.bfloat16)
    expanded = product(normed_low, full_expand) + bias_expand.astype(jnp.float32)
    activated, gelu_pull = jax.vjp(partial(jax.nn.gelu, approximate=False), expanded)
    activated_low = activated.astype(jnp.bfloat16)
    reduced = product(activated_low, full_reduce) + bias_reduce.astype(jnp.float32)
    final_rows, second_pull = jax.vjp(
        layer_norm,
        normed + reduced,
        gain_second.astype(jnp.float32),
        shift_second.astype(jnp.float32),
    )
    layer_out = (final_rows * valid_rows).astype(jnp.bfloat16).reshape(inputs.shape)
    d_output = cotangent.reshape(total_rows, model_width).astype(jnp.float32) * valid_rows
    d_second, second_gain_grad, second_shift_grad = second_pull(d_output)
    d_reduced = d_second.astype(jnp.bfloat16)
    reduce_grad = outer_sum(activated_low, d_reduced)
    reduce_bias_grad = jnp.sum(d_reduced.astype(jnp.float32), 0)
    (d_expanded_full,) = gelu_pull(back_product(d_reduced, full_reduce))
    d_expanded = d_expanded_full.astype(jnp.bfloat16)
    expand_grad = outer_sum(normed_low, d_expanded)
    expand_bias_grad = jnp.sum(d_expanded.astype(jnp.float32), 0)
    d_normed = d_second + back_product(d_expanded, full_expand)
    d_first, first_gain_grad, first_shift_grad = first_pull(d_normed)
    d_attended = d_first.astype(jnp.bfloat16)
    out_grad = outer_sum(context, d_attended)
    out_bias_grad = jnp.sum(d_attended.astype(jnp.float32), 0)
    d_context = back_product(d_attended, full_out).astype(jnp.bfloat16)
    d_context_heads = d_context.reshape(seq_count, block_rows, HEADS, head_size)
    delta = jnp.transpose(
        jnp.sum(d_context_heads.astype(jnp.float32) * context_full, -1), (0, 2, 1)
    )
    whole_length = block_rows * lax.axis_size("ctx")

    def score_grads(key_heads, value_heads, allowed):
        scores = (
            jnp.einsum(
                "sqhd,skhd->shqk", query_heads, key_heads, preferred_element_type=jnp.float32
            )
            * score_scale
        )
        probabilities = jnp.where(allowed, jnp.exp(scores - log_total[..., None]), 0.0)
        d_probs = jnp.einsum(
            "sqhd,skhd->shqk", d_context_heads, value_heads, preferred_element_type=jnp.float32
        )
        d_scores = (probabilities * (d_probs - delta[..., None])).astype(jnp.bfloat16)
        return (probabilities, d_scores)

    def backward_step(carry_state, block_pairs, first_row):
        grad_query, grad_pairs = carry_state
        key_heads, value_heads, key_count = split_pairs(block_pairs)
        probabilities, d_scores = score_grads(
            key_heads, value_heads, key_allowed(first_row, key_count)
        )
        grad_query = (
            grad_query
            + jnp.einsum("shqk,skhd->sqhd", d_scores, key_heads, preferred_element_type=jnp.float32)
            * score_scale
        )
        key_part = (
            jnp.einsum("shqk,sqhd->skhd", d_scores, query_heads, preferred_element_type=jnp.float32)
            * score_scale
        )
        value_part = jnp.einsum(
            "shqk,sqhd->skhd",
            probabilities.astype(jnp.bfloat16),
            d_context_heads,
            preferred_element_type=jnp.float32,
        )
        fresh = jnp.concatenate(
            [
                key_part.reshape(seq_count, key_count, model_width),
                value_part.reshape(seq_count, key_count, model_width),
            ],
            -1,
        )
        before = lax.dynamic_slice_in_dim(grad_pairs, first_row, key_count, 1)
        grad_pairs = lax.dynamic_update_slice_in_dim(grad_pairs, before + fresh, first_row, 1)
        return (grad_query, grad_pairs)

    query_zero = jnp.zeros((seq_count, block_rows, HEADS, head_size), jnp.float32)
    back_state = (query_zero, jnp.zeros((seq_count, whole_length, 2 * model_width), jnp.float32))
    back_result = over_blocks(
        backward_step, back_state, lax.all_gather(local_pairs, "ctx", axis=1, tiled=True)
    )
    grad_query = back_result[0]
    own_pairs = lax.psum_scatter(
        back_result[1].astype(jnp.bfloat16), "ctx", scatter_dimension=1, tiled=True
    ).astype(jnp.float32)
    d_keys = own_pairs[:, :, :model_width].reshape(total_rows, model_width).astype(jnp.bfloat16)
    d_values = own_pairs[:, :, model_width:].reshape(total_rows, model_width).astype(jnp.bfloat16)
    d_queries = grad_query.reshape(total_rows, model_width).astype(jnp.bfloat16)
    query_grad = outer_sum(flat_rows, d_queries)
    query_bias_grad = jnp.sum(d_queries.astype(jnp.float32), 0)
    key_grad = outer_sum(flat_rows, d_keys)
    value_grad = outer_sum(flat_rows, d_values)
    value_bias_grad = jnp.sum(d_values.astype(jnp.float32), 0)
    input_grad = (
        d_first
        + back_product(d_queries, full_query)
        + back_product(d_keys, full_key)
        + back_product(d_values, full_value)
    ).reshape(inputs.shape)
    shares = (
        lax.psum_scatter(query_grad, ("fsdp", "ctx"), scatter_dimension=0, tiled=True),
        lax.psum_scatter(query_bias_grad, ("fsdp", "ctx"), scatter_dimension=0, tiled=True),
        lax.psum_scatter(key_grad, ("fsdp", "ctx"), scatter_dimension=0, tiled=True),
        lax.psum_scatter(value_grad, ("fsdp", "ctx"), scatter_dimension=0, tiled=True),
        lax.psum_scatter(value_bias_grad, ("fsdp", "ctx"), scatter_dimension=0, tiled=True),
        lax.psum_scatter(out_grad, ("fsdp", "ctx"), scatter_dimension=0, tiled=True),
        lax.psum_scatter(out_bias_grad, ("fsdp", "ctx"), scatter_dimension=0, tiled=True),
        lax.psum_scatter(first_gain_grad, ("fsdp", "ctx"), scatter_dimension=0, tiled=True),
        lax.psum_scatter(first_shift_grad, ("fsdp", "ctx"), scatter_dimension=0, tiled=True),
        lax.psum_scatter(expand_grad, ("fsdp", "ctx"), scatter_dimension=0, tiled=True),
        lax.psum_scatter(expand_bias_grad, ("fsdp", "ctx"), scatter_dimension=0, tiled=True),
        lax.psum_scatter(reduce_grad, ("fsdp", "ctx"), scatter_dimension=0, tiled=True),
        lax.psum_scatter(reduce_bias_grad, ("fsdp", "ctx"), scatter_dimension=0, tiled=True),
        lax.psum_scatter(second_gain_grad, ("fsdp", "ctx"), scatter_dimension=0, tiled=True),
        lax.psum_scatter(second_shift_grad, ("fsdp", "ctx"), scatter_dimension=0, tiled=True),
    )
    return (
        layer_out,
        input_grad,
        shares[0],
        shares[1],
        shares[2],
        shares[3],
        shares[4],
        shares[5],
        shares[6],
        shares[7],
        shares[8],
        shares[9],
        shares[10],
        shares[11],
        shares[12],
        shares[13],
        shares[14],
    )


MESH = pl.DeviceIdType.MESH
MIB = 1024*1024

def place():
    core = lax.axis_index("fsdp"); chip = lax.axis_index("ctx")
    return core, chip

def greet(peers):
    barrier = pltpu.get_barrier_semaphore()
    for peer in peers:
        pl.semaphore_signal(barrier, inc=1, device_id=peer, device_id_type=MESH)
    pl.semaphore_wait(barrier, len(peers))

def flip(v, bits):
    for b in (1, 2, 4, 8):
        if bits & b:
            v = v + b - 2 * b * lax.rem(lax.div(v, b), 2)
    return v

LOG2E = math.log2(math.e)


def nt(a, b):
    return lax.dot_general(a, b, (((1,), (1,)), ((), ())), preferred_element_type=jnp.float32)


FULL_ORDER = (12, 8, 4, 15, 11, 7, 14, 13, 10, 9, 6, 5, 3, 2, 1)


class Copies:
    def __init__(self, send_sem, recv_sem):
        self.send_sem, self.recv_sem = send_sem, recv_sem
        self.names, self.sent = {}, []

    def pair(self, name, src, dst, peer):
        i = self.names.setdefault(name, len(self.names))
        return pltpu.make_async_remote_copy(
            src_ref=src,
            dst_ref=dst,
            send_sem=self.send_sem.at[i],
            recv_sem=self.recv_sem.at[i],
            device_id=peer,
            device_id_type=MESH,
        )

    def send(self, name, src, dst, peer, like):
        self.pair(name, src, dst, peer).start()
        self.sent.append((name, like))

    def arrived(self, name, dst, peer):
        self.pair(name, dst, dst, peer).wait_recv()

    def drain(self, peer):
        for name, like in self.sent:
            self.pair(name, like, like, peer).wait_send()


class Gather:
    def __init__(self, copies, name, src, out, local_sem):
        self.copies, self.name, self.src, self.out, self.local_sem = copies, name, src, out, local_sem
        self.core, self.chip = place()
        self.sib = (1 - self.core, self.chip)
        self.half = src.shape[0] // 2

    def at(self, bits):
        return (self.core, flip(self.chip, bits))

    def block(self, bits, core=None):
        return self.out.at[(self.core if core is None else core) * 16 + flip(self.chip, bits)]

    def part(self, bits, upper):
        return self.out.at[self.core * 16 + flip(self.chip, bits), pl.ds(self.half if upper else 0, self.half)]

    def send(self, tag, src, dst, peer, half=False):
        like = self.src.at[pl.ds(0, self.half)] if half else self.src
        self.copies.send((self.name, tag), src, dst, peer, like)

    def arrived(self, tag, dst):
        self.copies.arrived((self.name, tag), dst, self.sib)

    def start_z(self):
        for z in (12, 8, 4):
            self.send(("z", z), self.src, self.block(0), self.at(z))

    def start_plane(self):
        self.send(("x", 0), self.src, self.block(0), self.at(1))
        self.send(("y", 0), self.src, self.block(0), self.at(2))
        self.send(("s", 0), self.src, self.block(0), self.sib)
        self.local = pltpu.make_async_copy(self.src, self.block(0), self.local_sem)
        self.local.start()

    def on_z(self, z):
        b = self.block(z)
        self.arrived(("z", z), b)
        self.send(("x", z), b, b, self.at(1))
        self.send(("y", z), b, b, self.at(2))
        self.send(("s", z), b, b, self.sib)

    def on_plane(self, z):
        for bit, tag, further, upper in ((1, "x", 2, False), (2, "y", 1, True)):
            b = self.block(z + bit)
            self.arrived((tag, z), b)
            h = self.part(z + bit, upper)
            self.send(("d" + tag, z), h, h, self.at(further), True)
            self.send(("s", z + bit), b, b, self.sib)

    def on_diagonal(self, z):
        self.arrived(("dx", z), self.part(z + 3, False))
        self.arrived(("dy", z), self.part(z + 3, True))
        b = self.block(z + 3)
        self.send(("s", z + 3), b, b, self.sib)

    def on_sibling(self):
        for bits in range(16):
            self.arrived(("s", bits), self.block(bits, 1 - self.core))
        self.local.wait()


def load_sequence(r_ref, s, kk_ref, vt_ref=None, vv_ref=None):
    for j in range(r_ref.shape[1]):
        span = pl.ds(j * 128, 128)
        kk_ref[span] = r_ref[s, j, 64:128, :].astype(jnp.float32).T.astype(jnp.bfloat16)
        if vt_ref is not None:
            vt_ref[:, span] = r_ref[s, j, 128:192, :]
        if vv_ref is not None:
            vv_ref[span] = r_ref[s, j, 128:192, :].astype(jnp.float32).T.astype(jnp.bfloat16)


def fwd_kernel(
    x_ref, lengths_ref, s_qkv, s_bias, s_vec, s_out, s_expand, s_reduce,
    o_vec, o_out, o_expand, o_reduce, o_qkv, o_pairs, o_ctx, o_full, lse_ref,
    w_qkv, w_bias, send_blk, recv_blk, ctx_blk, ctx_recv, kk, vt,
    send_sem, recv_sem, local_sem, hsend, hrecv, csend, crecv,
):
    f32, bf16 = jnp.float32, jnp.bfloat16
    core, chip = place()
    sib = (1 - core, chip)
    greet([sib] + [(core, flip(chip, b)) for b in range(1, 16)])
    copies = Copies(send_sem, recv_sem)
    first = [
        Gather(copies, 0, s_qkv, w_qkv, local_sem.at[0]),
        Gather(copies, 1, s_bias, w_bias, local_sem.at[1]),
    ]
    rest = [
        Gather(copies, 2, s_out, o_out, local_sem.at[2]),
        Gather(copies, 3, s_vec, o_vec, local_sem.at[3]),
        Gather(copies, 4, s_expand, o_expand, local_sem.at[4]),
        Gather(copies, 5, s_reduce, o_reduce, local_sem.at[5]),
    ]
    for g in first:
        g.start_z()
        g.start_plane()
    for z in (4, 8, 12):
        for g in first:
            g.on_z(z)
    for g in rest[:3]:
        g.start_z()
    for z in (0, 4, 8, 12):
        for g in first:
            g.on_plane(z)
    for g in rest:
        g.start_plane()
    for z in (0, 4, 8, 12):
        for g in first:
            g.on_diagonal(z)
    for g in first:
        g.on_sibling()
    keep = pltpu.make_async_copy(w_qkv, o_qkv, local_sem.at[6])
    keep.start()

    for part in range(3):

        @pl.loop(0, 4)
        def _(p):
            w = w_qkv[:, :, pl.ds(pl.multiple_of(part * 1024 + p * 256, 256), 256)].reshape(1024, 256)
            t = jnp.dot(x_ref[...], w, preferred_element_type=f32).T
            for i in range(4):
                h = 4 * p + i
                rows = t[64 * i : 64 * i + 64]
                if part != 1:
                    own = pl.ds(0 if part == 0 else 32, 32)
                    bias = jnp.concatenate([w_bias[2 * h + k, own] for k in range(2)], 0).astype(f32)
                    rows = rows + jnp.concatenate([bias, bias], 1)
                send_blk[h, pl.ds(64 * part, 64)] = rows.astype(bf16)

    heads = []
    for s in range(2):
        for b in FULL_ORDER:
            to = flip(chip, b)
            i = s * 16 + b
            c = pltpu.make_async_remote_copy(
                src_ref=send_blk.at[to, :, pl.ds(128 * s, 128)],
                dst_ref=recv_blk.at[s, chip],
                send_sem=hsend.at[i],
                recv_sem=hrecv.at[i],
                device_id=(core, to),
                device_id_type=MESH,
            )
            c.start()
            heads.append(c)
        recv_blk[s, chip] = send_blk[chip, :, pl.ds(128 * s, 128)]

    def heads_here(s):
        for b in FULL_ORDER:
            i = s * 16 + b
            here = recv_blk.at[s, flip(chip, b)]
            pltpu.make_async_remote_copy(
                src_ref=here, dst_ref=here, send_sem=hsend.at[i], recv_sem=hrecv.at[i], device_id=sib, device_id_type=MESH
            ).wait_recv()

    rest[3].start_z()
    events = []
    events.append(lambda: [g.on_plane(0) for g in rest])
    for z in (4, 8, 12):
        events.append(lambda z=z: [g.on_z(z) for g in rest[:3]])
    events.append(lambda: [g.on_diagonal(0) for g in rest])
    for z in (4, 8, 12):
        events.append(lambda z=z: [g.on_plane(z) for g in rest[:3]])
    for z in (4, 8, 12):
        events.append(lambda z=z: [rest[3].on_z(z)])
    for z in (4, 8, 12):
        events.append(lambda z=z: [g.on_diagonal(z) for g in rest[:3]])
    for z in (4, 8, 12):
        events.append(lambda z=z: [rest[3].on_plane(z)])
    for z in (4, 8, 12):
        events.append(lambda z=z: [rest[3].on_diagonal(z)])
    events.append(lambda: [g.on_sibling() for g in rest])

    def attend_sequence(s, during):
        load_sequence(recv_blk, s, kk, vt_ref=vt)

        @pl.loop(0, 8)
        def _(step):
            for k, event in enumerate(during):

                @pl.when(step == k)
                def _():
                    event()

            q = flip_by(step, chip // 2)
            query = jnp.concatenate([recv_blk[s, 2 * q, 0:64, :], recv_blk[s, 2 * q + 1, 0:64, :]], 1)
            scores = jnp.dot(kk[...], query, preferred_element_type=f32) * (0.125 * LOG2E)
            key = lax.broadcasted_iota(jnp.int32, scores.shape, 0)
            scores = jnp.where(key < lengths_ref[s], scores, masked_score)
            top = jnp.max(scores, 0, keepdims=True)
            e = jnp.exp2(scores - top)
            mass = jnp.sum(e, 0, keepdims=True)
            o = jnp.dot(vt[...], e.astype(bf16), preferred_element_type=f32) / mass
            lse_ref[s, pl.ds(q, 1), :] = top + jnp.log2(mass)
            o_full[s, :, pl.ds(pl.multiple_of(q * 256, 256), 256)] = o
            for i in range(2):
                to = 2 * q + i
                ctx_blk[s, to] = o[:, 128 * i : 128 * i + 128].astype(bf16)

                @pl.when(to != chip)
                def _():
                    pltpu.make_async_remote_copy(
                        src_ref=ctx_blk.at[s, to],
                        dst_ref=ctx_recv.at[chip, :, pl.ds(128 * s, 128)],
                        send_sem=csend.at[s * 16 + to],
                        recv_sem=crecv.at[s * 16 + chip],
                        device_id=(core, to),
                        device_id_type=MESH,
                    ).start()

        ctx_recv[chip, :, pl.ds(128 * s, 128)] = ctx_blk[s, chip]

    PRE, FIRST, SECOND = 5, 3, 6
    for event in events[:PRE]:
        event()
    heads_here(0)
    attend_sequence(0, events[PRE : PRE + FIRST])
    heads_here(1)
    pairs_out = pltpu.make_async_copy(recv_blk, o_pairs, local_sem.at[7])
    pairs_out.start()
    attend_sequence(1, events[PRE + FIRST : PRE + FIRST + SECOND])
    for event in events[PRE + FIRST + SECOND :]:
        event()
    for s in range(2):
        for b in range(1, 16):
            other = flip(chip, b)
            here = ctx_recv.at[other, :, pl.ds(128 * s, 128)]
            pltpu.make_async_remote_copy(
                src_ref=ctx_blk.at[s, other],
                dst_ref=here,
                send_sem=csend.at[s * 16 + other],
                recv_sem=crecv.at[s * 16 + other],
                device_id=sib,
                device_id_type=MESH,
            ).wait()
    ctx_out = pltpu.make_async_copy(ctx_recv, o_ctx, local_sem.at[8])
    ctx_out.start()
    for c in heads:
        c.wait_send()
    copies.drain(sib)
    keep.wait()
    pairs_out.wait()
    ctx_out.wait()


def flip_by(v, w):
    out = 0
    for b in (1, 2, 4):
        p, q = lax.rem(lax.div(v, b), 2), lax.rem(lax.div(w, b), 2)
        out = out + b * (p + q - 2 * p * q)
    return out


def forward_attention(rows, lengths, qkv, bias, vec, w_out, w_expand, w_reduce, collective_id):
    v, hbm = pl.BlockSpec(memory_space=pltpu.VMEM), pl.BlockSpec(memory_space=pl.ANY)
    f32, bf16 = jnp.float32, jnp.bfloat16
    gathered = lambda x: jax.ShapeDtypeStruct((32,) + x.shape, x.dtype)
    dma = pltpu.SemaphoreType.DMA
    return pl.pallas_call(
        fwd_kernel,
        out_shape=[
            gathered(vec),
            gathered(w_out),
            gathered(w_expand),
            gathered(w_reduce),
            gathered(qkv),
            jax.ShapeDtypeStruct((2, 16, 192, 128), bf16),
            jax.ShapeDtypeStruct((16, 64, 256), bf16),
            jax.ShapeDtypeStruct((2, 64, 2048), f32),
            jax.ShapeDtypeStruct((2, 8, 256), f32),
        ],
        in_specs=[v, pl.BlockSpec(memory_space=pltpu.SMEM)] + [hbm] * 6,
        out_specs=[hbm] * 7 + [v, v],
        scratch_shapes=[
            pltpu.VMEM((32,) + qkv.shape, bf16),
            pltpu.VMEM((32,) + bias.shape, bf16),
            pltpu.VMEM((16, 192, 256), bf16),
            pltpu.VMEM((2, 16, 192, 128), bf16),
            pltpu.VMEM((2, 16, 64, 128), bf16),
            pltpu.VMEM((16, 64, 256), bf16),
            pltpu.VMEM((2048, 64), bf16),
            pltpu.VMEM((64, 2048), bf16),
            dma((210,)),
            dma((210,)),
            dma((9,)),
            dma((32,)),
            dma((32,)),
            dma((32,)),
            dma((32,)),
        ],
        compiler_params=pltpu.CompilerParams(
            collective_id=collective_id, has_side_effects=True, vmem_limit_bytes=56 * MIB
        ),
        name="forward_attention",
    )(rows, lengths, qkv, bias, vec, w_out, w_expand, w_reduce)


class Scatter:
    ORDER = (12, 8, 4, 0)

    def __init__(self, copies, name, grads, out, bufs):
        self.copies, self.name, self.grads, self.out = copies, name, grads, out
        self.first, self.second, self.third = bufs
        self.core, self.chip = place()
        self.rows = grads.shape[1]
        self.half = self.rows // 2
        self.lo, self.hi = pl.ds(0, self.half), pl.ds(self.half, self.half)
        self.first_at = [[self.first.at[k, i] for i in range(2)] for k in range(4)]
        self.second_at = [[self.second.at[k, i] for i in range(2)] for k in range(4)]
        self.third_at = [self.third.at[k] for k in range(3)]

    def at(self, bits):
        return (self.core, flip(self.chip, bits))

    def send(self, tag, src, dst, bits, half=True):
        like = self.first_at[0][0] if half else self.third_at[0]
        self.copies.send((self.name, tag), src, dst, self.at(bits), like)

    def arrived(self, tag, dst):
        self.copies.arrived((self.name, tag), dst, self.at(1))

    def add(self, rows, fn):
        step = min(rows, 16)
        if rows == step:
            fn(0, step)
            return

        def turn(i, carry):
            fn(pl.multiple_of(i * step, step), step)
            return carry

        lax.fori_loop(0, rows // step, turn, 0)

    def start(self):
        for k, z in enumerate(self.ORDER):
            diag = flip(self.chip, z + 3)
            self.send(("1a", k), self.grads.at[diag, self.lo], self.first_at[k][0], 2)
            self.send(("1b", k), self.grads.at[diag, self.hi], self.first_at[k][1], 1)

    def start_direct(self):
        for k, z in enumerate(self.ORDER):
            xb, yb = flip(self.chip, z + 1), flip(self.chip, z + 2)
            self.send(("2xh", k), self.grads.at[xb, self.hi], self.second_at[k][0].at[self.hi], 1)
            self.send(("2yl", k), self.grads.at[yb, self.lo], self.second_at[k][1].at[self.lo], 2)

    def on_first(self, k):
        z = self.ORDER[k]
        for i, (tag, bit, upper) in enumerate((("1a", 1, False), ("1b", 2, True))):
            owner = flip(self.chip, z + bit)
            here = self.first_at[k][i]
            self.arrived((tag, k), here)

            def fn(start, size):
                rows = pl.ds(start, size)
                theirs = pl.ds(start + (self.half if upper else 0), size)
                here[rows] = here[rows] + self.grads.at[owner][theirs]

            self.add(self.half, fn)
            self.send(("2" + "xy"[i] + "lh"[i], k), here, self.second_at[k][i].at[self.hi if upper else self.lo], bit)

    def on_second(self, k):
        z = self.ORDER[k]
        self.arrived(("2xh", k), self.second_at[k][0].at[self.hi])
        self.arrived(("2yl", k), self.second_at[k][1].at[self.lo])
        self.arrived(("2xl", k), self.second_at[k][0].at[self.lo])
        self.arrived(("2yh", k), self.second_at[k][1].at[self.hi])
        owner = flip(self.chip, z)

        def fn(start, size):
            rows = pl.ds(start, size)
            f32 = jnp.float32
            total = self.grads.at[owner][rows].astype(f32) + self.second_at[k][0][rows].astype(f32)
            total = total + self.second_at[k][1][rows].astype(f32)
            if k < 3:
                self.second_at[k][0][rows] = total.astype(self.second.dtype)
            else:
                self.out[rows] = total

        self.add(self.rows, fn)
        if k < 3:
            self.send(("3", k), self.second_at[k][0], self.third_at[k], z, False)

    def on_third(self):
        for k in range(3):
            self.arrived(("3", k), self.third_at[k])

        def fn(start, size):
            rows = pl.ds(start, size)
            total = self.out[rows]
            for k in range(3):
                total = total + self.third_at[k][rows].astype(jnp.float32)
            self.out[rows] = total

        self.add(self.rows, fn)


def scatter_buffers(block, dtype):
    rows, cols = block
    return [
        pltpu.VMEM((4, 2, rows // 2, cols), dtype),
        pltpu.VMEM((4, 2, rows, cols), dtype),
        pltpu.VMEM((3, rows, cols), dtype),
    ]


def bwd_kernel(*refs):
    f32, bf16 = jnp.float32, jnp.bfloat16
    (
        lengths_ref, pairs, o_full, lse_ref, x_t, normed_t, context_t, d_second, scaled, spread, gain, g_reduce, vec_in,
        h_slope, h_reduce, h_expand, h_out, h_qkv,
    ) = refs[:18]
    (o_reduce, o_expand, o_out, o_vec, o_qkv, o_input, o_bias) = refs[18:25]
    bufs = [refs[25 + 3 * i : 28 + 3 * i] for i in range(5)]
    (
        g_expand, g_out, g_vec, g_qkv, w_qkv, d_recv, kk, vv, kt, acc, d_send, d_own, d_sib, b_own, b_sib, b_in,
        slopes, w_reduce, w_expand, w_out, e_own, e_sib, d_first, a_own, a_sib, d_ctx, rows_sum, e_sum, vec_own, vec_sib,
        send_sem, recv_sem, local_sem, dsend, drecv, qsend, qrecv, esend, erecv, wsem,
    ) = refs[40:]
    core, chip = place()
    sib = (1 - core, chip)
    greet([sib] + [(core, flip(chip, b)) for b in range(1, 16)])
    copies = Copies(send_sem, recv_sem)
    rest = [
        Scatter(copies, i, g, o, bufs[i])
        for i, (g, o) in enumerate(((g_reduce, o_reduce), (g_expand, o_expand), (g_out, o_out), (g_vec, o_vec)))
    ]
    last = Scatter(copies, 4, g_qkv, o_qkv, bufs[4])
    rest[0].start()
    rest[0].start_direct()
    out_weights = pltpu.make_async_copy(h_out, w_out, local_sem.at[4])
    out_weights.start()

    def fetch(c, slot):
        return (
            pltpu.make_async_copy(h_reduce.at[pl.ds(c * 4, 4)], w_reduce.at[slot], wsem.at[slot, 0]),
            pltpu.make_async_copy(
                h_expand.at[:, :, pl.ds(pl.multiple_of(c * 512, 512), 512)], w_expand.at[slot], wsem.at[slot, 1]
            ),
            pltpu.make_async_copy(h_slope.at[:, pl.ds(pl.multiple_of(c * 512, 512), 512)], slopes.at[slot], wsem.at[slot, 2]),
        )

    for c in fetch(0, 0):
        c.start()
    a_own[...] = d_second[...].astype(bf16)
    d_first[...] = d_second[...]

    def e_copy(c):
        return pltpu.make_async_remote_copy(
            src_ref=e_own.at[c],
            dst_ref=e_sib.at[c],
            send_sem=esend.at[c],
            recv_sem=erecv.at[c],
            device_id=sib,
            device_id_type=MESH,
        )

    @pl.loop(0, 8)
    def _(c):
        slot = lax.rem(c, 2)

        @pl.when(c < 7)
        def _():
            for copy in fetch(c + 1, 1 - slot):
                copy.start()

        for copy in fetch(c, slot):
            copy.wait()
        d_active = nt(a_own[...], w_reduce[slot].reshape(512, 1024))
        d_expanded = (d_active * slopes[slot].astype(f32)).astype(bf16)
        e_own[c] = d_expanded
        e_copy(c).start()
        e_sum[pl.ds(c, 1)] = jnp.sum(d_expanded.astype(f32), 0, keepdims=True)
        d_first[...] += nt(d_expanded, w_expand[slot].reshape(1024, 512))

    rows_sum[...] = jnp.zeros_like(rows_sum)

    @pl.loop(0, 4)
    def _(i):
        span = pl.ds(pl.multiple_of(i * 64, 64), 64)
        d_normed, x_hat = d_first[span], scaled[span]
        pulled = d_normed * gain[...]
        level = jnp.mean(pulled, -1, keepdims=True)
        slope = jnp.mean(pulled * x_hat, -1, keepdims=True)
        d_rows = spread[span] * (pulled - level - x_hat * slope)
        d_low = d_rows.astype(bf16)
        d_first[span] = d_rows
        a_own[span] = d_low
        rows_sum[0:1] += jnp.sum(d_low.astype(f32), 0, keepdims=True)
        rows_sum[1:2] += jnp.sum(d_normed * x_hat, 0, keepdims=True)
        rows_sum[2:3] += jnp.sum(d_normed, 0, keepdims=True)

    out_weights.wait()

    @pl.loop(0, 4)
    def _(i):
        t = nt(w_out[pl.ds(i * 8, 8)].reshape(256, 1024), a_own[...])
        d_ctx[pl.ds(i * 4, 4)] = t.astype(bf16).reshape(4, 64, 256)

    sent = []

    def exchange_out(s, b, src, dst, sends, recvs):
        c = pltpu.make_async_remote_copy(
            src_ref=src,
            dst_ref=dst,
            send_sem=sends.at[s * 16 + b],
            recv_sem=recvs.at[s * 16 + b],
            device_id=(core, flip(chip, b)),
            device_id_type=MESH,
        )
        c.start()
        sent.append(c)

    def exchange_in(s, b, here, sends, recvs):
        pltpu.make_async_remote_copy(
            src_ref=here,
            dst_ref=here,
            send_sem=sends.at[s * 16 + b],
            recv_sem=recvs.at[s * 16 + b],
            device_id=sib,
            device_id_type=MESH,
        ).wait_recv()

    for s in range(2):
        lane = pl.ds(128 * s, 128)
        for b in FULL_ORDER:
            exchange_out(s, b, d_ctx.at[flip(chip, b), :, lane], d_recv.at[s, chip], dsend, drecv)
        d_recv[s, chip] = d_ctx[chip, :, lane]
    copies.send("a", a_own, a_sib, sib, a_own)

    vec_own[...] = vec_in[...]
    owner = lax.broadcasted_iota(jnp.int32, (32, 1024), 0)
    column = lax.broadcasted_iota(jnp.int32, (32, 1024), 1)
    place_in = lax.rem(lax.broadcasted_iota(jnp.int32, (1024, 128), 0), 32)
    pick = jnp.where(place_in == lax.broadcasted_iota(jnp.int32, (1024, 128), 1), 1.0, 0.0).astype(bf16)
    for r in range(3):
        spread_row = jnp.where(lax.div(column, 32) == owner, rows_sum[r : r + 1], 0.0)
        top = spread_row.astype(bf16)
        low = (spread_row - top.astype(f32)).astype(bf16)
        vec_own[:, r, :] = jnp.dot(top, pick, preferred_element_type=f32) + jnp.dot(low, pick, preferred_element_type=f32)
    for o in range(32):
        vec_own[o, 3:4, :] = e_sum[o // 4 : o // 4 + 1, 128 * (o % 4) : 128 * (o % 4) + 128]
    own_half, other_half = pl.ds(core * 16, 16), pl.ds((1 - core) * 16, 16)
    copies.send("v", vec_own.at[other_half], vec_sib, sib, vec_sib)

    for k in range(4):
        rest[0].on_first(k)

    @pl.loop(0, 8)
    def _(c):
        e_copy(c).wait()
        g = jnp.dot(normed_t[:, :256], e_own[c], preferred_element_type=f32)
        g = g + jnp.dot(normed_t[:, 256:], e_sib[c], preferred_element_type=f32)
        g_expand[:, :, pl.ds(pl.multiple_of(c * 512, 512), 512)] = g.astype(bf16).reshape(16, 32, 512)

    rest[1].start()
    rest[1].start_direct()
    copies.arrived("a", a_sib, sib)
    for i in range(4):
        cols = slice(256 * i, 256 * i + 256)
        g = jnp.dot(context_t[:, :256], a_own[:, cols], preferred_element_type=f32)
        g = g + jnp.dot(context_t[:, 256:], a_sib[:, cols], preferred_element_type=f32)
        g_out[:, :, cols] = g.astype(bf16).reshape(16, 32, 256)
    copies.arrived("v", vec_sib, sib)
    g_vec[...] = vec_own[own_half] + vec_sib[...]
    for r in rest[2:]:
        r.start()
        r.start_direct()
    b_own[...] = jnp.zeros_like(b_own)

    def fetch_qkv(i, slot):
        return pltpu.make_async_copy(h_qkv.at[pl.ds(i * 8, 8)], w_qkv.at[slot], local_sem.at[5 + slot])

    fetch_qkv(0, 0).start()
    fetch_qkv(1, 1).start()

    def back_sequence(s, during):
        load_sequence(pairs, s, kk, vt_ref=None, vv_ref=vv)
        for j in range(16):
            kt[:, pl.ds(j * 128, 128)] = pairs[s, j, 64:128, :]
        acc[...] = jnp.zeros_like(acc)

        @pl.loop(0, 8)
        def _(q):
            for k, event in enumerate(during):

                @pl.when(q == k)
                def _():
                    event()

            both = lambda ref, lo, hi: jnp.concatenate([ref[s, 2 * q, lo:hi, :], ref[s, 2 * q + 1, lo:hi, :]], 1)
            query, d_out = both(pairs, 0, 64), both(d_recv, 0, 64)
            span = pl.ds(pl.multiple_of(q * 256, 256), 256)
            delta = jnp.sum(d_out.astype(f32) * o_full[s, :, span], 0, keepdims=True)
            scores = jnp.dot(kk[...], query, preferred_element_type=f32) * (0.125 * LOG2E)
            key = lax.broadcasted_iota(jnp.int32, scores.shape, 0)
            probs = jnp.where(key < lengths_ref[s], jnp.exp2(scores - lse_ref[s, pl.ds(q, 1), :]), 0.0)
            d_probs = jnp.dot(vv[...], d_out, preferred_element_type=f32)
            d_scores = (probs * (d_probs - delta)).astype(bf16)
            zero = jnp.zeros((64, 256), f32)
            query_rows = jnp.concatenate([query.astype(f32), zero], 0).T.astype(bf16)
            d_rows = jnp.concatenate([zero, d_out.astype(f32)], 0).T.astype(bf16)
            acc[...] += jnp.dot(d_scores, query_rows, preferred_element_type=f32) + jnp.dot(
                probs.astype(bf16), d_rows, preferred_element_type=f32
            )
            d_query = (jnp.dot(kt[...], d_scores, preferred_element_type=f32) * 0.125).astype(bf16)
            for i in range(2):
                part = d_query[:, 128 * i : 128 * i + 128]
                d_send[s, 2 * q + i, 0:64, :] = part
                b_own[0] += part.astype(f32)

        for j in range(16):
            t = acc[pl.ds(j * 128, 128)].T
            d_send[s, j, 64:128, :] = (t[:64] * 0.125).astype(bf16)
            value = t[64:].astype(bf16)
            d_send[s, j, 128:192, :] = value
            b_own[1] += value.astype(f32)
        lane = pl.ds(128 * s, 128)
        for b in FULL_ORDER:
            exchange_out(s, b, d_send.at[s, flip(chip, b)], d_own.at[chip, :, lane], qsend, qrecv)
        d_own[chip, :, lane] = d_send[s, chip]

    for k in range(4):
        rest[0].on_second(k)
    events = [lambda k=k: [r.on_first(k) for r in rest[1:]] for k in range(4)]
    events += [lambda k=k: [r.on_second(k) for r in rest[1:]] for k in range(4)]
    FIRST, SECOND, WAIT = 0, 4, 2
    for b in FULL_ORDER:
        exchange_in(0, b, d_recv.at[0, flip(chip, b)], dsend, drecv)
    back_sequence(0, events[:FIRST])
    for b in FULL_ORDER:
        exchange_in(1, b, d_recv.at[1, flip(chip, b)], dsend, drecv)
    back_sequence(1, events[FIRST : FIRST + SECOND])

    copies.send("bias sib", b_own, b_sib, sib, b_own)
    for event in events[FIRST + SECOND : FIRST + SECOND + WAIT]:
        event()
    for s in range(2):
        lane = pl.ds(128 * s, 128)
        for b in FULL_ORDER:
            exchange_in(s, b, d_own.at[flip(chip, b), :, lane], qsend, qrecv)
        copies.send(("rows", s), d_own.at[:, :, lane], d_sib.at[:, :, lane], sib, d_own.at[:, :, lane])

    copies.arrived("bias sib", b_sib, sib)
    for s in range(2):
        copies.arrived(("rows", s), d_sib.at[:, :, pl.ds(128 * s, 128)], sib)

    for part in range(3):

        @pl.loop(0, 4)
        def _(p):
            total = None
            for i, rows in enumerate((d_own, d_sib)):
                right = rows[pl.ds(4 * p, 4), pl.ds(64 * part, 64)].reshape(256, 256)
                term = nt(x_t[:, 256 * i : 256 * i + 256], right)
                total = term if total is None else total + term
            cols = pl.ds(pl.multiple_of(part * 1024 + p * 256, 256), 256)
            g_qkv[:, :, cols] = total.astype(bf16).reshape(16, 32, 256)

    last.start()
    last.start_direct()

    b_sib[...] = b_sib[...] + b_own[...]
    sender = core == lax.div(chip, 8)
    for i in range(2):
        to = lax.rem(2 * chip + i, 16)
        rows = pl.ds(32 * i, 32)
        c = pltpu.make_async_remote_copy(
            src_ref=b_sib.at[:, rows],
            dst_ref=b_in,
            send_sem=local_sem.at[1 + i],
            recv_sem=local_sem.at[3],
            device_id=(core, to),
            device_id_type=MESH,
        )

        @pl.when(sender & (to != chip))
        def _():
            c.start()

        @pl.when(sender & (to == chip))
        def _():
            b_in[...] = b_sib[:, rows]

    for i in range(4):
        fetch_qkv(i, i % 2).wait()
        t = None
        for part in range(3):
            w = w_qkv[i % 2, :, :, 1024 * part : 1024 * part + 1024].reshape(256, 1024)
            term = jnp.dot(w, d_own[:, 64 * part : 64 * part + 64].reshape(1024, 256), preferred_element_type=f32)
            t = term if t is None else t + term
        if i < 2:
            fetch_qkv(i + 2, i).start()
        cols = slice(256 * i, 256 * i + 256)
        o_input[:, cols] = d_first[:, cols] + t.T

    for event in events[FIRST + SECOND + WAIT :]:
        event()
    for k in range(4):
        last.on_first(k)
    for r in rest:
        r.on_third()
    for k in range(4):
        last.on_second(k)
    last.on_third()
    for i in range(2):
        to = lax.rem(2 * chip + i, 16)

        @pl.when(sender & (to != chip))
        def _():
            pltpu.make_async_remote_copy(
                src_ref=b_sib.at[:, pl.ds(32 * i, 32)],
                dst_ref=b_in,
                send_sem=local_sem.at[1 + i],
                recv_sem=local_sem.at[3],
                device_id=(core, to),
                device_id_type=MESH,
            ).wait_send()

    @pl.when(8 * core + lax.div(chip, 2) != chip)
    def _():
        pltpu.make_async_remote_copy(
            src_ref=b_in, dst_ref=b_in, send_sem=local_sem.at[1], recv_sem=local_sem.at[3], device_id=sib, device_id_type=MESH
        ).wait_recv()

    o_bias[...] = b_in[...]
    for c in sent:
        c.wait_send()
    copies.drain(sib)


def backward_attention(
    lengths, pairs, o_full, lse, x_t, normed_t, context_t, d_second, scaled, spread, gain, g_reduce, vec_in,
    slope, w_reduce, w_expand, w_out, w_qkv, collective_id,
):
    v, hbm = pl.BlockSpec(memory_space=pltpu.VMEM), pl.BlockSpec(memory_space=pl.ANY)
    f32, bf16 = jnp.float32, jnp.bfloat16
    dma = pltpu.SemaphoreType.DMA
    blocks = [((128, 1024), bf16), ((32, 4096), bf16), ((32, 1024), bf16), ((16, 128), f32), ((32, 3072), bf16)]
    bufs = []
    for block, dtype in blocks:
        bufs += scatter_buffers(block, dtype)
    vmem = lambda shape, dtype=bf16: pltpu.VMEM(shape, dtype)
    return pl.pallas_call(
        bwd_kernel,
        out_shape=[jax.ShapeDtypeStruct(block, f32) for block, _ in blocks]
        + [jax.ShapeDtypeStruct((256, 1024), f32), jax.ShapeDtypeStruct((2, 32, 128), f32)],
        in_specs=[pl.BlockSpec(memory_space=pltpu.SMEM)] + [v] * 12 + [hbm] * 5,
        out_specs=[v] * 7,
        scratch_shapes=bufs
        + [
            vmem((16, 32, 4096)),
            vmem((16, 32, 1024)),
            vmem((16, 16, 128), f32),
            vmem((16, 32, 3072)),
            vmem((2, 8, 32, 3072)),
            vmem((2, 16, 64, 128)),
            vmem((2048, 64)),
            vmem((2048, 64)),
            vmem((64, 2048)),
            vmem((2048, 128), f32),
            vmem((2, 16, 192, 128)),
            vmem((16, 192, 256)),
            vmem((16, 192, 256)),
            vmem((2, 64, 128), f32),
            vmem((2, 64, 128), f32),
            vmem((2, 32, 128), f32),
            vmem((2, 256, 512)),
            vmem((2, 4, 128, 1024)),
            vmem((2, 32, 32, 512)),
            vmem((32, 32, 1024)),
            vmem((8, 256, 512)),
            vmem((8, 256, 512)),
            vmem((256, 1024), f32),
            vmem((256, 1024)),
            vmem((256, 1024)),
            vmem((16, 64, 256)),
            vmem((8, 1024), f32),
            vmem((8, 512), f32),
            vmem((32, 16, 128), f32),
            vmem((16, 16, 128), f32),
            dma((144,)),
            dma((144,)),
            dma((7,)),
            dma((32,)),
            dma((32,)),
            dma((32,)),
            dma((32,)),
            dma((8,)),
            dma((8,)),
            dma((2, 3)),
        ],
        compiler_params=pltpu.CompilerParams(
            collective_id=collective_id, has_side_effects=True, vmem_limit_bytes=63 * MIB
        ),
        name="backward_attention",
    )(
        lengths, pairs, o_full, lse, x_t, normed_t, context_t, d_second, scaled, spread, gain, g_reduce, vec_in,
        slope, w_reduce, w_expand, w_out, w_qkv,
    )


def swap(x):
    return lax.ppermute(x, "fsdp", [(0, 1), (1, 0)])


def halves(left_t):
    core = lax.axis_index("fsdp")
    h = left_t.shape[0] // 2
    own = lax.dynamic_slice_in_dim(left_t, core * h, h, 0)
    return own, swap(lax.dynamic_slice_in_dim(left_t, (1 - core) * h, h, 0))


def chip_sum(left, right):
    core = lax.axis_index("fsdp")
    h = left.shape[1] // 2
    own = lax.dynamic_slice_in_dim(left, core * h, h, 1)
    other = swap(lax.dynamic_slice_in_dim(left, (1 - core) * h, h, 1))
    grad = outer_sum(own, right) + outer_sum(other, swap(right))
    return grad.astype(jnp.bfloat16).reshape(16, h // 16, right.shape[1])


def fast_shards(
    inputs,
    lengths,
    w_query,
    b_query,
    w_key,
    w_value,
    b_value,
    w_out,
    b_out,
    first_gain,
    first_shift,
    w_expand,
    b_expand,
    w_reduce,
    b_reduce,
    second_gain,
    second_shift,
    cotangent,
):
    f32, bf16 = jnp.float32, jnp.bfloat16
    seqs, count, width = inputs.shape
    total = seqs * count
    part = width // 32
    ff = w_expand.shape[1]
    qkv = jnp.concatenate([w_query, w_key, w_value], 1)
    bias = jnp.concatenate([b_query, b_value])[:, None] + jnp.zeros((2 * part, 128), bf16)
    small = [b_out, first_gain, first_shift, b_expand, b_reduce, second_gain, second_shift]
    vec = sum(jnp.pad(b[None, :], ((r, part - 1 - r), (0, 128 - b.shape[0]))) for r, b in enumerate(small))
    flat_rows = inputs.reshape(total, width)
    g_vec, g_out, g_expand, g_reduce, g_qkv, pairs, context_t, o_full, lse = forward_attention(
        flat_rows, lengths, qkv, bias, vec, w_out, w_expand, w_reduce, 1
    )
    full_out = g_out.reshape(width, width)
    full_expand = g_expand.reshape(width, ff)
    full_reduce = g_reduce.reshape(ff, width)
    bias_out, gain_first, shift_first, bias_expand, bias_reduce, gain_second, shift_second = (
        g_vec[:, r, : b.shape[0]].reshape(1, -1).astype(f32) for r, b in enumerate(small)
    )
    own_first = lax.axis_index("ctx") * count
    positions = own_first + jnp.arange(count, dtype=jnp.int32)
    valid_rows = (positions[None, :] < lengths[:, None]).astype(f32).reshape(total, 1)
    context_t = context_t.reshape(width, total)
    residual = flat_rows.astype(f32) + outer_sum(context_t, full_out) + bias_out
    center = residual - jnp.mean(residual, -1, keepdims=True)
    spread = lax.rsqrt(jnp.mean(center * center, -1, keepdims=True) + epsilon)
    scaled = center * spread
    normed = scaled * gain_first + shift_first
    normed_low = normed.astype(bf16)
    expanded = product(normed_low, full_expand) + bias_expand
    share = 0.5 * (1.0 + lax.erf(expanded * math.sqrt(0.5)))
    slope = (share + expanded * jnp.exp(-0.5 * expanded * expanded) * (1.0 / math.sqrt(2.0 * math.pi))).astype(bf16)
    activated_low = (expanded * share).astype(bf16)
    reduced = product(activated_low, full_reduce) + bias_reduce
    final_rows, second_pull = jax.vjp(layer_norm, normed + reduced, gain_second, shift_second)
    layer_out = (final_rows * valid_rows).astype(bf16).reshape(inputs.shape)
    d_output = cotangent.reshape(total, width).astype(f32) * valid_rows
    d_second, second_gain_grad, second_shift_grad = second_pull(d_output)
    d_reduced = d_second.astype(bf16)
    reduce_grad = chip_sum(activated_low, d_reduced)
    reduce_bias_grad = jnp.sum(d_reduced.astype(f32), 0)
    vec_in = sum(
        jnp.pad(g.reshape(32, 1, part), ((0, 0), (r, 15 - r), (0, 128 - part)))
        for r, g in ((4, reduce_bias_grad), (5, second_gain_grad), (6, second_shift_grad))
    )
    both = lambda rows_t: jnp.concatenate(halves(rows_t), 1)
    s_reduce, s_expand, s_out, s_vec, s_qkv, input_grad, s_bias = backward_attention(
        lengths, pairs, o_full, lse, both(flat_rows.T), both(normed_low.T), both(context_t), d_second, scaled, spread,
        gain_first, reduce_grad, vec_in, slope, g_reduce, g_expand, g_out, g_qkv, 2,
    )
    s_query, s_key, s_value = (s_qkv[:, width * i : width * (i + 1)] for i in range(3))
    s_bias = jnp.sum(s_bias, -1)
    v = [s_vec[r, : b.shape[0]] for r, b in enumerate(small)]
    return (
        layer_out,
        input_grad.reshape(inputs.shape),
        s_query,
        s_bias[0],
        s_key,
        s_value,
        s_bias[1],
        s_out,
        v[0],
        v[1],
        v[2],
        s_expand,
        v[3],
        s_reduce,
        v[4],
        v[5],
        v[6],
    )


def solution(mesh):
    fast = mesh.shape["fsdp"] == 2 and mesh.shape["ctx"] == HEADS
    shards = fast_shards if fast else general_shards
    return jax.shard_map(
        shards,
        mesh=mesh,
        in_specs=(
            P("fsdp", "ctx", None),
            P("fsdp"),
            P(("fsdp", "ctx"), None),
            P(("fsdp", "ctx")),
            P(("fsdp", "ctx"), None),
            P(("fsdp", "ctx"), None),
            P(("fsdp", "ctx")),
            P(("fsdp", "ctx"), None),
            P(("fsdp", "ctx")),
            P(("fsdp", "ctx")),
            P(("fsdp", "ctx")),
            P(("fsdp", "ctx"), None),
            P(("fsdp", "ctx")),
            P(("fsdp", "ctx"), None),
            P(("fsdp", "ctx")),
            P(("fsdp", "ctx")),
            P(("fsdp", "ctx")),
            P("fsdp", "ctx", None),
        ),
        out_specs=(
            P("fsdp", "ctx", None),
            P("fsdp", "ctx", None),
            P(("fsdp", "ctx"), None),
            P(("fsdp", "ctx")),
            P(("fsdp", "ctx"), None),
            P(("fsdp", "ctx"), None),
            P(("fsdp", "ctx")),
            P(("fsdp", "ctx"), None),
            P(("fsdp", "ctx")),
            P(("fsdp", "ctx")),
            P(("fsdp", "ctx")),
            P(("fsdp", "ctx"), None),
            P(("fsdp", "ctx")),
            P(("fsdp", "ctx"), None),
            P(("fsdp", "ctx")),
            P(("fsdp", "ctx")),
            P(("fsdp", "ctx")),
        ),
        check_vma=False,
    )
```

```python
from functools import partial
import math

import jax
import jax.numpy as jnp
from jax import lax
from jax.experimental import pallas as pl
from jax.experimental.pallas import tpu as pltpu
from jax.sharding import PartitionSpec as P

HEADS = 16


epsilon = 1e-05
masked_score = -1e30


def layer_norm(rows_in, gain, shift):
    center = rows_in - jnp.mean(rows_in, -1, keepdims=True)
    spread = jnp.mean(center * center, -1, keepdims=True)
    return center * lax.rsqrt(spread + epsilon) * gain + shift


def product(left, right):
    return jnp.dot(left, right, preferred_element_type=jnp.float32)


def outer_sum(left, right):
    return jnp.einsum("rd,re->de", left, right, preferred_element_type=jnp.float32)


def back_product(grad_rows, weight):
    return jnp.einsum("re,de->rd", grad_rows, weight, preferred_element_type=jnp.float32)


def over_blocks(step_fn, carry_state, pair_rows):
    key_count = pair_rows.shape[1]
    block_width = math.gcd(key_count, 512)

    def turn(turn_index, inner_state):
        block_pairs = lax.dynamic_slice_in_dim(pair_rows, turn_index * block_width, block_width, 1)
        return step_fn(inner_state, block_pairs, turn_index * block_width)

    return lax.fori_loop(0, key_count // block_width, turn, carry_state)


def general_shards(
    inputs,
    lengths,
    w_query,
    b_query,
    w_key,
    w_value,
    b_value,
    w_out,
    b_out,
    first_gain,
    first_shift,
    w_expand,
    b_expand,
    w_reduce,
    b_reduce,
    second_gain,
    second_shift,
    cotangent,
):
    gathered = (
        lax.all_gather(w_query, ("fsdp", "ctx"), axis=0, tiled=True),
        lax.all_gather(b_query, ("fsdp", "ctx"), axis=0, tiled=True),
        lax.all_gather(w_key, ("fsdp", "ctx"), axis=0, tiled=True),
        lax.all_gather(w_value, ("fsdp", "ctx"), axis=0, tiled=True),
        lax.all_gather(b_value, ("fsdp", "ctx"), axis=0, tiled=True),
        lax.all_gather(w_out, ("fsdp", "ctx"), axis=0, tiled=True),
        lax.all_gather(b_out, ("fsdp", "ctx"), axis=0, tiled=True),
        lax.all_gather(first_gain, ("fsdp", "ctx"), axis=0, tiled=True),
        lax.all_gather(first_shift, ("fsdp", "ctx"), axis=0, tiled=True),
        lax.all_gather(w_expand, ("fsdp", "ctx"), axis=0, tiled=True),
        lax.all_gather(b_expand, ("fsdp", "ctx"), axis=0, tiled=True),
        lax.all_gather(w_reduce, ("fsdp", "ctx"), axis=0, tiled=True),
        lax.all_gather(b_reduce, ("fsdp", "ctx"), axis=0, tiled=True),
        lax.all_gather(second_gain, ("fsdp", "ctx"), axis=0, tiled=True),
        lax.all_gather(second_shift, ("fsdp", "ctx"), axis=0, tiled=True),
    )
    (
        full_query,
        bias_query,
        full_key,
        full_value,
        bias_value,
        full_out,
        bias_out,
        gain_first,
        shift_first,
        full_expand,
        bias_expand,
        full_reduce,
        bias_reduce,
        gain_second,
        shift_second,
    ) = gathered
    seq_count, block_rows, model_width = inputs.shape
    total_rows = seq_count * block_rows
    head_size = model_width // HEADS
    score_scale = head_size ** (-0.5)
    own_first = lax.axis_index("ctx") * block_rows
    positions = own_first + jnp.arange(block_rows, dtype=jnp.int32)
    valid_rows = (positions[None, :] < lengths[:, None]).astype(jnp.float32).reshape(total_rows, 1)
    flat_rows = inputs.reshape(total_rows, model_width)
    queries = (product(flat_rows, full_query) + bias_query.astype(jnp.float32)).astype(jnp.bfloat16)
    key_rows = product(flat_rows, full_key).astype(jnp.bfloat16)
    value_rows = (product(flat_rows, full_value) + bias_value.astype(jnp.float32)).astype(
        jnp.bfloat16
    )
    query_heads = queries.reshape(seq_count, block_rows, HEADS, head_size)
    local_pairs = jnp.concatenate([key_rows, value_rows], -1).reshape(
        seq_count, block_rows, 2 * model_width
    )

    def key_allowed(first_row, key_count):
        return ((first_row + jnp.arange(key_count, dtype=jnp.int32))[None, :] < lengths[:, None])[
            :, None, None, :
        ]

    def split_pairs(block_pairs):
        key_count = block_pairs.shape[1]
        key_heads = block_pairs[:, :, :model_width].reshape(seq_count, key_count, HEADS, head_size)
        value_heads = block_pairs[:, :, model_width:].reshape(
            seq_count, key_count, HEADS, head_size
        )
        return (key_heads, value_heads, key_count)

    def forward_step(carry_state, block_pairs, first_row):
        running_max, running_sum, running_acc = carry_state
        key_heads, value_heads, key_count = split_pairs(block_pairs)
        allowed = key_allowed(first_row, key_count)
        scores = (
            jnp.einsum(
                "sqhd,skhd->shqk", query_heads, key_heads, preferred_element_type=jnp.float32
            )
            * score_scale
        )
        scores = jnp.where(allowed, scores, masked_score)
        new_max = jnp.maximum(running_max, jnp.max(scores, -1))
        factor = jnp.exp(running_max - new_max)
        exponents = jnp.where(allowed, jnp.exp(scores - new_max[..., None]), 0.0)
        new_sum = running_sum * factor + jnp.sum(exponents, -1)
        update = jnp.einsum(
            "shqk,skhd->sqhd",
            exponents.astype(jnp.bfloat16),
            value_heads,
            preferred_element_type=jnp.float32,
        )
        new_acc = running_acc * jnp.transpose(factor, (0, 2, 1))[..., None] + update
        return (new_max, new_sum, new_acc)

    start_state = (
        jnp.full((seq_count, HEADS, block_rows), masked_score, jnp.float32),
        jnp.zeros((seq_count, HEADS, block_rows), jnp.float32),
        jnp.zeros((seq_count, block_rows, HEADS, head_size), jnp.float32),
    )
    running_max, running_sum, running_acc = over_blocks(
        forward_step, start_state, lax.all_gather(local_pairs, "ctx", axis=1, tiled=True)
    )
    context_full = running_acc / jnp.transpose(running_sum, (0, 2, 1))[..., None]
    log_total = running_max + jnp.log(running_sum)
    context = context_full.reshape(total_rows, model_width).astype(jnp.bfloat16)
    attended = product(context, full_out) + bias_out.astype(jnp.float32)
    residual = flat_rows.astype(jnp.float32) + attended
    normed, first_pull = jax.vjp(
        layer_norm, residual, gain_first.astype(jnp.float32), shift_first.astype(jnp.float32)
    )
    normed_low = normed.astype(jnp.bfloat16)
    expanded = product(normed_low, full_expand) + bias_expand.astype(jnp.float32)
    activated, gelu_pull = jax.vjp(partial(jax.nn.gelu, approximate=False), expanded)
    activated_low = activated.astype(jnp.bfloat16)
    reduced = product(activated_low, full_reduce) + bias_reduce.astype(jnp.float32)
    final_rows, second_pull = jax.vjp(
        layer_norm,
        normed + reduced,
        gain_second.astype(jnp.float32),
        shift_second.astype(jnp.float32),
    )
    layer_out = (final_rows * valid_rows).astype(jnp.bfloat16).reshape(inputs.shape)
    d_output = cotangent.reshape(total_rows, model_width).astype(jnp.float32) * valid_rows
    d_second, second_gain_grad, second_shift_grad = second_pull(d_output)
    d_reduced = d_second.astype(jnp.bfloat16)
    reduce_grad = outer_sum(activated_low, d_reduced)
    reduce_bias_grad = jnp.sum(d_reduced.astype(jnp.float32), 0)
    (d_expanded_full,) = gelu_pull(back_product(d_reduced, full_reduce))
    d_expanded = d_expanded_full.astype(jnp.bfloat16)
    expand_grad = outer_sum(normed_low, d_expanded)
    expand_bias_grad = jnp.sum(d_expanded.astype(jnp.float32), 0)
    d_normed = d_second + back_product(d_expanded, full_expand)
    d_first, first_gain_grad, first_shift_grad = first_pull(d_normed)
    d_attended = d_first.astype(jnp.bfloat16)
    out_grad = outer_sum(context, d_attended)
    out_bias_grad = jnp.sum(d_attended.astype(jnp.float32), 0)
    d_context = back_product(d_attended, full_out).astype(jnp.bfloat16)
    d_context_heads = d_context.reshape(seq_count, block_rows, HEADS, head_size)
    delta = jnp.transpose(
        jnp.sum(d_context_heads.astype(jnp.float32) * context_full, -1), (0, 2, 1)
    )
    whole_length = block_rows * lax.axis_size("ctx")

    def score_grads(key_heads, value_heads, allowed):
        scores = (
            jnp.einsum(
                "sqhd,skhd->shqk", query_heads, key_heads, preferred_element_type=jnp.float32
            )
            * score_scale
        )
        probabilities = jnp.where(allowed, jnp.exp(scores - log_total[..., None]), 0.0)
        d_probs = jnp.einsum(
            "sqhd,skhd->shqk", d_context_heads, value_heads, preferred_element_type=jnp.float32
        )
        d_scores = (probabilities * (d_probs - delta[..., None])).astype(jnp.bfloat16)
        return (probabilities, d_scores)

    def backward_step(carry_state, block_pairs, first_row):
        grad_query, grad_pairs = carry_state
        key_heads, value_heads, key_count = split_pairs(block_pairs)
        probabilities, d_scores = score_grads(
            key_heads, value_heads, key_allowed(first_row, key_count)
        )
        grad_query = (
            grad_query
            + jnp.einsum("shqk,skhd->sqhd", d_scores, key_heads, preferred_element_type=jnp.float32)
            * score_scale
        )
        key_part = (
            jnp.einsum("shqk,sqhd->skhd", d_scores, query_heads, preferred_element_type=jnp.float32)
            * score_scale
        )
        value_part = jnp.einsum(
            "shqk,sqhd->skhd",
            probabilities.astype(jnp.bfloat16),
            d_context_heads,
            preferred_element_type=jnp.float32,
        )
        fresh = jnp.concatenate(
            [
                key_part.reshape(seq_count, key_count, model_width),
                value_part.reshape(seq_count, key_count, model_width),
            ],
            -1,
        )
        before = lax.dynamic_slice_in_dim(grad_pairs, first_row, key_count, 1)
        grad_pairs = lax.dynamic_update_slice_in_dim(grad_pairs, before + fresh, first_row, 1)
        return (grad_query, grad_pairs)

    query_zero = jnp.zeros((seq_count, block_rows, HEADS, head_size), jnp.float32)
    back_state = (query_zero, jnp.zeros((seq_count, whole_length, 2 * model_width), jnp.float32))
    back_result = over_blocks(
        backward_step, back_state, lax.all_gather(local_pairs, "ctx", axis=1, tiled=True)
    )
    grad_query = back_result[0]
    own_pairs = lax.psum_scatter(
        back_result[1].astype(jnp.bfloat16), "ctx", scatter_dimension=1, tiled=True
    ).astype(jnp.float32)
    d_keys = own_pairs[:, :, :model_width].reshape(total_rows, model_width).astype(jnp.bfloat16)
    d_values = own_pairs[:, :, model_width:].reshape(total_rows, model_width).astype(jnp.bfloat16)
    d_queries = grad_query.reshape(total_rows, model_width).astype(jnp.bfloat16)
    query_grad = outer_sum(flat_rows, d_queries)
    query_bias_grad = jnp.sum(d_queries.astype(jnp.float32), 0)
    key_grad = outer_sum(flat_rows, d_keys)
    value_grad = outer_sum(flat_rows, d_values)
    value_bias_grad = jnp.sum(d_values.astype(jnp.float32), 0)
    input_grad = (
        d_first
        + back_product(d_queries, full_query)
        + back_product(d_keys, full_key)
        + back_product(d_values, full_value)
    ).reshape(inputs.shape)
    shares = (
        lax.psum_scatter(query_grad, ("fsdp", "ctx"), scatter_dimension=0, tiled=True),
        lax.psum_scatter(query_bias_grad, ("fsdp", "ctx"), scatter_dimension=0, tiled=True),
        lax.psum_scatter(key_grad, ("fsdp", "ctx"), scatter_dimension=0, tiled=True),
        lax.psum_scatter(value_grad, ("fsdp", "ctx"), scatter_dimension=0, tiled=True),
        lax.psum_scatter(value_bias_grad, ("fsdp", "ctx"), scatter_dimension=0, tiled=True),
        lax.psum_scatter(out_grad, ("fsdp", "ctx"), scatter_dimension=0, tiled=True),
        lax.psum_scatter(out_bias_grad, ("fsdp", "ctx"), scatter_dimension=0, tiled=True),
        lax.psum_scatter(first_gain_grad, ("fsdp", "ctx"), scatter_dimension=0, tiled=True),
        lax.psum_scatter(first_shift_grad, ("fsdp", "ctx"), scatter_dimension=0, tiled=True),
        lax.psum_scatter(expand_grad, ("fsdp", "ctx"), scatter_dimension=0, tiled=True),
        lax.psum_scatter(expand_bias_grad, ("fsdp", "ctx"), scatter_dimension=0, tiled=True),
        lax.psum_scatter(reduce_grad, ("fsdp", "ctx"), scatter_dimension=0, tiled=True),
        lax.psum_scatter(reduce_bias_grad, ("fsdp", "ctx"), scatter_dimension=0, tiled=True),
        lax.psum_scatter(second_gain_grad, ("fsdp", "ctx"), scatter_dimension=0, tiled=True),
        lax.psum_scatter(second_shift_grad, ("fsdp", "ctx"), scatter_dimension=0, tiled=True),
    )
    return (
        layer_out,
        input_grad,
        shares[0],
        shares[1],
        shares[2],
        shares[3],
        shares[4],
        shares[5],
        shares[6],
        shares[7],
        shares[8],
        shares[9],
        shares[10],
        shares[11],
        shares[12],
        shares[13],
        shares[14],
    )


MESH = pl.DeviceIdType.MESH
MIB = 1024*1024

def place():
    core = lax.axis_index("fsdp"); chip = lax.axis_index("ctx")
    return core, chip

def greet(peers):
    barrier = pltpu.get_barrier_semaphore()
    for peer in peers:
        pl.semaphore_signal(barrier, inc=1, device_id=peer, device_id_type=MESH)
    pl.semaphore_wait(barrier, len(peers))

def flip(v, bits):
    for b in (1, 2, 4, 8):
        if bits & b:
            v = v + b - 2 * b * lax.rem(lax.div(v, b), 2)
    return v

LOG2E = math.log2(math.e)


def nt(a, b):
    return lax.dot_general(a, b, (((1,), (1,)), ((), ())), preferred_element_type=jnp.float32)


FULL_ORDER = (12, 8, 4, 15, 11, 7, 14, 13, 10, 9, 6, 5, 3, 2, 1)


class Copies:
    def __init__(self, send_sem, recv_sem):
        self.send_sem, self.recv_sem = send_sem, recv_sem
        self.names, self.sent = {}, []

    def pair(self, name, src, dst, peer):
        i = self.names.setdefault(name, len(self.names))
        return pltpu.make_async_remote_copy(
            src_ref=src,
            dst_ref=dst,
            send_sem=self.send_sem.at[i],
            recv_sem=self.recv_sem.at[i],
            device_id=peer,
            device_id_type=MESH,
        )

    def send(self, name, src, dst, peer, like):
        self.pair(name, src, dst, peer).start()
        self.sent.append((name, like))

    def arrived(self, name, dst, peer):
        self.pair(name, dst, dst, peer).wait_recv()

    def drain(self, peer):
        for name, like in self.sent:
            self.pair(name, like, like, peer).wait_send()


class Gather:
    def __init__(self, copies, name, src, out, local_sem):
        self.copies, self.name, self.src, self.out, self.local_sem = copies, name, src, out, local_sem
        self.core, self.chip = place()
        self.sib = (1 - self.core, self.chip)
        self.half = src.shape[0] // 2

    def at(self, bits):
        return (self.core, flip(self.chip, bits))

    def block(self, bits, core=None):
        return self.out.at[(self.core if core is None else core) * 16 + flip(self.chip, bits)]

    def part(self, bits, upper):
        return self.out.at[self.core * 16 + flip(self.chip, bits), pl.ds(self.half if upper else 0, self.half)]

    def send(self, tag, src, dst, peer, half=False):
        like = self.src.at[pl.ds(0, self.half)] if half else self.src
        self.copies.send((self.name, tag), src, dst, peer, like)

    def arrived(self, tag, dst):
        self.copies.arrived((self.name, tag), dst, self.sib)

    def start_z(self):
        for z in (12, 8, 4):
            self.send(("z", z), self.src, self.block(0), self.at(z))

    def start_plane(self):
        self.send(("x", 0), self.src, self.block(0), self.at(1))
        self.send(("y", 0), self.src, self.block(0), self.at(2))
        self.send(("s", 0), self.src, self.block(0), self.sib)
        self.local = pltpu.make_async_copy(self.src, self.block(0), self.local_sem)
        self.local.start()

    def on_z(self, z):
        b = self.block(z)
        self.arrived(("z", z), b)
        self.send(("x", z), b, b, self.at(1))
        self.send(("y", z), b, b, self.at(2))
        self.send(("s", z), b, b, self.sib)

    def on_plane(self, z):
        for bit, tag, further, upper in ((1, "x", 2, False), (2, "y", 1, True)):
            b = self.block(z + bit)
            self.arrived((tag, z), b)
            h = self.part(z + bit, upper)
            self.send(("d" + tag, z), h, h, self.at(further), True)
            self.send(("s", z + bit), b, b, self.sib)

    def on_diagonal(self, z):
        self.arrived(("dx", z), self.part(z + 3, False))
        self.arrived(("dy", z), self.part(z + 3, True))
        b = self.block(z + 3)
        self.send(("s", z + 3), b, b, self.sib)

    def on_sibling(self):
        for bits in range(16):
            self.arrived(("s", bits), self.block(bits, 1 - self.core))
        self.local.wait()


def load_sequence(r_ref, s, kk_ref, vt_ref=None, vv_ref=None):
    for j in range(r_ref.shape[1]):
        span = pl.ds(j * 128, 128)
        kk_ref[span] = r_ref[s, j, 64:128, :].astype(jnp.float32).T.astype(jnp.bfloat16)
        if vt_ref is not None:
            vt_ref[:, span] = r_ref[s, j, 128:192, :]
        if vv_ref is not None:
            vv_ref[span] = r_ref[s, j, 128:192, :].astype(jnp.float32).T.astype(jnp.bfloat16)


def fwd_kernel(
    x_ref, lengths_ref, s_qkv, s_bias, s_vec, s_out, s_expand, s_reduce,
    o_out, o_expand, o_reduce, o_qkv, o_pairs, o_full, lse_ref,
    o_rows, o_scaled, o_spread, o_active, o_slope, o_turned, o_active_t,
    w_qkv, w_bias, w_vec, w_out, w_expand, send_blk, recv_blk, ctx_blk, ctx_recv, kk, vt,
    e_row, x_turned, n_turned, normed, stage, turned, active_t, ctx_sib,
    send_sem, recv_sem, local_sem, hsend, hrecv, csend, crecv, tsend, trecv, wsem,
):
    f32, bf16 = jnp.float32, jnp.bfloat16
    core, chip = place()
    sib = (1 - core, chip)
    greet([sib] + [(core, flip(chip, b)) for b in range(1, 16)])
    copies = Copies(send_sem, recv_sem)
    first = [
        Gather(copies, 0, s_qkv, w_qkv, local_sem.at[0]),
        Gather(copies, 1, s_bias, w_bias, local_sem.at[1]),
    ]
    rest = [
        Gather(copies, 2, s_out, o_out, local_sem.at[2]),
        Gather(copies, 3, s_vec, w_vec, local_sem.at[3]),
        Gather(copies, 4, s_expand, o_expand, local_sem.at[4]),
        Gather(copies, 5, s_reduce, o_reduce, local_sem.at[5]),
    ]
    for g in first:
        g.start_z()
        g.start_plane()

    def turn(slot, src, kept):
        c = pltpu.make_async_remote_copy(
            src_ref=src,
            dst_ref=turned.at[slot, 1],
            send_sem=tsend.at[slot],
            recv_sem=trecv.at[slot],
            device_id=sib,
            device_id_type=MESH,
        )
        c.start()
        turned[slot, 0] = kept[...]
        return c

    for i in range(4):
        x_turned[i // 2, 256 * (i % 2) : 256 * (i % 2) + 256] = x_ref[:, 256 * i : 256 * i + 256].astype(f32).T.astype(bf16)
    swaps = [turn(0, x_turned.at[1 - core], x_turned.at[core])]
    for z in (4, 8, 12):
        for g in first:
            g.on_z(z)
    for g in rest[:3]:
        g.start_z()
    for z in (0, 4, 8, 12):
        for g in first:
            g.on_plane(z)
    for g in rest:
        g.start_plane()
    for z in (0, 4, 8, 12):
        for g in first:
            g.on_diagonal(z)
    for g in first:
        g.on_sibling()
    keep = pltpu.make_async_copy(w_qkv, o_qkv, local_sem.at[6])
    keep.start()

    for part in range(3):

        @pl.loop(0, 4)
        def _(p):
            w = w_qkv[:, :, pl.ds(pl.multiple_of(part * 1024 + p * 256, 256), 256)].reshape(1024, 256)
            t = jnp.dot(x_ref[...], w, preferred_element_type=f32).T
            for i in range(4):
                h = 4 * p + i
                rows = t[64 * i : 64 * i + 64]
                if part != 1:
                    own = pl.ds(0 if part == 0 else 32, 32)
                    bias = jnp.concatenate([w_bias[2 * h + k, own] for k in range(2)], 0).astype(f32)
                    rows = rows + jnp.concatenate([bias, bias], 1)
                send_blk[h, pl.ds(64 * part, 64)] = rows.astype(bf16)

    heads = []
    for s in range(2):
        for b in FULL_ORDER:
            to = flip(chip, b)
            i = s * 16 + b
            c = pltpu.make_async_remote_copy(
                src_ref=send_blk.at[to, :, pl.ds(128 * s, 128)],
                dst_ref=recv_blk.at[s, chip],
                send_sem=hsend.at[i],
                recv_sem=hrecv.at[i],
                device_id=(core, to),
                device_id_type=MESH,
            )
            c.start()
            heads.append(c)
        recv_blk[s, chip] = send_blk[chip, :, pl.ds(128 * s, 128)]

    def heads_here(s):
        for b in FULL_ORDER:
            i = s * 16 + b
            here = recv_blk.at[s, flip(chip, b)]
            pltpu.make_async_remote_copy(
                src_ref=here, dst_ref=here, send_sem=hsend.at[i], recv_sem=hrecv.at[i], device_id=sib, device_id_type=MESH
            ).wait_recv()

    rest[3].start_z()
    events = [lambda: [g.on_plane(0) for g in rest]]
    for z in (4, 8, 12):
        events.append(lambda z=z: [g.on_z(z) for g in rest[:3]])
    events.append(lambda: [g.on_diagonal(0) for g in rest])
    for z in (4, 8, 12):
        events.append(lambda z=z: [g.on_plane(z) for g in rest[:3]])
    for z in (4, 8, 12):
        events.append(lambda z=z: [rest[3].on_z(z)])
    for z in (4, 8, 12):
        events.append(lambda z=z: [g.on_diagonal(z) for g in rest[:3]])
    READY = len(events)
    for z in (4, 8, 12):
        events.append(lambda z=z: [rest[3].on_plane(z)])
    for z in (4, 8, 12):
        events.append(lambda z=z: [rest[3].on_diagonal(z)])

    def attend_sequence(s, during):
        load_sequence(recv_blk, s, kk, vt_ref=vt)

        @pl.loop(0, 8)
        def _(step):
            for k, event in enumerate(during):

                @pl.when(step == k)
                def _():
                    event()

            q = flip_by(step, chip // 2)
            query = jnp.concatenate([recv_blk[s, 2 * q, 0:64, :], recv_blk[s, 2 * q + 1, 0:64, :]], 1)
            scores = jnp.dot(kk[...], query, preferred_element_type=f32) * (0.125 * LOG2E)
            key = lax.broadcasted_iota(jnp.int32, scores.shape, 0)
            scores = jnp.where(key < lengths_ref[s], scores, masked_score)
            top = jnp.max(scores, 0, keepdims=True)
            e = jnp.exp2(scores - top)
            mass = jnp.sum(e, 0, keepdims=True)
            o = jnp.dot(vt[...], e.astype(bf16), preferred_element_type=f32) / mass
            lse_ref[s, pl.ds(q, 1), :] = top + jnp.log2(mass)
            o_full[s, :, pl.ds(pl.multiple_of(q * 256, 256), 256)] = o
            for i in range(2):
                to = 2 * q + i
                ctx_blk[s, to] = o[:, 128 * i : 128 * i + 128].astype(bf16)

                @pl.when(to != chip)
                def _():
                    pltpu.make_async_remote_copy(
                        src_ref=ctx_blk.at[s, to],
                        dst_ref=ctx_recv.at[chip, :, pl.ds(128 * s, 128)],
                        send_sem=csend.at[s * 16 + to],
                        recv_sem=crecv.at[s * 16 + chip],
                        device_id=(core, to),
                        device_id_type=MESH,
                    ).start()

        ctx_recv[chip, :, pl.ds(128 * s, 128)] = ctx_blk[s, chip]

    PRE, FIRST, SECOND = 5, 3, 3
    for event in events[:PRE]:
        event()
    heads_here(0)
    attend_sequence(0, events[PRE : PRE + FIRST])
    heads_here(1)
    pairs_out = pltpu.make_async_copy(recv_blk, o_pairs, local_sem.at[7])
    pairs_out.start()
    attend_sequence(1, events[PRE + FIRST : PRE + FIRST + SECOND])
    for event in events[PRE + FIRST + SECOND : READY]:
        event()
    for g in rest[:3]:
        g.on_sibling()
    out_weights = pltpu.make_async_copy(o_out, w_out, local_sem.at[6 + 2])
    out_weights.start()

    def fetch(c, slot):
        cols = pl.ds(pl.multiple_of(c * 512, 512), 512)
        return pltpu.make_async_copy(o_expand.at[:, :, cols], w_expand.at[slot], wsem.at[slot])

    fetch(0, 0).start()

    owner = lax.broadcasted_iota(jnp.int32, (32, 1024), 0)
    column = lax.broadcasted_iota(jnp.int32, (32, 1024), 1)
    lane = lax.broadcasted_iota(jnp.int32, (128, 1024), 0)
    pick = jnp.where(lax.rem(lax.broadcasted_iota(jnp.int32, (128, 1024), 1), 32) == lane, 1.0, 0.0).astype(bf16)
    o_rows[...] = jnp.zeros_like(o_rows)
    for r in range(7):
        choose = jnp.where(column == owner * 32 + r, 1.0, 0.0).astype(bf16)
        piece = jnp.dot(choose, w_vec[...].reshape(1024, 128), preferred_element_type=f32)
        if r == 3:
            for o in range(32):
                e_row[o // 4 : o // 4 + 1, 128 * (o % 4) : 128 * (o % 4) + 128] = piece[o : o + 1]
        else:
            spread_row = jnp.dot(piece.astype(bf16), pick, preferred_element_type=f32)
            o_rows[r : r + 1] = jnp.sum(jnp.where(lax.div(column, 32) == owner, spread_row, 0.0), 0, keepdims=True)

    for s in range(2):
        for b in range(1, 16):
            other = flip(chip, b)
            here = ctx_recv.at[other, :, pl.ds(128 * s, 128)]
            pltpu.make_async_remote_copy(
                src_ref=ctx_blk.at[s, other],
                dst_ref=here,
                send_sem=csend.at[s * 16 + other],
                recv_sem=crecv.at[s * 16 + other],
                device_id=sib,
                device_id_type=MESH,
            ).wait()
    mine, others = pl.ds(core * 8, 8), pl.ds((1 - core) * 8, 8)
    swaps.append(
        pltpu.make_async_remote_copy(
            src_ref=ctx_recv.at[others],
            dst_ref=ctx_sib,
            send_sem=tsend.at[2],
            recv_sem=trecv.at[2],
            device_id=sib,
            device_id_type=MESH,
        )
    )
    swaps[-1].start()
    turned[2, 0] = ctx_recv[mine].reshape(512, 256)
    out_weights.wait()
    for i in range(4):
        rows = ctx_recv[4 * i : 4 * i + 4].reshape(256, 256).astype(f32).T.astype(bf16)
        term = jnp.dot(rows, w_out[8 * i : 8 * i + 8].reshape(256, 1024), preferred_element_type=f32)
        if i == 0:
            o_scaled[...] = term + (x_ref[...].astype(f32) + o_rows[0:1])
        else:
            o_scaled[...] += term

    @pl.loop(0, 4)
    def _(i):
        span = pl.ds(pl.multiple_of(i * 64, 64), 64)
        residual = o_scaled[span]
        center = residual - jnp.mean(residual, -1, keepdims=True)
        spread = lax.rsqrt(jnp.mean(center * center, -1, keepdims=True) + epsilon)
        x_hat = center * spread
        o_scaled[span] = x_hat
        o_spread[span] = jnp.broadcast_to(spread, (64, 128))
        normed[span] = (x_hat * o_rows[1:2] + o_rows[2:3]).astype(bf16)

    for i in range(4):
        n_turned[i // 2, 256 * (i % 2) : 256 * (i % 2) + 256] = normed[:, 256 * i : 256 * i + 256].astype(f32).T.astype(bf16)
    swaps.append(turn(1, n_turned.at[1 - core], n_turned.at[core]))

    def active_copy(j):
        return pltpu.make_async_remote_copy(
            src_ref=stage.at[j],
            dst_ref=active_t.at[1, j],
            send_sem=tsend.at[3 + j],
            recv_sem=trecv.at[3 + j],
            device_id=sib,
            device_id_type=MESH,
        )

    last_events = events[READY:]

    @pl.loop(0, 8)
    def _(c):
        for k, event in enumerate(last_events[:8]):

            @pl.when(c == k)
            def _():
                event()

        slot = lax.rem(c, 2)

        @pl.when(c < 7)
        def _():
            fetch(c + 1, 1 - slot).start()

        fetch(c, slot).wait()
        expanded = jnp.dot(normed[...], w_expand[slot].reshape(1024, 512), preferred_element_type=f32) + e_row[pl.ds(c, 1)]
        share = 0.5 * (1.0 + lax.erf(expanded * math.sqrt(0.5)))
        bell = jnp.exp(-0.5 * expanded * expanded) * (1.0 / math.sqrt(2.0 * math.pi))
        o_slope[c] = (share + expanded * bell).astype(bf16)
        active = (expanded * share).astype(bf16)
        o_active[c] = active
        across = active.astype(f32).T.astype(bf16)
        j = lax.rem(c, 4)

        @pl.when(lax.div(c, 4) == core)
        def _():
            active_t[0, j] = across

        @pl.when(lax.div(c, 4) != core)
        def _():
            stage[j] = across
            active_copy(j).start()

    for event in last_events[8:]:
        event()
    rest[3].on_sibling()
    for c in swaps:
        c.wait()
    turned[2, 1] = ctx_sib[...].reshape(512, 256)
    for j in range(4):
        active_copy(j).wait()
    o_turned[...] = turned[...]
    o_active_t[...] = active_t[...]
    for c in heads:
        c.wait_send()
    copies.drain(sib)
    keep.wait()
    pairs_out.wait()


def flip_by(v, w):
    out = 0
    for b in (1, 2, 4):
        p, q = lax.rem(lax.div(v, b), 2), lax.rem(lax.div(w, b), 2)
        out = out + b * (p + q - 2 * p * q)
    return out


def forward_attention(rows, lengths, qkv, bias, vec, w_out, w_expand, w_reduce, collective_id):
    v, hbm = pl.BlockSpec(memory_space=pltpu.VMEM), pl.BlockSpec(memory_space=pl.ANY)
    f32, bf16 = jnp.float32, jnp.bfloat16
    gathered = lambda x: jax.ShapeDtypeStruct((32,) + x.shape, x.dtype)
    dma = pltpu.SemaphoreType.DMA
    array = jax.ShapeDtypeStruct
    vmem = lambda shape, dtype=bf16: pltpu.VMEM(shape, dtype)
    return pl.pallas_call(
        fwd_kernel,
        out_shape=[
            gathered(w_out),
            gathered(w_expand),
            gathered(w_reduce),
            gathered(qkv),
            array((2, 16, 192, 128), bf16),
            array((2, 64, 2048), f32),
            array((2, 8, 256), f32),
            array((8, 1024), f32),
            array((256, 1024), f32),
            array((256, 128), f32),
            array((8, 256, 512), bf16),
            array((8, 256, 512), bf16),
            array((3, 2, 512, 256), bf16),
            array((2, 4, 512, 256), bf16),
        ],
        in_specs=[v, pl.BlockSpec(memory_space=pltpu.SMEM)] + [hbm] * 6,
        out_specs=[hbm] * 5 + [v] * 9,
        scratch_shapes=[
            vmem((32,) + qkv.shape),
            vmem((32,) + bias.shape),
            vmem((32,) + vec.shape),
            vmem((32,) + w_out.shape),
            vmem((2, 32, 32, 512)),
            vmem((16, 192, 256)),
            vmem((2, 16, 192, 128)),
            vmem((2, 16, 64, 128)),
            vmem((16, 64, 256)),
            vmem((2048, 64)),
            vmem((64, 2048)),
            vmem((8, 512), f32),
            vmem((2, 512, 256)),
            vmem((2, 512, 256)),
            vmem((256, 1024)),
            vmem((4, 512, 256)),
            vmem((3, 2, 512, 256)),
            vmem((2, 4, 512, 256)),
            vmem((8, 64, 256)),
            dma((210,)),
            dma((210,)),
            dma((9,)),
            dma((32,)),
            dma((32,)),
            dma((32,)),
            dma((32,)),
            dma((7,)),
            dma((7,)),
            dma((2,)),
        ],
        compiler_params=pltpu.CompilerParams(
            collective_id=collective_id, has_side_effects=True, vmem_limit_bytes=60 * MIB
        ),
        name="forward_attention",
    )(rows, lengths, qkv, bias, vec, w_out, w_expand, w_reduce)


class Scatter:
    ORDER = (12, 8, 4, 0)

    def __init__(self, copies, name, grads, out, bufs):
        self.copies, self.name, self.grads, self.out = copies, name, grads, out
        self.first, self.second, self.third = bufs
        self.core, self.chip = place()
        self.rows = grads.shape[1]
        self.half = self.rows // 2
        self.lo, self.hi = pl.ds(0, self.half), pl.ds(self.half, self.half)
        self.first_at = [[self.first.at[k, i] for i in range(2)] for k in range(4)]
        self.second_at = [[self.second.at[k, i] for i in range(2)] for k in range(4)]
        self.third_at = [self.third.at[k] for k in range(3)]

    def at(self, bits):
        return (self.core, flip(self.chip, bits))

    def send(self, tag, src, dst, bits, half=True):
        like = self.first_at[0][0] if half else self.third_at[0]
        self.copies.send((self.name, tag), src, dst, self.at(bits), like)

    def arrived(self, tag, dst):
        self.copies.arrived((self.name, tag), dst, self.at(1))

    def add(self, rows, fn):
        step = min(rows, 16)
        if rows == step:
            fn(0, step)
            return

        def turn(i, carry):
            fn(pl.multiple_of(i * step, step), step)
            return carry

        lax.fori_loop(0, rows // step, turn, 0)

    def start(self):
        for k, z in enumerate(self.ORDER):
            diag = flip(self.chip, z + 3)
            self.send(("1a", k), self.grads.at[diag, self.lo], self.first_at[k][0], 2)
            self.send(("1b", k), self.grads.at[diag, self.hi], self.first_at[k][1], 1)

    def start_direct(self):
        for k, z in enumerate(self.ORDER):
            xb, yb = flip(self.chip, z + 1), flip(self.chip, z + 2)
            self.send(("2xh", k), self.grads.at[xb, self.hi], self.second_at[k][0].at[self.hi], 1)
            self.send(("2yl", k), self.grads.at[yb, self.lo], self.second_at[k][1].at[self.lo], 2)

    def on_first(self, k):
        z = self.ORDER[k]
        for i, (tag, bit, upper) in enumerate((("1a", 1, False), ("1b", 2, True))):
            owner = flip(self.chip, z + bit)
            here = self.first_at[k][i]
            self.arrived((tag, k), here)

            def fn(start, size):
                rows = pl.ds(start, size)
                theirs = pl.ds(start + (self.half if upper else 0), size)
                here[rows] = here[rows] + self.grads.at[owner][theirs]

            self.add(self.half, fn)
            self.send(("2" + "xy"[i] + "lh"[i], k), here, self.second_at[k][i].at[self.hi if upper else self.lo], bit)

    def on_second(self, k):
        z = self.ORDER[k]
        self.arrived(("2xh", k), self.second_at[k][0].at[self.hi])
        self.arrived(("2yl", k), self.second_at[k][1].at[self.lo])
        self.arrived(("2xl", k), self.second_at[k][0].at[self.lo])
        self.arrived(("2yh", k), self.second_at[k][1].at[self.hi])
        owner = flip(self.chip, z)

        def fn(start, size):
            rows = pl.ds(start, size)
            f32 = jnp.float32
            total = self.grads.at[owner][rows].astype(f32) + self.second_at[k][0][rows].astype(f32)
            total = total + self.second_at[k][1][rows].astype(f32)
            if k < 3:
                self.second_at[k][0][rows] = total.astype(self.second.dtype)
            else:
                self.out[rows] = total

        self.add(self.rows, fn)
        if k < 3:
            self.send(("3", k), self.second_at[k][0], self.third_at[k], z, False)

    def on_third(self):
        for k in range(3):
            self.arrived(("3", k), self.third_at[k])

        def fn(start, size):
            rows = pl.ds(start, size)
            total = self.out[rows]
            for k in range(3):
                total = total + self.third_at[k][rows].astype(jnp.float32)
            self.out[rows] = total

        self.add(self.rows, fn)


def scatter_buffers(block, dtype):
    rows, cols = block
    return [
        pltpu.VMEM((4, 2, rows // 2, cols), dtype),
        pltpu.VMEM((4, 2, rows, cols), dtype),
        pltpu.VMEM((3, rows, cols), dtype),
    ]


def bwd_kernel(*refs):
    f32, bf16 = jnp.float32, jnp.bfloat16
    (
        lengths_ref, pairs, o_full, lse_ref, rows_t, active_t, cotangent, scaled, spread, vectors,
        h_active, h_slope, h_reduce, h_expand, h_out, h_qkv,
    ) = refs[:16]
    (o_layer, o_reduce, o_expand, o_out, o_vec, o_qkv, o_input, o_bias) = refs[16:24]
    bufs = [refs[24 + 3 * i : 27 + 3 * i] for i in range(5)]
    (
        g_reduce, g_expand, g_out, g_vec, g_qkv, w_qkv, d_recv, kk, vv, kt, acc, d_send, d_own, d_sib, b_own, b_sib, b_in,
        slopes, w_reduce, w_expand, w_out, e_own, e_sib, d_first, a_own, a_sib, d_ctx, rows_sum, e_sum, vec_own, vec_sib, r_own, r_sib,
        send_sem, recv_sem, local_sem, dsend, drecv, qsend, qrecv, esend, erecv, wsem,
    ) = refs[39:]
    core, chip = place()
    sib = (1 - core, chip)
    greet([sib] + [(core, flip(chip, b)) for b in range(1, 16)])
    copies = Copies(send_sem, recv_sem)
    rest = [
        Scatter(copies, i, g, o, bufs[i])
        for i, (g, o) in enumerate(((g_reduce, o_reduce), (g_expand, o_expand), (g_out, o_out), (g_vec, o_vec)))
    ]
    last = Scatter(copies, 4, g_qkv, o_qkv, bufs[4])
    out_weights = pltpu.make_async_copy(h_out, w_out, local_sem.at[4])
    out_weights.start()

    def fetch(c, slot, back):
        cols = pl.ds(pl.multiple_of(c * 512, 512), 512)
        copies_in = [
            pltpu.make_async_copy(h_reduce.at[pl.ds(c * 4, 4)], w_reduce.at[slot], wsem.at[slot, 0]),
            pltpu.make_async_copy((h_slope if back else h_active).at[c], slopes.at[slot], wsem.at[slot, 2]),
        ]
        if back:
            copies_in.append(pltpu.make_async_copy(h_expand.at[:, :, cols], w_expand.at[slot], wsem.at[slot, 1]))
        return copies_in

    for c in fetch(0, 0, False):
        c.start()
    d_first[...] = scaled[...] * vectors[1:2] + (vectors[2:3] + vectors[4:5])

    @pl.loop(0, 8)
    def _(c):
        slot = lax.rem(c, 2)

        @pl.when(c < 7)
        def _():
            for copy in fetch(c + 1, 1 - slot, False):
                copy.start()

        @pl.when(c == 7)
        def _():
            for copy in fetch(0, 0, True):
                copy.start()

        for copy in fetch(c, slot, False):
            copy.wait()
        d_first[...] += jnp.dot(slopes[slot], w_reduce[slot].reshape(512, 1024), preferred_element_type=f32)

    rows_sum[...] = jnp.zeros_like(rows_sum)

    @pl.loop(0, 4)
    def _(i):
        span = pl.ds(pl.multiple_of(i * 64, 64), 64)
        total = d_first[span]
        center = total - jnp.mean(total, -1, keepdims=True)
        width = lax.rsqrt(jnp.mean(center * center, -1, keepdims=True) + epsilon)
        x_hat = center * width
        row = chip * 128 + lax.rem(i, 2) * 64 + lax.broadcasted_iota(jnp.int32, (64, 1024), 0)
        valid = row < lengths_ref[lax.div(i, 2)]
        o_layer[span] = jnp.where(valid, x_hat * vectors[5:6] + vectors[6:7], 0.0).astype(bf16)
        d_output = jnp.where(valid, cotangent[span].astype(f32), 0.0)
        pulled = d_output * vectors[5:6]
        level = jnp.mean(pulled, -1, keepdims=True)
        slope = jnp.mean(pulled * x_hat, -1, keepdims=True)
        d_rows = width * (pulled - level - x_hat * slope)
        d_low = d_rows.astype(bf16)
        d_first[span] = d_rows
        r_own[span] = d_low
        rows_sum[4:5] += jnp.sum(d_low.astype(f32), 0, keepdims=True)
        rows_sum[5:6] += jnp.sum(d_output * x_hat, 0, keepdims=True)
        rows_sum[6:7] += jnp.sum(d_output, 0, keepdims=True)

    copies.send("r", r_own, r_sib, sib, r_own)
    copies.arrived("r", r_sib, sib)

    @pl.loop(0, 4)
    def _(j):
        g = jnp.dot(active_t[0, j], r_own[...], preferred_element_type=f32)
        g = g + jnp.dot(active_t[1, j], r_sib[...], preferred_element_type=f32)
        g_reduce[pl.ds(j * 4, 4)] = g.astype(bf16).reshape(4, 128, 1024)

    rest[0].start()
    rest[0].start_direct()

    def e_copy(c):
        return pltpu.make_async_remote_copy(
            src_ref=e_own.at[c],
            dst_ref=e_sib.at[c],
            send_sem=esend.at[c],
            recv_sem=erecv.at[c],
            device_id=sib,
            device_id_type=MESH,
        )

    @pl.loop(0, 8)
    def _(c):
        slot = lax.rem(c, 2)

        @pl.when(c < 7)
        def _():
            for copy in fetch(c + 1, 1 - slot, True):
                copy.start()

        for copy in fetch(c, slot, True):
            copy.wait()
        d_active = nt(r_own[...], w_reduce[slot].reshape(512, 1024))
        d_expanded = (d_active * slopes[slot].astype(f32)).astype(bf16)
        e_own[c] = d_expanded
        e_copy(c).start()
        e_sum[pl.ds(c, 1)] = jnp.sum(d_expanded.astype(f32), 0, keepdims=True)
        d_first[...] += nt(d_expanded, w_expand[slot].reshape(1024, 512))

    @pl.loop(0, 4)
    def _(i):
        span = pl.ds(pl.multiple_of(i * 64, 64), 64)
        d_normed, x_hat = d_first[span], scaled[span]
        pulled = d_normed * vectors[1:2]
        level = jnp.mean(pulled, -1, keepdims=True)
        slope = jnp.mean(pulled * x_hat, -1, keepdims=True)
        d_rows = spread[span, 0:1] * (pulled - level - x_hat * slope)
        d_low = d_rows.astype(bf16)
        d_first[span] = d_rows
        a_own[span] = d_low
        rows_sum[0:1] += jnp.sum(d_low.astype(f32), 0, keepdims=True)
        rows_sum[1:2] += jnp.sum(d_normed * x_hat, 0, keepdims=True)
        rows_sum[2:3] += jnp.sum(d_normed, 0, keepdims=True)

    out_weights.wait()

    @pl.loop(0, 4)
    def _(i):
        t = nt(w_out[pl.ds(i * 8, 8)].reshape(256, 1024), a_own[...])
        d_ctx[pl.ds(i * 4, 4)] = t.astype(bf16).reshape(4, 64, 256)

    sent = []

    def exchange_out(s, b, src, dst, sends, recvs):
        c = pltpu.make_async_remote_copy(
            src_ref=src,
            dst_ref=dst,
            send_sem=sends.at[s * 16 + b],
            recv_sem=recvs.at[s * 16 + b],
            device_id=(core, flip(chip, b)),
            device_id_type=MESH,
        )
        c.start()
        sent.append(c)

    def exchange_in(s, b, here, sends, recvs):
        pltpu.make_async_remote_copy(
            src_ref=here,
            dst_ref=here,
            send_sem=sends.at[s * 16 + b],
            recv_sem=recvs.at[s * 16 + b],
            device_id=sib,
            device_id_type=MESH,
        ).wait_recv()

    for s in range(2):
        lane = pl.ds(128 * s, 128)
        for b in FULL_ORDER:
            exchange_out(s, b, d_ctx.at[flip(chip, b), :, lane], d_recv.at[s, chip], dsend, drecv)
        d_recv[s, chip] = d_ctx[chip, :, lane]
    copies.send("a", a_own, a_sib, sib, a_own)

    vec_own[...] = jnp.zeros_like(vec_own)
    owner = lax.broadcasted_iota(jnp.int32, (32, 1024), 0)
    column = lax.broadcasted_iota(jnp.int32, (32, 1024), 1)
    place_in = lax.rem(lax.broadcasted_iota(jnp.int32, (1024, 128), 0), 32)
    pick = jnp.where(place_in == lax.broadcasted_iota(jnp.int32, (1024, 128), 1), 1.0, 0.0).astype(bf16)
    for r in (0, 1, 2, 4, 5, 6):
        spread_row = jnp.where(lax.div(column, 32) == owner, rows_sum[r : r + 1], 0.0)
        top = spread_row.astype(bf16)
        low = (spread_row - top.astype(f32)).astype(bf16)
        vec_own[:, r, :] = jnp.dot(top, pick, preferred_element_type=f32) + jnp.dot(low, pick, preferred_element_type=f32)
    for o in range(32):
        vec_own[o, 3:4, :] = e_sum[o // 4 : o // 4 + 1, 128 * (o % 4) : 128 * (o % 4) + 128]
    own_half, other_half = pl.ds(core * 16, 16), pl.ds((1 - core) * 16, 16)
    copies.send("v", vec_own.at[other_half], vec_sib, sib, vec_sib)

    for k in range(4):
        rest[0].on_first(k)

    @pl.loop(0, 8)
    def _(c):
        e_copy(c).wait()
        g = jnp.dot(rows_t[1, 0], e_own[c], preferred_element_type=f32)
        g = g + jnp.dot(rows_t[1, 1], e_sib[c], preferred_element_type=f32)
        g_expand[:, :, pl.ds(pl.multiple_of(c * 512, 512), 512)] = g.astype(bf16).reshape(16, 32, 512)

    rest[1].start()
    rest[1].start_direct()
    copies.arrived("a", a_sib, sib)
    for i in range(4):
        cols = slice(256 * i, 256 * i + 256)
        g = jnp.dot(rows_t[2, 0], a_own[:, cols], preferred_element_type=f32)
        g = g + jnp.dot(rows_t[2, 1], a_sib[:, cols], preferred_element_type=f32)
        g_out[:, :, cols] = g.astype(bf16).reshape(16, 32, 256)
    copies.arrived("v", vec_sib, sib)
    g_vec[...] = vec_own[own_half] + vec_sib[...]
    for r in rest[2:]:
        r.start()
        r.start_direct()
    b_own[...] = jnp.zeros_like(b_own)

    def fetch_qkv(i, slot):
        return pltpu.make_async_copy(h_qkv.at[pl.ds(i * 8, 8)], w_qkv.at[slot], local_sem.at[5 + slot])

    fetch_qkv(0, 0).start()
    fetch_qkv(1, 1).start()

    def back_sequence(s, during):
        load_sequence(pairs, s, kk, vt_ref=None, vv_ref=vv)
        for j in range(16):
            kt[:, pl.ds(j * 128, 128)] = pairs[s, j, 64:128, :]
        acc[...] = jnp.zeros_like(acc)

        @pl.loop(0, 8)
        def _(q):
            for k, event in enumerate(during):

                @pl.when(q == k)
                def _():
                    event()

            both = lambda ref, lo, hi: jnp.concatenate([ref[s, 2 * q, lo:hi, :], ref[s, 2 * q + 1, lo:hi, :]], 1)
            query, d_out = both(pairs, 0, 64), both(d_recv, 0, 64)
            span = pl.ds(pl.multiple_of(q * 256, 256), 256)
            delta = jnp.sum(d_out.astype(f32) * o_full[s, :, span], 0, keepdims=True)
            scores = jnp.dot(kk[...], query, preferred_element_type=f32) * (0.125 * LOG2E)
            key = lax.broadcasted_iota(jnp.int32, scores.shape, 0)
            probs = jnp.where(key < lengths_ref[s], jnp.exp2(scores - lse_ref[s, pl.ds(q, 1), :]), 0.0)
            d_probs = jnp.dot(vv[...], d_out, preferred_element_type=f32)
            d_scores = (probs * (d_probs - delta)).astype(bf16)
            zero = jnp.zeros((64, 256), f32)
            query_rows = jnp.concatenate([query.astype(f32), zero], 0).T.astype(bf16)
            d_rows = jnp.concatenate([zero, d_out.astype(f32)], 0).T.astype(bf16)
            acc[...] += jnp.dot(d_scores, query_rows, preferred_element_type=f32) + jnp.dot(
                probs.astype(bf16), d_rows, preferred_element_type=f32
            )
            d_query = (jnp.dot(kt[...], d_scores, preferred_element_type=f32) * 0.125).astype(bf16)
            for i in range(2):
                part = d_query[:, 128 * i : 128 * i + 128]
                d_send[s, 2 * q + i, 0:64, :] = part
                b_own[0] += part.astype(f32)

        for j in range(16):
            t = acc[pl.ds(j * 128, 128)].T
            d_send[s, j, 64:128, :] = (t[:64] * 0.125).astype(bf16)
            value = t[64:].astype(bf16)
            d_send[s, j, 128:192, :] = value
            b_own[1] += value.astype(f32)
        lane = pl.ds(128 * s, 128)
        for b in FULL_ORDER:
            exchange_out(s, b, d_send.at[s, flip(chip, b)], d_own.at[chip, :, lane], qsend, qrecv)
        d_own[chip, :, lane] = d_send[s, chip]

    for k in range(4):
        rest[0].on_second(k)
    events = [lambda k=k: [r.on_first(k) for r in rest[1:]] for k in range(4)]
    events += [lambda k=k: [r.on_second(k) for r in rest[1:]] for k in range(4)]
    FIRST, SECOND, WAIT = 0, 0, 4
    for b in FULL_ORDER:
        exchange_in(0, b, d_recv.at[0, flip(chip, b)], dsend, drecv)
    back_sequence(0, events[:FIRST])
    for b in FULL_ORDER:
        exchange_in(1, b, d_recv.at[1, flip(chip, b)], dsend, drecv)
    back_sequence(1, events[FIRST : FIRST + SECOND])

    copies.send("bias sib", b_own, b_sib, sib, b_own)
    for event in events[FIRST + SECOND : FIRST + SECOND + WAIT]:
        event()
    for s in range(2):
        lane = pl.ds(128 * s, 128)
        for b in FULL_ORDER:
            exchange_in(s, b, d_own.at[flip(chip, b), :, lane], qsend, qrecv)
        copies.send(("rows", s), d_own.at[:, :, lane], d_sib.at[:, :, lane], sib, d_own.at[:, :, lane])

    copies.arrived("bias sib", b_sib, sib)
    for s in range(2):
        copies.arrived(("rows", s), d_sib.at[:, :, pl.ds(128 * s, 128)], sib)

    for part in range(3):

        @pl.loop(0, 4)
        def _(p):
            total = None
            for i, rows in enumerate((d_own, d_sib)):
                right = rows[pl.ds(4 * p, 4), pl.ds(64 * part, 64)].reshape(256, 256)
                term = nt(rows_t[0, i], right)
                total = term if total is None else total + term
            cols = pl.ds(pl.multiple_of(part * 1024 + p * 256, 256), 256)
            g_qkv[:, :, cols] = total.astype(bf16).reshape(16, 32, 256)

    last.start()
    last.start_direct()

    b_sib[...] = b_sib[...] + b_own[...]
    sender = core == lax.div(chip, 8)
    for i in range(2):
        to = lax.rem(2 * chip + i, 16)
        rows = pl.ds(32 * i, 32)
        c = pltpu.make_async_remote_copy(
            src_ref=b_sib.at[:, rows],
            dst_ref=b_in,
            send_sem=local_sem.at[1 + i],
            recv_sem=local_sem.at[3],
            device_id=(core, to),
            device_id_type=MESH,
        )

        @pl.when(sender & (to != chip))
        def _():
            c.start()

        @pl.when(sender & (to == chip))
        def _():
            b_in[...] = b_sib[:, rows]

    for i in range(4):
        fetch_qkv(i, i % 2).wait()
        t = None
        for part in range(3):
            w = w_qkv[i % 2, :, :, 1024 * part : 1024 * part + 1024].reshape(256, 1024)
            term = jnp.dot(w, d_own[:, 64 * part : 64 * part + 64].reshape(1024, 256), preferred_element_type=f32)
            t = term if t is None else t + term
        if i < 2:
            fetch_qkv(i + 2, i).start()
        cols = slice(256 * i, 256 * i + 256)
        o_input[:, cols] = d_first[:, cols] + t.T

    for event in events[FIRST + SECOND + WAIT :]:
        event()
    for k in range(4):
        last.on_first(k)
    for r in rest:
        r.on_third()
    for k in range(4):
        last.on_second(k)
    last.on_third()
    for i in range(2):
        to = lax.rem(2 * chip + i, 16)

        @pl.when(sender & (to != chip))
        def _():
            pltpu.make_async_remote_copy(
                src_ref=b_sib.at[:, pl.ds(32 * i, 32)],
                dst_ref=b_in,
                send_sem=local_sem.at[1 + i],
                recv_sem=local_sem.at[3],
                device_id=(core, to),
                device_id_type=MESH,
            ).wait_send()

    @pl.when(8 * core + lax.div(chip, 2) != chip)
    def _():
        pltpu.make_async_remote_copy(
            src_ref=b_in, dst_ref=b_in, send_sem=local_sem.at[1], recv_sem=local_sem.at[3], device_id=sib, device_id_type=MESH
        ).wait_recv()

    o_bias[...] = b_in[...]
    for c in sent:
        c.wait_send()
    copies.drain(sib)


def backward_attention(
    lengths, pairs, o_full, lse, rows_t, active_t, cotangent, scaled, spread, vectors,
    active, slope, w_reduce, w_expand, w_out, w_qkv, collective_id,
):
    v, hbm = pl.BlockSpec(memory_space=pltpu.VMEM), pl.BlockSpec(memory_space=pl.ANY)
    f32, bf16 = jnp.float32, jnp.bfloat16
    dma = pltpu.SemaphoreType.DMA
    blocks = [((128, 1024), bf16), ((32, 4096), bf16), ((32, 1024), bf16), ((16, 128), f32), ((32, 3072), bf16)]
    bufs = []
    for block, dtype in blocks:
        bufs += scatter_buffers(block, dtype)
    vmem = lambda shape, dtype=bf16: pltpu.VMEM(shape, dtype)
    return pl.pallas_call(
        bwd_kernel,
        out_shape=[jax.ShapeDtypeStruct((256, 1024), bf16)]
        + [jax.ShapeDtypeStruct(block, f32) for block, _ in blocks]
        + [jax.ShapeDtypeStruct((256, 1024), f32), jax.ShapeDtypeStruct((2, 32, 128), f32)],
        in_specs=[pl.BlockSpec(memory_space=pltpu.SMEM)] + [v] * 9 + [hbm] * 6,
        out_specs=[v] * 8,
        scratch_shapes=bufs
        + [
            vmem((16, 128, 1024)),
            vmem((16, 32, 4096)),
            vmem((16, 32, 1024)),
            vmem((16, 16, 128), f32),
            vmem((16, 32, 3072)),
            vmem((2, 8, 32, 3072)),
            vmem((2, 16, 64, 128)),
            vmem((2048, 64)),
            vmem((2048, 64)),
            vmem((64, 2048)),
            vmem((2048, 128), f32),
            vmem((2, 16, 192, 128)),
            vmem((16, 192, 256)),
            vmem((16, 192, 256)),
            vmem((2, 64, 128), f32),
            vmem((2, 64, 128), f32),
            vmem((2, 32, 128), f32),
            vmem((2, 256, 512)),
            vmem((2, 4, 128, 1024)),
            vmem((2, 32, 32, 512)),
            vmem((32, 32, 1024)),
            vmem((8, 256, 512)),
            vmem((8, 256, 512)),
            vmem((256, 1024), f32),
            vmem((256, 1024)),
            vmem((256, 1024)),
            vmem((16, 64, 256)),
            vmem((8, 1024), f32),
            vmem((8, 512), f32),
            vmem((32, 16, 128), f32),
            vmem((16, 16, 128), f32),
            vmem((256, 1024)),
            vmem((256, 1024)),
            dma((144,)),
            dma((144,)),
            dma((7,)),
            dma((32,)),
            dma((32,)),
            dma((32,)),
            dma((32,)),
            dma((8,)),
            dma((8,)),
            dma((2, 3)),
        ],
        compiler_params=pltpu.CompilerParams(
            collective_id=collective_id, has_side_effects=True, vmem_limit_bytes=63 * MIB
        ),
        name="backward_attention",
    )(
        lengths, pairs, o_full, lse, rows_t, active_t, cotangent, scaled, spread, vectors,
        active, slope, w_reduce, w_expand, w_out, w_qkv,
    )


def fast_shards(
    inputs,
    lengths,
    w_query,
    b_query,
    w_key,
    w_value,
    b_value,
    w_out,
    b_out,
    first_gain,
    first_shift,
    w_expand,
    b_expand,
    w_reduce,
    b_reduce,
    second_gain,
    second_shift,
    cotangent,
):
    f32, bf16 = jnp.float32, jnp.bfloat16
    seqs, count, width = inputs.shape
    total = seqs * count
    part = width // 32
    ff = w_expand.shape[1]
    qkv = jnp.concatenate([w_query, w_key, w_value], 1)
    bias = jnp.concatenate([b_query, b_value])[:, None] + jnp.zeros((2 * part, 128), bf16)
    small = [b_out, first_gain, first_shift, b_expand, b_reduce, second_gain, second_shift]
    vec = sum(jnp.pad(b[None, :], ((r, part - 1 - r), (0, 128 - b.shape[0]))) for r, b in enumerate(small))
    flat_rows = inputs.reshape(total, width)
    (
        g_out, g_expand, g_reduce, g_qkv, pairs, o_full, lse, vectors, scaled, spread, active, slope, rows_t, active_t,
    ) = forward_attention(flat_rows, lengths, qkv, bias, vec, w_out, w_expand, w_reduce, 1)
    layer_out, s_reduce, s_expand, s_out, s_vec, s_qkv, input_grad, s_bias = backward_attention(
        lengths, pairs, o_full, lse, rows_t, active_t, cotangent.reshape(total, width), scaled, spread, vectors,
        active, slope, g_reduce, g_expand, g_out, g_qkv, 2,
    )
    s_query, s_key, s_value = (s_qkv[:, width * i : width * (i + 1)] for i in range(3))
    s_bias = jnp.sum(s_bias, -1)
    v = [s_vec[r, : b.shape[0]] for r, b in enumerate(small)]
    return (
        layer_out.reshape(inputs.shape),
        input_grad.reshape(inputs.shape),
        s_query,
        s_bias[0],
        s_key,
        s_value,
        s_bias[1],
        s_out,
        v[0],
        v[1],
        v[2],
        s_expand,
        v[3],
        s_reduce,
        v[4],
        v[5],
        v[6],
    )


def solution(mesh):
    fast = mesh.shape["fsdp"] == 2 and mesh.shape["ctx"] == HEADS
    shards = fast_shards if fast else general_shards
    return jax.shard_map(
        shards,
        mesh=mesh,
        in_specs=(
            P("fsdp", "ctx", None),
            P("fsdp"),
            P(("fsdp", "ctx"), None),
            P(("fsdp", "ctx")),
            P(("fsdp", "ctx"), None),
            P(("fsdp", "ctx"), None),
            P(("fsdp", "ctx")),
            P(("fsdp", "ctx"), None),
            P(("fsdp", "ctx")),
            P(("fsdp", "ctx")),
            P(("fsdp", "ctx")),
            P(("fsdp", "ctx"), None),
            P(("fsdp", "ctx")),
            P(("fsdp", "ctx"), None),
            P(("fsdp", "ctx")),
            P(("fsdp", "ctx")),
            P(("fsdp", "ctx")),
            P("fsdp", "ctx", None),
        ),
        out_specs=(
            P("fsdp", "ctx", None),
            P("fsdp", "ctx", None),
            P(("fsdp", "ctx"), None),
            P(("fsdp", "ctx")),
            P(("fsdp", "ctx"), None),
            P(("fsdp", "ctx"), None),
            P(("fsdp", "ctx")),
            P(("fsdp", "ctx"), None),
            P(("fsdp", "ctx")),
            P(("fsdp", "ctx")),
            P(("fsdp", "ctx")),
            P(("fsdp", "ctx"), None),
            P(("fsdp", "ctx")),
            P(("fsdp", "ctx"), None),
            P(("fsdp", "ctx")),
            P(("fsdp", "ctx")),
            P(("fsdp", "ctx")),
        ),
        check_vma=False,
    )
```

```python
from functools import partial
import math

import jax
import jax.numpy as jnp
from jax import lax
from jax.experimental import pallas as pl
from jax.experimental.pallas import tpu as pltpu
from jax.sharding import PartitionSpec as P

HEADS = 16


epsilon = 1e-05
masked_score = -1e30


def layer_norm(rows_in, gain, shift):
    center = rows_in - jnp.mean(rows_in, -1, keepdims=True)
    spread = jnp.mean(center * center, -1, keepdims=True)
    return center * lax.rsqrt(spread + epsilon) * gain + shift


def product(left, right):
    return jnp.dot(left, right, preferred_element_type=jnp.float32)


def outer_sum(left, right):
    return jnp.einsum("rd,re->de", left, right, preferred_element_type=jnp.float32)


def back_product(grad_rows, weight):
    return jnp.einsum("re,de->rd", grad_rows, weight, preferred_element_type=jnp.float32)


def over_blocks(step_fn, carry_state, pair_rows):
    key_count = pair_rows.shape[1]
    block_width = math.gcd(key_count, 512)

    def turn(turn_index, inner_state):
        block_pairs = lax.dynamic_slice_in_dim(pair_rows, turn_index * block_width, block_width, 1)
        return step_fn(inner_state, block_pairs, turn_index * block_width)

    return lax.fori_loop(0, key_count // block_width, turn, carry_state)


def general_shards(
    inputs,
    lengths,
    w_query,
    b_query,
    w_key,
    w_value,
    b_value,
    w_out,
    b_out,
    first_gain,
    first_shift,
    w_expand,
    b_expand,
    w_reduce,
    b_reduce,
    second_gain,
    second_shift,
    cotangent,
):
    gathered = (
        lax.all_gather(w_query, ("fsdp", "ctx"), axis=0, tiled=True),
        lax.all_gather(b_query, ("fsdp", "ctx"), axis=0, tiled=True),
        lax.all_gather(w_key, ("fsdp", "ctx"), axis=0, tiled=True),
        lax.all_gather(w_value, ("fsdp", "ctx"), axis=0, tiled=True),
        lax.all_gather(b_value, ("fsdp", "ctx"), axis=0, tiled=True),
        lax.all_gather(w_out, ("fsdp", "ctx"), axis=0, tiled=True),
        lax.all_gather(b_out, ("fsdp", "ctx"), axis=0, tiled=True),
        lax.all_gather(first_gain, ("fsdp", "ctx"), axis=0, tiled=True),
        lax.all_gather(first_shift, ("fsdp", "ctx"), axis=0, tiled=True),
        lax.all_gather(w_expand, ("fsdp", "ctx"), axis=0, tiled=True),
        lax.all_gather(b_expand, ("fsdp", "ctx"), axis=0, tiled=True),
        lax.all_gather(w_reduce, ("fsdp", "ctx"), axis=0, tiled=True),
        lax.all_gather(b_reduce, ("fsdp", "ctx"), axis=0, tiled=True),
        lax.all_gather(second_gain, ("fsdp", "ctx"), axis=0, tiled=True),
        lax.all_gather(second_shift, ("fsdp", "ctx"), axis=0, tiled=True),
    )
    (
        full_query,
        bias_query,
        full_key,
        full_value,
        bias_value,
        full_out,
        bias_out,
        gain_first,
        shift_first,
        full_expand,
        bias_expand,
        full_reduce,
        bias_reduce,
        gain_second,
        shift_second,
    ) = gathered
    seq_count, block_rows, model_width = inputs.shape
    total_rows = seq_count * block_rows
    head_size = model_width // HEADS
    score_scale = head_size ** (-0.5)
    own_first = lax.axis_index("ctx") * block_rows
    positions = own_first + jnp.arange(block_rows, dtype=jnp.int32)
    valid_rows = (positions[None, :] < lengths[:, None]).astype(jnp.float32).reshape(total_rows, 1)
    flat_rows = inputs.reshape(total_rows, model_width)
    queries = (product(flat_rows, full_query) + bias_query.astype(jnp.float32)).astype(jnp.bfloat16)
    key_rows = product(flat_rows, full_key).astype(jnp.bfloat16)
    value_rows = (product(flat_rows, full_value) + bias_value.astype(jnp.float32)).astype(
        jnp.bfloat16
    )
    query_heads = queries.reshape(seq_count, block_rows, HEADS, head_size)
    local_pairs = jnp.concatenate([key_rows, value_rows], -1).reshape(
        seq_count, block_rows, 2 * model_width
    )

    def key_allowed(first_row, key_count):
        return ((first_row + jnp.arange(key_count, dtype=jnp.int32))[None, :] < lengths[:, None])[
            :, None, None, :
        ]

    def split_pairs(block_pairs):
        key_count = block_pairs.shape[1]
        key_heads = block_pairs[:, :, :model_width].reshape(seq_count, key_count, HEADS, head_size)
        value_heads = block_pairs[:, :, model_width:].reshape(
            seq_count, key_count, HEADS, head_size
        )
        return (key_heads, value_heads, key_count)

    def forward_step(carry_state, block_pairs, first_row):
        running_max, running_sum, running_acc = carry_state
        key_heads, value_heads, key_count = split_pairs(block_pairs)
        allowed = key_allowed(first_row, key_count)
        scores = (
            jnp.einsum(
                "sqhd,skhd->shqk", query_heads, key_heads, preferred_element_type=jnp.float32
            )
            * score_scale
        )
        scores = jnp.where(allowed, scores, masked_score)
        new_max = jnp.maximum(running_max, jnp.max(scores, -1))
        factor = jnp.exp(running_max - new_max)
        exponents = jnp.where(allowed, jnp.exp(scores - new_max[..., None]), 0.0)
        new_sum = running_sum * factor + jnp.sum(exponents, -1)
        update = jnp.einsum(
            "shqk,skhd->sqhd",
            exponents.astype(jnp.bfloat16),
            value_heads,
            preferred_element_type=jnp.float32,
        )
        new_acc = running_acc * jnp.transpose(factor, (0, 2, 1))[..., None] + update
        return (new_max, new_sum, new_acc)

    start_state = (
        jnp.full((seq_count, HEADS, block_rows), masked_score, jnp.float32),
        jnp.zeros((seq_count, HEADS, block_rows), jnp.float32),
        jnp.zeros((seq_count, block_rows, HEADS, head_size), jnp.float32),
    )
    running_max, running_sum, running_acc = over_blocks(
        forward_step, start_state, lax.all_gather(local_pairs, "ctx", axis=1, tiled=True)
    )
    context_full = running_acc / jnp.transpose(running_sum, (0, 2, 1))[..., None]
    log_total = running_max + jnp.log(running_sum)
    context = context_full.reshape(total_rows, model_width).astype(jnp.bfloat16)
    attended = product(context, full_out) + bias_out.astype(jnp.float32)
    residual = flat_rows.astype(jnp.float32) + attended
    normed, first_pull = jax.vjp(
        layer_norm, residual, gain_first.astype(jnp.float32), shift_first.astype(jnp.float32)
    )
    normed_low = normed.astype(jnp.bfloat16)
    expanded = product(normed_low, full_expand) + bias_expand.astype(jnp.float32)
    activated, gelu_pull = jax.vjp(partial(jax.nn.gelu, approximate=False), expanded)
    activated_low = activated.astype(jnp.bfloat16)
    reduced = product(activated_low, full_reduce) + bias_reduce.astype(jnp.float32)
    final_rows, second_pull = jax.vjp(
        layer_norm,
        normed + reduced,
        gain_second.astype(jnp.float32),
        shift_second.astype(jnp.float32),
    )
    layer_out = (final_rows * valid_rows).astype(jnp.bfloat16).reshape(inputs.shape)
    d_output = cotangent.reshape(total_rows, model_width).astype(jnp.float32) * valid_rows
    d_second, second_gain_grad, second_shift_grad = second_pull(d_output)
    d_reduced = d_second.astype(jnp.bfloat16)
    reduce_grad = outer_sum(activated_low, d_reduced)
    reduce_bias_grad = jnp.sum(d_reduced.astype(jnp.float32), 0)
    (d_expanded_full,) = gelu_pull(back_product(d_reduced, full_reduce))
    d_expanded = d_expanded_full.astype(jnp.bfloat16)
    expand_grad = outer_sum(normed_low, d_expanded)
    expand_bias_grad = jnp.sum(d_expanded.astype(jnp.float32), 0)
    d_normed = d_second + back_product(d_expanded, full_expand)
    d_first, first_gain_grad, first_shift_grad = first_pull(d_normed)
    d_attended = d_first.astype(jnp.bfloat16)
    out_grad = outer_sum(context, d_attended)
    out_bias_grad = jnp.sum(d_attended.astype(jnp.float32), 0)
    d_context = back_product(d_attended, full_out).astype(jnp.bfloat16)
    d_context_heads = d_context.reshape(seq_count, block_rows, HEADS, head_size)
    delta = jnp.transpose(
        jnp.sum(d_context_heads.astype(jnp.float32) * context_full, -1), (0, 2, 1)
    )
    whole_length = block_rows * lax.axis_size("ctx")

    def score_grads(key_heads, value_heads, allowed):
        scores = (
            jnp.einsum(
                "sqhd,skhd->shqk", query_heads, key_heads, preferred_element_type=jnp.float32
            )
            * score_scale
        )
        probabilities = jnp.where(allowed, jnp.exp(scores - log_total[..., None]), 0.0)
        d_probs = jnp.einsum(
            "sqhd,skhd->shqk", d_context_heads, value_heads, preferred_element_type=jnp.float32
        )
        d_scores = (probabilities * (d_probs - delta[..., None])).astype(jnp.bfloat16)
        return (probabilities, d_scores)

    def backward_step(carry_state, block_pairs, first_row):
        grad_query, grad_pairs = carry_state
        key_heads, value_heads, key_count = split_pairs(block_pairs)
        probabilities, d_scores = score_grads(
            key_heads, value_heads, key_allowed(first_row, key_count)
        )
        grad_query = (
            grad_query
            + jnp.einsum("shqk,skhd->sqhd", d_scores, key_heads, preferred_element_type=jnp.float32)
            * score_scale
        )
        key_part = (
            jnp.einsum("shqk,sqhd->skhd", d_scores, query_heads, preferred_element_type=jnp.float32)
            * score_scale
        )
        value_part = jnp.einsum(
            "shqk,sqhd->skhd",
            probabilities.astype(jnp.bfloat16),
            d_context_heads,
            preferred_element_type=jnp.float32,
        )
        fresh = jnp.concatenate(
            [
                key_part.reshape(seq_count, key_count, model_width),
                value_part.reshape(seq_count, key_count, model_width),
            ],
            -1,
        )
        before = lax.dynamic_slice_in_dim(grad_pairs, first_row, key_count, 1)
        grad_pairs = lax.dynamic_update_slice_in_dim(grad_pairs, before + fresh, first_row, 1)
        return (grad_query, grad_pairs)

    query_zero = jnp.zeros((seq_count, block_rows, HEADS, head_size), jnp.float32)
    back_state = (query_zero, jnp.zeros((seq_count, whole_length, 2 * model_width), jnp.float32))
    back_result = over_blocks(
        backward_step, back_state, lax.all_gather(local_pairs, "ctx", axis=1, tiled=True)
    )
    grad_query = back_result[0]
    own_pairs = lax.psum_scatter(
        back_result[1].astype(jnp.bfloat16), "ctx", scatter_dimension=1, tiled=True
    ).astype(jnp.float32)
    d_keys = own_pairs[:, :, :model_width].reshape(total_rows, model_width).astype(jnp.bfloat16)
    d_values = own_pairs[:, :, model_width:].reshape(total_rows, model_width).astype(jnp.bfloat16)
    d_queries = grad_query.reshape(total_rows, model_width).astype(jnp.bfloat16)
    query_grad = outer_sum(flat_rows, d_queries)
    query_bias_grad = jnp.sum(d_queries.astype(jnp.float32), 0)
    key_grad = outer_sum(flat_rows, d_keys)
    value_grad = outer_sum(flat_rows, d_values)
    value_bias_grad = jnp.sum(d_values.astype(jnp.float32), 0)
    input_grad = (
        d_first
        + back_product(d_queries, full_query)
        + back_product(d_keys, full_key)
        + back_product(d_values, full_value)
    ).reshape(inputs.shape)
    shares = (
        lax.psum_scatter(query_grad, ("fsdp", "ctx"), scatter_dimension=0, tiled=True),
        lax.psum_scatter(query_bias_grad, ("fsdp", "ctx"), scatter_dimension=0, tiled=True),
        lax.psum_scatter(key_grad, ("fsdp", "ctx"), scatter_dimension=0, tiled=True),
        lax.psum_scatter(value_grad, ("fsdp", "ctx"), scatter_dimension=0, tiled=True),
        lax.psum_scatter(value_bias_grad, ("fsdp", "ctx"), scatter_dimension=0, tiled=True),
        lax.psum_scatter(out_grad, ("fsdp", "ctx"), scatter_dimension=0, tiled=True),
        lax.psum_scatter(out_bias_grad, ("fsdp", "ctx"), scatter_dimension=0, tiled=True),
        lax.psum_scatter(first_gain_grad, ("fsdp", "ctx"), scatter_dimension=0, tiled=True),
        lax.psum_scatter(first_shift_grad, ("fsdp", "ctx"), scatter_dimension=0, tiled=True),
        lax.psum_scatter(expand_grad, ("fsdp", "ctx"), scatter_dimension=0, tiled=True),
        lax.psum_scatter(expand_bias_grad, ("fsdp", "ctx"), scatter_dimension=0, tiled=True),
        lax.psum_scatter(reduce_grad, ("fsdp", "ctx"), scatter_dimension=0, tiled=True),
        lax.psum_scatter(reduce_bias_grad, ("fsdp", "ctx"), scatter_dimension=0, tiled=True),
        lax.psum_scatter(second_gain_grad, ("fsdp", "ctx"), scatter_dimension=0, tiled=True),
        lax.psum_scatter(second_shift_grad, ("fsdp", "ctx"), scatter_dimension=0, tiled=True),
    )
    return (
        layer_out,
        input_grad,
        shares[0],
        shares[1],
        shares[2],
        shares[3],
        shares[4],
        shares[5],
        shares[6],
        shares[7],
        shares[8],
        shares[9],
        shares[10],
        shares[11],
        shares[12],
        shares[13],
        shares[14],
    )


MESH = pl.DeviceIdType.MESH
MIB = 1024*1024

def place():
    core = lax.axis_index("fsdp"); chip = lax.axis_index("ctx")
    return core, chip

def greet(peers):
    barrier = pltpu.get_barrier_semaphore()
    for peer in peers:
        pl.semaphore_signal(barrier, inc=1, device_id=peer, device_id_type=MESH)
    pl.semaphore_wait(barrier, len(peers))

def flip(v, bits):
    for b in (1, 2, 4, 8):
        if bits & b:
            v = v + b - 2 * b * lax.rem(lax.div(v, b), 2)
    return v

LOG2E = math.log2(math.e)


def nt(a, b):
    return lax.dot_general(a, b, (((1,), (1,)), ((), ())), preferred_element_type=jnp.float32)


FULL_ORDER = (12, 8, 4, 15, 11, 7, 14, 13, 10, 9, 6, 5, 3, 2, 1)


class Copies:
    def __init__(self, send_sem, recv_sem):
        self.send_sem, self.recv_sem = send_sem, recv_sem
        self.names, self.sent = {}, []

    def pair(self, name, src, dst, peer):
        i = self.names.setdefault(name, len(self.names))
        return pltpu.make_async_remote_copy(
            src_ref=src,
            dst_ref=dst,
            send_sem=self.send_sem.at[i],
            recv_sem=self.recv_sem.at[i],
            device_id=peer,
            device_id_type=MESH,
        )

    def send(self, name, src, dst, peer, like):
        self.pair(name, src, dst, peer).start()
        self.sent.append((name, like))

    def arrived(self, name, dst, peer):
        self.pair(name, dst, dst, peer).wait_recv()

    def drain(self, peer):
        for name, like in self.sent:
            self.pair(name, like, like, peer).wait_send()


class Line:
    def __init__(self, chip):
        self.z = lax.div(chip, 4)
        self.rest = chip - 4 * self.z
        even = lax.rem(self.z, 2) == 0
        low = self.z < 2
        one, two, three = jnp.int32(1), jnp.int32(2), jnp.int32(3)
        near = jnp.where(even, one, -one)
        mid = jnp.where(low, jnp.where(even, two, one), jnp.where(even, -one, -two))
        far = jnp.where(low, jnp.where(even, three, two), jnp.where(even, -two, -three))
        self.offsets = [jnp.int32(0), near, mid, far]

    def source(self, k):
        return self.z + self.offsets[k]

    def onward_up(self, k):
        return (self.offsets[k] < 0) & (self.z < 3)

    def onward_down(self, k):
        return (self.offsets[k] > 0) & (self.z > 0)


class Gather:
    def __init__(self, copies, line, name, src, out, local_sem, zsend, zrecv):
        self.copies, self.line, self.name, self.src, self.out, self.local_sem = copies, line, name, src, out, local_sem
        self.zsend, self.zrecv = zsend, zrecv
        self.core, self.chip = place()
        self.sib = (1 - self.core, self.chip)
        self.half = src.shape[0] // 2

    def at(self, bits):
        return (self.core, flip(self.chip, bits))

    def index(self, k, bits, core=None):
        core = self.core if core is None else core
        return core * 16 + self.line.source(k) * 4 + flip(self.line.rest, bits)

    def block(self, k, bits, core=None):
        return self.out.at[self.index(k, bits, core)]

    def part(self, k, bits, upper):
        return self.out.at[self.index(k, bits), pl.ds(self.half if upper else 0, self.half)]

    def send(self, tag, src, dst, peer, half=False):
        like = self.src.at[pl.ds(0, self.half)] if half else self.src
        self.copies.send((self.name, tag), src, dst, peer, like)

    def arrived(self, tag, dst):
        self.copies.arrived((self.name, tag), dst, self.sib)

    def along(self, slot, source, src, dst, up):
        return pltpu.make_async_remote_copy(
            src_ref=src,
            dst_ref=dst,
            send_sem=self.zsend.at[self.name * 6 + slot],
            recv_sem=self.zrecv.at[self.name * 4 + source],
            device_id=(self.core, self.chip + 4 if up else self.chip - 4),
            device_id_type=MESH,
        )

    def start_z(self):
        z = self.line.z

        @pl.when(z < 3)
        def _():
            self.along(4, z, self.src, self.block(0, 0), True).start()

        @pl.when(z > 0)
        def _():
            self.along(5, z, self.src, self.block(0, 0), False).start()

    def start_plane(self):
        self.send(("x", 0), self.src, self.block(0, 0), self.at(1))
        self.send(("y", 0), self.src, self.block(0, 0), self.at(2))
        self.send(("s", 0, 0), self.src, self.block(0, 0), self.sib)
        self.local = pltpu.make_async_copy(self.src, self.block(0, 0), self.local_sem)
        self.local.start()

    def on_z(self, k):
        b = self.block(k, 0)
        source = self.line.source(k)
        self.along(source, source, b, b, True).wait_recv()

        @pl.when(self.line.onward_up(k))
        def _():
            self.along(source, source, b, b, True).start()

        @pl.when(self.line.onward_down(k))
        def _():
            self.along(source, source, b, b, False).start()

        self.send(("x", k), b, b, self.at(1))
        self.send(("y", k), b, b, self.at(2))
        self.send(("s", k, 0), b, b, self.sib)

    def on_plane(self, k):
        for bit, tag, further, upper in ((1, "x", 2, False), (2, "y", 1, True)):
            b = self.block(k, bit)
            self.arrived((tag, k), b)
            h = self.part(k, bit, upper)
            self.send(("d" + tag, k), h, h, self.at(further), True)
            self.send(("s", k, bit), b, b, self.sib)

    def on_diagonal(self, k):
        self.arrived(("dx", k), self.part(k, 3, False))
        self.arrived(("dy", k), self.part(k, 3, True))
        b = self.block(k, 3)
        self.send(("s", k, 3), b, b, self.sib)

    def on_sibling(self):
        for k in range(4):
            for bits in range(4):
                self.arrived(("s", k, bits), self.block(k, bits, 1 - self.core))
        self.local.wait()

    def drain(self):
        z = self.line.z

        @pl.when(z < 3)
        def _():
            self.along(4, z, self.src, self.src, True).wait_send()

        @pl.when(z > 0)
        def _():
            self.along(5, z, self.src, self.src, True).wait_send()

        for k in range(1, 4):
            source = self.line.source(k)

            @pl.when(self.line.onward_up(k) | self.line.onward_down(k))
            def _():
                self.along(source, source, self.src, self.src, True).wait_send()


def load_sequence(r_ref, s, kk_ref, vt_ref=None, vv_ref=None):
    for j in range(r_ref.shape[1]):
        span = pl.ds(j * 128, 128)
        kk_ref[span] = r_ref[s, j, 64:128, :].astype(jnp.float32).T.astype(jnp.bfloat16)
        if vt_ref is not None:
            vt_ref[:, span] = r_ref[s, j, 128:192, :]
        if vv_ref is not None:
            vv_ref[span] = r_ref[s, j, 128:192, :].astype(jnp.float32).T.astype(jnp.bfloat16)


def fwd_kernel(
    x_ref, lengths_ref, s_qkv, s_bias, s_vec, s_out, s_expand, s_reduce,
    o_out, o_expand, o_reduce, o_qkv, o_pairs, o_full, lse_ref,
    o_rows, o_scaled, o_spread, o_active, o_slope, o_turned, o_active_t,
    w_qkv, w_bias, w_vec, w_out, w_expand, send_blk, recv_blk, ctx_blk, ctx_recv, kk, vt,
    e_row, x_turned, n_turned, normed, stage, turned, active_t, ctx_sib, active_all, slope_all,
    send_sem, recv_sem, local_sem, hsend, hrecv, csend, crecv, tsend, trecv, wsem, zsend, zrecv, ksem,
):
    f32, bf16 = jnp.float32, jnp.bfloat16
    core, chip = place()
    sib = (1 - core, chip)
    greet([sib] + [(core, flip(chip, b)) for b in range(1, 16)])
    copies = Copies(send_sem, recv_sem)
    line = Line(chip)
    first = [
        Gather(copies, line, 0, s_qkv, w_qkv, local_sem.at[0], zsend, zrecv),
        Gather(copies, line, 1, s_bias, w_bias, local_sem.at[1], zsend, zrecv),
    ]
    rest = [
        Gather(copies, line, 2, s_out, o_out, local_sem.at[2], zsend, zrecv),
        Gather(copies, line, 3, s_vec, w_vec, local_sem.at[3], zsend, zrecv),
        Gather(copies, line, 4, s_expand, o_expand, local_sem.at[4], zsend, zrecv),
        Gather(copies, line, 5, s_reduce, o_reduce, local_sem.at[5], zsend, zrecv),
    ]
    for g in first:
        g.start_z()
        g.start_plane()

    def turn(slot, src, kept):
        c = pltpu.make_async_remote_copy(
            src_ref=src,
            dst_ref=turned.at[slot, 1],
            send_sem=tsend.at[slot],
            recv_sem=trecv.at[slot],
            device_id=sib,
            device_id_type=MESH,
        )
        c.start()
        turned[slot, 0] = kept[...]
        return c

    for i in range(4):
        x_turned[i // 2, 256 * (i % 2) : 256 * (i % 2) + 256] = x_ref[:, 256 * i : 256 * i + 256].astype(f32).T.astype(bf16)
    swaps = [turn(0, x_turned.at[1 - core], x_turned.at[core])]
    for z in (1, 2, 3):
        for g in first:
            g.on_z(z)
    for g in rest[:3]:
        g.start_z()
    for z in range(4):
        for g in first:
            g.on_plane(z)
    for g in rest:
        g.start_plane()
    for z in range(4):
        for g in first:
            g.on_diagonal(z)
    for g in first:
        g.on_sibling()
    keep = pltpu.make_async_copy(w_qkv, o_qkv, local_sem.at[6])
    keep.start()

    for g in rest[:3]:
        g.on_z(1)
    for part in range(3):

        @pl.loop(0, 4)
        def _(p):
            w = w_qkv[:, :, pl.ds(pl.multiple_of(part * 1024 + p * 256, 256), 256)].reshape(1024, 256)
            t = jnp.dot(x_ref[...], w, preferred_element_type=f32).T
            for i in range(4):
                h = 4 * p + i
                rows = t[64 * i : 64 * i + 64]
                if part != 1:
                    own = pl.ds(0 if part == 0 else 32, 32)
                    bias = jnp.concatenate([w_bias[2 * h + k, own] for k in range(2)], 0).astype(f32)
                    rows = rows + jnp.concatenate([bias, bias], 1)
                send_blk[h, pl.ds(64 * part, 64)] = rows.astype(bf16)

    for g in rest[:3]:
        g.on_z(2)
    heads = []
    for s in range(2):
        for b in FULL_ORDER:
            to = flip(chip, b)
            i = s * 16 + b
            c = pltpu.make_async_remote_copy(
                src_ref=send_blk.at[to, :, pl.ds(128 * s, 128)],
                dst_ref=recv_blk.at[s, chip],
                send_sem=hsend.at[i],
                recv_sem=hrecv.at[i],
                device_id=(core, to),
                device_id_type=MESH,
            )
            c.start()
            heads.append(c)
        recv_blk[s, chip] = send_blk[chip, :, pl.ds(128 * s, 128)]

    def heads_here(s):
        for b in FULL_ORDER:
            i = s * 16 + b
            here = recv_blk.at[s, flip(chip, b)]
            pltpu.make_async_remote_copy(
                src_ref=here, dst_ref=here, send_sem=hsend.at[i], recv_sem=hrecv.at[i], device_id=sib, device_id_type=MESH
            ).wait_recv()

    rest[3].start_z()
    events = [lambda: [g.on_plane(0) for g in rest]]
    events.append(lambda: [g.on_z(3) for g in rest[:3]])
    events.append(lambda: [g.on_diagonal(0) for g in rest])
    for z in (1, 2, 3):
        events.append(lambda z=z: [g.on_plane(z) for g in rest[:3]])
    for z in (1, 2, 3):
        events.append(lambda z=z: [rest[3].on_z(z)])
    for z in (1, 2, 3):
        events.append(lambda z=z: [g.on_diagonal(z) for g in rest[:3]])
    READY = len(events)
    for z in (1, 2, 3):
        events.append(lambda z=z: [rest[3].on_plane(z)])
    for z in (1, 2, 3):
        events.append(lambda z=z: [rest[3].on_diagonal(z)])

    def attend_sequence(s, during):
        load_sequence(recv_blk, s, kk, vt_ref=vt)

        @pl.loop(0, 8)
        def _(step):
            for k, event in enumerate(during):

                @pl.when(step == k)
                def _():
                    event()

            q = flip_by(step, chip // 2)
            query = jnp.concatenate([recv_blk[s, 2 * q, 0:64, :], recv_blk[s, 2 * q + 1, 0:64, :]], 1)
            scores = jnp.dot(kk[...], query, preferred_element_type=f32) * (0.125 * LOG2E)
            key = lax.broadcasted_iota(jnp.int32, scores.shape, 0)
            scores = jnp.where(key < lengths_ref[s], scores, masked_score)
            top = jnp.max(scores, 0, keepdims=True)
            e = jnp.exp2(scores - top)
            mass = jnp.sum(e, 0, keepdims=True)
            o = jnp.dot(vt[...], e.astype(bf16), preferred_element_type=f32) / mass
            lse_ref[s, pl.ds(q, 1), :] = top + jnp.log2(mass)
            o_full[s, :, pl.ds(pl.multiple_of(q * 256, 256), 256)] = o
            for i in range(2):
                to = 2 * q + i
                ctx_blk[s, to] = o[:, 128 * i : 128 * i + 128].astype(bf16)

                @pl.when(to != chip)
                def _():
                    pltpu.make_async_remote_copy(
                        src_ref=ctx_blk.at[s, to],
                        dst_ref=ctx_recv.at[chip, :, pl.ds(128 * s, 128)],
                        send_sem=csend.at[s * 16 + to],
                        recv_sem=crecv.at[s * 16 + chip],
                        device_id=(core, to),
                        device_id_type=MESH,
                    ).start()

        ctx_recv[chip, :, pl.ds(128 * s, 128)] = ctx_blk[s, chip]

    PRE, FIRST, SECOND = 3, 3, 5
    for event in events[:PRE]:
        event()
    heads_here(0)
    attend_sequence(0, events[PRE : PRE + FIRST])
    heads_here(1)
    pairs_out = pltpu.make_async_copy(recv_blk, o_pairs, local_sem.at[7])
    pairs_out.start()
    attend_sequence(1, events[PRE + FIRST : PRE + FIRST + SECOND])
    for event in events[PRE + FIRST + SECOND : READY]:
        event()
    for g in rest[:3]:
        g.on_sibling()
    out_weights = pltpu.make_async_copy(o_out, w_out, local_sem.at[6 + 2])
    out_weights.start()

    def fetch(c, slot):
        cols = pl.ds(pl.multiple_of(c * 512, 512), 512)
        return pltpu.make_async_copy(o_expand.at[:, :, cols], w_expand.at[slot], wsem.at[slot])

    fetch(0, 0).start()

    owner = lax.broadcasted_iota(jnp.int32, (32, 1024), 0)
    column = lax.broadcasted_iota(jnp.int32, (32, 1024), 1)
    lane = lax.broadcasted_iota(jnp.int32, (128, 1024), 0)
    pick = jnp.where(lax.rem(lax.broadcasted_iota(jnp.int32, (128, 1024), 1), 32) == lane, 1.0, 0.0).astype(bf16)
    o_rows[...] = jnp.zeros_like(o_rows)
    for r in range(7):
        choose = jnp.where(column == owner * 32 + r, 1.0, 0.0).astype(bf16)
        piece = jnp.dot(choose, w_vec[...].reshape(1024, 128), preferred_element_type=f32)
        if r == 3:
            for o in range(32):
                e_row[o // 4 : o // 4 + 1, 128 * (o % 4) : 128 * (o % 4) + 128] = piece[o : o + 1]
        else:
            spread_row = jnp.dot(piece.astype(bf16), pick, preferred_element_type=f32)
            o_rows[r : r + 1] = jnp.sum(jnp.where(lax.div(column, 32) == owner, spread_row, 0.0), 0, keepdims=True)

    for s in range(2):
        for b in range(1, 16):
            other = flip(chip, b)
            here = ctx_recv.at[other, :, pl.ds(128 * s, 128)]
            pltpu.make_async_remote_copy(
                src_ref=ctx_blk.at[s, other],
                dst_ref=here,
                send_sem=csend.at[s * 16 + other],
                recv_sem=crecv.at[s * 16 + other],
                device_id=sib,
                device_id_type=MESH,
            ).wait()
    mine, others = pl.ds(core * 8, 8), pl.ds((1 - core) * 8, 8)
    swaps.append(
        pltpu.make_async_remote_copy(
            src_ref=ctx_recv.at[others],
            dst_ref=ctx_sib,
            send_sem=tsend.at[2],
            recv_sem=trecv.at[2],
            device_id=sib,
            device_id_type=MESH,
        )
    )
    swaps[-1].start()
    turned[2, 0] = ctx_recv[mine].reshape(512, 256)
    out_weights.wait()
    for i in range(4):
        rows = ctx_recv[4 * i : 4 * i + 4].reshape(256, 256).astype(f32).T.astype(bf16)
        term = jnp.dot(rows, w_out[8 * i : 8 * i + 8].reshape(256, 1024), preferred_element_type=f32)
        if i == 0:
            o_scaled[...] = term + (x_ref[...].astype(f32) + o_rows[0:1])
        else:
            o_scaled[...] += term

    @pl.loop(0, 4)
    def _(i):
        span = pl.ds(pl.multiple_of(i * 64, 64), 64)
        residual = o_scaled[span]
        center = residual - jnp.mean(residual, -1, keepdims=True)
        spread = lax.rsqrt(jnp.mean(center * center, -1, keepdims=True) + epsilon)
        x_hat = center * spread
        o_scaled[span] = x_hat
        o_spread[span] = jnp.broadcast_to(spread, (64, 128))
        normed[span] = (x_hat * o_rows[1:2] + o_rows[2:3]).astype(bf16)

    for i in range(4):
        n_turned[i // 2, 256 * (i % 2) : 256 * (i % 2) + 256] = normed[:, 256 * i : 256 * i + 256].astype(f32).T.astype(bf16)
    swaps.append(turn(1, n_turned.at[1 - core], n_turned.at[core]))

    def active_copy(j):
        return pltpu.make_async_remote_copy(
            src_ref=stage.at[j],
            dst_ref=active_t.at[1, j],
            send_sem=tsend.at[3 + j],
            recv_sem=trecv.at[3 + j],
            device_id=sib,
            device_id_type=MESH,
        )

    def keep_chunk(c):
        return (
            pltpu.make_async_copy(active_all.at[c], o_active.at[c], ksem.at[0, c]),
            pltpu.make_async_copy(slope_all.at[c], o_slope.at[c], ksem.at[1, c]),
        )

    last_events = events[READY:]

    @pl.loop(0, 8)
    def _(c):
        for k, event in enumerate(last_events[:8]):

            @pl.when(c == k)
            def _():
                event()

        slot = lax.rem(c, 2)

        @pl.when(c < 7)
        def _():
            fetch(c + 1, 1 - slot).start()

        fetch(c, slot).wait()
        expanded = jnp.dot(normed[...], w_expand[slot].reshape(1024, 512), preferred_element_type=f32) + e_row[pl.ds(c, 1)]
        share = 0.5 * (1.0 + lax.erf(expanded * math.sqrt(0.5)))
        bell = jnp.exp(-0.5 * expanded * expanded) * (1.0 / math.sqrt(2.0 * math.pi))
        slope_all[c] = (share + expanded * bell).astype(bf16)
        active = (expanded * share).astype(bf16)
        active_all[c] = active
        for copy in keep_chunk(c):
            copy.start()
        across = active.astype(f32).T.astype(bf16)
        j = lax.rem(c, 4)

        @pl.when(lax.div(c, 4) == core)
        def _():
            active_t[0, j] = across

        @pl.when(lax.div(c, 4) != core)
        def _():
            stage[j] = across
            active_copy(j).start()

    for event in last_events[8:]:
        event()
    for c in swaps:
        c.wait()
    turned[2, 1] = ctx_sib[...].reshape(512, 256)
    for j in range(4):
        active_copy(j).wait()
    kept = [
        pltpu.make_async_copy(turned, o_turned, local_sem.at[0]),
        pltpu.make_async_copy(active_t, o_active_t, local_sem.at[1]),
    ]
    for c in kept:
        c.start()
    rest[3].on_sibling()
    for c in range(8):
        for copy in keep_chunk(c):
            copy.wait()
    for c in kept:
        c.wait()
    for c in heads:
        c.wait_send()
    copies.drain(sib)
    for g in first + rest:
        g.drain()
    keep.wait()
    pairs_out.wait()


def flip_by(v, w):
    out = 0
    for b in (1, 2, 4):
        p, q = lax.rem(lax.div(v, b), 2), lax.rem(lax.div(w, b), 2)
        out = out + b * (p + q - 2 * p * q)
    return out


def forward_attention(rows, lengths, qkv, bias, vec, w_out, w_expand, w_reduce, collective_id):
    v, hbm = pl.BlockSpec(memory_space=pltpu.VMEM), pl.BlockSpec(memory_space=pl.ANY)
    f32, bf16 = jnp.float32, jnp.bfloat16
    gathered = lambda x: jax.ShapeDtypeStruct((32,) + x.shape, x.dtype)
    dma = pltpu.SemaphoreType.DMA
    array = jax.ShapeDtypeStruct
    vmem = lambda shape, dtype=bf16: pltpu.VMEM(shape, dtype)
    return pl.pallas_call(
        fwd_kernel,
        out_shape=[
            gathered(w_out),
            gathered(w_expand),
            gathered(w_reduce),
            gathered(qkv),
            array((2, 16, 192, 128), bf16),
            array((2, 64, 2048), f32),
            array((2, 8, 256), f32),
            array((8, 1024), f32),
            array((256, 1024), f32),
            array((256, 128), f32),
            array((8, 256, 512), bf16),
            array((8, 256, 512), bf16),
            array((3, 2, 512, 256), bf16),
            array((2, 4, 512, 256), bf16),
        ],
        in_specs=[v, pl.BlockSpec(memory_space=pltpu.SMEM)] + [hbm] * 6,
        out_specs=[hbm] * 5 + [v] * 5 + [hbm] * 4,
        scratch_shapes=[
            vmem((32,) + qkv.shape),
            vmem((32,) + bias.shape),
            vmem((32,) + vec.shape),
            vmem((32,) + w_out.shape),
            vmem((2, 32, 32, 512)),
            vmem((16, 192, 256)),
            vmem((2, 16, 192, 128)),
            vmem((2, 16, 64, 128)),
            vmem((16, 64, 256)),
            vmem((2048, 64)),
            vmem((64, 2048)),
            vmem((8, 512), f32),
            vmem((2, 512, 256)),
            vmem((2, 512, 256)),
            vmem((256, 1024)),
            vmem((4, 512, 256)),
            vmem((3, 2, 512, 256)),
            vmem((2, 4, 512, 256)),
            vmem((8, 64, 256)),
            vmem((8, 256, 512)),
            vmem((8, 256, 512)),
            dma((210,)),
            dma((210,)),
            dma((9,)),
            dma((32,)),
            dma((32,)),
            dma((32,)),
            dma((32,)),
            dma((7,)),
            dma((7,)),
            dma((2,)),
            dma((36,)),
            dma((24,)),
            dma((2, 8)),
        ],
        compiler_params=pltpu.CompilerParams(
            collective_id=collective_id, has_side_effects=True, vmem_limit_bytes=60 * MIB
        ),
        name="forward_attention",
    )(rows, lengths, qkv, bias, vec, w_out, w_expand, w_reduce)


class Scatter:
    ORDER = (12, 8, 4, 0)

    def __init__(self, copies, name, grads, out, bufs):
        self.copies, self.name, self.grads, self.out = copies, name, grads, out
        self.first, self.second, self.third = bufs
        self.core, self.chip = place()
        self.rows = grads.shape[1]
        self.half = self.rows // 2
        self.lo, self.hi = pl.ds(0, self.half), pl.ds(self.half, self.half)
        self.first_at = [[self.first.at[k, i] for i in range(2)] for k in range(4)]
        self.second_at = [[self.second.at[k, i] for i in range(2)] for k in range(4)]
        self.third_at = [self.third.at[k] for k in range(3)]

    def at(self, bits):
        return (self.core, flip(self.chip, bits))

    def send(self, tag, src, dst, bits, half=True):
        like = self.first_at[0][0] if half else self.third_at[0]
        self.copies.send((self.name, tag), src, dst, self.at(bits), like)

    def arrived(self, tag, dst):
        self.copies.arrived((self.name, tag), dst, self.at(1))

    def add(self, rows, fn):
        step = min(rows, 16)
        if rows == step:
            fn(0, step)
            return

        def turn(i, carry):
            fn(pl.multiple_of(i * step, step), step)
            return carry

        lax.fori_loop(0, rows // step, turn, 0)

    def start(self):
        for k, z in enumerate(self.ORDER):
            diag = flip(self.chip, z + 3)
            self.send(("1a", k), self.grads.at[diag, self.lo], self.first_at[k][0], 2)
            self.send(("1b", k), self.grads.at[diag, self.hi], self.first_at[k][1], 1)

    def start_direct(self):
        for k, z in enumerate(self.ORDER):
            xb, yb = flip(self.chip, z + 1), flip(self.chip, z + 2)
            self.send(("2xh", k), self.grads.at[xb, self.hi], self.second_at[k][0].at[self.hi], 1)
            self.send(("2yl", k), self.grads.at[yb, self.lo], self.second_at[k][1].at[self.lo], 2)

    def on_first(self, k):
        z = self.ORDER[k]
        for i, (tag, bit, upper) in enumerate((("1a", 1, False), ("1b", 2, True))):
            owner = flip(self.chip, z + bit)
            here = self.first_at[k][i]
            self.arrived((tag, k), here)

            def fn(start, size):
                rows = pl.ds(start, size)
                theirs = pl.ds(start + (self.half if upper else 0), size)
                here[rows] = here[rows] + self.grads.at[owner][theirs]

            self.add(self.half, fn)
            self.send(("2" + "xy"[i] + "lh"[i], k), here, self.second_at[k][i].at[self.hi if upper else self.lo], bit)

    def on_second(self, k):
        z = self.ORDER[k]
        self.arrived(("2xh", k), self.second_at[k][0].at[self.hi])
        self.arrived(("2yl", k), self.second_at[k][1].at[self.lo])
        self.arrived(("2xl", k), self.second_at[k][0].at[self.lo])
        self.arrived(("2yh", k), self.second_at[k][1].at[self.hi])
        owner = flip(self.chip, z)

        def fn(start, size):
            rows = pl.ds(start, size)
            f32 = jnp.float32
            total = self.grads.at[owner][rows].astype(f32) + self.second_at[k][0][rows].astype(f32)
            total = total + self.second_at[k][1][rows].astype(f32)
            if k < 3:
                self.second_at[k][0][rows] = total.astype(self.second.dtype)
            else:
                self.out[rows] = total

        self.add(self.rows, fn)
        if k < 3:
            self.send(("3", k), self.second_at[k][0], self.third_at[k], z, False)

    def on_third(self):
        for k in range(3):
            self.arrived(("3", k), self.third_at[k])

        def fn(start, size):
            rows = pl.ds(start, size)
            total = self.out[rows]
            for k in range(3):
                total = total + self.third_at[k][rows].astype(jnp.float32)
            self.out[rows] = total

        self.add(self.rows, fn)


def scatter_buffers(block, dtype):
    rows, cols = block
    return [
        pltpu.VMEM((4, 2, rows // 2, cols), dtype),
        pltpu.VMEM((4, 2, rows, cols), dtype),
        pltpu.VMEM((3, rows, cols), dtype),
    ]


def bwd_kernel(*refs):
    f32, bf16 = jnp.float32, jnp.bfloat16
    (
        lengths_ref, h_pairs, h_full, lse_ref, h_rows, h_active_t, cotangent, scaled, spread, vectors,
        h_active, h_slope, h_reduce, h_expand, h_out, h_qkv,
    ) = refs[:16]
    (o_layer, o_reduce, o_expand, o_out, o_vec, o_qkv, o_input, o_bias) = refs[16:24]
    bufs = [refs[24 + 3 * i : 27 + 3 * i] for i in range(5)]
    (
        g_reduce, g_expand, g_out, g_vec, g_qkv, w_qkv, d_recv, kk, vv, kt, acc, d_send, d_own, d_sib, b_own, b_sib, b_in,
        slopes, w_reduce, w_expand, w_out, e_own, e_sib, d_first, a_own, a_sib, d_ctx, rows_sum, e_sum, vec_own, vec_sib, r_own, r_sib, pairs, o_full, rows_t, active_t,
        send_sem, recv_sem, local_sem, dsend, drecv, qsend, qrecv, esend, erecv, wsem, lsem,
    ) = refs[39:]
    core, chip = place()
    sib = (1 - core, chip)
    greet([sib] + [(core, flip(chip, b)) for b in range(1, 16)])
    copies = Copies(send_sem, recv_sem)
    rest = [
        Scatter(copies, i, g, o, bufs[i])
        for i, (g, o) in enumerate(((g_reduce, o_reduce), (g_expand, o_expand), (g_out, o_out), (g_vec, o_vec)))
    ]
    last = Scatter(copies, 4, g_qkv, o_qkv, bufs[4])
    out_weights = pltpu.make_async_copy(h_out, w_out, local_sem.at[4])
    out_weights.start()

    def fetch(c, slot, back):
        cols = pl.ds(pl.multiple_of(c * 512, 512), 512)
        copies_in = [
            pltpu.make_async_copy(h_reduce.at[pl.ds(c * 4, 4)], w_reduce.at[slot], wsem.at[slot, 0]),
            pltpu.make_async_copy((h_slope if back else h_active).at[c], slopes.at[slot], wsem.at[slot, 2]),
        ]
        if back:
            copies_in.append(pltpu.make_async_copy(h_expand.at[:, :, cols], w_expand.at[slot], wsem.at[slot, 1]))
        return copies_in

    for c in fetch(0, 0, False):
        c.start()
    loads = [
        pltpu.make_async_copy(src, dst, lsem.at[i])
        for i, (src, dst) in enumerate(((h_active_t, active_t), (h_rows, rows_t), (h_pairs, pairs), (h_full, o_full)))
    ]
    for c in loads:
        c.start()
    d_first[...] = scaled[...] * vectors[1:2] + (vectors[2:3] + vectors[4:5])

    @pl.loop(0, 8)
    def _(c):
        slot = lax.rem(c, 2)

        @pl.when(c < 7)
        def _():
            for copy in fetch(c + 1, 1 - slot, False):
                copy.start()

        @pl.when(c == 7)
        def _():
            for copy in fetch(0, 0, True):
                copy.start()

        for copy in fetch(c, slot, False):
            copy.wait()
        d_first[...] += jnp.dot(slopes[slot], w_reduce[slot].reshape(512, 1024), preferred_element_type=f32)

    rows_sum[...] = jnp.zeros_like(rows_sum)

    @pl.loop(0, 4)
    def _(i):
        span = pl.ds(pl.multiple_of(i * 64, 64), 64)
        total = d_first[span]
        center = total - jnp.mean(total, -1, keepdims=True)
        width = lax.rsqrt(jnp.mean(center * center, -1, keepdims=True) + epsilon)
        x_hat = center * width
        row = chip * 128 + lax.rem(i, 2) * 64 + lax.broadcasted_iota(jnp.int32, (64, 1024), 0)
        valid = row < lengths_ref[lax.div(i, 2)]
        o_layer[span] = jnp.where(valid, x_hat * vectors[5:6] + vectors[6:7], 0.0).astype(bf16)
        d_output = jnp.where(valid, cotangent[span].astype(f32), 0.0)
        pulled = d_output * vectors[5:6]
        level = jnp.mean(pulled, -1, keepdims=True)
        slope = jnp.mean(pulled * x_hat, -1, keepdims=True)
        d_rows = width * (pulled - level - x_hat * slope)
        d_low = d_rows.astype(bf16)
        d_first[span] = d_rows
        r_own[span] = d_low
        rows_sum[4:5] += jnp.sum(d_low.astype(f32), 0, keepdims=True)
        rows_sum[5:6] += jnp.sum(d_output * x_hat, 0, keepdims=True)
        rows_sum[6:7] += jnp.sum(d_output, 0, keepdims=True)

    copies.send("r", r_own, r_sib, sib, r_own)
    copies.arrived("r", r_sib, sib)
    for c in loads:
        c.wait()

    @pl.loop(0, 4)
    def _(j):
        g = jnp.dot(active_t[0, j], r_own[...], preferred_element_type=f32)
        g = g + jnp.dot(active_t[1, j], r_sib[...], preferred_element_type=f32)
        g_reduce[pl.ds(j * 4, 4)] = g.astype(bf16).reshape(4, 128, 1024)

    rest[0].start()
    rest[0].start_direct()

    def e_copy(c):
        return pltpu.make_async_remote_copy(
            src_ref=e_own.at[c],
            dst_ref=e_sib.at[c],
            send_sem=esend.at[c],
            recv_sem=erecv.at[c],
            device_id=sib,
            device_id_type=MESH,
        )

    @pl.loop(0, 8)
    def _(c):
        slot = lax.rem(c, 2)

        @pl.when(c < 7)
        def _():
            for copy in fetch(c + 1, 1 - slot, True):
                copy.start()

        for copy in fetch(c, slot, True):
            copy.wait()
        d_active = nt(r_own[...], w_reduce[slot].reshape(512, 1024))
        d_expanded = (d_active * slopes[slot].astype(f32)).astype(bf16)
        e_own[c] = d_expanded
        e_copy(c).start()
        e_sum[pl.ds(c, 1)] = jnp.sum(d_expanded.astype(f32), 0, keepdims=True)
        d_first[...] += nt(d_expanded, w_expand[slot].reshape(1024, 512))

    @pl.loop(0, 4)
    def _(i):
        span = pl.ds(pl.multiple_of(i * 64, 64), 64)
        d_normed, x_hat = d_first[span], scaled[span]
        pulled = d_normed * vectors[1:2]
        level = jnp.mean(pulled, -1, keepdims=True)
        slope = jnp.mean(pulled * x_hat, -1, keepdims=True)
        d_rows = spread[span, 0:1] * (pulled - level - x_hat * slope)
        d_low = d_rows.astype(bf16)
        d_first[span] = d_rows
        a_own[span] = d_low
        rows_sum[0:1] += jnp.sum(d_low.astype(f32), 0, keepdims=True)
        rows_sum[1:2] += jnp.sum(d_normed * x_hat, 0, keepdims=True)
        rows_sum[2:3] += jnp.sum(d_normed, 0, keepdims=True)

    for k in range(4):
        rest[0].on_first(k)
    out_weights.wait()

    @pl.loop(0, 4)
    def _(i):
        t = nt(w_out[pl.ds(i * 8, 8)].reshape(256, 1024), a_own[...])
        d_ctx[pl.ds(i * 4, 4)] = t.astype(bf16).reshape(4, 64, 256)

    sent = []

    def exchange_out(s, b, src, dst, sends, recvs):
        c = pltpu.make_async_remote_copy(
            src_ref=src,
            dst_ref=dst,
            send_sem=sends.at[s * 16 + b],
            recv_sem=recvs.at[s * 16 + b],
            device_id=(core, flip(chip, b)),
            device_id_type=MESH,
        )
        c.start()
        sent.append(c)

    def exchange_in(s, b, here, sends, recvs):
        pltpu.make_async_remote_copy(
            src_ref=here,
            dst_ref=here,
            send_sem=sends.at[s * 16 + b],
            recv_sem=recvs.at[s * 16 + b],
            device_id=sib,
            device_id_type=MESH,
        ).wait_recv()

    for s in range(2):
        lane = pl.ds(128 * s, 128)
        for b in FULL_ORDER:
            exchange_out(s, b, d_ctx.at[flip(chip, b), :, lane], d_recv.at[s, chip], dsend, drecv)
        d_recv[s, chip] = d_ctx[chip, :, lane]
    copies.send("a", a_own, a_sib, sib, a_own)

    vec_own[...] = jnp.zeros_like(vec_own)
    owner = lax.broadcasted_iota(jnp.int32, (32, 1024), 0)
    column = lax.broadcasted_iota(jnp.int32, (32, 1024), 1)
    place_in = lax.rem(lax.broadcasted_iota(jnp.int32, (1024, 128), 0), 32)
    pick = jnp.where(place_in == lax.broadcasted_iota(jnp.int32, (1024, 128), 1), 1.0, 0.0).astype(bf16)
    for r in (0, 1, 2, 4, 5, 6):
        spread_row = jnp.where(lax.div(column, 32) == owner, rows_sum[r : r + 1], 0.0)
        top = spread_row.astype(bf16)
        low = (spread_row - top.astype(f32)).astype(bf16)
        vec_own[:, r, :] = jnp.dot(top, pick, preferred_element_type=f32) + jnp.dot(low, pick, preferred_element_type=f32)
    for o in range(32):
        vec_own[o, 3:4, :] = e_sum[o // 4 : o // 4 + 1, 128 * (o % 4) : 128 * (o % 4) + 128]
    own_half, other_half = pl.ds(core * 16, 16), pl.ds((1 - core) * 16, 16)
    copies.send("v", vec_own.at[other_half], vec_sib, sib, vec_sib)


    @pl.loop(0, 8)
    def _(c):
        e_copy(c).wait()
        g = jnp.dot(rows_t[1, 0], e_own[c], preferred_element_type=f32)
        g = g + jnp.dot(rows_t[1, 1], e_sib[c], preferred_element_type=f32)
        g_expand[:, :, pl.ds(pl.multiple_of(c * 512, 512), 512)] = g.astype(bf16).reshape(16, 32, 512)

    rest[1].start()
    rest[1].start_direct()
    copies.arrived("a", a_sib, sib)
    for i in range(4):
        cols = slice(256 * i, 256 * i + 256)
        g = jnp.dot(rows_t[2, 0], a_own[:, cols], preferred_element_type=f32)
        g = g + jnp.dot(rows_t[2, 1], a_sib[:, cols], preferred_element_type=f32)
        g_out[:, :, cols] = g.astype(bf16).reshape(16, 32, 256)
    copies.arrived("v", vec_sib, sib)
    g_vec[...] = vec_own[own_half] + vec_sib[...]
    for r in rest[2:]:
        r.start()
        r.start_direct()
    b_own[...] = jnp.zeros_like(b_own)

    def fetch_qkv(i, slot):
        return pltpu.make_async_copy(h_qkv.at[pl.ds(i * 8, 8)], w_qkv.at[slot], local_sem.at[5 + slot])

    fetch_qkv(0, 0).start()
    fetch_qkv(1, 1).start()

    def back_sequence(s, during):
        load_sequence(pairs, s, kk, vt_ref=None, vv_ref=vv)
        for j in range(16):
            kt[:, pl.ds(j * 128, 128)] = pairs[s, j, 64:128, :]
        acc[...] = jnp.zeros_like(acc)

        @pl.loop(0, 8)
        def _(q):
            for k, event in enumerate(during):

                @pl.when(q == k)
                def _():
                    event()

            both = lambda ref, lo, hi: jnp.concatenate([ref[s, 2 * q, lo:hi, :], ref[s, 2 * q + 1, lo:hi, :]], 1)
            query, d_out = both(pairs, 0, 64), both(d_recv, 0, 64)
            span = pl.ds(pl.multiple_of(q * 256, 256), 256)
            delta = jnp.sum(d_out.astype(f32) * o_full[s, :, span], 0, keepdims=True)
            scores = jnp.dot(kk[...], query, preferred_element_type=f32) * (0.125 * LOG2E)
            key = lax.broadcasted_iota(jnp.int32, scores.shape, 0)
            probs = jnp.where(key < lengths_ref[s], jnp.exp2(scores - lse_ref[s, pl.ds(q, 1), :]), 0.0)
            d_probs = jnp.dot(vv[...], d_out, preferred_element_type=f32)
            d_scores = (probs * (d_probs - delta)).astype(bf16)
            zero = jnp.zeros((64, 256), f32)
            query_rows = jnp.concatenate([query.astype(f32), zero], 0).T.astype(bf16)
            d_rows = jnp.concatenate([zero, d_out.astype(f32)], 0).T.astype(bf16)
            acc[...] += jnp.dot(d_scores, query_rows, preferred_element_type=f32) + jnp.dot(
                probs.astype(bf16), d_rows, preferred_element_type=f32
            )
            d_query = (jnp.dot(kt[...], d_scores, preferred_element_type=f32) * 0.125).astype(bf16)
            for i in range(2):
                part = d_query[:, 128 * i : 128 * i + 128]
                d_send[s, 2 * q + i, 0:64, :] = part
                b_own[0] += part.astype(f32)

        for j in range(16):
            t = acc[pl.ds(j * 128, 128)].T
            d_send[s, j, 64:128, :] = (t[:64] * 0.125).astype(bf16)
            value = t[64:].astype(bf16)
            d_send[s, j, 128:192, :] = value
            b_own[1] += value.astype(f32)
        lane = pl.ds(128 * s, 128)
        for b in FULL_ORDER:
            exchange_out(s, b, d_send.at[s, flip(chip, b)], d_own.at[chip, :, lane], qsend, qrecv)
        d_own[chip, :, lane] = d_send[s, chip]

    for k in range(4):
        rest[0].on_second(k)
    events = [lambda k=k: [r.on_first(k) for r in rest[1:]] for k in range(4)]
    events += [lambda k=k: [r.on_second(k) for r in rest[1:]] for k in range(4)]
    FIRST, SECOND, WAIT = 0, 0, 4
    for b in FULL_ORDER:
        exchange_in(0, b, d_recv.at[0, flip(chip, b)], dsend, drecv)
    back_sequence(0, events[:FIRST])
    for b in FULL_ORDER:
        exchange_in(1, b, d_recv.at[1, flip(chip, b)], dsend, drecv)
    back_sequence(1, events[FIRST : FIRST + SECOND])

    copies.send("bias sib", b_own, b_sib, sib, b_own)
    for event in events[FIRST + SECOND : FIRST + SECOND + WAIT]:
        event()
    for s in range(2):
        lane = pl.ds(128 * s, 128)
        for b in FULL_ORDER:
            exchange_in(s, b, d_own.at[flip(chip, b), :, lane], qsend, qrecv)
        copies.send(("rows", s), d_own.at[:, :, lane], d_sib.at[:, :, lane], sib, d_own.at[:, :, lane])

    copies.arrived("bias sib", b_sib, sib)
    for s in range(2):
        copies.arrived(("rows", s), d_sib.at[:, :, pl.ds(128 * s, 128)], sib)

    for part in range(3):

        @pl.loop(0, 4)
        def _(p):
            total = None
            for i, rows in enumerate((d_own, d_sib)):
                right = rows[pl.ds(4 * p, 4), pl.ds(64 * part, 64)].reshape(256, 256)
                term = nt(rows_t[0, i], right)
                total = term if total is None else total + term
            cols = pl.ds(pl.multiple_of(part * 1024 + p * 256, 256), 256)
            g_qkv[:, :, cols] = total.astype(bf16).reshape(16, 32, 256)

    last.start()
    last.start_direct()

    b_sib[...] = b_sib[...] + b_own[...]
    sender = core == lax.div(chip, 8)
    for i in range(2):
        to = lax.rem(2 * chip + i, 16)
        rows = pl.ds(32 * i, 32)
        c = pltpu.make_async_remote_copy(
            src_ref=b_sib.at[:, rows],
            dst_ref=b_in,
            send_sem=local_sem.at[1 + i],
            recv_sem=local_sem.at[3],
            device_id=(core, to),
            device_id_type=MESH,
        )

        @pl.when(sender & (to != chip))
        def _():
            c.start()

        @pl.when(sender & (to == chip))
        def _():
            b_in[...] = b_sib[:, rows]

    for event in events[FIRST + SECOND + WAIT :]:
        event()
    for i in range(4):
        fetch_qkv(i, i % 2).wait()
        t = None
        for part in range(3):
            w = w_qkv[i % 2, :, :, 1024 * part : 1024 * part + 1024].reshape(256, 1024)
            term = jnp.dot(w, d_own[:, 64 * part : 64 * part + 64].reshape(1024, 256), preferred_element_type=f32)
            t = term if t is None else t + term
        if i < 2:
            fetch_qkv(i + 2, i).start()
        cols = slice(256 * i, 256 * i + 256)
        o_input[:, cols] = d_first[:, cols] + t.T

    for k in range(4):
        last.on_first(k)
    for r in rest:
        r.on_third()
    for k in range(4):
        last.on_second(k)
    last.on_third()
    for i in range(2):
        to = lax.rem(2 * chip + i, 16)

        @pl.when(sender & (to != chip))
        def _():
            pltpu.make_async_remote_copy(
                src_ref=b_sib.at[:, pl.ds(32 * i, 32)],
                dst_ref=b_in,
                send_sem=local_sem.at[1 + i],
                recv_sem=local_sem.at[3],
                device_id=(core, to),
                device_id_type=MESH,
            ).wait_send()

    @pl.when(8 * core + lax.div(chip, 2) != chip)
    def _():
        pltpu.make_async_remote_copy(
            src_ref=b_in, dst_ref=b_in, send_sem=local_sem.at[1], recv_sem=local_sem.at[3], device_id=sib, device_id_type=MESH
        ).wait_recv()

    o_bias[...] = b_in[...]
    for c in sent:
        c.wait_send()
    copies.drain(sib)


def backward_attention(
    lengths, pairs, o_full, lse, rows_t, active_t, cotangent, scaled, spread, vectors,
    active, slope, w_reduce, w_expand, w_out, w_qkv, collective_id,
):
    v, hbm = pl.BlockSpec(memory_space=pltpu.VMEM), pl.BlockSpec(memory_space=pl.ANY)
    f32, bf16 = jnp.float32, jnp.bfloat16
    dma = pltpu.SemaphoreType.DMA
    blocks = [((128, 1024), bf16), ((32, 4096), bf16), ((32, 1024), bf16), ((16, 128), f32), ((32, 3072), bf16)]
    bufs = []
    for block, dtype in blocks:
        bufs += scatter_buffers(block, dtype)
    vmem = lambda shape, dtype=bf16: pltpu.VMEM(shape, dtype)
    return pl.pallas_call(
        bwd_kernel,
        out_shape=[jax.ShapeDtypeStruct((256, 1024), bf16)]
        + [jax.ShapeDtypeStruct(block, f32) for block, _ in blocks]
        + [jax.ShapeDtypeStruct((256, 1024), f32), jax.ShapeDtypeStruct((2, 32, 128), f32)],
        in_specs=[pl.BlockSpec(memory_space=pltpu.SMEM), hbm, hbm, v, hbm, hbm] + [v] * 4 + [hbm] * 6,
        out_specs=[v] * 8,
        scratch_shapes=bufs
        + [
            vmem((16, 128, 1024)),
            vmem((16, 32, 4096)),
            vmem((16, 32, 1024)),
            vmem((16, 16, 128), f32),
            vmem((16, 32, 3072)),
            vmem((2, 8, 32, 3072)),
            vmem((2, 16, 64, 128)),
            vmem((2048, 64)),
            vmem((2048, 64)),
            vmem((64, 2048)),
            vmem((2048, 128), f32),
            vmem((2, 16, 192, 128)),
            vmem((16, 192, 256)),
            vmem((16, 192, 256)),
            vmem((2, 64, 128), f32),
            vmem((2, 64, 128), f32),
            vmem((2, 32, 128), f32),
            vmem((2, 256, 512)),
            vmem((2, 4, 128, 1024)),
            vmem((2, 32, 32, 512)),
            vmem((32, 32, 1024)),
            vmem((8, 256, 512)),
            vmem((8, 256, 512)),
            vmem((256, 1024), f32),
            vmem((256, 1024)),
            vmem((256, 1024)),
            vmem((16, 64, 256)),
            vmem((8, 1024), f32),
            vmem((8, 512), f32),
            vmem((32, 16, 128), f32),
            vmem((16, 16, 128), f32),
            vmem((256, 1024)),
            vmem((256, 1024)),
            vmem((2, 16, 192, 128)),
            vmem((2, 64, 2048), f32),
            vmem((3, 2, 512, 256)),
            vmem((2, 4, 512, 256)),
            dma((144,)),
            dma((144,)),
            dma((7,)),
            dma((32,)),
            dma((32,)),
            dma((32,)),
            dma((32,)),
            dma((8,)),
            dma((8,)),
            dma((2, 3)),
            dma((4,)),
        ],
        compiler_params=pltpu.CompilerParams(
            collective_id=collective_id, has_side_effects=True, vmem_limit_bytes=63 * MIB
        ),
        name="backward_attention",
    )(
        lengths, pairs, o_full, lse, rows_t, active_t, cotangent, scaled, spread, vectors,
        active, slope, w_reduce, w_expand, w_out, w_qkv,
    )


def fast_shards(
    inputs,
    lengths,
    w_query,
    b_query,
    w_key,
    w_value,
    b_value,
    w_out,
    b_out,
    first_gain,
    first_shift,
    w_expand,
    b_expand,
    w_reduce,
    b_reduce,
    second_gain,
    second_shift,
    cotangent,
):
    f32, bf16 = jnp.float32, jnp.bfloat16
    seqs, count, width = inputs.shape
    total = seqs * count
    part = width // 32
    ff = w_expand.shape[1]
    qkv = jnp.concatenate([w_query, w_key, w_value], 1)
    bias = jnp.concatenate([b_query, b_value])[:, None] + jnp.zeros((2 * part, 128), bf16)
    small = [b_out, first_gain, first_shift, b_expand, b_reduce, second_gain, second_shift]
    vec = sum(jnp.pad(b[None, :], ((r, part - 1 - r), (0, 128 - b.shape[0]))) for r, b in enumerate(small))
    flat_rows = inputs.reshape(total, width)
    (
        g_out, g_expand, g_reduce, g_qkv, pairs, o_full, lse, vectors, scaled, spread, active, slope, rows_t, active_t,
    ) = forward_attention(flat_rows, lengths, qkv, bias, vec, w_out, w_expand, w_reduce, 1)
    layer_out, s_reduce, s_expand, s_out, s_vec, s_qkv, input_grad, s_bias = backward_attention(
        lengths, pairs, o_full, lse, rows_t, active_t, cotangent.reshape(total, width), scaled, spread, vectors,
        active, slope, g_reduce, g_expand, g_out, g_qkv, 2,
    )
    s_query, s_key, s_value = (s_qkv[:, width * i : width * (i + 1)] for i in range(3))
    s_bias = jnp.sum(s_bias, -1)
    v = [s_vec[r, : b.shape[0]] for r, b in enumerate(small)]
    return (
        layer_out.reshape(inputs.shape),
        input_grad.reshape(inputs.shape),
        s_query,
        s_bias[0],
        s_key,
        s_value,
        s_bias[1],
        s_out,
        v[0],
        v[1],
        v[2],
        s_expand,
        v[3],
        s_reduce,
        v[4],
        v[5],
        v[6],
    )


def solution(mesh):
    fast = mesh.shape["fsdp"] == 2 and mesh.shape["ctx"] == HEADS
    shards = fast_shards if fast else general_shards
    return jax.shard_map(
        shards,
        mesh=mesh,
        in_specs=(
            P("fsdp", "ctx", None),
            P("fsdp"),
            P(("fsdp", "ctx"), None),
            P(("fsdp", "ctx")),
            P(("fsdp", "ctx"), None),
            P(("fsdp", "ctx"), None),
            P(("fsdp", "ctx")),
            P(("fsdp", "ctx"), None),
            P(("fsdp", "ctx")),
            P(("fsdp", "ctx")),
            P(("fsdp", "ctx")),
            P(("fsdp", "ctx"), None),
            P(("fsdp", "ctx")),
            P(("fsdp", "ctx"), None),
            P(("fsdp", "ctx")),
            P(("fsdp", "ctx")),
            P(("fsdp", "ctx")),
            P("fsdp", "ctx", None),
        ),
        out_specs=(
            P("fsdp", "ctx", None),
            P("fsdp", "ctx", None),
            P(("fsdp", "ctx"), None),
            P(("fsdp", "ctx")),
            P(("fsdp", "ctx"), None),
            P(("fsdp", "ctx"), None),
            P(("fsdp", "ctx")),
            P(("fsdp", "ctx"), None),
            P(("fsdp", "ctx")),
            P(("fsdp", "ctx")),
            P(("fsdp", "ctx")),
            P(("fsdp", "ctx"), None),
            P(("fsdp", "ctx")),
            P(("fsdp", "ctx"), None),
            P(("fsdp", "ctx")),
            P(("fsdp", "ctx")),
            P(("fsdp", "ctx")),
        ),
        check_vma=False,
    )
```

```python
from functools import partial
import math

import jax
import jax.numpy as jnp
from jax import lax
from jax.experimental import pallas as pl
from jax.experimental.pallas import tpu as pltpu
from jax.sharding import PartitionSpec as P

HEADS = 16


epsilon = 1e-05
masked_score = -1e30


def layer_norm(rows_in, gain, shift):
    center = rows_in - jnp.mean(rows_in, -1, keepdims=True)
    spread = jnp.mean(center * center, -1, keepdims=True)
    return center * lax.rsqrt(spread + epsilon) * gain + shift


def product(left, right):
    return jnp.dot(left, right, preferred_element_type=jnp.float32)


def outer_sum(left, right):
    return jnp.einsum("rd,re->de", left, right, preferred_element_type=jnp.float32)


def back_product(grad_rows, weight):
    return jnp.einsum("re,de->rd", grad_rows, weight, preferred_element_type=jnp.float32)


def over_blocks(step_fn, carry_state, pair_rows):
    key_count = pair_rows.shape[1]
    block_width = math.gcd(key_count, 512)

    def turn(turn_index, inner_state):
        block_pairs = lax.dynamic_slice_in_dim(pair_rows, turn_index * block_width, block_width, 1)
        return step_fn(inner_state, block_pairs, turn_index * block_width)

    return lax.fori_loop(0, key_count // block_width, turn, carry_state)


def general_shards(
    inputs,
    lengths,
    w_query,
    b_query,
    w_key,
    w_value,
    b_value,
    w_out,
    b_out,
    first_gain,
    first_shift,
    w_expand,
    b_expand,
    w_reduce,
    b_reduce,
    second_gain,
    second_shift,
    cotangent,
):
    gathered = (
        lax.all_gather(w_query, ("fsdp", "ctx"), axis=0, tiled=True),
        lax.all_gather(b_query, ("fsdp", "ctx"), axis=0, tiled=True),
        lax.all_gather(w_key, ("fsdp", "ctx"), axis=0, tiled=True),
        lax.all_gather(w_value, ("fsdp", "ctx"), axis=0, tiled=True),
        lax.all_gather(b_value, ("fsdp", "ctx"), axis=0, tiled=True),
        lax.all_gather(w_out, ("fsdp", "ctx"), axis=0, tiled=True),
        lax.all_gather(b_out, ("fsdp", "ctx"), axis=0, tiled=True),
        lax.all_gather(first_gain, ("fsdp", "ctx"), axis=0, tiled=True),
        lax.all_gather(first_shift, ("fsdp", "ctx"), axis=0, tiled=True),
        lax.all_gather(w_expand, ("fsdp", "ctx"), axis=0, tiled=True),
        lax.all_gather(b_expand, ("fsdp", "ctx"), axis=0, tiled=True),
        lax.all_gather(w_reduce, ("fsdp", "ctx"), axis=0, tiled=True),
        lax.all_gather(b_reduce, ("fsdp", "ctx"), axis=0, tiled=True),
        lax.all_gather(second_gain, ("fsdp", "ctx"), axis=0, tiled=True),
        lax.all_gather(second_shift, ("fsdp", "ctx"), axis=0, tiled=True),
    )
    (
        full_query,
        bias_query,
        full_key,
        full_value,
        bias_value,
        full_out,
        bias_out,
        gain_first,
        shift_first,
        full_expand,
        bias_expand,
        full_reduce,
        bias_reduce,
        gain_second,
        shift_second,
    ) = gathered
    seq_count, block_rows, model_width = inputs.shape
    total_rows = seq_count * block_rows
    head_size = model_width // HEADS
    score_scale = head_size ** (-0.5)
    own_first = lax.axis_index("ctx") * block_rows
    positions = own_first + jnp.arange(block_rows, dtype=jnp.int32)
    valid_rows = (positions[None, :] < lengths[:, None]).astype(jnp.float32).reshape(total_rows, 1)
    flat_rows = inputs.reshape(total_rows, model_width)
    queries = (product(flat_rows, full_query) + bias_query.astype(jnp.float32)).astype(jnp.bfloat16)
    key_rows = product(flat_rows, full_key).astype(jnp.bfloat16)
    value_rows = (product(flat_rows, full_value) + bias_value.astype(jnp.float32)).astype(
        jnp.bfloat16
    )
    query_heads = queries.reshape(seq_count, block_rows, HEADS, head_size)
    local_pairs = jnp.concatenate([key_rows, value_rows], -1).reshape(
        seq_count, block_rows, 2 * model_width
    )

    def key_allowed(first_row, key_count):
        return ((first_row + jnp.arange(key_count, dtype=jnp.int32))[None, :] < lengths[:, None])[
            :, None, None, :
        ]

    def split_pairs(block_pairs):
        key_count = block_pairs.shape[1]
        key_heads = block_pairs[:, :, :model_width].reshape(seq_count, key_count, HEADS, head_size)
        value_heads = block_pairs[:, :, model_width:].reshape(
            seq_count, key_count, HEADS, head_size
        )
        return (key_heads, value_heads, key_count)

    def forward_step(carry_state, block_pairs, first_row):
        running_max, running_sum, running_acc = carry_state
        key_heads, value_heads, key_count = split_pairs(block_pairs)
        allowed = key_allowed(first_row, key_count)
        scores = (
            jnp.einsum(
                "sqhd,skhd->shqk", query_heads, key_heads, preferred_element_type=jnp.float32
            )
            * score_scale
        )
        scores = jnp.where(allowed, scores, masked_score)
        new_max = jnp.maximum(running_max, jnp.max(scores, -1))
        factor = jnp.exp(running_max - new_max)
        exponents = jnp.where(allowed, jnp.exp(scores - new_max[..., None]), 0.0)
        new_sum = running_sum * factor + jnp.sum(exponents, -1)
        update = jnp.einsum(
            "shqk,skhd->sqhd",
            exponents.astype(jnp.bfloat16),
            value_heads,
            preferred_element_type=jnp.float32,
        )
        new_acc = running_acc * jnp.transpose(factor, (0, 2, 1))[..., None] + update
        return (new_max, new_sum, new_acc)

    start_state = (
        jnp.full((seq_count, HEADS, block_rows), masked_score, jnp.float32),
        jnp.zeros((seq_count, HEADS, block_rows), jnp.float32),
        jnp.zeros((seq_count, block_rows, HEADS, head_size), jnp.float32),
    )
    running_max, running_sum, running_acc = over_blocks(
        forward_step, start_state, lax.all_gather(local_pairs, "ctx", axis=1, tiled=True)
    )
    context_full = running_acc / jnp.transpose(running_sum, (0, 2, 1))[..., None]
    log_total = running_max + jnp.log(running_sum)
    context = context_full.reshape(total_rows, model_width).astype(jnp.bfloat16)
    attended = product(context, full_out) + bias_out.astype(jnp.float32)
    residual = flat_rows.astype(jnp.float32) + attended
    normed, first_pull = jax.vjp(
        layer_norm, residual, gain_first.astype(jnp.float32), shift_first.astype(jnp.float32)
    )
    normed_low = normed.astype(jnp.bfloat16)
    expanded = product(normed_low, full_expand) + bias_expand.astype(jnp.float32)
    activated, gelu_pull = jax.vjp(partial(jax.nn.gelu, approximate=False), expanded)
    activated_low = activated.astype(jnp.bfloat16)
    reduced = product(activated_low, full_reduce) + bias_reduce.astype(jnp.float32)
    final_rows, second_pull = jax.vjp(
        layer_norm,
        normed + reduced,
        gain_second.astype(jnp.float32),
        shift_second.astype(jnp.float32),
    )
    layer_out = (final_rows * valid_rows).astype(jnp.bfloat16).reshape(inputs.shape)
    d_output = cotangent.reshape(total_rows, model_width).astype(jnp.float32) * valid_rows
    d_second, second_gain_grad, second_shift_grad = second_pull(d_output)
    d_reduced = d_second.astype(jnp.bfloat16)
    reduce_grad = outer_sum(activated_low, d_reduced)
    reduce_bias_grad = jnp.sum(d_reduced.astype(jnp.float32), 0)
    (d_expanded_full,) = gelu_pull(back_product(d_reduced, full_reduce))
    d_expanded = d_expanded_full.astype(jnp.bfloat16)
    expand_grad = outer_sum(normed_low, d_expanded)
    expand_bias_grad = jnp.sum(d_expanded.astype(jnp.float32), 0)
    d_normed = d_second + back_product(d_expanded, full_expand)
    d_first, first_gain_grad, first_shift_grad = first_pull(d_normed)
    d_attended = d_first.astype(jnp.bfloat16)
    out_grad = outer_sum(context, d_attended)
    out_bias_grad = jnp.sum(d_attended.astype(jnp.float32), 0)
    d_context = back_product(d_attended, full_out).astype(jnp.bfloat16)
    d_context_heads = d_context.reshape(seq_count, block_rows, HEADS, head_size)
    delta = jnp.transpose(
        jnp.sum(d_context_heads.astype(jnp.float32) * context_full, -1), (0, 2, 1)
    )
    whole_length = block_rows * lax.axis_size("ctx")

    def score_grads(key_heads, value_heads, allowed):
        scores = (
            jnp.einsum(
                "sqhd,skhd->shqk", query_heads, key_heads, preferred_element_type=jnp.float32
            )
            * score_scale
        )
        probabilities = jnp.where(allowed, jnp.exp(scores - log_total[..., None]), 0.0)
        d_probs = jnp.einsum(
            "sqhd,skhd->shqk", d_context_heads, value_heads, preferred_element_type=jnp.float32
        )
        d_scores = (probabilities * (d_probs - delta[..., None])).astype(jnp.bfloat16)
        return (probabilities, d_scores)

    def backward_step(carry_state, block_pairs, first_row):
        grad_query, grad_pairs = carry_state
        key_heads, value_heads, key_count = split_pairs(block_pairs)
        probabilities, d_scores = score_grads(
            key_heads, value_heads, key_allowed(first_row, key_count)
        )
        grad_query = (
            grad_query
            + jnp.einsum("shqk,skhd->sqhd", d_scores, key_heads, preferred_element_type=jnp.float32)
            * score_scale
        )
        key_part = (
            jnp.einsum("shqk,sqhd->skhd", d_scores, query_heads, preferred_element_type=jnp.float32)
            * score_scale
        )
        value_part = jnp.einsum(
            "shqk,sqhd->skhd",
            probabilities.astype(jnp.bfloat16),
            d_context_heads,
            preferred_element_type=jnp.float32,
        )
        fresh = jnp.concatenate(
            [
                key_part.reshape(seq_count, key_count, model_width),
                value_part.reshape(seq_count, key_count, model_width),
            ],
            -1,
        )
        before = lax.dynamic_slice_in_dim(grad_pairs, first_row, key_count, 1)
        grad_pairs = lax.dynamic_update_slice_in_dim(grad_pairs, before + fresh, first_row, 1)
        return (grad_query, grad_pairs)

    query_zero = jnp.zeros((seq_count, block_rows, HEADS, head_size), jnp.float32)
    back_state = (query_zero, jnp.zeros((seq_count, whole_length, 2 * model_width), jnp.float32))
    back_result = over_blocks(
        backward_step, back_state, lax.all_gather(local_pairs, "ctx", axis=1, tiled=True)
    )
    grad_query = back_result[0]
    own_pairs = lax.psum_scatter(
        back_result[1].astype(jnp.bfloat16), "ctx", scatter_dimension=1, tiled=True
    ).astype(jnp.float32)
    d_keys = own_pairs[:, :, :model_width].reshape(total_rows, model_width).astype(jnp.bfloat16)
    d_values = own_pairs[:, :, model_width:].reshape(total_rows, model_width).astype(jnp.bfloat16)
    d_queries = grad_query.reshape(total_rows, model_width).astype(jnp.bfloat16)
    query_grad = outer_sum(flat_rows, d_queries)
    query_bias_grad = jnp.sum(d_queries.astype(jnp.float32), 0)
    key_grad = outer_sum(flat_rows, d_keys)
    value_grad = outer_sum(flat_rows, d_values)
    value_bias_grad = jnp.sum(d_values.astype(jnp.float32), 0)
    input_grad = (
        d_first
        + back_product(d_queries, full_query)
        + back_product(d_keys, full_key)
        + back_product(d_values, full_value)
    ).reshape(inputs.shape)
    shares = (
        lax.psum_scatter(query_grad, ("fsdp", "ctx"), scatter_dimension=0, tiled=True),
        lax.psum_scatter(query_bias_grad, ("fsdp", "ctx"), scatter_dimension=0, tiled=True),
        lax.psum_scatter(key_grad, ("fsdp", "ctx"), scatter_dimension=0, tiled=True),
        lax.psum_scatter(value_grad, ("fsdp", "ctx"), scatter_dimension=0, tiled=True),
        lax.psum_scatter(value_bias_grad, ("fsdp", "ctx"), scatter_dimension=0, tiled=True),
        lax.psum_scatter(out_grad, ("fsdp", "ctx"), scatter_dimension=0, tiled=True),
        lax.psum_scatter(out_bias_grad, ("fsdp", "ctx"), scatter_dimension=0, tiled=True),
        lax.psum_scatter(first_gain_grad, ("fsdp", "ctx"), scatter_dimension=0, tiled=True),
        lax.psum_scatter(first_shift_grad, ("fsdp", "ctx"), scatter_dimension=0, tiled=True),
        lax.psum_scatter(expand_grad, ("fsdp", "ctx"), scatter_dimension=0, tiled=True),
        lax.psum_scatter(expand_bias_grad, ("fsdp", "ctx"), scatter_dimension=0, tiled=True),
        lax.psum_scatter(reduce_grad, ("fsdp", "ctx"), scatter_dimension=0, tiled=True),
        lax.psum_scatter(reduce_bias_grad, ("fsdp", "ctx"), scatter_dimension=0, tiled=True),
        lax.psum_scatter(second_gain_grad, ("fsdp", "ctx"), scatter_dimension=0, tiled=True),
        lax.psum_scatter(second_shift_grad, ("fsdp", "ctx"), scatter_dimension=0, tiled=True),
    )
    return (
        layer_out,
        input_grad,
        shares[0],
        shares[1],
        shares[2],
        shares[3],
        shares[4],
        shares[5],
        shares[6],
        shares[7],
        shares[8],
        shares[9],
        shares[10],
        shares[11],
        shares[12],
        shares[13],
        shares[14],
    )


MESH = pl.DeviceIdType.MESH
MIB = 1024*1024

def place():
    core = lax.axis_index("fsdp"); chip = lax.axis_index("ctx")
    return core, chip

def greet(peers):
    barrier = pltpu.get_barrier_semaphore()
    for peer in peers:
        pl.semaphore_signal(barrier, inc=1, device_id=peer, device_id_type=MESH)
    pl.semaphore_wait(barrier, len(peers))

def flip(v, bits):
    for b in (1, 2, 4, 8):
        if bits & b:
            v = v + b - 2 * b * lax.rem(lax.div(v, b), 2)
    return v

LOG2E = math.log2(math.e)


def nt(a, b):
    return lax.dot_general(a, b, (((1,), (1,)), ((), ())), preferred_element_type=jnp.float32)


FULL_ORDER = (12, 8, 4, 15, 11, 7, 14, 13, 10, 9, 6, 5, 3, 2, 1)


class Copies:
    def __init__(self, send_sem, recv_sem):
        self.send_sem, self.recv_sem = send_sem, recv_sem
        self.names, self.sent = {}, []

    def pair(self, name, src, dst, peer):
        i = self.names.setdefault(name, len(self.names))
        return pltpu.make_async_remote_copy(
            src_ref=src,
            dst_ref=dst,
            send_sem=self.send_sem.at[i],
            recv_sem=self.recv_sem.at[i],
            device_id=peer,
            device_id_type=MESH,
        )

    def send(self, name, src, dst, peer, like):
        self.pair(name, src, dst, peer).start()
        self.sent.append((name, like))

    def arrived(self, name, dst, peer):
        self.pair(name, dst, dst, peer).wait_recv()

    def drain(self, peer):
        for name, like in self.sent:
            self.pair(name, like, like, peer).wait_send()


class Line:
    def __init__(self, chip):
        self.z = lax.div(chip, 4)
        self.rest = chip - 4 * self.z
        even = lax.rem(self.z, 2) == 0
        low = self.z < 2
        one, two, three = jnp.int32(1), jnp.int32(2), jnp.int32(3)
        near = jnp.where(even, one, -one)
        mid = jnp.where(low, jnp.where(even, two, one), jnp.where(even, -one, -two))
        far = jnp.where(low, jnp.where(even, three, two), jnp.where(even, -two, -three))
        self.offsets = [jnp.int32(0), near, mid, far]

    def source(self, k):
        return self.z + self.offsets[k]

    def onward_up(self, k):
        return (self.offsets[k] < 0) & (self.z < 3)

    def onward_down(self, k):
        return (self.offsets[k] > 0) & (self.z > 0)


class Gather:
    def __init__(self, copies, line, name, src, out, local_sem, zsend, zrecv):
        self.copies, self.line, self.name, self.src, self.out, self.local_sem = copies, line, name, src, out, local_sem
        self.zsend, self.zrecv = zsend, zrecv
        self.core, self.chip = place()
        self.sib = (1 - self.core, self.chip)
        self.half = src.shape[0] // 2

    def at(self, bits):
        return (self.core, flip(self.chip, bits))

    def index(self, k, bits, core=None):
        core = self.core if core is None else core
        return core * 16 + self.line.source(k) * 4 + flip(self.line.rest, bits)

    def block(self, k, bits, core=None):
        return self.out.at[self.index(k, bits, core)]

    def part(self, k, bits, upper):
        return self.out.at[self.index(k, bits), pl.ds(self.half if upper else 0, self.half)]

    def send(self, tag, src, dst, peer, half=False):
        like = self.src.at[pl.ds(0, self.half)] if half else self.src
        self.copies.send((self.name, tag), src, dst, peer, like)

    def arrived(self, tag, dst):
        self.copies.arrived((self.name, tag), dst, self.sib)

    def along(self, slot, source, src, dst, up):
        return pltpu.make_async_remote_copy(
            src_ref=src,
            dst_ref=dst,
            send_sem=self.zsend.at[self.name * 6 + slot],
            recv_sem=self.zrecv.at[self.name * 4 + source],
            device_id=(self.core, self.chip + 4 if up else self.chip - 4),
            device_id_type=MESH,
        )

    def start_z(self):
        z = self.line.z

        @pl.when(z < 3)
        def _():
            self.along(4, z, self.src, self.block(0, 0), True).start()

        @pl.when(z > 0)
        def _():
            self.along(5, z, self.src, self.block(0, 0), False).start()

    def start_plane(self):
        self.send(("x", 0), self.src, self.block(0, 0), self.at(1))
        self.send(("y", 0), self.src, self.block(0, 0), self.at(2))
        self.send(("s", 0, 0), self.src, self.block(0, 0), self.sib)
        self.local = pltpu.make_async_copy(self.src, self.block(0, 0), self.local_sem)
        self.local.start()

    def on_z(self, k):
        b = self.block(k, 0)
        source = self.line.source(k)
        self.along(source, source, b, b, True).wait_recv()

        @pl.when(self.line.onward_up(k))
        def _():
            self.along(source, source, b, b, True).start()

        @pl.when(self.line.onward_down(k))
        def _():
            self.along(source, source, b, b, False).start()

        self.send(("x", k), b, b, self.at(1))
        self.send(("y", k), b, b, self.at(2))
        self.send(("s", k, 0), b, b, self.sib)

    def on_plane(self, k):
        for bit, tag, further, upper in ((1, "x", 2, False), (2, "y", 1, True)):
            b = self.block(k, bit)
            self.arrived((tag, k), b)
            h = self.part(k, bit, upper)
            self.send(("d" + tag, k), h, h, self.at(further), True)
            self.send(("s", k, bit), b, b, self.sib)

    def on_diagonal(self, k):
        self.arrived(("dx", k), self.part(k, 3, False))
        self.arrived(("dy", k), self.part(k, 3, True))
        b = self.block(k, 3)
        self.send(("s", k, 3), b, b, self.sib)

    def on_sibling(self):
        for k in range(4):
            for bits in range(4):
                self.arrived(("s", k, bits), self.block(k, bits, 1 - self.core))
        self.local.wait()

    def drain(self):
        z = self.line.z

        @pl.when(z < 3)
        def _():
            self.along(4, z, self.src, self.src, True).wait_send()

        @pl.when(z > 0)
        def _():
            self.along(5, z, self.src, self.src, True).wait_send()

        for k in range(1, 4):
            source = self.line.source(k)

            @pl.when(self.line.onward_up(k) | self.line.onward_down(k))
            def _():
                self.along(source, source, self.src, self.src, True).wait_send()


def load_sequence(r_ref, s, kk_ref, vt_ref=None, vv_ref=None):
    for j in range(r_ref.shape[1]):
        span = pl.ds(j * 128, 128)
        kk_ref[span] = r_ref[s, j, 64:128, :].astype(jnp.float32).T.astype(jnp.bfloat16)
        if vt_ref is not None:
            vt_ref[:, span] = r_ref[s, j, 128:192, :]
        if vv_ref is not None:
            vv_ref[span] = r_ref[s, j, 128:192, :].astype(jnp.float32).T.astype(jnp.bfloat16)


def fwd_kernel(
    x_ref, lengths_ref, s_qkv, s_bias, s_vec, s_out, s_expand, s_reduce,
    o_out, o_expand, o_reduce, o_qkv, o_pairs, o_full, lse_ref,
    o_rows, o_scaled, o_spread, o_active, o_slope, o_turned, o_active_t,
    w_qkv, w_bias, w_vec, w_out, w_expand, send_blk, recv_blk, ctx_blk, ctx_recv, kk, vt,
    e_row, x_turned, n_turned, normed, stage, turned, active_t, ctx_sib, active_all, slope_all,
    send_sem, recv_sem, local_sem, hsend, hrecv, csend, crecv, tsend, trecv, wsem, zsend, zrecv, ksem,
):
    f32, bf16 = jnp.float32, jnp.bfloat16
    core, chip = place()
    sib = (1 - core, chip)
    greet([sib] + [(core, flip(chip, b)) for b in range(1, 16)])
    copies = Copies(send_sem, recv_sem)
    line = Line(chip)
    first = [
        Gather(copies, line, 0, s_qkv, w_qkv, local_sem.at[0], zsend, zrecv),
        Gather(copies, line, 1, s_bias, w_bias, local_sem.at[1], zsend, zrecv),
    ]
    rest = [
        Gather(copies, line, 2, s_out, o_out, local_sem.at[2], zsend, zrecv),
        Gather(copies, line, 3, s_vec, w_vec, local_sem.at[3], zsend, zrecv),
        Gather(copies, line, 4, s_expand, o_expand, local_sem.at[4], zsend, zrecv),
        Gather(copies, line, 5, s_reduce, o_reduce, local_sem.at[5], zsend, zrecv),
    ]
    for g in first:
        g.start_z()
        g.start_plane()

    def turn(slot, src, kept):
        c = pltpu.make_async_remote_copy(
            src_ref=src,
            dst_ref=turned.at[slot, 1],
            send_sem=tsend.at[slot],
            recv_sem=trecv.at[slot],
            device_id=sib,
            device_id_type=MESH,
        )
        c.start()
        turned[slot, 0] = kept[...]
        return c

    for i in range(4):
        x_turned[i // 2, 256 * (i % 2) : 256 * (i % 2) + 256] = x_ref[:, 256 * i : 256 * i + 256].astype(f32).T.astype(bf16)
    swaps = [turn(0, x_turned.at[1 - core], x_turned.at[core])]
    for z in (1, 2, 3):
        for g in first:
            g.on_z(z)
    for g in rest[:3]:
        g.start_z()
    for z in range(4):
        for g in first:
            g.on_plane(z)
    for g in rest:
        g.start_plane()
    for z in range(4):
        for g in first:
            g.on_diagonal(z)
    for g in first:
        g.on_sibling()
    keep = pltpu.make_async_copy(w_qkv, o_qkv, local_sem.at[6])
    keep.start()

    for g in rest[:3]:
        g.on_z(1)
    for part in range(3):

        @pl.loop(0, 4)
        def _(p):
            w = w_qkv[:, :, pl.ds(pl.multiple_of(part * 1024 + p * 256, 256), 256)].reshape(1024, 256)
            t = jnp.dot(x_ref[...], w, preferred_element_type=f32).T
            for i in range(4):
                h = 4 * p + i
                rows = t[64 * i : 64 * i + 64]
                if part != 1:
                    own = pl.ds(0 if part == 0 else 32, 32)
                    bias = jnp.concatenate([w_bias[2 * h + k, own] for k in range(2)], 0).astype(f32)
                    rows = rows + jnp.concatenate([bias, bias], 1)
                send_blk[h, pl.ds(64 * part, 64)] = rows.astype(bf16)

    for g in rest[:3]:
        g.on_z(2)
    heads = []
    for s in range(2):
        for b in FULL_ORDER:
            to = flip(chip, b)
            i = s * 16 + b
            c = pltpu.make_async_remote_copy(
                src_ref=send_blk.at[to, :, pl.ds(128 * s, 128)],
                dst_ref=recv_blk.at[s, chip],
                send_sem=hsend.at[i],
                recv_sem=hrecv.at[i],
                device_id=(core, to),
                device_id_type=MESH,
            )
            c.start()
            heads.append(c)
        recv_blk[s, chip] = send_blk[chip, :, pl.ds(128 * s, 128)]

    def heads_here(s):
        for b in FULL_ORDER:
            i = s * 16 + b
            here = recv_blk.at[s, flip(chip, b)]
            pltpu.make_async_remote_copy(
                src_ref=here, dst_ref=here, send_sem=hsend.at[i], recv_sem=hrecv.at[i], device_id=sib, device_id_type=MESH
            ).wait_recv()

    rest[3].start_z()
    events = [lambda: [g.on_plane(0) for g in rest]]
    events.append(lambda: [g.on_z(3) for g in rest[:3]])
    events.append(lambda: [g.on_diagonal(0) for g in rest])
    for z in (1, 2, 3):
        events.append(lambda z=z: [g.on_plane(z) for g in rest[:3]])
    for z in (1, 2, 3):
        events.append(lambda z=z: [rest[3].on_z(z)])
    for z in (1, 2, 3):
        events.append(lambda z=z: [g.on_diagonal(z) for g in rest[:3]])
    READY = len(events)
    for z in (1, 2, 3):
        events.append(lambda z=z: [rest[3].on_plane(z)])
    for z in (1, 2, 3):
        events.append(lambda z=z: [rest[3].on_diagonal(z)])

    def attend_sequence(s, during):
        load_sequence(recv_blk, s, kk, vt_ref=vt)

        @pl.loop(0, 8)
        def _(step):
            for k, event in enumerate(during):

                @pl.when(step == k)
                def _():
                    event()

            q = flip_by(step, chip // 2)
            query = jnp.concatenate([recv_blk[s, 2 * q, 0:64, :], recv_blk[s, 2 * q + 1, 0:64, :]], 1)
            scores = jnp.dot(kk[...], query, preferred_element_type=f32) * (0.125 * LOG2E)
            key = lax.broadcasted_iota(jnp.int32, scores.shape, 0)
            scores = jnp.where(key < lengths_ref[s], scores, masked_score)
            top = jnp.max(scores, 0, keepdims=True)
            e = jnp.exp2(scores - top)
            mass = jnp.sum(e, 0, keepdims=True)
            o = jnp.dot(vt[...], e.astype(bf16), preferred_element_type=f32) / mass
            lse_ref[s, pl.ds(q, 1), :] = top + jnp.log2(mass)
            o_full[s, :, pl.ds(pl.multiple_of(q * 256, 256), 256)] = o
            for i in range(2):
                to = 2 * q + i
                ctx_blk[s, to] = o[:, 128 * i : 128 * i + 128].astype(bf16)

                @pl.when(to != chip)
                def _():
                    pltpu.make_async_remote_copy(
                        src_ref=ctx_blk.at[s, to],
                        dst_ref=ctx_recv.at[chip, :, pl.ds(128 * s, 128)],
                        send_sem=csend.at[s * 16 + to],
                        recv_sem=crecv.at[s * 16 + chip],
                        device_id=(core, to),
                        device_id_type=MESH,
                    ).start()

        ctx_recv[chip, :, pl.ds(128 * s, 128)] = ctx_blk[s, chip]

    PRE, FIRST, SECOND = 3, 4, 4
    for event in events[:PRE]:
        event()
    heads_here(0)
    attend_sequence(0, events[PRE : PRE + FIRST])
    heads_here(1)
    pairs_out = pltpu.make_async_copy(recv_blk, o_pairs, local_sem.at[7])
    pairs_out.start()
    attend_sequence(1, events[PRE + FIRST : PRE + FIRST + SECOND])
    for event in events[PRE + FIRST + SECOND : READY]:
        event()
    for g in rest[:3]:
        g.on_sibling()
    out_weights = pltpu.make_async_copy(o_out, w_out, local_sem.at[6 + 2])
    out_weights.start()

    def fetch(c, slot):
        cols = pl.ds(pl.multiple_of(c * 512, 512), 512)
        return pltpu.make_async_copy(o_expand.at[:, :, cols], w_expand.at[slot], wsem.at[slot])

    fetch(0, 0).start()

    owner = lax.broadcasted_iota(jnp.int32, (32, 1024), 0)
    column = lax.broadcasted_iota(jnp.int32, (32, 1024), 1)
    lane = lax.broadcasted_iota(jnp.int32, (128, 1024), 0)
    pick = jnp.where(lax.rem(lax.broadcasted_iota(jnp.int32, (128, 1024), 1), 32) == lane, 1.0, 0.0).astype(bf16)
    o_rows[...] = jnp.zeros_like(o_rows)
    for r in range(7):
        choose = jnp.where(column == owner * 32 + r, 1.0, 0.0).astype(bf16)
        piece = jnp.dot(choose, w_vec[...].reshape(1024, 128), preferred_element_type=f32)
        if r == 3:
            for o in range(32):
                e_row[o // 4 : o // 4 + 1, 128 * (o % 4) : 128 * (o % 4) + 128] = piece[o : o + 1]
        else:
            spread_row = jnp.dot(piece.astype(bf16), pick, preferred_element_type=f32)
            o_rows[r : r + 1] = jnp.sum(jnp.where(lax.div(column, 32) == owner, spread_row, 0.0), 0, keepdims=True)

    for s in range(2):
        for b in range(1, 16):
            other = flip(chip, b)
            here = ctx_recv.at[other, :, pl.ds(128 * s, 128)]
            pltpu.make_async_remote_copy(
                src_ref=ctx_blk.at[s, other],
                dst_ref=here,
                send_sem=csend.at[s * 16 + other],
                recv_sem=crecv.at[s * 16 + other],
                device_id=sib,
                device_id_type=MESH,
            ).wait()
    mine, others = pl.ds(core * 8, 8), pl.ds((1 - core) * 8, 8)
    swaps.append(
        pltpu.make_async_remote_copy(
            src_ref=ctx_recv.at[others],
            dst_ref=ctx_sib,
            send_sem=tsend.at[2],
            recv_sem=trecv.at[2],
            device_id=sib,
            device_id_type=MESH,
        )
    )
    swaps[-1].start()
    turned[2, 0] = ctx_recv[mine].reshape(512, 256)
    out_weights.wait()
    for i in range(4):
        rows = ctx_recv[4 * i : 4 * i + 4].reshape(256, 256).astype(f32).T.astype(bf16)
        term = jnp.dot(rows, w_out[8 * i : 8 * i + 8].reshape(256, 1024), preferred_element_type=f32)
        if i == 0:
            o_scaled[...] = term + (x_ref[...].astype(f32) + o_rows[0:1])
        else:
            o_scaled[...] += term

    @pl.loop(0, 4)
    def _(i):
        span = pl.ds(pl.multiple_of(i * 64, 64), 64)
        residual = o_scaled[span]
        center = residual - jnp.mean(residual, -1, keepdims=True)
        spread = lax.rsqrt(jnp.mean(center * center, -1, keepdims=True) + epsilon)
        x_hat = center * spread
        o_scaled[span] = x_hat
        o_spread[span] = jnp.broadcast_to(spread, (64, 128))
        normed[span] = (x_hat * o_rows[1:2] + o_rows[2:3]).astype(bf16)

    for i in range(4):
        n_turned[i // 2, 256 * (i % 2) : 256 * (i % 2) + 256] = normed[:, 256 * i : 256 * i + 256].astype(f32).T.astype(bf16)
    swaps.append(turn(1, n_turned.at[1 - core], n_turned.at[core]))

    def active_copy(j):
        return pltpu.make_async_remote_copy(
            src_ref=stage.at[j],
            dst_ref=active_t.at[1, j],
            send_sem=tsend.at[3 + j],
            recv_sem=trecv.at[3 + j],
            device_id=sib,
            device_id_type=MESH,
        )

    def keep_chunk(c):
        return (
            pltpu.make_async_copy(active_all.at[c], o_active.at[c], ksem.at[0, c]),
            pltpu.make_async_copy(slope_all.at[c], o_slope.at[c], ksem.at[1, c]),
        )

    last_events = events[READY:]

    @pl.loop(0, 8)
    def _(c):
        for k, event in enumerate(last_events[:8]):

            @pl.when(c == k)
            def _():
                event()

        slot = lax.rem(c, 2)

        @pl.when(c < 7)
        def _():
            fetch(c + 1, 1 - slot).start()

        fetch(c, slot).wait()
        expanded = jnp.dot(normed[...], w_expand[slot].reshape(1024, 512), preferred_element_type=f32) + e_row[pl.ds(c, 1)]
        share = 0.5 * (1.0 + lax.erf(expanded * math.sqrt(0.5)))
        bell = jnp.exp(-0.5 * expanded * expanded) * (1.0 / math.sqrt(2.0 * math.pi))
        slope_all[c] = (share + expanded * bell).astype(bf16)
        active = (expanded * share).astype(bf16)
        active_all[c] = active
        for copy in keep_chunk(c):
            copy.start()
        across = active.astype(f32).T.astype(bf16)
        j = lax.rem(c, 4)

        @pl.when(lax.div(c, 4) == core)
        def _():
            active_t[0, j] = across

        @pl.when(lax.div(c, 4) != core)
        def _():
            stage[j] = across
            active_copy(j).start()

    for event in last_events[8:]:
        event()
    for c in swaps:
        c.wait()
    turned[2, 1] = ctx_sib[...].reshape(512, 256)
    for j in range(4):
        active_copy(j).wait()
    kept = [
        pltpu.make_async_copy(turned, o_turned, local_sem.at[0]),
        pltpu.make_async_copy(active_t, o_active_t, local_sem.at[1]),
    ]
    for c in kept:
        c.start()
    rest[3].on_sibling()
    for c in range(8):
        for copy in keep_chunk(c):
            copy.wait()
    for c in kept:
        c.wait()
    for c in heads:
        c.wait_send()
    copies.drain(sib)
    for g in first + rest:
        g.drain()
    keep.wait()
    pairs_out.wait()


def flip_by(v, w):
    out = 0
    for b in (1, 2, 4):
        p, q = lax.rem(lax.div(v, b), 2), lax.rem(lax.div(w, b), 2)
        out = out + b * (p + q - 2 * p * q)
    return out


def forward_attention(rows, lengths, qkv, bias, vec, w_out, w_expand, w_reduce, collective_id):
    v, hbm = pl.BlockSpec(memory_space=pltpu.VMEM), pl.BlockSpec(memory_space=pl.ANY)
    f32, bf16 = jnp.float32, jnp.bfloat16
    gathered = lambda x: jax.ShapeDtypeStruct((32,) + x.shape, x.dtype)
    dma = pltpu.SemaphoreType.DMA
    array = jax.ShapeDtypeStruct
    vmem = lambda shape, dtype=bf16: pltpu.VMEM(shape, dtype)
    return pl.pallas_call(
        fwd_kernel,
        out_shape=[
            gathered(w_out),
            gathered(w_expand),
            gathered(w_reduce),
            gathered(qkv),
            array((2, 16, 192, 128), bf16),
            array((2, 64, 2048), f32),
            array((2, 8, 256), f32),
            array((8, 1024), f32),
            array((256, 1024), f32),
            array((256, 128), f32),
            array((8, 256, 512), bf16),
            array((8, 256, 512), bf16),
            array((3, 2, 512, 256), bf16),
            array((2, 4, 512, 256), bf16),
        ],
        in_specs=[v, pl.BlockSpec(memory_space=pltpu.SMEM)] + [hbm] * 6,
        out_specs=[hbm] * 5 + [v] * 5 + [hbm] * 4,
        scratch_shapes=[
            vmem((32,) + qkv.shape),
            vmem((32,) + bias.shape),
            vmem((32,) + vec.shape),
            vmem((32,) + w_out.shape),
            vmem((2, 32, 32, 512)),
            vmem((16, 192, 256)),
            vmem((2, 16, 192, 128)),
            vmem((2, 16, 64, 128)),
            vmem((16, 64, 256)),
            vmem((2048, 64)),
            vmem((64, 2048)),
            vmem((8, 512), f32),
            vmem((2, 512, 256)),
            vmem((2, 512, 256)),
            vmem((256, 1024)),
            vmem((4, 512, 256)),
            vmem((3, 2, 512, 256)),
            vmem((2, 4, 512, 256)),
            vmem((8, 64, 256)),
            vmem((8, 256, 512)),
            vmem((8, 256, 512)),
            dma((210,)),
            dma((210,)),
            dma((9,)),
            dma((32,)),
            dma((32,)),
            dma((32,)),
            dma((32,)),
            dma((7,)),
            dma((7,)),
            dma((2,)),
            dma((36,)),
            dma((24,)),
            dma((2, 8)),
        ],
        compiler_params=pltpu.CompilerParams(
            collective_id=collective_id, has_side_effects=True, vmem_limit_bytes=60 * MIB
        ),
        name="forward_attention",
    )(rows, lengths, qkv, bias, vec, w_out, w_expand, w_reduce)


class Scatter:
    ORDER = (12, 8, 4, 0)

    def __init__(self, copies, name, grads, out, bufs):
        self.copies, self.name, self.grads, self.out = copies, name, grads, out
        self.first, self.second, self.third = bufs
        self.core, self.chip = place()
        self.rows = grads.shape[1]
        self.half = self.rows // 2
        self.lo, self.hi = pl.ds(0, self.half), pl.ds(self.half, self.half)
        self.first_at = [[self.first.at[k, i] for i in range(2)] for k in range(4)]
        self.second_at = [[self.second.at[k, i] for i in range(2)] for k in range(4)]
        self.third_at = [self.third.at[k] for k in range(3)]

    def at(self, bits):
        return (self.core, flip(self.chip, bits))

    def send(self, tag, src, dst, bits, half=True):
        like = self.first_at[0][0] if half else self.third_at[0]
        self.copies.send((self.name, tag), src, dst, self.at(bits), like)

    def arrived(self, tag, dst):
        self.copies.arrived((self.name, tag), dst, self.at(1))

    def add(self, rows, fn):
        step = min(rows, 16)
        if rows == step:
            fn(0, step)
            return

        def turn(i, carry):
            fn(pl.multiple_of(i * step, step), step)
            return carry

        lax.fori_loop(0, rows // step, turn, 0)

    def start(self):
        for k, z in enumerate(self.ORDER):
            diag = flip(self.chip, z + 3)
            self.send(("1a", k), self.grads.at[diag, self.lo], self.first_at[k][0], 2)
            self.send(("1b", k), self.grads.at[diag, self.hi], self.first_at[k][1], 1)

    def start_direct(self):
        for k, z in enumerate(self.ORDER):
            xb, yb = flip(self.chip, z + 1), flip(self.chip, z + 2)
            self.send(("2xh", k), self.grads.at[xb, self.hi], self.second_at[k][0].at[self.hi], 1)
            self.send(("2yl", k), self.grads.at[yb, self.lo], self.second_at[k][1].at[self.lo], 2)

    def on_first(self, k):
        z = self.ORDER[k]
        for i, (tag, bit, upper) in enumerate((("1a", 1, False), ("1b", 2, True))):
            owner = flip(self.chip, z + bit)
            here = self.first_at[k][i]
            self.arrived((tag, k), here)

            def fn(start, size):
                rows = pl.ds(start, size)
                theirs = pl.ds(start + (self.half if upper else 0), size)
                here[rows] = here[rows] + self.grads.at[owner][theirs]

            self.add(self.half, fn)
            self.send(("2" + "xy"[i] + "lh"[i], k), here, self.second_at[k][i].at[self.hi if upper else self.lo], bit)

    def on_second(self, k):
        z = self.ORDER[k]
        self.arrived(("2xh", k), self.second_at[k][0].at[self.hi])
        self.arrived(("2yl", k), self.second_at[k][1].at[self.lo])
        self.arrived(("2xl", k), self.second_at[k][0].at[self.lo])
        self.arrived(("2yh", k), self.second_at[k][1].at[self.hi])
        owner = flip(self.chip, z)

        def fn(start, size):
            rows = pl.ds(start, size)
            f32 = jnp.float32
            total = self.grads.at[owner][rows].astype(f32) + self.second_at[k][0][rows].astype(f32)
            total = total + self.second_at[k][1][rows].astype(f32)
            if k < 3:
                self.second_at[k][0][rows] = total.astype(self.second.dtype)
            else:
                self.out[rows] = total

        self.add(self.rows, fn)
        if k < 3:
            self.send(("3", k), self.second_at[k][0], self.third_at[k], z, False)

    def on_third(self):
        for k in range(3):
            self.arrived(("3", k), self.third_at[k])

        def fn(start, size):
            rows = pl.ds(start, size)
            total = self.out[rows]
            for k in range(3):
                total = total + self.third_at[k][rows].astype(jnp.float32)
            self.out[rows] = total

        self.add(self.rows, fn)


def scatter_buffers(block, dtype):
    rows, cols = block
    return [
        pltpu.VMEM((4, 2, rows // 2, cols), dtype),
        pltpu.VMEM((4, 2, rows, cols), dtype),
        pltpu.VMEM((3, rows, cols), dtype),
    ]


def bwd_kernel(*refs):
    f32, bf16 = jnp.float32, jnp.bfloat16
    (
        lengths_ref, h_pairs, h_full, lse_ref, h_rows, h_active_t, cotangent, scaled, spread, vectors,
        h_active, h_slope, h_reduce, h_expand, h_out, h_qkv,
    ) = refs[:16]
    (o_layer, o_reduce, o_expand, o_out, o_vec, o_qkv, o_input, o_bias) = refs[16:24]
    bufs = [refs[24 + 3 * i : 27 + 3 * i] for i in range(5)]
    (
        g_reduce, g_expand, g_out, g_vec, g_qkv, w_qkv, d_recv, kk, vv, kt, acc, d_send, d_own, d_sib, b_own, b_sib, b_in,
        slopes, w_reduce, w_expand, w_out, e_own, e_sib, d_first, a_own, a_sib, d_ctx, rows_sum, e_sum, vec_own, vec_sib, r_own, r_sib, pairs, o_full, rows_t, active_t,
        send_sem, recv_sem, local_sem, dsend, drecv, qsend, qrecv, esend, erecv, wsem, lsem,
    ) = refs[39:]
    core, chip = place()
    sib = (1 - core, chip)
    greet([sib] + [(core, flip(chip, b)) for b in range(1, 16)])
    copies = Copies(send_sem, recv_sem)
    rest = [
        Scatter(copies, i, g, o, bufs[i])
        for i, (g, o) in enumerate(((g_reduce, o_reduce), (g_expand, o_expand), (g_out, o_out), (g_vec, o_vec)))
    ]
    last = Scatter(copies, 4, g_qkv, o_qkv, bufs[4])
    out_weights = pltpu.make_async_copy(h_out, w_out, local_sem.at[4])
    out_weights.start()

    def fetch(c, slot, back):
        cols = pl.ds(pl.multiple_of(c * 512, 512), 512)
        copies_in = [
            pltpu.make_async_copy(h_reduce.at[pl.ds(c * 4, 4)], w_reduce.at[slot], wsem.at[slot, 0]),
            pltpu.make_async_copy((h_slope if back else h_active).at[c], slopes.at[slot], wsem.at[slot, 2]),
        ]
        if back:
            copies_in.append(pltpu.make_async_copy(h_expand.at[:, :, cols], w_expand.at[slot], wsem.at[slot, 1]))
        return copies_in

    for c in fetch(0, 0, False):
        c.start()
    loads = [
        pltpu.make_async_copy(src, dst, lsem.at[i])
        for i, (src, dst) in enumerate(((h_active_t, active_t), (h_rows, rows_t), (h_pairs, pairs), (h_full, o_full)))
    ]
    for c in loads:
        c.start()
    d_first[...] = scaled[...] * vectors[1:2] + (vectors[2:3] + vectors[4:5])

    @pl.loop(0, 8)
    def _(c):
        slot = lax.rem(c, 2)

        @pl.when(c < 7)
        def _():
            for copy in fetch(c + 1, 1 - slot, False):
                copy.start()

        @pl.when(c == 7)
        def _():
            for copy in fetch(0, 0, True):
                copy.start()

        for copy in fetch(c, slot, False):
            copy.wait()
        d_first[...] += jnp.dot(slopes[slot], w_reduce[slot].reshape(512, 1024), preferred_element_type=f32)

    rows_sum[...] = jnp.zeros_like(rows_sum)

    @pl.loop(0, 4)
    def _(i):
        span = pl.ds(pl.multiple_of(i * 64, 64), 64)
        total = d_first[span]
        center = total - jnp.mean(total, -1, keepdims=True)
        width = lax.rsqrt(jnp.mean(center * center, -1, keepdims=True) + epsilon)
        x_hat = center * width
        row = chip * 128 + lax.rem(i, 2) * 64 + lax.broadcasted_iota(jnp.int32, (64, 1024), 0)
        valid = row < lengths_ref[lax.div(i, 2)]
        o_layer[span] = jnp.where(valid, x_hat * vectors[5:6] + vectors[6:7], 0.0).astype(bf16)
        d_output = jnp.where(valid, cotangent[span].astype(f32), 0.0)
        pulled = d_output * vectors[5:6]
        level = jnp.mean(pulled, -1, keepdims=True)
        slope = jnp.mean(pulled * x_hat, -1, keepdims=True)
        d_rows = width * (pulled - level - x_hat * slope)
        d_low = d_rows.astype(bf16)
        d_first[span] = d_rows
        r_own[span] = d_low
        rows_sum[4:5] += jnp.sum(d_low.astype(f32), 0, keepdims=True)
        rows_sum[5:6] += jnp.sum(d_output * x_hat, 0, keepdims=True)
        rows_sum[6:7] += jnp.sum(d_output, 0, keepdims=True)

    copies.send("r", r_own, r_sib, sib, r_own)
    copies.arrived("r", r_sib, sib)
    for c in loads:
        c.wait()

    @pl.loop(0, 4)
    def _(j):
        g = jnp.dot(active_t[0, j], r_own[...], preferred_element_type=f32)
        g = g + jnp.dot(active_t[1, j], r_sib[...], preferred_element_type=f32)
        g_reduce[pl.ds(j * 4, 4)] = g.astype(bf16).reshape(4, 128, 1024)

    rest[0].start()
    rest[0].start_direct()

    def e_copy(c):
        return pltpu.make_async_remote_copy(
            src_ref=e_own.at[c],
            dst_ref=e_sib.at[c],
            send_sem=esend.at[c],
            recv_sem=erecv.at[c],
            device_id=sib,
            device_id_type=MESH,
        )

    @pl.loop(0, 8)
    def _(c):
        slot = lax.rem(c, 2)

        @pl.when(c < 7)
        def _():
            for copy in fetch(c + 1, 1 - slot, True):
                copy.start()

        for copy in fetch(c, slot, True):
            copy.wait()
        d_active = nt(r_own[...], w_reduce[slot].reshape(512, 1024))
        d_expanded = (d_active * slopes[slot].astype(f32)).astype(bf16)
        e_own[c] = d_expanded
        e_copy(c).start()
        e_sum[pl.ds(c, 1)] = jnp.sum(d_expanded.astype(f32), 0, keepdims=True)
        d_first[...] += nt(d_expanded, w_expand[slot].reshape(1024, 512))

    @pl.loop(0, 4)
    def _(i):
        span = pl.ds(pl.multiple_of(i * 64, 64), 64)
        d_normed, x_hat = d_first[span], scaled[span]
        pulled = d_normed * vectors[1:2]
        level = jnp.mean(pulled, -1, keepdims=True)
        slope = jnp.mean(pulled * x_hat, -1, keepdims=True)
        d_rows = spread[span, 0:1] * (pulled - level - x_hat * slope)
        d_low = d_rows.astype(bf16)
        d_first[span] = d_rows
        a_own[span] = d_low
        rows_sum[0:1] += jnp.sum(d_low.astype(f32), 0, keepdims=True)
        rows_sum[1:2] += jnp.sum(d_normed * x_hat, 0, keepdims=True)
        rows_sum[2:3] += jnp.sum(d_normed, 0, keepdims=True)

    for k in range(4):
        rest[0].on_first(k)
    out_weights.wait()

    @pl.loop(0, 4)
    def _(i):
        t = nt(w_out[pl.ds(i * 8, 8)].reshape(256, 1024), a_own[...])
        d_ctx[pl.ds(i * 4, 4)] = t.astype(bf16).reshape(4, 64, 256)

    sent = []

    def exchange_out(s, b, src, dst, sends, recvs):
        c = pltpu.make_async_remote_copy(
            src_ref=src,
            dst_ref=dst,
            send_sem=sends.at[s * 16 + b],
            recv_sem=recvs.at[s * 16 + b],
            device_id=(core, flip(chip, b)),
            device_id_type=MESH,
        )
        c.start()
        sent.append(c)

    def exchange_in(s, b, here, sends, recvs):
        pltpu.make_async_remote_copy(
            src_ref=here,
            dst_ref=here,
            send_sem=sends.at[s * 16 + b],
            recv_sem=recvs.at[s * 16 + b],
            device_id=sib,
            device_id_type=MESH,
        ).wait_recv()

    for s in range(2):
        lane = pl.ds(128 * s, 128)
        for b in FULL_ORDER:
            exchange_out(s, b, d_ctx.at[flip(chip, b), :, lane], d_recv.at[s, chip], dsend, drecv)
        d_recv[s, chip] = d_ctx[chip, :, lane]
    copies.send("a", a_own, a_sib, sib, a_own)

    vec_own[...] = jnp.zeros_like(vec_own)
    owner = lax.broadcasted_iota(jnp.int32, (32, 1024), 0)
    column = lax.broadcasted_iota(jnp.int32, (32, 1024), 1)
    place_in = lax.rem(lax.broadcasted_iota(jnp.int32, (1024, 128), 0), 32)
    pick = jnp.where(place_in == lax.broadcasted_iota(jnp.int32, (1024, 128), 1), 1.0, 0.0).astype(bf16)
    for r in (0, 1, 2, 4, 5, 6):
        spread_row = jnp.where(lax.div(column, 32) == owner, rows_sum[r : r + 1], 0.0)
        top = spread_row.astype(bf16)
        low = (spread_row - top.astype(f32)).astype(bf16)
        vec_own[:, r, :] = jnp.dot(top, pick, preferred_element_type=f32) + jnp.dot(low, pick, preferred_element_type=f32)
    for o in range(32):
        vec_own[o, 3:4, :] = e_sum[o // 4 : o // 4 + 1, 128 * (o % 4) : 128 * (o % 4) + 128]
    own_half, other_half = pl.ds(core * 16, 16), pl.ds((1 - core) * 16, 16)
    copies.send("v", vec_own.at[other_half], vec_sib, sib, vec_sib)


    @pl.loop(0, 8)
    def _(c):
        e_copy(c).wait()
        g = jnp.dot(rows_t[1, 0], e_own[c], preferred_element_type=f32)
        g = g + jnp.dot(rows_t[1, 1], e_sib[c], preferred_element_type=f32)
        g_expand[:, :, pl.ds(pl.multiple_of(c * 512, 512), 512)] = g.astype(bf16).reshape(16, 32, 512)

    rest[1].start()
    rest[1].start_direct()
    copies.arrived("a", a_sib, sib)
    for i in range(4):
        cols = slice(256 * i, 256 * i + 256)
        g = jnp.dot(rows_t[2, 0], a_own[:, cols], preferred_element_type=f32)
        g = g + jnp.dot(rows_t[2, 1], a_sib[:, cols], preferred_element_type=f32)
        g_out[:, :, cols] = g.astype(bf16).reshape(16, 32, 256)
    copies.arrived("v", vec_sib, sib)
    g_vec[...] = vec_own[own_half] + vec_sib[...]
    for r in rest[2:]:
        r.start()
        r.start_direct()
    b_own[...] = jnp.zeros_like(b_own)

    def fetch_qkv(i, slot):
        return pltpu.make_async_copy(h_qkv.at[pl.ds(i * 8, 8)], w_qkv.at[slot], local_sem.at[5 + slot])

    fetch_qkv(0, 0).start()
    fetch_qkv(1, 1).start()

    def back_sequence(s, during):
        load_sequence(pairs, s, kk, vt_ref=None, vv_ref=vv)
        for j in range(16):
            kt[:, pl.ds(j * 128, 128)] = pairs[s, j, 64:128, :]
        acc[...] = jnp.zeros_like(acc)

        @pl.loop(0, 8)
        def _(q):
            for k, event in enumerate(during):

                @pl.when(q == k)
                def _():
                    event()

            both = lambda ref, lo, hi: jnp.concatenate([ref[s, 2 * q, lo:hi, :], ref[s, 2 * q + 1, lo:hi, :]], 1)
            query, d_out = both(pairs, 0, 64), both(d_recv, 0, 64)
            span = pl.ds(pl.multiple_of(q * 256, 256), 256)
            delta = jnp.sum(d_out.astype(f32) * o_full[s, :, span], 0, keepdims=True)
            scores = jnp.dot(kk[...], query, preferred_element_type=f32) * (0.125 * LOG2E)
            key = lax.broadcasted_iota(jnp.int32, scores.shape, 0)
            probs = jnp.where(key < lengths_ref[s], jnp.exp2(scores - lse_ref[s, pl.ds(q, 1), :]), 0.0)
            d_probs = jnp.dot(vv[...], d_out, preferred_element_type=f32)
            d_scores = (probs * (d_probs - delta)).astype(bf16)
            zero = jnp.zeros((64, 256), f32)
            query_rows = jnp.concatenate([query.astype(f32), zero], 0).T.astype(bf16)
            d_rows = jnp.concatenate([zero, d_out.astype(f32)], 0).T.astype(bf16)
            acc[...] += jnp.dot(d_scores, query_rows, preferred_element_type=f32) + jnp.dot(
                probs.astype(bf16), d_rows, preferred_element_type=f32
            )
            d_query = (jnp.dot(kt[...], d_scores, preferred_element_type=f32) * 0.125).astype(bf16)
            for i in range(2):
                part = d_query[:, 128 * i : 128 * i + 128]
                d_send[s, 2 * q + i, 0:64, :] = part
                b_own[0] += part.astype(f32)

        for j in range(16):
            t = acc[pl.ds(j * 128, 128)].T
            d_send[s, j, 64:128, :] = (t[:64] * 0.125).astype(bf16)
            value = t[64:].astype(bf16)
            d_send[s, j, 128:192, :] = value
            b_own[1] += value.astype(f32)
        lane = pl.ds(128 * s, 128)
        for b in FULL_ORDER:
            exchange_out(s, b, d_send.at[s, flip(chip, b)], d_own.at[chip, :, lane], qsend, qrecv)
        d_own[chip, :, lane] = d_send[s, chip]

    for k in range(4):
        rest[0].on_second(k)
    events = [lambda k=k: [r.on_first(k) for r in rest[1:]] for k in range(4)]
    events += [lambda k=k: [r.on_second(k) for r in rest[1:]] for k in range(4)]
    FIRST, SECOND, WAIT = 0, 0, 5
    for b in FULL_ORDER:
        exchange_in(0, b, d_recv.at[0, flip(chip, b)], dsend, drecv)
    back_sequence(0, events[:FIRST])
    for b in FULL_ORDER:
        exchange_in(1, b, d_recv.at[1, flip(chip, b)], dsend, drecv)
    back_sequence(1, events[FIRST : FIRST + SECOND])

    copies.send("bias sib", b_own, b_sib, sib, b_own)
    for event in events[FIRST + SECOND : FIRST + SECOND + WAIT]:
        event()
    for s in range(2):
        lane = pl.ds(128 * s, 128)
        for b in FULL_ORDER:
            exchange_in(s, b, d_own.at[flip(chip, b), :, lane], qsend, qrecv)
        copies.send(("rows", s), d_own.at[:, :, lane], d_sib.at[:, :, lane], sib, d_own.at[:, :, lane])

    copies.arrived("bias sib", b_sib, sib)
    for s in range(2):
        copies.arrived(("rows", s), d_sib.at[:, :, pl.ds(128 * s, 128)], sib)

    for part in range(3):

        @pl.loop(0, 4)
        def _(p):
            total = None
            for i, rows in enumerate((d_own, d_sib)):
                right = rows[pl.ds(4 * p, 4), pl.ds(64 * part, 64)].reshape(256, 256)
                term = nt(rows_t[0, i], right)
                total = term if total is None else total + term
            cols = pl.ds(pl.multiple_of(part * 1024 + p * 256, 256), 256)
            g_qkv[:, :, cols] = total.astype(bf16).reshape(16, 32, 256)

    last.start()
    last.start_direct()

    b_sib[...] = b_sib[...] + b_own[...]
    sender = core == lax.div(chip, 8)
    for i in range(2):
        to = lax.rem(2 * chip + i, 16)
        rows = pl.ds(32 * i, 32)
        c = pltpu.make_async_remote_copy(
            src_ref=b_sib.at[:, rows],
            dst_ref=b_in,
            send_sem=local_sem.at[1 + i],
            recv_sem=local_sem.at[3],
            device_id=(core, to),
            device_id_type=MESH,
        )

        @pl.when(sender & (to != chip))
        def _():
            c.start()

        @pl.when(sender & (to == chip))
        def _():
            b_in[...] = b_sib[:, rows]

    for event in events[FIRST + SECOND + WAIT :]:
        event()
    for i in range(4):
        fetch_qkv(i, i % 2).wait()
        t = None
        for part in range(3):
            w = w_qkv[i % 2, :, :, 1024 * part : 1024 * part + 1024].reshape(256, 1024)
            term = jnp.dot(w, d_own[:, 64 * part : 64 * part + 64].reshape(1024, 256), preferred_element_type=f32)
            t = term if t is None else t + term
        if i < 2:
            fetch_qkv(i + 2, i).start()
        cols = slice(256 * i, 256 * i + 256)
        o_input[:, cols] = d_first[:, cols] + t.T

    for k in range(4):
        last.on_first(k)
    for r in rest:
        r.on_third()
    for k in range(4):
        last.on_second(k)
    last.on_third()
    for i in range(2):
        to = lax.rem(2 * chip + i, 16)

        @pl.when(sender & (to != chip))
        def _():
            pltpu.make_async_remote_copy(
                src_ref=b_sib.at[:, pl.ds(32 * i, 32)],
                dst_ref=b_in,
                send_sem=local_sem.at[1 + i],
                recv_sem=local_sem.at[3],
                device_id=(core, to),
                device_id_type=MESH,
            ).wait_send()

    @pl.when(8 * core + lax.div(chip, 2) != chip)
    def _():
        pltpu.make_async_remote_copy(
            src_ref=b_in, dst_ref=b_in, send_sem=local_sem.at[1], recv_sem=local_sem.at[3], device_id=sib, device_id_type=MESH
        ).wait_recv()

    o_bias[...] = b_in[...]
    for c in sent:
        c.wait_send()
    copies.drain(sib)


def backward_attention(
    lengths, pairs, o_full, lse, rows_t, active_t, cotangent, scaled, spread, vectors,
    active, slope, w_reduce, w_expand, w_out, w_qkv, collective_id,
):
    v, hbm = pl.BlockSpec(memory_space=pltpu.VMEM), pl.BlockSpec(memory_space=pl.ANY)
    f32, bf16 = jnp.float32, jnp.bfloat16
    dma = pltpu.SemaphoreType.DMA
    blocks = [((128, 1024), bf16), ((32, 4096), bf16), ((32, 1024), bf16), ((16, 128), f32), ((32, 3072), bf16)]
    bufs = []
    for block, dtype in blocks:
        bufs += scatter_buffers(block, dtype)
    vmem = lambda shape, dtype=bf16: pltpu.VMEM(shape, dtype)
    return pl.pallas_call(
        bwd_kernel,
        out_shape=[jax.ShapeDtypeStruct((256, 1024), bf16)]
        + [jax.ShapeDtypeStruct(block, f32) for block, _ in blocks]
        + [jax.ShapeDtypeStruct((256, 1024), f32), jax.ShapeDtypeStruct((2, 32, 128), f32)],
        in_specs=[pl.BlockSpec(memory_space=pltpu.SMEM), hbm, hbm, v, hbm, hbm] + [v] * 4 + [hbm] * 6,
        out_specs=[v] * 8,
        scratch_shapes=bufs
        + [
            vmem((16, 128, 1024)),
            vmem((16, 32, 4096)),
            vmem((16, 32, 1024)),
            vmem((16, 16, 128), f32),
            vmem((16, 32, 3072)),
            vmem((2, 8, 32, 3072)),
            vmem((2, 16, 64, 128)),
            vmem((2048, 64)),
            vmem((2048, 64)),
            vmem((64, 2048)),
            vmem((2048, 128), f32),
            vmem((2, 16, 192, 128)),
            vmem((16, 192, 256)),
            vmem((16, 192, 256)),
            vmem((2, 64, 128), f32),
            vmem((2, 64, 128), f32),
            vmem((2, 32, 128), f32),
            vmem((2, 256, 512)),
            vmem((2, 4, 128, 1024)),
            vmem((2, 32, 32, 512)),
            vmem((32, 32, 1024)),
            vmem((8, 256, 512)),
            vmem((8, 256, 512)),
            vmem((256, 1024), f32),
            vmem((256, 1024)),
            vmem((256, 1024)),
            vmem((16, 64, 256)),
            vmem((8, 1024), f32),
            vmem((8, 512), f32),
            vmem((32, 16, 128), f32),
            vmem((16, 16, 128), f32),
            vmem((256, 1024)),
            vmem((256, 1024)),
            vmem((2, 16, 192, 128)),
            vmem((2, 64, 2048), f32),
            vmem((3, 2, 512, 256)),
            vmem((2, 4, 512, 256)),
            dma((144,)),
            dma((144,)),
            dma((7,)),
            dma((32,)),
            dma((32,)),
            dma((32,)),
            dma((32,)),
            dma((8,)),
            dma((8,)),
            dma((2, 3)),
            dma((4,)),
        ],
        compiler_params=pltpu.CompilerParams(
            collective_id=collective_id, has_side_effects=True, vmem_limit_bytes=63 * MIB
        ),
        name="backward_attention",
    )(
        lengths, pairs, o_full, lse, rows_t, active_t, cotangent, scaled, spread, vectors,
        active, slope, w_reduce, w_expand, w_out, w_qkv,
    )


def fast_shards(
    inputs,
    lengths,
    w_query,
    b_query,
    w_key,
    w_value,
    b_value,
    w_out,
    b_out,
    first_gain,
    first_shift,
    w_expand,
    b_expand,
    w_reduce,
    b_reduce,
    second_gain,
    second_shift,
    cotangent,
):
    f32, bf16 = jnp.float32, jnp.bfloat16
    seqs, count, width = inputs.shape
    total = seqs * count
    part = width // 32
    ff = w_expand.shape[1]
    qkv = jnp.concatenate([w_query, w_key, w_value], 1)
    bias = jnp.concatenate([b_query, b_value])[:, None] + jnp.zeros((2 * part, 128), bf16)
    small = [b_out, first_gain, first_shift, b_expand, b_reduce, second_gain, second_shift]
    vec = sum(jnp.pad(b[None, :], ((r, part - 1 - r), (0, 128 - b.shape[0]))) for r, b in enumerate(small))
    flat_rows = inputs.reshape(total, width)
    (
        g_out, g_expand, g_reduce, g_qkv, pairs, o_full, lse, vectors, scaled, spread, active, slope, rows_t, active_t,
    ) = forward_attention(flat_rows, lengths, qkv, bias, vec, w_out, w_expand, w_reduce, 1)
    layer_out, s_reduce, s_expand, s_out, s_vec, s_qkv, input_grad, s_bias = backward_attention(
        lengths, pairs, o_full, lse, rows_t, active_t, cotangent.reshape(total, width), scaled, spread, vectors,
        active, slope, g_reduce, g_expand, g_out, g_qkv, 2,
    )
    s_query, s_key, s_value = (s_qkv[:, width * i : width * (i + 1)] for i in range(3))
    s_bias = jnp.sum(s_bias, -1)
    v = [s_vec[r, : b.shape[0]] for r, b in enumerate(small)]
    return (
        layer_out.reshape(inputs.shape),
        input_grad.reshape(inputs.shape),
        s_query,
        s_bias[0],
        s_key,
        s_value,
        s_bias[1],
        s_out,
        v[0],
        v[1],
        v[2],
        s_expand,
        v[3],
        s_reduce,
        v[4],
        v[5],
        v[6],
    )


def solution(mesh):
    fast = mesh.shape["fsdp"] == 2 and mesh.shape["ctx"] == HEADS
    shards = fast_shards if fast else general_shards
    return jax.shard_map(
        shards,
        mesh=mesh,
        in_specs=(
            P("fsdp", "ctx", None),
            P("fsdp"),
            P(("fsdp", "ctx"), None),
            P(("fsdp", "ctx")),
            P(("fsdp", "ctx"), None),
            P(("fsdp", "ctx"), None),
            P(("fsdp", "ctx")),
            P(("fsdp", "ctx"), None),
            P(("fsdp", "ctx")),
            P(("fsdp", "ctx")),
            P(("fsdp", "ctx")),
            P(("fsdp", "ctx"), None),
            P(("fsdp", "ctx")),
            P(("fsdp", "ctx"), None),
            P(("fsdp", "ctx")),
            P(("fsdp", "ctx")),
            P(("fsdp", "ctx")),
            P("fsdp", "ctx", None),
        ),
        out_specs=(
            P("fsdp", "ctx", None),
            P("fsdp", "ctx", None),
            P(("fsdp", "ctx"), None),
            P(("fsdp", "ctx")),
            P(("fsdp", "ctx"), None),
            P(("fsdp", "ctx"), None),
            P(("fsdp", "ctx")),
            P(("fsdp", "ctx"), None),
            P(("fsdp", "ctx")),
            P(("fsdp", "ctx")),
            P(("fsdp", "ctx")),
            P(("fsdp", "ctx"), None),
            P(("fsdp", "ctx")),
            P(("fsdp", "ctx"), None),
            P(("fsdp", "ctx")),
            P(("fsdp", "ctx")),
            P(("fsdp", "ctx")),
        ),
        check_vma=False,
    )
```

```python
from functools import partial
import math

import jax
import jax.numpy as jnp
from jax import lax
from jax.experimental import pallas as pl
from jax.experimental.pallas import tpu as pltpu
from jax.sharding import PartitionSpec as P

HEADS = 16


epsilon = 1e-05
masked_score = -1e30


def layer_norm(rows_in, gain, shift):
    center = rows_in - jnp.mean(rows_in, -1, keepdims=True)
    spread = jnp.mean(center * center, -1, keepdims=True)
    return center * lax.rsqrt(spread + epsilon) * gain + shift


def product(left, right):
    return jnp.dot(left, right, preferred_element_type=jnp.float32)


def outer_sum(left, right):
    return jnp.einsum("rd,re->de", left, right, preferred_element_type=jnp.float32)


def back_product(grad_rows, weight):
    return jnp.einsum("re,de->rd", grad_rows, weight, preferred_element_type=jnp.float32)


def over_blocks(step_fn, carry_state, pair_rows):
    key_count = pair_rows.shape[1]
    block_width = math.gcd(key_count, 512)

    def turn(turn_index, inner_state):
        block_pairs = lax.dynamic_slice_in_dim(pair_rows, turn_index * block_width, block_width, 1)
        return step_fn(inner_state, block_pairs, turn_index * block_width)

    return lax.fori_loop(0, key_count // block_width, turn, carry_state)


def general_shards(
    inputs,
    lengths,
    w_query,
    b_query,
    w_key,
    w_value,
    b_value,
    w_out,
    b_out,
    first_gain,
    first_shift,
    w_expand,
    b_expand,
    w_reduce,
    b_reduce,
    second_gain,
    second_shift,
    cotangent,
):
    gathered = (
        lax.all_gather(w_query, ("fsdp", "ctx"), axis=0, tiled=True),
        lax.all_gather(b_query, ("fsdp", "ctx"), axis=0, tiled=True),
        lax.all_gather(w_key, ("fsdp", "ctx"), axis=0, tiled=True),
        lax.all_gather(w_value, ("fsdp", "ctx"), axis=0, tiled=True),
        lax.all_gather(b_value, ("fsdp", "ctx"), axis=0, tiled=True),
        lax.all_gather(w_out, ("fsdp", "ctx"), axis=0, tiled=True),
        lax.all_gather(b_out, ("fsdp", "ctx"), axis=0, tiled=True),
        lax.all_gather(first_gain, ("fsdp", "ctx"), axis=0, tiled=True),
        lax.all_gather(first_shift, ("fsdp", "ctx"), axis=0, tiled=True),
        lax.all_gather(w_expand, ("fsdp", "ctx"), axis=0, tiled=True),
        lax.all_gather(b_expand, ("fsdp", "ctx"), axis=0, tiled=True),
        lax.all_gather(w_reduce, ("fsdp", "ctx"), axis=0, tiled=True),
        lax.all_gather(b_reduce, ("fsdp", "ctx"), axis=0, tiled=True),
        lax.all_gather(second_gain, ("fsdp", "ctx"), axis=0, tiled=True),
        lax.all_gather(second_shift, ("fsdp", "ctx"), axis=0, tiled=True),
    )
    (
        full_query,
        bias_query,
        full_key,
        full_value,
        bias_value,
        full_out,
        bias_out,
        gain_first,
        shift_first,
        full_expand,
        bias_expand,
        full_reduce,
        bias_reduce,
        gain_second,
        shift_second,
    ) = gathered
    seq_count, block_rows, model_width = inputs.shape
    total_rows = seq_count * block_rows
    head_size = model_width // HEADS
    score_scale = head_size ** (-0.5)
    own_first = lax.axis_index("ctx") * block_rows
    positions = own_first + jnp.arange(block_rows, dtype=jnp.int32)
    valid_rows = (positions[None, :] < lengths[:, None]).astype(jnp.float32).reshape(total_rows, 1)
    flat_rows = inputs.reshape(total_rows, model_width)
    queries = (product(flat_rows, full_query) + bias_query.astype(jnp.float32)).astype(jnp.bfloat16)
    key_rows = product(flat_rows, full_key).astype(jnp.bfloat16)
    value_rows = (product(flat_rows, full_value) + bias_value.astype(jnp.float32)).astype(
        jnp.bfloat16
    )
    query_heads = queries.reshape(seq_count, block_rows, HEADS, head_size)
    local_pairs = jnp.concatenate([key_rows, value_rows], -1).reshape(
        seq_count, block_rows, 2 * model_width
    )

    def key_allowed(first_row, key_count):
        return ((first_row + jnp.arange(key_count, dtype=jnp.int32))[None, :] < lengths[:, None])[
            :, None, None, :
        ]

    def split_pairs(block_pairs):
        key_count = block_pairs.shape[1]
        key_heads = block_pairs[:, :, :model_width].reshape(seq_count, key_count, HEADS, head_size)
        value_heads = block_pairs[:, :, model_width:].reshape(
            seq_count, key_count, HEADS, head_size
        )
        return (key_heads, value_heads, key_count)

    def forward_step(carry_state, block_pairs, first_row):
        running_max, running_sum, running_acc = carry_state
        key_heads, value_heads, key_count = split_pairs(block_pairs)
        allowed = key_allowed(first_row, key_count)
        scores = (
            jnp.einsum(
                "sqhd,skhd->shqk", query_heads, key_heads, preferred_element_type=jnp.float32
            )
            * score_scale
        )
        scores = jnp.where(allowed, scores, masked_score)
        new_max = jnp.maximum(running_max, jnp.max(scores, -1))
        factor = jnp.exp(running_max - new_max)
        exponents = jnp.where(allowed, jnp.exp(scores - new_max[..., None]), 0.0)
        new_sum = running_sum * factor + jnp.sum(exponents, -1)
        update = jnp.einsum(
            "shqk,skhd->sqhd",
            exponents.astype(jnp.bfloat16),
            value_heads,
            preferred_element_type=jnp.float32,
        )
        new_acc = running_acc * jnp.transpose(factor, (0, 2, 1))[..., None] + update
        return (new_max, new_sum, new_acc)

    start_state = (
        jnp.full((seq_count, HEADS, block_rows), masked_score, jnp.float32),
        jnp.zeros((seq_count, HEADS, block_rows), jnp.float32),
        jnp.zeros((seq_count, block_rows, HEADS, head_size), jnp.float32),
    )
    running_max, running_sum, running_acc = over_blocks(
        forward_step, start_state, lax.all_gather(local_pairs, "ctx", axis=1, tiled=True)
    )
    context_full = running_acc / jnp.transpose(running_sum, (0, 2, 1))[..., None]
    log_total = running_max + jnp.log(running_sum)
    context = context_full.reshape(total_rows, model_width).astype(jnp.bfloat16)
    attended = product(context, full_out) + bias_out.astype(jnp.float32)
    residual = flat_rows.astype(jnp.float32) + attended
    normed, first_pull = jax.vjp(
        layer_norm, residual, gain_first.astype(jnp.float32), shift_first.astype(jnp.float32)
    )
    normed_low = normed.astype(jnp.bfloat16)
    expanded = product(normed_low, full_expand) + bias_expand.astype(jnp.float32)
    activated, gelu_pull = jax.vjp(partial(jax.nn.gelu, approximate=False), expanded)
    activated_low = activated.astype(jnp.bfloat16)
    reduced = product(activated_low, full_reduce) + bias_reduce.astype(jnp.float32)
    final_rows, second_pull = jax.vjp(
        layer_norm,
        normed + reduced,
        gain_second.astype(jnp.float32),
        shift_second.astype(jnp.float32),
    )
    layer_out = (final_rows * valid_rows).astype(jnp.bfloat16).reshape(inputs.shape)
    d_output = cotangent.reshape(total_rows, model_width).astype(jnp.float32) * valid_rows
    d_second, second_gain_grad, second_shift_grad = second_pull(d_output)
    d_reduced = d_second.astype(jnp.bfloat16)
    reduce_grad = outer_sum(activated_low, d_reduced)
    reduce_bias_grad = jnp.sum(d_reduced.astype(jnp.float32), 0)
    (d_expanded_full,) = gelu_pull(back_product(d_reduced, full_reduce))
    d_expanded = d_expanded_full.astype(jnp.bfloat16)
    expand_grad = outer_sum(normed_low, d_expanded)
    expand_bias_grad = jnp.sum(d_expanded.astype(jnp.float32), 0)
    d_normed = d_second + back_product(d_expanded, full_expand)
    d_first, first_gain_grad, first_shift_grad = first_pull(d_normed)
    d_attended = d_first.astype(jnp.bfloat16)
    out_grad = outer_sum(context, d_attended)
    out_bias_grad = jnp.sum(d_attended.astype(jnp.float32), 0)
    d_context = back_product(d_attended, full_out).astype(jnp.bfloat16)
    d_context_heads = d_context.reshape(seq_count, block_rows, HEADS, head_size)
    delta = jnp.transpose(
        jnp.sum(d_context_heads.astype(jnp.float32) * context_full, -1), (0, 2, 1)
    )
    whole_length = block_rows * lax.axis_size("ctx")

    def score_grads(key_heads, value_heads, allowed):
        scores = (
            jnp.einsum(
                "sqhd,skhd->shqk", query_heads, key_heads, preferred_element_type=jnp.float32
            )
            * score_scale
        )
        probabilities = jnp.where(allowed, jnp.exp(scores - log_total[..., None]), 0.0)
        d_probs = jnp.einsum(
            "sqhd,skhd->shqk", d_context_heads, value_heads, preferred_element_type=jnp.float32
        )
        d_scores = (probabilities * (d_probs - delta[..., None])).astype(jnp.bfloat16)
        return (probabilities, d_scores)

    def backward_step(carry_state, block_pairs, first_row):
        grad_query, grad_pairs = carry_state
        key_heads, value_heads, key_count = split_pairs(block_pairs)
        probabilities, d_scores = score_grads(
            key_heads, value_heads, key_allowed(first_row, key_count)
        )
        grad_query = (
            grad_query
            + jnp.einsum("shqk,skhd->sqhd", d_scores, key_heads, preferred_element_type=jnp.float32)
            * score_scale
        )
        key_part = (
            jnp.einsum("shqk,sqhd->skhd", d_scores, query_heads, preferred_element_type=jnp.float32)
            * score_scale
        )
        value_part = jnp.einsum(
            "shqk,sqhd->skhd",
            probabilities.astype(jnp.bfloat16),
            d_context_heads,
            preferred_element_type=jnp.float32,
        )
        fresh = jnp.concatenate(
            [
                key_part.reshape(seq_count, key_count, model_width),
                value_part.reshape(seq_count, key_count, model_width),
            ],
            -1,
        )
        before = lax.dynamic_slice_in_dim(grad_pairs, first_row, key_count, 1)
        grad_pairs = lax.dynamic_update_slice_in_dim(grad_pairs, before + fresh, first_row, 1)
        return (grad_query, grad_pairs)

    query_zero = jnp.zeros((seq_count, block_rows, HEADS, head_size), jnp.float32)
    back_state = (query_zero, jnp.zeros((seq_count, whole_length, 2 * model_width), jnp.float32))
    back_result = over_blocks(
        backward_step, back_state, lax.all_gather(local_pairs, "ctx", axis=1, tiled=True)
    )
    grad_query = back_result[0]
    own_pairs = lax.psum_scatter(
        back_result[1].astype(jnp.bfloat16), "ctx", scatter_dimension=1, tiled=True
    ).astype(jnp.float32)
    d_keys = own_pairs[:, :, :model_width].reshape(total_rows, model_width).astype(jnp.bfloat16)
    d_values = own_pairs[:, :, model_width:].reshape(total_rows, model_width).astype(jnp.bfloat16)
    d_queries = grad_query.reshape(total_rows, model_width).astype(jnp.bfloat16)
    query_grad = outer_sum(flat_rows, d_queries)
    query_bias_grad = jnp.sum(d_queries.astype(jnp.float32), 0)
    key_grad = outer_sum(flat_rows, d_keys)
    value_grad = outer_sum(flat_rows, d_values)
    value_bias_grad = jnp.sum(d_values.astype(jnp.float32), 0)
    input_grad = (
        d_first
        + back_product(d_queries, full_query)
        + back_product(d_keys, full_key)
        + back_product(d_values, full_value)
    ).reshape(inputs.shape)
    shares = (
        lax.psum_scatter(query_grad, ("fsdp", "ctx"), scatter_dimension=0, tiled=True),
        lax.psum_scatter(query_bias_grad, ("fsdp", "ctx"), scatter_dimension=0, tiled=True),
        lax.psum_scatter(key_grad, ("fsdp", "ctx"), scatter_dimension=0, tiled=True),
        lax.psum_scatter(value_grad, ("fsdp", "ctx"), scatter_dimension=0, tiled=True),
        lax.psum_scatter(value_bias_grad, ("fsdp", "ctx"), scatter_dimension=0, tiled=True),
        lax.psum_scatter(out_grad, ("fsdp", "ctx"), scatter_dimension=0, tiled=True),
        lax.psum_scatter(out_bias_grad, ("fsdp", "ctx"), scatter_dimension=0, tiled=True),
        lax.psum_scatter(first_gain_grad, ("fsdp", "ctx"), scatter_dimension=0, tiled=True),
        lax.psum_scatter(first_shift_grad, ("fsdp", "ctx"), scatter_dimension=0, tiled=True),
        lax.psum_scatter(expand_grad, ("fsdp", "ctx"), scatter_dimension=0, tiled=True),
        lax.psum_scatter(expand_bias_grad, ("fsdp", "ctx"), scatter_dimension=0, tiled=True),
        lax.psum_scatter(reduce_grad, ("fsdp", "ctx"), scatter_dimension=0, tiled=True),
        lax.psum_scatter(reduce_bias_grad, ("fsdp", "ctx"), scatter_dimension=0, tiled=True),
        lax.psum_scatter(second_gain_grad, ("fsdp", "ctx"), scatter_dimension=0, tiled=True),
        lax.psum_scatter(second_shift_grad, ("fsdp", "ctx"), scatter_dimension=0, tiled=True),
    )
    return (
        layer_out,
        input_grad,
        shares[0],
        shares[1],
        shares[2],
        shares[3],
        shares[4],
        shares[5],
        shares[6],
        shares[7],
        shares[8],
        shares[9],
        shares[10],
        shares[11],
        shares[12],
        shares[13],
        shares[14],
    )


MESH = pl.DeviceIdType.MESH
MIB = 1024*1024

def place():
    core = lax.axis_index("fsdp"); chip = lax.axis_index("ctx")
    return core, chip

def greet(peers):
    barrier = pltpu.get_barrier_semaphore()
    for peer in peers:
        pl.semaphore_signal(barrier, inc=1, device_id=peer, device_id_type=MESH)
    pl.semaphore_wait(barrier, len(peers))

def flip(v, bits):
    for b in (1, 2, 4, 8):
        if bits & b:
            v = v + b - 2 * b * lax.rem(lax.div(v, b), 2)
    return v

LOG2E = math.log2(math.e)


def nt(a, b):
    return lax.dot_general(a, b, (((1,), (1,)), ((), ())), preferred_element_type=jnp.float32)


FULL_ORDER = (12, 8, 4, 15, 11, 7, 14, 13, 10, 9, 6, 5, 3, 2, 1)


class Copies:
    def __init__(self, send_sem, recv_sem):
        self.send_sem, self.recv_sem = send_sem, recv_sem
        self.names, self.sent = {}, []

    def pair(self, name, src, dst, peer):
        i = self.names.setdefault(name, len(self.names))
        return pltpu.make_async_remote_copy(
            src_ref=src,
            dst_ref=dst,
            send_sem=self.send_sem.at[i],
            recv_sem=self.recv_sem.at[i],
            device_id=peer,
            device_id_type=MESH,
        )

    def send(self, name, src, dst, peer, like):
        self.pair(name, src, dst, peer).start()
        self.sent.append((name, like))

    def arrived(self, name, dst, peer):
        self.pair(name, dst, dst, peer).wait_recv()

    def drain(self, peer):
        for name, like in self.sent:
            self.pair(name, like, like, peer).wait_send()


class Line:
    def __init__(self, chip):
        self.z = lax.div(chip, 4)
        self.rest = chip - 4 * self.z
        even = lax.rem(self.z, 2) == 0
        low = self.z < 2
        one, two, three = jnp.int32(1), jnp.int32(2), jnp.int32(3)
        near = jnp.where(even, one, -one)
        mid = jnp.where(low, jnp.where(even, two, one), jnp.where(even, -one, -two))
        far = jnp.where(low, jnp.where(even, three, two), jnp.where(even, -two, -three))
        self.offsets = [jnp.int32(0), near, mid, far]

    def source(self, k):
        return self.z + self.offsets[k]

    def onward_up(self, k):
        return (self.offsets[k] < 0) & (self.z < 3)

    def onward_down(self, k):
        return (self.offsets[k] > 0) & (self.z > 0)


class Gather:
    def __init__(self, copies, line, name, src, out, local_sem, zsend, zrecv):
        self.copies, self.line, self.name, self.src, self.out, self.local_sem = copies, line, name, src, out, local_sem
        self.zsend, self.zrecv = zsend, zrecv
        self.core, self.chip = place()
        self.sib = (1 - self.core, self.chip)
        self.half = src.shape[0] // 2

    def at(self, bits):
        return (self.core, flip(self.chip, bits))

    def index(self, k, bits, core=None):
        core = self.core if core is None else core
        return core * 16 + self.line.source(k) * 4 + flip(self.line.rest, bits)

    def block(self, k, bits, core=None):
        return self.out.at[self.index(k, bits, core)]

    def part(self, k, bits, upper):
        return self.out.at[self.index(k, bits), pl.ds(self.half if upper else 0, self.half)]

    def send(self, tag, src, dst, peer, half=False):
        like = self.src.at[pl.ds(0, self.half)] if half else self.src
        self.copies.send((self.name, tag), src, dst, peer, like)

    def arrived(self, tag, dst):
        self.copies.arrived((self.name, tag), dst, self.sib)

    def along(self, slot, source, src, dst, up):
        return pltpu.make_async_remote_copy(
            src_ref=src,
            dst_ref=dst,
            send_sem=self.zsend.at[self.name * 6 + slot],
            recv_sem=self.zrecv.at[self.name * 4 + source],
            device_id=(self.core, self.chip + 4 if up else self.chip - 4),
            device_id_type=MESH,
        )

    def start_z(self):
        z = self.line.z

        @pl.when(z < 3)
        def _():
            self.along(4, z, self.src, self.block(0, 0), True).start()

        @pl.when(z > 0)
        def _():
            self.along(5, z, self.src, self.block(0, 0), False).start()

    def start_plane(self):
        self.send(("x", 0), self.src, self.block(0, 0), self.at(1))
        self.send(("y", 0), self.src, self.block(0, 0), self.at(2))
        self.send(("s", 0, 0), self.src, self.block(0, 0), self.sib)
        self.local = pltpu.make_async_copy(self.src, self.block(0, 0), self.local_sem)
        self.local.start()

    def on_z(self, k):
        b = self.block(k, 0)
        source = self.line.source(k)
        self.along(source, source, b, b, True).wait_recv()

        @pl.when(self.line.onward_up(k))
        def _():
            self.along(source, source, b, b, True).start()

        @pl.when(self.line.onward_down(k))
        def _():
            self.along(source, source, b, b, False).start()

        self.send(("x", k), b, b, self.at(1))
        self.send(("y", k), b, b, self.at(2))
        self.send(("s", k, 0), b, b, self.sib)

    def on_plane(self, k):
        for bit, tag, further, upper in ((1, "x", 2, False), (2, "y", 1, True)):
            b = self.block(k, bit)
            self.arrived((tag, k), b)
            h = self.part(k, bit, upper)
            self.send(("d" + tag, k), h, h, self.at(further), True)
            self.send(("s", k, bit), b, b, self.sib)

    def on_diagonal(self, k):
        self.arrived(("dx", k), self.part(k, 3, False))
        self.arrived(("dy", k), self.part(k, 3, True))
        b = self.block(k, 3)
        self.send(("s", k, 3), b, b, self.sib)

    def on_sibling(self):
        for k in range(4):
            for bits in range(4):
                self.arrived(("s", k, bits), self.block(k, bits, 1 - self.core))
        self.local.wait()

    def drain(self):
        z = self.line.z

        @pl.when(z < 3)
        def _():
            self.along(4, z, self.src, self.src, True).wait_send()

        @pl.when(z > 0)
        def _():
            self.along(5, z, self.src, self.src, True).wait_send()

        for k in range(1, 4):
            source = self.line.source(k)

            @pl.when(self.line.onward_up(k) | self.line.onward_down(k))
            def _():
                self.along(source, source, self.src, self.src, True).wait_send()


def load_sequence(r_ref, s, kk_ref, vt_ref=None, vv_ref=None):
    for j in range(r_ref.shape[1]):
        span = pl.ds(j * 128, 128)
        kk_ref[span] = r_ref[s, j, 64:128, :].astype(jnp.float32).T.astype(jnp.bfloat16)
        if vt_ref is not None:
            vt_ref[:, span] = r_ref[s, j, 128:192, :]
        if vv_ref is not None:
            vv_ref[span] = r_ref[s, j, 128:192, :].astype(jnp.float32).T.astype(jnp.bfloat16)


def fwd_kernel(
    x_ref, lengths_ref, s_qkv, s_bias, s_vec, s_out, s_expand, s_reduce,
    o_out, o_expand, o_reduce, o_qkv, o_pairs, o_full, lse_ref,
    o_rows, o_scaled, o_spread, o_active, o_slope, o_turned, o_active_t,
    w_qkv, w_bias, w_vec, w_out, w_expand, send_blk, recv_blk, ctx_blk, ctx_recv, kk, vt,
    e_row, x_turned, n_turned, normed, stage, turned, active_t, ctx_sib, active_all, slope_all,
    send_sem, recv_sem, local_sem, hsend, hrecv, csend, crecv, tsend, trecv, wsem, zsend, zrecv, ksem,
):
    f32, bf16 = jnp.float32, jnp.bfloat16
    core, chip = place()
    sib = (1 - core, chip)
    greet([sib] + [(core, flip(chip, b)) for b in range(1, 16)])
    copies = Copies(send_sem, recv_sem)
    line = Line(chip)
    first = [
        Gather(copies, line, 0, s_qkv, w_qkv, local_sem.at[0], zsend, zrecv),
        Gather(copies, line, 1, s_bias, w_bias, local_sem.at[1], zsend, zrecv),
    ]
    rest = [
        Gather(copies, line, 2, s_out, o_out, local_sem.at[2], zsend, zrecv),
        Gather(copies, line, 3, s_vec, w_vec, local_sem.at[3], zsend, zrecv),
        Gather(copies, line, 4, s_expand, o_expand, local_sem.at[4], zsend, zrecv),
        Gather(copies, line, 5, s_reduce, o_reduce, local_sem.at[5], zsend, zrecv),
    ]
    for g in first:
        g.start_z()
        g.start_plane()

    def turn(slot, src, kept):
        c = pltpu.make_async_remote_copy(
            src_ref=src,
            dst_ref=turned.at[slot, 1],
            send_sem=tsend.at[slot],
            recv_sem=trecv.at[slot],
            device_id=sib,
            device_id_type=MESH,
        )
        c.start()
        turned[slot, 0] = kept[...]
        return c

    for i in range(4):
        x_turned[i // 2, 256 * (i % 2) : 256 * (i % 2) + 256] = x_ref[:, 256 * i : 256 * i + 256].astype(f32).T.astype(bf16)
    swaps = [turn(0, x_turned.at[1 - core], x_turned.at[core])]
    for z in (1, 2, 3):
        for g in first:
            g.on_z(z)
    for g in rest[:3]:
        g.start_z()
    for z in range(4):
        for g in first:
            g.on_plane(z)
    for g in rest:
        g.start_plane()
    for z in range(4):
        for g in first:
            g.on_diagonal(z)
    for g in first:
        g.on_sibling()
    keep = pltpu.make_async_copy(w_qkv, o_qkv, local_sem.at[6])
    keep.start()

    for g in rest[:3]:
        g.on_z(1)
    for part in range(3):

        @pl.loop(0, 4)
        def _(p):
            w = w_qkv[:, :, pl.ds(pl.multiple_of(part * 1024 + p * 256, 256), 256)].reshape(1024, 256)
            t = jnp.dot(x_ref[...], w, preferred_element_type=f32).T
            for i in range(4):
                h = 4 * p + i
                rows = t[64 * i : 64 * i + 64]
                if part != 1:
                    own = pl.ds(0 if part == 0 else 32, 32)
                    bias = jnp.concatenate([w_bias[2 * h + k, own] for k in range(2)], 0).astype(f32)
                    rows = rows + jnp.concatenate([bias, bias], 1)
                send_blk[h, pl.ds(64 * part, 64)] = rows.astype(bf16)

    rest[3].start_z()
    for g in rest[:3]:
        g.on_z(2)
    heads = []
    for s in range(2):
        for b in FULL_ORDER:
            to = flip(chip, b)
            i = s * 16 + b
            c = pltpu.make_async_remote_copy(
                src_ref=send_blk.at[to, :, pl.ds(128 * s, 128)],
                dst_ref=recv_blk.at[s, chip],
                send_sem=hsend.at[i],
                recv_sem=hrecv.at[i],
                device_id=(core, to),
                device_id_type=MESH,
            )
            c.start()
            heads.append(c)
        recv_blk[s, chip] = send_blk[chip, :, pl.ds(128 * s, 128)]

    def heads_here(s):
        for b in FULL_ORDER:
            i = s * 16 + b
            here = recv_blk.at[s, flip(chip, b)]
            pltpu.make_async_remote_copy(
                src_ref=here, dst_ref=here, send_sem=hsend.at[i], recv_sem=hrecv.at[i], device_id=sib, device_id_type=MESH
            ).wait_recv()

    events = [lambda: [g.on_plane(0) for g in rest]]
    events.append(lambda: [g.on_z(3) for g in rest[:3]])
    events.append(lambda: [g.on_diagonal(0) for g in rest])
    for z in (1, 2, 3):
        events.append(lambda z=z: [g.on_plane(z) for g in rest[:3]])
    for z in (1, 2, 3):
        events.append(lambda z=z: [rest[3].on_z(z)])
    for z in (1, 2, 3):
        events.append(lambda z=z: [g.on_diagonal(z) for g in rest[:3]])
    READY = len(events)
    for z in (1, 2, 3):
        events.append(lambda z=z: [rest[3].on_plane(z)])
    for z in (1, 2, 3):
        events.append(lambda z=z: [rest[3].on_diagonal(z)])

    def attend_sequence(s, during):
        load_sequence(recv_blk, s, kk, vt_ref=vt)

        @pl.loop(0, 8)
        def _(step):
            for k, event in enumerate(during):

                @pl.when(step == k)
                def _():
                    event()

            q = flip_by(step, chip // 2)
            query = jnp.concatenate([recv_blk[s, 2 * q, 0:64, :], recv_blk[s, 2 * q + 1, 0:64, :]], 1)
            scores = jnp.dot(kk[...], query, preferred_element_type=f32) * (0.125 * LOG2E)
            key = lax.broadcasted_iota(jnp.int32, scores.shape, 0)
            scores = jnp.where(key < lengths_ref[s], scores, masked_score)
            top = jnp.max(scores, 0, keepdims=True)
            e = jnp.exp2(scores - top)
            mass = jnp.sum(e, 0, keepdims=True)
            o = jnp.dot(vt[...], e.astype(bf16), preferred_element_type=f32) / mass
            lse_ref[s, pl.ds(q, 1), :] = top + jnp.log2(mass)
            o_full[s, :, pl.ds(pl.multiple_of(q * 256, 256), 256)] = o
            for i in range(2):
                to = 2 * q + i
                ctx_blk[s, to] = o[:, 128 * i : 128 * i + 128].astype(bf16)

                @pl.when(to != chip)
                def _():
                    pltpu.make_async_remote_copy(
                        src_ref=ctx_blk.at[s, to],
                        dst_ref=ctx_recv.at[chip, :, pl.ds(128 * s, 128)],
                        send_sem=csend.at[s * 16 + to],
                        recv_sem=crecv.at[s * 16 + chip],
                        device_id=(core, to),
                        device_id_type=MESH,
                    ).start()

        ctx_recv[chip, :, pl.ds(128 * s, 128)] = ctx_blk[s, chip]

    PRE, FIRST, SECOND = 3, 4, 4
    for event in events[:PRE]:
        event()
    heads_here(0)
    attend_sequence(0, events[PRE : PRE + FIRST])
    heads_here(1)
    pairs_out = pltpu.make_async_copy(recv_blk, o_pairs, local_sem.at[7])
    pairs_out.start()
    attend_sequence(1, events[PRE + FIRST : PRE + FIRST + SECOND])
    for event in events[PRE + FIRST + SECOND : READY]:
        event()
    for g in rest[:3]:
        g.on_sibling()
    out_weights = pltpu.make_async_copy(o_out, w_out, local_sem.at[6 + 2])
    out_weights.start()

    def fetch(c, slot):
        cols = pl.ds(pl.multiple_of(c * 512, 512), 512)
        return pltpu.make_async_copy(o_expand.at[:, :, cols], w_expand.at[slot], wsem.at[slot])

    fetch(0, 0).start()

    owner = lax.broadcasted_iota(jnp.int32, (32, 1024), 0)
    column = lax.broadcasted_iota(jnp.int32, (32, 1024), 1)
    lane = lax.broadcasted_iota(jnp.int32, (128, 1024), 0)
    pick = jnp.where(lax.rem(lax.broadcasted_iota(jnp.int32, (128, 1024), 1), 32) == lane, 1.0, 0.0).astype(bf16)
    o_rows[...] = jnp.zeros_like(o_rows)
    for r in range(7):
        choose = jnp.where(column == owner * 32 + r, 1.0, 0.0).astype(bf16)
        piece = jnp.dot(choose, w_vec[...].reshape(1024, 128), preferred_element_type=f32)
        if r == 3:
            for o in range(32):
                e_row[o // 4 : o // 4 + 1, 128 * (o % 4) : 128 * (o % 4) + 128] = piece[o : o + 1]
        else:
            spread_row = jnp.dot(piece.astype(bf16), pick, preferred_element_type=f32)
            o_rows[r : r + 1] = jnp.sum(jnp.where(lax.div(column, 32) == owner, spread_row, 0.0), 0, keepdims=True)

    for s in range(2):
        for b in range(1, 16):
            other = flip(chip, b)
            here = ctx_recv.at[other, :, pl.ds(128 * s, 128)]
            pltpu.make_async_remote_copy(
                src_ref=ctx_blk.at[s, other],
                dst_ref=here,
                send_sem=csend.at[s * 16 + other],
                recv_sem=crecv.at[s * 16 + other],
                device_id=sib,
                device_id_type=MESH,
            ).wait()
    mine, others = pl.ds(core * 8, 8), pl.ds((1 - core) * 8, 8)
    swaps.append(
        pltpu.make_async_remote_copy(
            src_ref=ctx_recv.at[others],
            dst_ref=ctx_sib,
            send_sem=tsend.at[2],
            recv_sem=trecv.at[2],
            device_id=sib,
            device_id_type=MESH,
        )
    )
    swaps[-1].start()
    turned[2, 0] = ctx_recv[mine].reshape(512, 256)
    out_weights.wait()
    for i in range(4):
        rows = ctx_recv[4 * i : 4 * i + 4].reshape(256, 256).astype(f32).T.astype(bf16)
        term = jnp.dot(rows, w_out[8 * i : 8 * i + 8].reshape(256, 1024), preferred_element_type=f32)
        if i == 0:
            o_scaled[...] = term + (x_ref[...].astype(f32) + o_rows[0:1])
        else:
            o_scaled[...] += term

    @pl.loop(0, 4)
    def _(i):
        span = pl.ds(pl.multiple_of(i * 64, 64), 64)
        residual = o_scaled[span]
        center = residual - jnp.mean(residual, -1, keepdims=True)
        spread = lax.rsqrt(jnp.mean(center * center, -1, keepdims=True) + epsilon)
        x_hat = center * spread
        o_scaled[span] = x_hat
        o_spread[span] = jnp.broadcast_to(spread, (64, 128))
        normed[span] = (x_hat * o_rows[1:2] + o_rows[2:3]).astype(bf16)

    for i in range(4):
        n_turned[i // 2, 256 * (i % 2) : 256 * (i % 2) + 256] = normed[:, 256 * i : 256 * i + 256].astype(f32).T.astype(bf16)
    swaps.append(turn(1, n_turned.at[1 - core], n_turned.at[core]))

    def active_copy(j):
        return pltpu.make_async_remote_copy(
            src_ref=stage.at[j],
            dst_ref=active_t.at[1, j],
            send_sem=tsend.at[3 + j],
            recv_sem=trecv.at[3 + j],
            device_id=sib,
            device_id_type=MESH,
        )

    def keep_chunk(c):
        return (
            pltpu.make_async_copy(active_all.at[c], o_active.at[c], ksem.at[0, c]),
            pltpu.make_async_copy(slope_all.at[c], o_slope.at[c], ksem.at[1, c]),
        )

    last_events = events[READY:]

    @pl.loop(0, 8)
    def _(c):
        for k, event in enumerate(last_events[:8]):

            @pl.when(c == k)
            def _():
                event()

        slot = lax.rem(c, 2)

        @pl.when(c < 7)
        def _():
            fetch(c + 1, 1 - slot).start()

        fetch(c, slot).wait()
        expanded = jnp.dot(normed[...], w_expand[slot].reshape(1024, 512), preferred_element_type=f32) + e_row[pl.ds(c, 1)]
        share = 0.5 * (1.0 + lax.erf(expanded * math.sqrt(0.5)))
        bell = jnp.exp(-0.5 * expanded * expanded) * (1.0 / math.sqrt(2.0 * math.pi))
        slope_all[c] = (share + expanded * bell).astype(bf16)
        active = (expanded * share).astype(bf16)
        active_all[c] = active
        for copy in keep_chunk(c):
            copy.start()
        across = active.astype(f32).T.astype(bf16)
        j = lax.rem(c, 4)

        @pl.when(lax.div(c, 4) == core)
        def _():
            active_t[0, j] = across

        @pl.when(lax.div(c, 4) != core)
        def _():
            stage[j] = across
            active_copy(j).start()

    for event in last_events[8:]:
        event()
    for c in swaps:
        c.wait()
    turned[2, 1] = ctx_sib[...].reshape(512, 256)
    for j in range(4):
        active_copy(j).wait()
    kept = [
        pltpu.make_async_copy(turned, o_turned, local_sem.at[0]),
        pltpu.make_async_copy(active_t, o_active_t, local_sem.at[1]),
    ]
    for c in kept:
        c.start()
    rest[3].on_sibling()
    for c in range(8):
        for copy in keep_chunk(c):
            copy.wait()
    for c in kept:
        c.wait()
    for c in heads:
        c.wait_send()
    copies.drain(sib)
    for g in first + rest:
        g.drain()
    keep.wait()
    pairs_out.wait()


def flip_by(v, w):
    out = 0
    for b in (1, 2, 4):
        p, q = lax.rem(lax.div(v, b), 2), lax.rem(lax.div(w, b), 2)
        out = out + b * (p + q - 2 * p * q)
    return out


def forward_attention(rows, lengths, qkv, bias, vec, w_out, w_expand, w_reduce, collective_id):
    v, hbm = pl.BlockSpec(memory_space=pltpu.VMEM), pl.BlockSpec(memory_space=pl.ANY)
    f32, bf16 = jnp.float32, jnp.bfloat16
    gathered = lambda x: jax.ShapeDtypeStruct((32,) + x.shape, x.dtype)
    dma = pltpu.SemaphoreType.DMA
    array = jax.ShapeDtypeStruct
    vmem = lambda shape, dtype=bf16: pltpu.VMEM(shape, dtype)
    return pl.pallas_call(
        fwd_kernel,
        out_shape=[
            gathered(w_out),
            gathered(w_expand),
            gathered(w_reduce),
            gathered(qkv),
            array((2, 16, 192, 128), bf16),
            array((2, 64, 2048), f32),
            array((2, 8, 256), f32),
            array((8, 1024), f32),
            array((256, 1024), f32),
            array((256, 128), f32),
            array((8, 256, 512), bf16),
            array((8, 256, 512), bf16),
            array((3, 2, 512, 256), bf16),
            array((2, 4, 512, 256), bf16),
        ],
        in_specs=[v, pl.BlockSpec(memory_space=pltpu.SMEM)] + [hbm] * 6,
        out_specs=[hbm] * 5 + [v] * 5 + [hbm] * 4,
        scratch_shapes=[
            vmem((32,) + qkv.shape),
            vmem((32,) + bias.shape),
            vmem((32,) + vec.shape),
            vmem((32,) + w_out.shape),
            vmem((2, 32, 32, 512)),
            vmem((16, 192, 256)),
            vmem((2, 16, 192, 128)),
            vmem((2, 16, 64, 128)),
            vmem((16, 64, 256)),
            vmem((2048, 64)),
            vmem((64, 2048)),
            vmem((8, 512), f32),
            vmem((2, 512, 256)),
            vmem((2, 512, 256)),
            vmem((256, 1024)),
            vmem((4, 512, 256)),
            vmem((3, 2, 512, 256)),
            vmem((2, 4, 512, 256)),
            vmem((8, 64, 256)),
            vmem((8, 256, 512)),
            vmem((8, 256, 512)),
            dma((210,)),
            dma((210,)),
            dma((9,)),
            dma((32,)),
            dma((32,)),
            dma((32,)),
            dma((32,)),
            dma((7,)),
            dma((7,)),
            dma((2,)),
            dma((36,)),
            dma((24,)),
            dma((2, 8)),
        ],
        compiler_params=pltpu.CompilerParams(
            collective_id=collective_id, has_side_effects=True, vmem_limit_bytes=60 * MIB
        ),
        name="forward_attention",
    )(rows, lengths, qkv, bias, vec, w_out, w_expand, w_reduce)


class Scatter:
    ORDER = (12, 8, 4, 0)

    def __init__(self, copies, name, grads, out, bufs):
        self.copies, self.name, self.grads, self.out = copies, name, grads, out
        self.first, self.second, self.third = bufs
        self.core, self.chip = place()
        self.rows = grads.shape[1]
        self.half = self.rows // 2
        self.lo, self.hi = pl.ds(0, self.half), pl.ds(self.half, self.half)
        self.first_at = [[self.first.at[k, i] for i in range(2)] for k in range(4)]
        self.second_at = [[self.second.at[k, i] for i in range(2)] for k in range(4)]
        self.third_at = [self.third.at[k] for k in range(3)]

    def at(self, bits):
        return (self.core, flip(self.chip, bits))

    def send(self, tag, src, dst, bits, half=True):
        like = self.first_at[0][0] if half else self.third_at[0]
        self.copies.send((self.name, tag), src, dst, self.at(bits), like)

    def arrived(self, tag, dst):
        self.copies.arrived((self.name, tag), dst, self.at(1))

    def add(self, rows, fn):
        step = min(rows, 16)
        if rows == step:
            fn(0, step)
            return

        def turn(i, carry):
            fn(pl.multiple_of(i * step, step), step)
            return carry

        lax.fori_loop(0, rows // step, turn, 0)

    def start(self):
        for k, z in enumerate(self.ORDER):
            diag = flip(self.chip, z + 3)
            self.send(("1a", k), self.grads.at[diag, self.lo], self.first_at[k][0], 2)
            self.send(("1b", k), self.grads.at[diag, self.hi], self.first_at[k][1], 1)

    def start_direct(self):
        for k, z in enumerate(self.ORDER):
            xb, yb = flip(self.chip, z + 1), flip(self.chip, z + 2)
            self.send(("2xh", k), self.grads.at[xb, self.hi], self.second_at[k][0].at[self.hi], 1)
            self.send(("2yl", k), self.grads.at[yb, self.lo], self.second_at[k][1].at[self.lo], 2)

    def on_first(self, k):
        z = self.ORDER[k]
        for i, (tag, bit, upper) in enumerate((("1a", 1, False), ("1b", 2, True))):
            owner = flip(self.chip, z + bit)
            here = self.first_at[k][i]
            self.arrived((tag, k), here)

            def fn(start, size):
                rows = pl.ds(start, size)
                theirs = pl.ds(start + (self.half if upper else 0), size)
                here[rows] = here[rows] + self.grads.at[owner][theirs]

            self.add(self.half, fn)
            self.send(("2" + "xy"[i] + "lh"[i], k), here, self.second_at[k][i].at[self.hi if upper else self.lo], bit)

    def on_second(self, k):
        z = self.ORDER[k]
        self.arrived(("2xh", k), self.second_at[k][0].at[self.hi])
        self.arrived(("2yl", k), self.second_at[k][1].at[self.lo])
        self.arrived(("2xl", k), self.second_at[k][0].at[self.lo])
        self.arrived(("2yh", k), self.second_at[k][1].at[self.hi])
        owner = flip(self.chip, z)

        def fn(start, size):
            rows = pl.ds(start, size)
            f32 = jnp.float32
            total = self.grads.at[owner][rows].astype(f32) + self.second_at[k][0][rows].astype(f32)
            total = total + self.second_at[k][1][rows].astype(f32)
            if k < 3:
                self.second_at[k][0][rows] = total.astype(self.second.dtype)
            else:
                self.out[rows] = total

        self.add(self.rows, fn)
        if k < 3:
            self.send(("3", k), self.second_at[k][0], self.third_at[k], z, False)

    def on_third(self):
        for k in range(3):
            self.arrived(("3", k), self.third_at[k])

        def fn(start, size):
            rows = pl.ds(start, size)
            total = self.out[rows]
            for k in range(3):
                total = total + self.third_at[k][rows].astype(jnp.float32)
            self.out[rows] = total

        self.add(self.rows, fn)


def scatter_buffers(block, dtype):
    rows, cols = block
    return [
        pltpu.VMEM((4, 2, rows // 2, cols), dtype),
        pltpu.VMEM((4, 2, rows, cols), dtype),
        pltpu.VMEM((3, rows, cols), dtype),
    ]


def bwd_kernel(*refs):
    f32, bf16 = jnp.float32, jnp.bfloat16
    (
        lengths_ref, h_pairs, h_full, lse_ref, h_rows, h_active_t, cotangent, scaled, spread, vectors,
        h_active, h_slope, h_reduce, h_expand, h_out, h_qkv,
    ) = refs[:16]
    (o_layer, o_reduce, o_expand, o_out, o_vec, o_qkv, o_input, o_bias) = refs[16:24]
    bufs = [refs[24 + 3 * i : 27 + 3 * i] for i in range(5)]
    (
        g_reduce, g_expand, g_out, g_vec, g_qkv, w_qkv, d_recv, kk, vv, kt, acc, d_send, d_own, d_sib, b_own, b_sib, b_in,
        slopes, w_reduce, w_expand, w_out, e_own, e_sib, d_first, a_own, a_sib, d_ctx, rows_sum, e_sum, vec_own, vec_sib, r_own, r_sib, pairs, o_full, rows_t, active_t,
        send_sem, recv_sem, local_sem, dsend, drecv, qsend, qrecv, esend, erecv, wsem, lsem,
    ) = refs[39:]
    core, chip = place()
    sib = (1 - core, chip)
    greet([sib] + [(core, flip(chip, b)) for b in range(1, 16)])
    copies = Copies(send_sem, recv_sem)
    rest = [
        Scatter(copies, i, g, o, bufs[i])
        for i, (g, o) in enumerate(((g_reduce, o_reduce), (g_expand, o_expand), (g_out, o_out), (g_vec, o_vec)))
    ]
    last = Scatter(copies, 4, g_qkv, o_qkv, bufs[4])
    out_weights = pltpu.make_async_copy(h_out, w_out, local_sem.at[4])
    out_weights.start()

    def fetch(c, slot, back):
        cols = pl.ds(pl.multiple_of(c * 512, 512), 512)
        copies_in = [
            pltpu.make_async_copy(h_reduce.at[pl.ds(c * 4, 4)], w_reduce.at[slot], wsem.at[slot, 0]),
            pltpu.make_async_copy((h_slope if back else h_active).at[c], slopes.at[slot], wsem.at[slot, 2]),
        ]
        if back:
            copies_in.append(pltpu.make_async_copy(h_expand.at[:, :, cols], w_expand.at[slot], wsem.at[slot, 1]))
        return copies_in

    for c in fetch(0, 0, False):
        c.start()
    loads = [
        pltpu.make_async_copy(src, dst, lsem.at[i])
        for i, (src, dst) in enumerate(((h_active_t, active_t), (h_rows, rows_t), (h_pairs, pairs), (h_full, o_full)))
    ]
    for c in loads:
        c.start()
    d_first[...] = scaled[...] * vectors[1:2] + (vectors[2:3] + vectors[4:5])

    @pl.loop(0, 8)
    def _(c):
        slot = lax.rem(c, 2)

        @pl.when(c < 7)
        def _():
            for copy in fetch(c + 1, 1 - slot, False):
                copy.start()

        @pl.when(c == 7)
        def _():
            for copy in fetch(0, 0, True):
                copy.start()

        for copy in fetch(c, slot, False):
            copy.wait()
        d_first[...] += jnp.dot(slopes[slot], w_reduce[slot].reshape(512, 1024), preferred_element_type=f32)

    rows_sum[...] = jnp.zeros_like(rows_sum)

    @pl.loop(0, 4)
    def _(i):
        span = pl.ds(pl.multiple_of(i * 64, 64), 64)
        total = d_first[span]
        center = total - jnp.mean(total, -1, keepdims=True)
        width = lax.rsqrt(jnp.mean(center * center, -1, keepdims=True) + epsilon)
        x_hat = center * width
        row = chip * 128 + lax.rem(i, 2) * 64 + lax.broadcasted_iota(jnp.int32, (64, 1024), 0)
        valid = row < lengths_ref[lax.div(i, 2)]
        o_layer[span] = jnp.where(valid, x_hat * vectors[5:6] + vectors[6:7], 0.0).astype(bf16)
        d_output = jnp.where(valid, cotangent[span].astype(f32), 0.0)
        pulled = d_output * vectors[5:6]
        level = jnp.mean(pulled, -1, keepdims=True)
        slope = jnp.mean(pulled * x_hat, -1, keepdims=True)
        d_rows = width * (pulled - level - x_hat * slope)
        d_low = d_rows.astype(bf16)
        d_first[span] = d_rows
        r_own[span] = d_low
        rows_sum[4:5] += jnp.sum(d_low.astype(f32), 0, keepdims=True)
        rows_sum[5:6] += jnp.sum(d_output * x_hat, 0, keepdims=True)
        rows_sum[6:7] += jnp.sum(d_output, 0, keepdims=True)

    copies.send("r", r_own, r_sib, sib, r_own)
    copies.arrived("r", r_sib, sib)
    for c in loads:
        c.wait()

    @pl.loop(0, 4)
    def _(j):
        g = jnp.dot(active_t[0, j], r_own[...], preferred_element_type=f32)
        g = g + jnp.dot(active_t[1, j], r_sib[...], preferred_element_type=f32)
        g_reduce[pl.ds(j * 4, 4)] = g.astype(bf16).reshape(4, 128, 1024)

    rest[0].start()
    rest[0].start_direct()

    def e_copy(c):
        return pltpu.make_async_remote_copy(
            src_ref=e_own.at[c],
            dst_ref=e_sib.at[c],
            send_sem=esend.at[c],
            recv_sem=erecv.at[c],
            device_id=sib,
            device_id_type=MESH,
        )

    @pl.loop(0, 8)
    def _(c):
        slot = lax.rem(c, 2)

        @pl.when(c < 7)
        def _():
            for copy in fetch(c + 1, 1 - slot, True):
                copy.start()

        for copy in fetch(c, slot, True):
            copy.wait()
        d_active = nt(r_own[...], w_reduce[slot].reshape(512, 1024))
        d_expanded = (d_active * slopes[slot].astype(f32)).astype(bf16)
        e_own[c] = d_expanded
        e_copy(c).start()
        e_sum[pl.ds(c, 1)] = jnp.sum(d_expanded.astype(f32), 0, keepdims=True)
        d_first[...] += nt(d_expanded, w_expand[slot].reshape(1024, 512))

    @pl.loop(0, 4)
    def _(i):
        span = pl.ds(pl.multiple_of(i * 64, 64), 64)
        d_normed, x_hat = d_first[span], scaled[span]
        pulled = d_normed * vectors[1:2]
        level = jnp.mean(pulled, -1, keepdims=True)
        slope = jnp.mean(pulled * x_hat, -1, keepdims=True)
        d_rows = spread[span, 0:1] * (pulled - level - x_hat * slope)
        d_low = d_rows.astype(bf16)
        d_first[span] = d_rows
        a_own[span] = d_low
        rows_sum[0:1] += jnp.sum(d_low.astype(f32), 0, keepdims=True)
        rows_sum[1:2] += jnp.sum(d_normed * x_hat, 0, keepdims=True)
        rows_sum[2:3] += jnp.sum(d_normed, 0, keepdims=True)

    for k in range(4):
        rest[0].on_first(k)
    out_weights.wait()

    @pl.loop(0, 4)
    def _(i):
        t = nt(w_out[pl.ds(i * 8, 8)].reshape(256, 1024), a_own[...])
        d_ctx[pl.ds(i * 4, 4)] = t.astype(bf16).reshape(4, 64, 256)

    sent = []

    def exchange_out(s, b, src, dst, sends, recvs):
        c = pltpu.make_async_remote_copy(
            src_ref=src,
            dst_ref=dst,
            send_sem=sends.at[s * 16 + b],
            recv_sem=recvs.at[s * 16 + b],
            device_id=(core, flip(chip, b)),
            device_id_type=MESH,
        )
        c.start()
        sent.append(c)

    def exchange_in(s, b, here, sends, recvs):
        pltpu.make_async_remote_copy(
            src_ref=here,
            dst_ref=here,
            send_sem=sends.at[s * 16 + b],
            recv_sem=recvs.at[s * 16 + b],
            device_id=sib,
            device_id_type=MESH,
        ).wait_recv()

    for s in range(2):
        lane = pl.ds(128 * s, 128)
        for b in FULL_ORDER:
            exchange_out(s, b, d_ctx.at[flip(chip, b), :, lane], d_recv.at[s, chip], dsend, drecv)
        d_recv[s, chip] = d_ctx[chip, :, lane]
    copies.send("a", a_own, a_sib, sib, a_own)

    vec_own[...] = jnp.zeros_like(vec_own)
    owner = lax.broadcasted_iota(jnp.int32, (32, 1024), 0)
    column = lax.broadcasted_iota(jnp.int32, (32, 1024), 1)
    place_in = lax.rem(lax.broadcasted_iota(jnp.int32, (1024, 128), 0), 32)
    pick = jnp.where(place_in == lax.broadcasted_iota(jnp.int32, (1024, 128), 1), 1.0, 0.0).astype(bf16)
    for r in (0, 1, 2, 4, 5, 6):
        spread_row = jnp.where(lax.div(column, 32) == owner, rows_sum[r : r + 1], 0.0)
        top = spread_row.astype(bf16)
        low = (spread_row - top.astype(f32)).astype(bf16)
        vec_own[:, r, :] = jnp.dot(top, pick, preferred_element_type=f32) + jnp.dot(low, pick, preferred_element_type=f32)
    for o in range(32):
        vec_own[o, 3:4, :] = e_sum[o // 4 : o // 4 + 1, 128 * (o % 4) : 128 * (o % 4) + 128]
    own_half, other_half = pl.ds(core * 16, 16), pl.ds((1 - core) * 16, 16)
    copies.send("v", vec_own.at[other_half], vec_sib, sib, vec_sib)


    @pl.loop(0, 8)
    def _(c):
        e_copy(c).wait()
        g = jnp.dot(rows_t[1, 0], e_own[c], preferred_element_type=f32)
        g = g + jnp.dot(rows_t[1, 1], e_sib[c], preferred_element_type=f32)
        g_expand[:, :, pl.ds(pl.multiple_of(c * 512, 512), 512)] = g.astype(bf16).reshape(16, 32, 512)

    rest[1].start()
    rest[1].start_direct()
    copies.arrived("a", a_sib, sib)
    for i in range(4):
        cols = slice(256 * i, 256 * i + 256)
        g = jnp.dot(rows_t[2, 0], a_own[:, cols], preferred_element_type=f32)
        g = g + jnp.dot(rows_t[2, 1], a_sib[:, cols], preferred_element_type=f32)
        g_out[:, :, cols] = g.astype(bf16).reshape(16, 32, 256)
    copies.arrived("v", vec_sib, sib)
    g_vec[...] = vec_own[own_half] + vec_sib[...]
    for r in rest[2:]:
        r.start()
        r.start_direct()
    b_own[...] = jnp.zeros_like(b_own)

    def fetch_qkv(i, slot):
        return pltpu.make_async_copy(h_qkv.at[pl.ds(i * 8, 8)], w_qkv.at[slot], local_sem.at[5 + slot])

    fetch_qkv(0, 0).start()
    fetch_qkv(1, 1).start()

    def back_sequence(s, during):
        load_sequence(pairs, s, kk, vt_ref=None, vv_ref=vv)
        for j in range(16):
            kt[:, pl.ds(j * 128, 128)] = pairs[s, j, 64:128, :]
        acc[...] = jnp.zeros_like(acc)

        @pl.loop(0, 8)
        def _(q):
            for k, event in enumerate(during):

                @pl.when(q == k)
                def _():
                    event()

            both = lambda ref, lo, hi: jnp.concatenate([ref[s, 2 * q, lo:hi, :], ref[s, 2 * q + 1, lo:hi, :]], 1)
            query, d_out = both(pairs, 0, 64), both(d_recv, 0, 64)
            span = pl.ds(pl.multiple_of(q * 256, 256), 256)
            delta = jnp.sum(d_out.astype(f32) * o_full[s, :, span], 0, keepdims=True)
            scores = jnp.dot(kk[...], query, preferred_element_type=f32) * (0.125 * LOG2E)
            key = lax.broadcasted_iota(jnp.int32, scores.shape, 0)
            probs = jnp.where(key < lengths_ref[s], jnp.exp2(scores - lse_ref[s, pl.ds(q, 1), :]), 0.0)
            d_probs = jnp.dot(vv[...], d_out, preferred_element_type=f32)
            d_scores = (probs * (d_probs - delta)).astype(bf16)
            zero = jnp.zeros((64, 256), f32)
            query_rows = jnp.concatenate([query.astype(f32), zero], 0).T.astype(bf16)
            d_rows = jnp.concatenate([zero, d_out.astype(f32)], 0).T.astype(bf16)
            acc[...] += jnp.dot(d_scores, query_rows, preferred_element_type=f32) + jnp.dot(
                probs.astype(bf16), d_rows, preferred_element_type=f32
            )
            d_query = (jnp.dot(kt[...], d_scores, preferred_element_type=f32) * 0.125).astype(bf16)
            for i in range(2):
                part = d_query[:, 128 * i : 128 * i + 128]
                d_send[s, 2 * q + i, 0:64, :] = part
                b_own[0] += part.astype(f32)

        for j in range(16):
            t = acc[pl.ds(j * 128, 128)].T
            d_send[s, j, 64:128, :] = (t[:64] * 0.125).astype(bf16)
            value = t[64:].astype(bf16)
            d_send[s, j, 128:192, :] = value
            b_own[1] += value.astype(f32)
        lane = pl.ds(128 * s, 128)
        for b in FULL_ORDER:
            exchange_out(s, b, d_send.at[s, flip(chip, b)], d_own.at[chip, :, lane], qsend, qrecv)
        d_own[chip, :, lane] = d_send[s, chip]

    for k in range(4):
        rest[0].on_second(k)
    events = [lambda k=k: [r.on_first(k) for r in rest[1:]] for k in range(4)]
    events += [lambda k=k: [r.on_second(k) for r in rest[1:]] for k in range(4)]
    FIRST, SECOND, WAIT = 0, 0, 5
    for b in FULL_ORDER:
        exchange_in(0, b, d_recv.at[0, flip(chip, b)], dsend, drecv)
    back_sequence(0, events[:FIRST])
    for b in FULL_ORDER:
        exchange_in(1, b, d_recv.at[1, flip(chip, b)], dsend, drecv)
    back_sequence(1, events[FIRST : FIRST + SECOND])

    copies.send("bias sib", b_own, b_sib, sib, b_own)
    for event in events[FIRST + SECOND : FIRST + SECOND + WAIT]:
        event()
    for s in range(2):
        lane = pl.ds(128 * s, 128)
        for b in FULL_ORDER:
            exchange_in(s, b, d_own.at[flip(chip, b), :, lane], qsend, qrecv)
        copies.send(("rows", s), d_own.at[:, :, lane], d_sib.at[:, :, lane], sib, d_own.at[:, :, lane])

    copies.arrived("bias sib", b_sib, sib)
    for s in range(2):
        copies.arrived(("rows", s), d_sib.at[:, :, pl.ds(128 * s, 128)], sib)

    for part in range(3):

        @pl.loop(0, 4)
        def _(p):
            total = None
            for i, rows in enumerate((d_own, d_sib)):
                right = rows[pl.ds(4 * p, 4), pl.ds(64 * part, 64)].reshape(256, 256)
                term = nt(rows_t[0, i], right)
                total = term if total is None else total + term
            cols = pl.ds(pl.multiple_of(part * 1024 + p * 256, 256), 256)
            g_qkv[:, :, cols] = total.astype(bf16).reshape(16, 32, 256)

    last.start()
    last.start_direct()

    b_sib[...] = b_sib[...] + b_own[...]
    sender = core == lax.div(chip, 8)
    for i in range(2):
        to = lax.rem(2 * chip + i, 16)
        rows = pl.ds(32 * i, 32)
        c = pltpu.make_async_remote_copy(
            src_ref=b_sib.at[:, rows],
            dst_ref=b_in,
            send_sem=local_sem.at[1 + i],
            recv_sem=local_sem.at[3],
            device_id=(core, to),
            device_id_type=MESH,
        )

        @pl.when(sender & (to != chip))
        def _():
            c.start()

        @pl.when(sender & (to == chip))
        def _():
            b_in[...] = b_sib[:, rows]

    for event in events[FIRST + SECOND + WAIT :]:
        event()
    for i in range(4):
        fetch_qkv(i, i % 2).wait()
        t = None
        for part in range(3):
            w = w_qkv[i % 2, :, :, 1024 * part : 1024 * part + 1024].reshape(256, 1024)
            term = jnp.dot(w, d_own[:, 64 * part : 64 * part + 64].reshape(1024, 256), preferred_element_type=f32)
            t = term if t is None else t + term
        if i < 2:
            fetch_qkv(i + 2, i).start()
        cols = slice(256 * i, 256 * i + 256)
        o_input[:, cols] = d_first[:, cols] + t.T

    for k in range(4):
        last.on_first(k)
    for r in rest:
        r.on_third()
    for k in range(4):
        last.on_second(k)
    last.on_third()
    for i in range(2):
        to = lax.rem(2 * chip + i, 16)

        @pl.when(sender & (to != chip))
        def _():
            pltpu.make_async_remote_copy(
                src_ref=b_sib.at[:, pl.ds(32 * i, 32)],
                dst_ref=b_in,
                send_sem=local_sem.at[1 + i],
                recv_sem=local_sem.at[3],
                device_id=(core, to),
                device_id_type=MESH,
            ).wait_send()

    @pl.when(8 * core + lax.div(chip, 2) != chip)
    def _():
        pltpu.make_async_remote_copy(
            src_ref=b_in, dst_ref=b_in, send_sem=local_sem.at[1], recv_sem=local_sem.at[3], device_id=sib, device_id_type=MESH
        ).wait_recv()

    o_bias[...] = b_in[...]
    for c in sent:
        c.wait_send()
    copies.drain(sib)


def backward_attention(
    lengths, pairs, o_full, lse, rows_t, active_t, cotangent, scaled, spread, vectors,
    active, slope, w_reduce, w_expand, w_out, w_qkv, collective_id,
):
    v, hbm = pl.BlockSpec(memory_space=pltpu.VMEM), pl.BlockSpec(memory_space=pl.ANY)
    f32, bf16 = jnp.float32, jnp.bfloat16
    dma = pltpu.SemaphoreType.DMA
    blocks = [((128, 1024), bf16), ((32, 4096), bf16), ((32, 1024), bf16), ((16, 128), f32), ((32, 3072), bf16)]
    bufs = []
    for block, dtype in blocks:
        bufs += scatter_buffers(block, dtype)
    vmem = lambda shape, dtype=bf16: pltpu.VMEM(shape, dtype)
    return pl.pallas_call(
        bwd_kernel,
        out_shape=[jax.ShapeDtypeStruct((256, 1024), bf16)]
        + [jax.ShapeDtypeStruct(block, f32) for block, _ in blocks]
        + [jax.ShapeDtypeStruct((256, 1024), f32), jax.ShapeDtypeStruct((2, 32, 128), f32)],
        in_specs=[pl.BlockSpec(memory_space=pltpu.SMEM), hbm, hbm, v, hbm, hbm] + [v] * 4 + [hbm] * 6,
        out_specs=[v] * 8,
        scratch_shapes=bufs
        + [
            vmem((16, 128, 1024)),
            vmem((16, 32, 4096)),
            vmem((16, 32, 1024)),
            vmem((16, 16, 128), f32),
            vmem((16, 32, 3072)),
            vmem((2, 8, 32, 3072)),
            vmem((2, 16, 64, 128)),
            vmem((2048, 64)),
            vmem((2048, 64)),
            vmem((64, 2048)),
            vmem((2048, 128), f32),
            vmem((2, 16, 192, 128)),
            vmem((16, 192, 256)),
            vmem((16, 192, 256)),
            vmem((2, 64, 128), f32),
            vmem((2, 64, 128), f32),
            vmem((2, 32, 128), f32),
            vmem((2, 256, 512)),
            vmem((2, 4, 128, 1024)),
            vmem((2, 32, 32, 512)),
            vmem((32, 32, 1024)),
            vmem((8, 256, 512)),
            vmem((8, 256, 512)),
            vmem((256, 1024), f32),
            vmem((256, 1024)),
            vmem((256, 1024)),
            vmem((16, 64, 256)),
            vmem((8, 1024), f32),
            vmem((8, 512), f32),
            vmem((32, 16, 128), f32),
            vmem((16, 16, 128), f32),
            vmem((256, 1024)),
            vmem((256, 1024)),
            vmem((2, 16, 192, 128)),
            vmem((2, 64, 2048), f32),
            vmem((3, 2, 512, 256)),
            vmem((2, 4, 512, 256)),
            dma((144,)),
            dma((144,)),
            dma((7,)),
            dma((32,)),
            dma((32,)),
            dma((32,)),
            dma((32,)),
            dma((8,)),
            dma((8,)),
            dma((2, 3)),
            dma((4,)),
        ],
        compiler_params=pltpu.CompilerParams(
            collective_id=collective_id, has_side_effects=True, vmem_limit_bytes=63 * MIB
        ),
        name="backward_attention",
    )(
        lengths, pairs, o_full, lse, rows_t, active_t, cotangent, scaled, spread, vectors,
        active, slope, w_reduce, w_expand, w_out, w_qkv,
    )


def fast_shards(
    inputs,
    lengths,
    w_query,
    b_query,
    w_key,
    w_value,
    b_value,
    w_out,
    b_out,
    first_gain,
    first_shift,
    w_expand,
    b_expand,
    w_reduce,
    b_reduce,
    second_gain,
    second_shift,
    cotangent,
):
    f32, bf16 = jnp.float32, jnp.bfloat16
    seqs, count, width = inputs.shape
    total = seqs * count
    part = width // 32
    ff = w_expand.shape[1]
    qkv = jnp.concatenate([w_query, w_key, w_value], 1)
    bias = jnp.concatenate([b_query, b_value])[:, None] + jnp.zeros((2 * part, 128), bf16)
    small = [b_out, first_gain, first_shift, b_expand, b_reduce, second_gain, second_shift]
    vec = sum(jnp.pad(b[None, :], ((r, part - 1 - r), (0, 128 - b.shape[0]))) for r, b in enumerate(small))
    flat_rows = inputs.reshape(total, width)
    (
        g_out, g_expand, g_reduce, g_qkv, pairs, o_full, lse, vectors, scaled, spread, active, slope, rows_t, active_t,
    ) = forward_attention(flat_rows, lengths, qkv, bias, vec, w_out, w_expand, w_reduce, 1)
    layer_out, s_reduce, s_expand, s_out, s_vec, s_qkv, input_grad, s_bias = backward_attention(
        lengths, pairs, o_full, lse, rows_t, active_t, cotangent.reshape(total, width), scaled, spread, vectors,
        active, slope, g_reduce, g_expand, g_out, g_qkv, 2,
    )
    s_query, s_key, s_value = (s_qkv[:, width * i : width * (i + 1)] for i in range(3))
    s_bias = jnp.sum(s_bias, -1)
    v = [s_vec[r, : b.shape[0]] for r, b in enumerate(small)]
    return (
        layer_out.reshape(inputs.shape),
        input_grad.reshape(inputs.shape),
        s_query,
        s_bias[0],
        s_key,
        s_value,
        s_bias[1],
        s_out,
        v[0],
        v[1],
        v[2],
        s_expand,
        v[3],
        s_reduce,
        v[4],
        v[5],
        v[6],
    )


def solution(mesh):
    fast = mesh.shape["fsdp"] == 2 and mesh.shape["ctx"] == HEADS
    shards = fast_shards if fast else general_shards
    return jax.shard_map(
        shards,
        mesh=mesh,
        in_specs=(
            P("fsdp", "ctx", None),
            P("fsdp"),
            P(("fsdp", "ctx"), None),
            P(("fsdp", "ctx")),
            P(("fsdp", "ctx"), None),
            P(("fsdp", "ctx"), None),
            P(("fsdp", "ctx")),
            P(("fsdp", "ctx"), None),
            P(("fsdp", "ctx")),
            P(("fsdp", "ctx")),
            P(("fsdp", "ctx")),
            P(("fsdp", "ctx"), None),
            P(("fsdp", "ctx")),
            P(("fsdp", "ctx"), None),
            P(("fsdp", "ctx")),
            P(("fsdp", "ctx")),
            P(("fsdp", "ctx")),
            P("fsdp", "ctx", None),
        ),
        out_specs=(
            P("fsdp", "ctx", None),
            P("fsdp", "ctx", None),
            P(("fsdp", "ctx"), None),
            P(("fsdp", "ctx")),
            P(("fsdp", "ctx"), None),
            P(("fsdp", "ctx"), None),
            P(("fsdp", "ctx")),
            P(("fsdp", "ctx"), None),
            P(("fsdp", "ctx")),
            P(("fsdp", "ctx")),
            P(("fsdp", "ctx")),
            P(("fsdp", "ctx"), None),
            P(("fsdp", "ctx")),
            P(("fsdp", "ctx"), None),
            P(("fsdp", "ctx")),
            P(("fsdp", "ctx")),
            P(("fsdp", "ctx")),
        ),
        check_vma=False,
    )
```
